32 devices in a mesh: parts: 2 (over y), patch: 4 (over z), level: 2 (over x), sub: 2 (over core).
Axes of the slice: x: 2, y: 2, z: 4, core: 2. Of those that a mesh axis runs over, the one named last changes fastest.
Arguments:
- adjoint_height: float32 [4, 1024, 1024], P(('parts', 'level'), ('patch', 'sub')), parts along dimension 0, may hold values from -6 to 6
- adjoint_momenta: float32 [2, 4, 1024, 1024], P(None, ('parts', 'level'), ('patch', 'sub')), parts along dimension 1, may hold values from -6 to 6
- depth: float32 [2, 1024, 1024], P('level', ('patch', 'sub')), may hold values from 0.2 to 1
- wet_mask: int32 [2, 1024, 1024], P('level', ('patch', 'sub')), may hold values 0 or 1
- adjacency: int32 [2, 4, 4], P('level'), may hold values from -1 to 3, as said below
- nest_gain: float32 [2, 8192], P(None, ('patch', 'sub')), may hold values from 0.75 to 1
- nest_index: int32 [2, 8192], P(None, ('patch', 'sub')), may hold values from 0 to 1023, as said below
Outputs:
- height_out: float32 [4, 1024, 1024], P(('parts', 'level'), ('patch', 'sub')), parts along dimension 0
- momenta_out: float32 [2, 4, 1024, 1024], P(None, ('parts', 'level'), ('patch', 'sub')), parts along dimension 1
The draws below stay inside these ranges and needn't reach their ends.
There are 2 independent parts, one for each index of `parts`. The reference program is written for one: setup_inputs(seed, part) draws one part's arguments, and reference() takes and returns one part's arrays. A program takes and returns all parts, laid end to end along the dimension named above; an argument that names none is the same for every part. Nothing has to cross between parts.
Inputs may be any that keep to these rules, and one draw needn't show every extreme that they name: `adjacency`: the patches of a level sit on a grid of cells in an order drawn from the seed; each row of a patch lists its grid neighbours, -1 at the grid's edge, and neighbour links are symmetric. `nest_index`: entries index a cell of the same half patch's strip, 1024 cells long.
All inputs are finite; a program needn't handle non-finite values. No bound on the sum of `wet_mask` on one device may be relied on, other than what follows from the above.
Results may differ from the reference program's by a relative error of at most 0.00002.
Values sent between devices are 32-bit elements; how exact they have to be, the bound alone decides.
No kernel may reach another device: no remote copies, remote signals or barrier semaphores. Data moves between devices by JAX's collectives and lax.ppermute only.
A program may use at most 64 MiB of HBM per device.

```python
import math
import jax
import jax.numpy as jnp

BR = 128
COLS = 1024
STEPS = 2
LEVELS = 2
PATCHES = 4
ROWS = 256
TOTAL_ROWS = 1024
SEGS = 8


def level_links(key):
    gcols = 1 << (PATCHES.bit_length() - 1) // 2
    grows = PATCHES // gcols
    order = jax.random.permutation(key, PATCHES).astype(jnp.int32)
    places = jnp.arange(PATCHES, dtype=jnp.int32)
    row_of = places // gcols
    col_of = places % gcols
    none = jnp.full((PATCHES,), -1, jnp.int32)
    north_place = jnp.where(row_of > 0, places - gcols, none)
    south_place = jnp.where(row_of < grows - 1, places + gcols, none)
    west_place = jnp.where(col_of > 0, places - 1, none)
    east_place = jnp.where(col_of < gcols - 1, places + 1, none)
    stacked = jnp.stack([north_place, south_place, west_place, east_place], axis=1)
    named = jnp.where(stacked >= 0, order[jnp.clip(stacked, 0, PATCHES - 1)], -1)
    return jnp.zeros((PATCHES, 4), jnp.int32).at[order].set(named)


def draw_adjacency(key, part):
    keys = jax.random.split(jax.random.fold_in(key, 11), LEVELS)
    return jax.vmap(level_links)(keys)


def draw_nest_index(key, part):
    first, second = jax.random.split(jax.random.fold_in(key, 23))
    offsets = jax.random.randint(first, (LEVELS, SEGS, 1), 0, COLS)
    jitter = jax.random.randint(second, (LEVELS, SEGS, COLS), 0, 3)
    cells = jnp.arange(COLS, dtype=jnp.int32)[None, None, :]
    table = (3 * cells + offsets + jitter) % COLS
    return table.reshape(LEVELS, SEGS * COLS).astype(jnp.int32)


def set_ends(result, rng, low, largest):
    place = [jax.random.randint(jax.random.fold_in(rng, axis), (), 0, length) for axis, length in enumerate(result.shape)]
    longest = result.shape.index(max(result.shape))
    beside = place[:longest] + [(place[longest] + 1) % result.shape[longest]] + place[longest + 1:]
    return result.at[tuple(place)].set(low).at[tuple(beside)].set(largest)


def block_levels(rng, shape, shards, least, high):
    loudness = 1.0
    for dim, shards_of in shards:
        heights = jax.random.uniform(jax.random.fold_in(jax.random.fold_in(rng, 6), dim), (shards_of,), jnp.float32, least / len(shards), high / len(shards))
        loudness = loudness * jnp.repeat(jnp.exp(heights), shape[dim] // shards_of).reshape((-1,) + (1,) * (len(shape) - 1 - dim))
    return loudness


def centred(rng, extent, spread, most, cuts=(), kind=jnp.bfloat16):
    factor_of = block_levels(rng, extent, cuts, -0.22, 0.18) if cuts else 1.0
    entries = jax.random.normal(rng, extent, jnp.float32) * spread * factor_of
    return jnp.minimum(jnp.maximum(entries, -most), most).astype(kind)


def setup_inputs(seed: int = 0, part: int = 0) -> dict:
    arg_keys = jax.random.split(jax.random.key(seed), 8)
    part_splits = jax.random.split(jax.random.fold_in(arg_keys[7], part), 8)
    return {
        "adjoint_height": centred(part_splits[0], (LEVELS, TOTAL_ROWS, COLS), 1.0, 6.0, ((0, 2), (1, 8)), jnp.float32),
        "adjoint_momenta": centred(part_splits[1], (2, LEVELS, TOTAL_ROWS, COLS), 1.0, 6.0, ((1, 2), (2, 8)), jnp.float32),
        "depth": jnp.clip(0.2 + 0.8 * jax.random.uniform(arg_keys[2], (LEVELS, TOTAL_ROWS, COLS), jnp.float32) ** block_levels(arg_keys[2], (LEVELS, TOTAL_ROWS, COLS), ((0, 2), (1, 8)), -0.2, 0.2), 0.2, 1.0),
        "wet_mask": set_ends((jax.random.randint(arg_keys[3], (LEVELS, TOTAL_ROWS, COLS), 0, 4) < 3).astype(jnp.int32), jax.random.fold_in(arg_keys[3], 1), 0, 1),
        "adjacency": draw_adjacency(jax.random.fold_in(arg_keys[7], 71), part),
        "nest_gain": jnp.clip(jnp.exp(math.log(1.0) - 0.2876821 * jax.random.uniform(arg_keys[5], (LEVELS, SEGS * COLS), jnp.float32) ** block_levels(arg_keys[5], (LEVELS, SEGS * COLS), ((1, 8),), -0.2, 0.2)), 0.75, 1.0),
        "nest_index": draw_nest_index(jax.random.fold_in(arg_keys[7], 71), part),
    }


courant = 0.45


def neighbour(field, links, level_ids):
    picked = field[level_ids, jnp.clip(links, 0, PATCHES - 1)]
    return picked * (links >= 0).astype(jnp.float32)[:, :, None, None]


def reference(adjoint_height, adjoint_momenta, depth, wet_mask, adjacency, nest_gain, nest_index):
    shape4 = (LEVELS, PATCHES, ROWS, COLS)
    eta = adjoint_height.reshape(shape4)
    mom_row = adjoint_momenta[0].reshape(shape4)
    mom_col = adjoint_momenta[1].reshape(shape4)
    height = depth.reshape(shape4)
    wet = wet_mask.astype(jnp.float32).reshape(shape4)
    north = adjacency[:, :, 0]
    south = adjacency[:, :, 1]
    west = adjacency[:, :, 2]
    east = adjacency[:, :, 3]
    level_ids = jnp.arange(LEVELS)[:, None]
    gains = nest_gain.reshape(LEVELS, SEGS, COLS)
    tables = nest_index.reshape(LEVELS, SEGS, COLS)
    for step in range(STEPS):
        halves = eta.reshape(LEVELS, SEGS, BR, COLS)
        strips = halves[:, :, 0, :]
        flux = jnp.zeros((SEGS, COLS), jnp.float32)
        inflows = []
        for lev in range(LEVELS - 1, -1, -1):
            inflow = gains[lev] * jnp.take_along_axis(flux, tables[lev], axis=1)
            flux = inflow + strips[lev]
            inflows.insert(0, inflow)
        halves = halves.at[:, :, 0, :].add(jnp.stack(inflows))
        eta = halves.reshape(shape4)
        east_eta = jnp.concatenate([eta[..., 1:], neighbour(eta, east, level_ids)[..., :1]], axis=3)
        south_eta = jnp.concatenate([eta[:, :, 1:, :], neighbour(eta, south, level_ids)[:, :, :1, :]], axis=2)
        mom_row = wet * (mom_row - courant * (east_eta - eta))
        mom_col = wet * (mom_col - courant * (south_eta - eta))
        west_row = jnp.concatenate([neighbour(mom_row, west, level_ids)[..., -1:], mom_row[..., :-1]], axis=3)
        north_col = jnp.concatenate([neighbour(mom_col, north, level_ids)[:, :, -1:, :], mom_col[:, :, :-1, :]], axis=2)
        eta = wet * (eta - courant * height * ((mom_row - west_row) + (mom_col - north_col)))
    flat = (LEVELS, TOTAL_ROWS, COLS)
    return eta.reshape(flat), jnp.stack([mom_row.reshape(flat), mom_col.reshape(flat)])
```

```python
import jax
import jax.numpy as jnp
from jax import lax
from jax.sharding import PartitionSpec as P

STEPS = 2


courant = 0.45


def passed_along(value, axis, steps):
    count = lax.axis_size(axis)
    initial, last = (max(0, -steps), min(count, count - steps))
    return lax.ppermute(value, axis, [(source, source + steps) for source in range(initial, last)])


def from_all(value, axes):
    count = lax.axis_size(axes)
    others = [lax.ppermute(value, axes, [(source, source ^ turn) for source in range(count)]) for turn in range(1, count)]
    return jnp.stack([value] + others)


def pick_row(table, index):
    return lax.dynamic_index_in_dim(table, index, 0, keepdims=False)


def body(adjoint_height, adjoint_momenta, depth, wet_mask, adjacency, nest_gain, nest_index):
    eta = adjoint_height[0]
    mom_row = adjoint_momenta[0, 0]
    mom_col = adjoint_momenta[1, 0]
    height = depth[0]
    wet = wet_mask[0].astype(jnp.float32)
    level = lax.axis_index("level")
    patch = lax.axis_index("patch")
    half = lax.axis_index("sub")
    levels = lax.axis_size("level")
    subs = lax.axis_size("sub")
    own = patch * subs + half
    cols = eta.shape[1]
    links = pick_row(adjacency[0], patch)
    north = links[0]
    south = links[1]
    west = links[2]
    east = links[3]
    has_north = (north >= 0).astype(jnp.float32)
    has_south = (south >= 0).astype(jnp.float32)
    has_west = (west >= 0).astype(jnp.float32)
    has_east = (east >= 0).astype(jnp.float32)
    own_gain = pick_row(nest_gain, level)
    own_table = pick_row(nest_index, level)
    for step in range(STEPS):
        strip = eta[0]
        flux = strip
        inflow = jnp.zeros_like(strip)
        for turn in range(levels - 1):
            received = passed_along(flux, "level", -1)
            inflow = own_gain * jnp.take(received, own_table)
            flux = inflow + strip
        eta = eta.at[0].add(inflow)
        first_col = eta[:, 0]
        first_row = eta[0, :]
        edges = from_all(jnp.concatenate([first_row, first_col]), ("patch", "sub"))
        east_col = pick_row(edges, own ^ (jnp.maximum(east, 0) * subs + half))[cols:] * has_east
        across = jnp.where(half == subs - 1, jnp.maximum(south, 0) * subs, own + 1)
        keep = jnp.where(half == subs - 1, has_south, 1.0)
        south_row = pick_row(edges, own ^ across)[:cols] * keep
        east_eta = jnp.concatenate([eta[:, 1:], east_col[:, None]], axis=1)
        south_eta = jnp.concatenate([eta[1:], south_row[None]], axis=0)
        mom_row = wet * (mom_row - courant * (east_eta - eta))
        mom_col = wet * (mom_col - courant * (south_eta - eta))
        last_col = mom_row[:, -1]
        last_row = mom_col[-1, :]
        edges = from_all(jnp.concatenate([last_row, last_col]), ("patch", "sub"))
        west_col = pick_row(edges, own ^ (jnp.maximum(west, 0) * subs + half))[cols:] * has_west
        across = jnp.where(half == 0, jnp.maximum(north, 0) * subs + subs - 1, own - 1)
        keep = jnp.where(half == 0, has_north, 1.0)
        north_row = pick_row(edges, own ^ across)[:cols] * keep
        west_row = jnp.concatenate([west_col[:, None], mom_row[:, :-1]], axis=1)
        north_col = jnp.concatenate([north_row[None], mom_col[:-1]], axis=0)
        eta = wet * (eta - courant * height * (mom_row - west_row + (mom_col - north_col)))
    return (eta[None], jnp.stack([mom_row, mom_col])[:, None])


def solution(mesh):
    in_specs = (
        P(("parts", "level"), ("patch", "sub"), None),
        P(None, ("parts", "level"), ("patch", "sub"), None),
        P("level", ("patch", "sub"), None),
        P("level", ("patch", "sub"), None),
        P("level", None, None),
        P(None, ("patch", "sub")),
        P(None, ("patch", "sub")),
    )
    out_specs = (
        P(("parts", "level"), ("patch", "sub"), None),
        P(None, ("parts", "level"), ("patch", "sub"), None),
    )
    return jax.shard_map(body, mesh=mesh, in_specs=in_specs, out_specs=out_specs, check_vma=False)
```

```python
import jax
import jax.numpy as jnp
from jax import lax
from jax.sharding import PartitionSpec as P

STEPS = 2


courant = 0.45


def passed_along(value, axis, steps):
    count = lax.axis_size(axis)
    initial, last = (max(0, -steps), min(count, count - steps))
    return lax.ppermute(value, axis, [(source, source + steps) for source in range(initial, last)])


def from_all(value, axes):
    copies = jnp.broadcast_to(value, (lax.axis_size(axes),) + value.shape)
    return lax.all_to_all(copies, axes, 0, 0, tiled=True)


def pick_row(table, index):
    return lax.dynamic_index_in_dim(table, index, 0, keepdims=False)


def body(adjoint_height, adjoint_momenta, depth, wet_mask, adjacency, nest_gain, nest_index):
    eta = adjoint_height[0]
    mom_row = adjoint_momenta[0, 0]
    mom_col = adjoint_momenta[1, 0]
    height = depth[0]
    wet = wet_mask[0].astype(jnp.float32)
    level = lax.axis_index("level")
    patch = lax.axis_index("patch")
    half = lax.axis_index("sub")
    levels = lax.axis_size("level")
    subs = lax.axis_size("sub")
    own = patch * subs + half
    cols = eta.shape[1]
    links = pick_row(adjacency[0], patch)
    north = links[0]
    south = links[1]
    west = links[2]
    east = links[3]
    has_north = (north >= 0).astype(jnp.float32)
    has_south = (south >= 0).astype(jnp.float32)
    has_west = (west >= 0).astype(jnp.float32)
    has_east = (east >= 0).astype(jnp.float32)
    own_gain = pick_row(nest_gain, level)
    own_table = pick_row(nest_index, level)
    for step in range(STEPS):
        strip = eta[0]
        flux = strip
        inflow = jnp.zeros_like(strip)
        for turn in range(levels - 1):
            received = passed_along(flux, "level", -1)
            inflow = own_gain * jnp.take(received, own_table)
            flux = inflow + strip
        eta = eta.at[0].add(inflow)
        first_col = eta[:, 0]
        first_row = eta[0, :]
        edges = from_all(jnp.concatenate([first_row, first_col]), ("patch", "sub"))
        east_col = pick_row(edges, jnp.maximum(east, 0) * subs + half)[cols:] * has_east
        across = jnp.where(half == subs - 1, jnp.maximum(south, 0) * subs, own + 1)
        keep = jnp.where(half == subs - 1, has_south, 1.0)
        south_row = pick_row(edges, across)[:cols] * keep
        east_eta = jnp.concatenate([eta[:, 1:], east_col[:, None]], axis=1)
        south_eta = jnp.concatenate([eta[1:], south_row[None]], axis=0)
        mom_row = wet * (mom_row - courant * (east_eta - eta))
        mom_col = wet * (mom_col - courant * (south_eta - eta))
        last_col = mom_row[:, -1]
        last_row = mom_col[-1, :]
        edges = from_all(jnp.concatenate([last_row, last_col]), ("patch", "sub"))
        west_col = pick_row(edges, jnp.maximum(west, 0) * subs + half)[cols:] * has_west
        across = jnp.where(half == 0, jnp.maximum(north, 0) * subs + subs - 1, own - 1)
        keep = jnp.where(half == 0, has_north, 1.0)
        north_row = pick_row(edges, across)[:cols] * keep
        west_row = jnp.concatenate([west_col[:, None], mom_row[:, :-1]], axis=1)
        north_col = jnp.concatenate([north_row[None], mom_col[:-1]], axis=0)
        eta = wet * (eta - courant * height * (mom_row - west_row + (mom_col - north_col)))
    return (eta[None], jnp.stack([mom_row, mom_col])[:, None])


def solution(mesh):
    in_specs = (
        P(("parts", "level"), ("patch", "sub"), None),
        P(None, ("parts", "level"), ("patch", "sub"), None),
        P("level", ("patch", "sub"), None),
        P("level", ("patch", "sub"), None),
        P("level", None, None),
        P(None, ("patch", "sub")),
        P(None, ("patch", "sub")),
    )
    out_specs = (
        P(("parts", "level"), ("patch", "sub"), None),
        P(None, ("parts", "level"), ("patch", "sub"), None),
    )
    return jax.shard_map(body, mesh=mesh, in_specs=in_specs, out_specs=out_specs, check_vma=False)
```

```python
import functools

import jax
import jax.numpy as jnp
from jax import lax
from jax.experimental import pallas as pl
from jax.experimental.pallas import tpu as pltpu
from jax.sharding import PartitionSpec as P

STEPS = 2
LANES = 128
TILE = 8
VMEM_LIMIT = 48 * 1024 * 1024

courant = 0.45

STRIP_SUM, STRIP, STRIP_DEPTH, GAIN, INDEX, EDGE_FLOW, EDGE_DEPTH, EDGE_SUM = range(8)
(FIRST_ETA, SECOND_ETA, FIRST_ROW, FIRST_COL, FIRST_DEPTH, NEXT_ETA, LAST_ETA, NEXT_ROW,
 LAST_ROW, LAST_COL, NEXT_DEPTH, LAST_DEPTH) = range(12)


def iota(shape, axis):
    return lax.broadcasted_iota(jnp.int32, shape, axis)


def rolled(value, shift, axis):
    return pltpu.roll(value, shift % value.shape[axis], axis)


def wet(depth):
    return (depth > 0).astype(jnp.float32)


def pack_kernel(*refs):
    (eta_top, eta_low, eta_left, eta_right, row_top, row_low, row_left, row_right,
     col_top, col_low, col_left, col_right, depth_top, depth_low, depth_left, depth_right,
     wet_top, wet_low, wet_left, wet_right, gain_ref, index_ref, out_ref) = refs
    count, _, width = out_ref.shape
    cols = width - 2 * LANES
    level = lax.axis_index("level")
    lane = iota((TILE, cols), 1)

    def loaded(eta, row, col, depth, mask):
        mask = mask[0].astype(jnp.float32)
        return eta[0], row[0, 0], col[0, 0], mask * depth[0], mask

    eta, row, col, depth, mask = loaded(eta_top, row_top, col_top, depth_top, wet_top)
    east = jnp.where(lane == cols - 1, 0.0, rolled(eta, -1, 1))
    row = mask * (row - courant * (east - eta))
    west = jnp.where(lane == 0, 0.0, rolled(row, 1, 1))
    col = mask * (col - courant * (rolled(eta, -1, 0) - eta))
    strip_sum = mask * eta - courant * depth * (row - west + col)
    out_ref[0, STRIP_SUM:STRIP_SUM + 1, :cols] = strip_sum[:1]
    out_ref[0, STRIP:STRIP + 1, :cols] = eta[:1]
    out_ref[0, STRIP_DEPTH:STRIP_DEPTH + 1, :cols] = depth[:1]
    out_ref[0, GAIN:GAIN + 1, :cols] = gain_ref[pl.ds(level, 1), :]
    out_ref[0, INDEX:INDEX + 1, :cols] = index_ref[pl.ds(level, 1), :].astype(jnp.float32)

    eta, row, col, depth, mask = loaded(eta_low, row_low, col_low, depth_low, wet_low)
    east = jnp.where(lane == cols - 1, 0.0, rolled(eta, -1, 1))
    row = mask * (row - courant * (east - eta))
    west = jnp.where(lane == 0, 0.0, rolled(row, 1, 1))
    flow = mask * (col + courant * eta)
    above = rolled(flow - courant * mask * rolled(eta, -1, 0), 1, 0)
    edge_sum = mask * eta - courant * depth * (row - west - above)
    out_ref[0, EDGE_FLOW:EDGE_FLOW + 1, :cols] = flow[TILE - 1:]
    out_ref[0, EDGE_DEPTH:EDGE_DEPTH + 1, :cols] = depth[TILE - 1:]
    out_ref[0, EDGE_SUM:EDGE_SUM + 1, :cols] = edge_sum[TILE - 1:]

    lane = iota(eta_left.shape[1:], 1)
    columns = jnp.zeros(eta_left.shape[1:], jnp.float32)
    depth_first = depth_left[0] * wet_left[0].astype(jnp.float32)
    depth_last = depth_right[0] * wet_right[0].astype(jnp.float32)
    for place, value, at in (
        (FIRST_ETA, eta_left[0], 0), (SECOND_ETA, eta_left[0], 1), (FIRST_ROW, row_left[0, 0], 0),
        (FIRST_COL, col_left[0, 0], 0), (FIRST_DEPTH, depth_first, 0),
        (NEXT_ETA, eta_right[0], LANES - 2), (LAST_ETA, eta_right[0], LANES - 1),
        (NEXT_ROW, row_right[0, 0], LANES - 2), (LAST_ROW, row_right[0, 0], LANES - 1),
        (LAST_COL, col_right[0, 0], LANES - 1),
        (NEXT_DEPTH, depth_last, LANES - 2), (LAST_DEPTH, depth_last, LANES - 1),
    ):
        moved = value if place == at else rolled(value, place - at, 1)
        columns = jnp.where(lane == place, moved, columns)
    columns = columns.T
    out_ref[0, :, cols:cols + LANES] = columns[:TILE]
    out_ref[0, :, cols + LANES:] = columns[TILE:2 * TILE]
    packet = out_ref[0]
    for turn in range(1, count):
        out_ref[turn] = packet


class Links:
    def __init__(self, links_ref, subs):
        self.links_ref, self.subs = links_ref, subs

    def across(self, segment, way):
        patch = self.links_ref[0, segment // self.subs, way]
        return jnp.maximum(patch, 0), jnp.where(patch >= 0, 1.0, 0.0)

    def north(self, segment):
        patch, there = self.across(segment, 0)
        inside = segment % self.subs > 0
        return jnp.where(inside, segment - 1, patch * self.subs + self.subs - 1), jnp.where(inside, 1.0, there)

    def south(self, segment):
        patch, there = self.across(segment, 1)
        inside = segment % self.subs < self.subs - 1
        return jnp.where(inside, segment + 1, patch * self.subs), jnp.where(inside, 1.0, there)

    def west(self, segment):
        patch, there = self.across(segment, 2)
        return patch * self.subs + segment % self.subs, there

    def east(self, segment):
        patch, there = self.across(segment, 3)
        return patch * self.subs + segment % self.subs, there


def nested(table, flux, index):
    segments, cols = index.shape
    del table
    rows = []
    for low in range(0, segments, TILE):
        tiles = []
        for left in range(0, cols, LANES):
            at = index[low:low + TILE, left:left + LANES]
            lane, tile = at % LANES, at // LANES
            taken = jnp.zeros(at.shape, jnp.float32)
            for source in range(cols // LANES):
                values = flux[low:low + TILE, source * LANES:(source + 1) * LANES]
                found = jnp.take_along_axis(values, lane, axis=1, mode="promise_in_bounds")
                taken = jnp.where(tile == source, found, taken)
            tiles.append(taken)
        rows.append(jnp.concatenate(tiles, axis=1))
    return jnp.concatenate(rows, axis=0) if len(rows) > 1 else rows[0]


def strips_of(links, got_ref, finer, picked_ref, narrow_ref):
    count, _, width = got_ref.shape
    cols = width - 2 * LANES
    lane = iota((count, LANES), 1)
    strip, depth = got_ref[:, STRIP, :cols], got_ref[:, STRIP_DEPTH, :cols]
    mask = wet(depth)
    if finer is None:
        inflow = jnp.zeros_like(strip)
    else:
        gain = got_ref[:, GAIN, :cols]
        index = got_ref[:, INDEX, :cols].astype(jnp.int32)
        inflow = gain * nested(None, finer[0], index)
    eta = strip + inflow

    narrow_ref[...] = eta[:, :LANES]
    for segment in range(count):
        east, there = links.east(segment)
        picked_ref[segment:segment + 1, :LANES] = narrow_ref[pl.ds(east, 1), :] * there
    east_eta = rolled(picked_ref[:, :LANES], -1, 1)
    after = rolled(inflow, -1, 1)
    after = jnp.concatenate(
        [after[:, :-LANES], jnp.where(lane == LANES - 1, east_eta, after[:, -LANES:])], axis=1)
    more_row = courant * mask * (inflow - after)

    last_eta = got_ref[:, LAST_ETA % TILE, cols:cols + LANES]
    last_row = got_ref[:, LAST_ROW % TILE, cols + LANES:]
    first_of_last = rolled(last_row + courant * last_eta, -1, 1)
    narrow_ref[...] = mask[:, -LANES:] * first_of_last + more_row[:, -LANES:]
    for segment in range(count):
        west, there = links.west(segment)
        picked_ref[segment:segment + 1, :LANES] = narrow_ref[pl.ds(west, 1), :] * there
    west_row = rolled(picked_ref[:, :LANES], 1, 1)
    before = rolled(more_row, 1, 1)
    before = jnp.concatenate([jnp.where(lane == 0, west_row, before[:, :LANES]), before[:, LANES:]], axis=1)

    for segment in range(count):
        north, there = links.north(segment)
        picked_ref[segment:segment + 1, :] = got_ref[pl.ds(north, 1), EDGE_FLOW, :cols] * there
    flow = picked_ref[...]
    for segment in range(count):
        north, there = links.north(segment)
        picked_ref[segment:segment + 1, :] = got_ref[pl.ds(north, 1), EDGE_DEPTH, :cols] * there
    north_col = flow - courant * wet(picked_ref[...]) * eta
    later = (got_ref[:, STRIP_SUM, :cols] + mask * inflow
             - courant * depth * (more_row - before + courant * mask * inflow - north_col))
    if finer is None:
        return inflow, eta, inflow, later
    later_inflow = gain * nested(None, finer[1], index)
    return inflow, eta, later_inflow, later + later_inflow


def strips_kernel(subs, *refs):
    links_ref, got_ref = refs[:2]
    out_ref, picked_ref, narrow_ref = refs[-3:]
    finer = (refs[2][0], refs[2][1]) if len(refs) == 6 else None
    _, eta, _, later = strips_of(Links(links_ref, subs), got_ref, finer, picked_ref, narrow_ref)
    out_ref[0] = eta
    out_ref[1] = later


def final_kernel(subs, links_ref, got_ref, finer_ref, eta_ref, momenta_ref, depth_ref, wet_ref,
                 eta_out, momenta_out, picked_ref, narrow_ref, strips_ref, eta_pad, col_pad):
    count, _, width = got_ref.shape
    rows, cols = eta_ref.shape[1:]
    links = Links(links_ref, subs)
    for place, value in enumerate(
            strips_of(links, got_ref, (finer_ref[0], finer_ref[1]), picked_ref, narrow_ref)):
        for segment in range(count):
            strips_ref[place * count + segment] = value[segment:segment + 1]
    own = lax.axis_index("patch") * subs + lax.axis_index("sub")
    lane = iota((1, LANES), 1)
    first, last = lane == 0, lane == LANES - 1

    def strip_tile(which, segment, left):
        return strips_ref[which * count + segment, :, left:left + LANES]

    def strip_row(which, segment):
        return strips_ref[which * count + segment]

    def packet_row(segment, row, left=0, size=cols):
        return got_ref[pl.ds(segment, 1), row, left:left + size]

    def packet_column(segment, column):
        left = cols + column // TILE * LANES
        return got_ref[pl.ds(segment, 1), column % TILE, left:left + LANES]

    def edge_col(segment, there, eta, left, turned):
        north, beyond = links.north(segment)
        flow = packet_row(north, EDGE_FLOW, left, LANES)
        mask = wet(packet_row(north, EDGE_DEPTH, left, LANES))
        return beyond * (rolled(flow, turned, 1) - courant * rolled(mask, turned, 1) * eta)

    end = cols - LANES
    west, there = links.west(own)
    eta = packet_column(west, LAST_ETA) + jnp.where(first, rolled(strip_tile(0, west, end), 1, 1), 0.0)
    next_eta = packet_column(west, NEXT_ETA) + jnp.where(first, rolled(strip_tile(0, west, end), 2, 1), 0.0)
    depth = packet_column(west, LAST_DEPTH) * there
    mask = wet(depth)
    next_row = wet(packet_column(west, NEXT_DEPTH)) * (
        packet_column(west, NEXT_ROW) - courant * (eta - next_eta))
    below, beyond = links.south(west)
    south_eta = jnp.where(last, strip_tile(1, below, end) * beyond, rolled(eta, -1, 1))
    col = mask * (packet_column(west, LAST_COL) - courant * (south_eta - eta))
    north_col = jnp.where(first, edge_col(west, there, eta, end, 1), rolled(col, 1, 1))
    west_flow = mask * (packet_column(west, LAST_ROW) + courant * eta)
    west_sum = (mask * eta - courant * depth * (col - next_row - north_col)
                + jnp.where(first, rolled(strip_tile(2, west, end), 1, 1), 0.0))
    west_depth = depth
    east, there = links.east(own)
    eta = there * (packet_column(east, FIRST_ETA) + jnp.where(first, strip_tile(0, east, 0), 0.0))
    second_eta = packet_column(east, SECOND_ETA) + jnp.where(first, rolled(strip_tile(0, east, 0), -1, 1), 0.0)
    depth = packet_column(east, FIRST_DEPTH) * there
    mask = wet(depth)
    row = mask * (packet_column(east, FIRST_ROW) - courant * (second_eta - eta))
    below, beyond = links.south(east)
    south_eta = jnp.where(last, rolled(strip_tile(1, below, 0), -1, 1) * beyond, rolled(eta, -1, 1))
    col = mask * (packet_column(east, FIRST_COL) - courant * (south_eta - eta))
    north_col = jnp.where(first, edge_col(east, there, eta, 0, 0), rolled(col, 1, 1))
    east_sum = (mask * eta - courant * depth * (row + col - north_col)
                + there * jnp.where(first, strip_tile(2, east, 0), 0.0))
    sides = jnp.concatenate(
        [west_flow, west_sum, west_depth, eta, east_sum, depth, jnp.zeros((2, LANES), jnp.float32)], axis=0).T
    west_flow, west_sum, west_depth, east_eta, east_sum, east_depth = [
        sides[:, place:place + 1] for place in range(6)]
    west_wet = wet(west_depth)
    north, there = links.north(own)
    north_depth = packet_row(north, EDGE_DEPTH) * there
    north_wet = wet(north_depth)
    north_col = packet_row(north, EDGE_FLOW) * there - courant * north_wet * strip_row(1, own)
    north_east, beyond = links.east(north)
    right_eta = beyond * packet_column(north_east, FIRST_ETA)
    north_west, beyond = links.west(north)
    left_row = beyond * wet(packet_column(north_west, LAST_DEPTH)) * (
        packet_column(north_west, LAST_ROW)
        - courant * (packet_column(north, FIRST_ETA) - packet_column(north_west, LAST_ETA)))
    nothing = jnp.zeros((1, cols - LANES), jnp.float32)
    corners = (jnp.concatenate([jnp.where(first, rolled(left_row, 1, 1), 0.0), nothing], axis=1)
               + jnp.concatenate([nothing, jnp.where(last, courant * right_eta, 0.0)], axis=1))
    north_eta = packet_row(north, EDGE_SUM) + courant * north_depth * (corners - north_col)
    south, there_south = links.south(own)

    lanes = iota((TILE, cols), 1)
    eta_pad[TILE:TILE + rows] = eta_ref[0]
    eta_pad[TILE:TILE + 1] = strip_row(1, own)
    eta_pad[TILE + rows:TILE + rows + 1] = strip_row(1, south) * there_south
    col_pad[TILE - 1:TILE] = north_col

    def step(number, east_of, west_of, last_step):
        for low in range(0, rows, TILE):
            chunk = slice(low, low + TILE)
            eta = eta_pad[TILE + low:2 * TILE + low]
            mask = wet_ref[0, chunk].astype(jnp.float32)
            depth = depth_ref[0, chunk]
            if number == 0:
                row, col = momenta_ref[0, 0, chunk], momenta_ref[1, 0, chunk]
            else:
                row, col = momenta_out[0, 0, chunk], col_pad[TILE + low:2 * TILE + low]
            east = jnp.where(lanes == cols - 1, east_of(low), rolled(eta, -1, 1))
            south = eta_pad[TILE + low + 1:2 * TILE + low + 1]
            row = mask * (row - courant * (east - eta))
            col = mask * (col - courant * (south - eta))
            momenta_out[0, 0, chunk] = row
            col_pad[TILE + low:2 * TILE + low] = col
            if last_step:
                momenta_out[1, 0, chunk] = col
            west = jnp.where(lanes == 0, west_of(low, eta), rolled(row, 1, 1))
            north = col_pad[TILE + low - 1:2 * TILE + low - 1]
            eta = mask * (eta - courant * depth * (row - west + (col - north)))
            if last_step:
                eta_out[0, chunk] = eta
            else:
                eta_pad[TILE + low:2 * TILE + low] = eta

    first_west = []

    def west_before(low, eta):
        value = west_flow[low:low + TILE] - courant * west_wet[low:low + TILE] * eta[:, :1]
        first_west.append(value)
        return value

    step(0, lambda low: east_eta[low:low + TILE], west_before, False)

    eta_pad[TILE:TILE + 1] += strip_row(2, own)
    eta_pad[TILE + rows:TILE + rows + 1] = strip_row(3, south) * there_south
    col_pad[TILE - 1:TILE] = north_col_after(north_col, north_wet, north_eta, eta_pad[TILE:TILE + 1])

    def east_after(low):
        chunk = slice(low, low + TILE)
        return east_sum[chunk] + courant * east_depth[chunk] * momenta_out[0, 0, chunk, cols - 1:]

    def west_after(low, eta):
        chunk = slice(low, low + TILE)
        row = first_west[low // TILE]
        west_eta = west_sum[chunk] - courant * west_depth[chunk] * row
        return west_wet[chunk] * (row - courant * (eta[:, :1] - west_eta))

    step(1, east_after, west_after, True)


def north_col_after(col, mask, eta, south_eta):
    return mask * (col - courant * (south_eta - eta))


def body(adjoint_height, adjoint_momenta, depth, wet_mask, adjacency, nest_gain, nest_index):
    rows, cols = adjoint_height.shape[1:]
    levels = lax.axis_size("level")
    subs = lax.axis_size("sub")
    count = lax.axis_size("patch") * subs
    params = pltpu.CompilerParams(vmem_limit_bytes=VMEM_LIMIT)
    whole = pl.BlockSpec(memory_space=pltpu.VMEM)
    scalars = pl.BlockSpec(memory_space=pltpu.SMEM)
    low, right = rows // TILE - 1, cols // LANES - 1

    def edges(leading):
        none = (0,) * len(leading)
        return [
            pl.BlockSpec(leading + shape, functools.partial(lambda place, step: none + place, place))
            for shape, place in (
                ((TILE, cols), (0, 0)), ((TILE, cols), (low, 0)),
                ((rows, LANES), (0, 0)), ((rows, LANES), (0, right)))
        ]

    def momentum(which):
        return [
            pl.BlockSpec((1, 1) + shape, functools.partial(lambda place, step: (which, 0) + place, place))
            for shape, place in (
                ((TILE, cols), (0, 0)), ((TILE, cols), (low, 0)),
                ((rows, LANES), (0, 0)), ((rows, LANES), (0, right)))
        ]

    table = pl.BlockSpec((levels, cols), lambda step: (0, 0))
    packet = (count, 8, cols + 2 * LANES)
    packed = pl.pallas_call(
        pack_kernel,
        grid=(1,),
        out_shape=jax.ShapeDtypeStruct(packet, jnp.float32),
        in_specs=edges((1,)) + momentum(0) + momentum(1) + edges((1,)) + edges((1,)) + [table, table],
        out_specs=pl.BlockSpec(packet, lambda step: (0, 0, 0)),
        compiler_params=params,
        name="pack",
    )(*[adjoint_height] * 4, *[adjoint_momenta] * 8, *[depth] * 4, *[wet_mask] * 4, nest_gain, nest_index)
    got = lax.all_to_all(packed, ("patch", "sub"), 0, 0, tiled=True)

    work = [pltpu.VMEM((count, cols), jnp.float32), pltpu.VMEM((count, LANES), jnp.float32)]
    flux = ()
    for turn in range(levels - 1):
        strips = pl.pallas_call(
            functools.partial(strips_kernel, subs),
            out_shape=jax.ShapeDtypeStruct((2, count, cols), jnp.float32),
            in_specs=[scalars, whole] + [whole] * len(flux),
            out_specs=whole,
            scratch_shapes=work,
            compiler_params=params,
            name="strips",
        )(adjacency, got, *flux)
        flux = (lax.ppermute(strips, "level", [(source, source - 1) for source in range(1, levels)]),)

    return pl.pallas_call(
        functools.partial(final_kernel, subs),
        out_shape=[
            jax.ShapeDtypeStruct(adjoint_height.shape, jnp.float32),
            jax.ShapeDtypeStruct(adjoint_momenta.shape, jnp.float32),
        ],
        in_specs=[scalars] + [whole] * 6,
        out_specs=[whole, whole],
        scratch_shapes=work + [
            pltpu.VMEM((4 * count, 1, cols), jnp.float32),
            pltpu.VMEM((rows + 2 * TILE, cols), jnp.float32),
            pltpu.VMEM((rows + 2 * TILE, cols), jnp.float32),
        ],
        compiler_params=params,
        name="final",
    )(adjacency, got, *flux, adjoint_height, adjoint_momenta, depth, wet_mask)


def solution(mesh):
    in_specs = (
        P(("parts", "level"), ("patch", "sub"), None),
        P(None, ("parts", "level"), ("patch", "sub"), None),
        P("level", ("patch", "sub"), None),
        P("level", ("patch", "sub"), None),
        P("level", None, None),
        P(None, ("patch", "sub")),
        P(None, ("patch", "sub")),
    )
    out_specs = (
        P(("parts", "level"), ("patch", "sub"), None),
        P(None, ("parts", "level"), ("patch", "sub"), None),
    )
    return jax.shard_map(body, mesh=mesh, in_specs=in_specs, out_specs=out_specs, check_vma=False)
```

```python
import functools

import jax
import jax.numpy as jnp
from jax import lax
from jax.experimental import pallas as pl
from jax.experimental.pallas import tpu as pltpu
from jax.sharding import PartitionSpec as P

STEPS = 2
LANES = 128
TILE = 8
VMEM_LIMIT = 48 * 1024 * 1024

courant = 0.45

STRIP_SUM, STRIP, STRIP_DEPTH, GAIN, INDEX, EDGE_FLOW, EDGE_DEPTH, EDGE_SUM = range(8)
(FIRST_ETA, SECOND_ETA, FIRST_ROW, FIRST_COL, FIRST_DEPTH, NEXT_ETA, LAST_ETA, NEXT_ROW,
 LAST_ROW, LAST_COL, NEXT_DEPTH, LAST_DEPTH) = range(12)


def iota(shape, axis):
    return lax.broadcasted_iota(jnp.int32, shape, axis)


def rolled(value, shift, axis):
    return pltpu.roll(value, shift % value.shape[axis], axis)


def wet(depth):
    return (depth > 0).astype(jnp.float32)


def copied(pairs, sems):
    copies = [pltpu.make_async_copy(source, target, sems.at[place]) for place, (source, target) in enumerate(pairs)]
    for copy in copies:
        copy.start()
    return copies


def pack_kernel(eta_ref, momenta_ref, depth_ref, wet_ref, gain_ref, index_ref, out_ref,
                ends, end_wet, sides, side_wet, gains, indices, sems):
    count, _, width = out_ref.shape
    rows, cols = eta_ref.shape[1:]
    fields = eta_ref.at[0], momenta_ref.at[0, 0], momenta_ref.at[1, 0], depth_ref.at[0]
    pairs = []
    for end in range(2):
        tall = pl.ds(end * (rows - TILE), TILE)
        wide = pl.ds(end * (cols - LANES), LANES)
        for place, field in enumerate(fields):
            pairs.append((field.at[tall, :], ends.at[end, place]))
            pairs.append((field.at[:, wide], sides.at[end, place]))
        pairs.append((wet_ref.at[0, tall, :], end_wet.at[end]))
        pairs.append((wet_ref.at[0, :, wide], side_wet.at[end]))
    for copy in copied(pairs + [(gain_ref, gains), (index_ref, indices)], sems):
        copy.wait()
    level = lax.axis_index("level")
    lane = iota((TILE, cols), 1)

    def loaded(end):
        mask = end_wet[end].astype(jnp.float32)
        return ends[end, 0], ends[end, 1], ends[end, 2], mask * ends[end, 3], mask

    eta, row, col, depth, mask = loaded(0)
    east = jnp.where(lane == cols - 1, 0.0, rolled(eta, -1, 1))
    row = mask * (row - courant * (east - eta))
    west = jnp.where(lane == 0, 0.0, rolled(row, 1, 1))
    col = mask * (col - courant * (rolled(eta, -1, 0) - eta))
    strip_sum = mask * eta - courant * depth * (row - west + col)
    out_ref[0, STRIP_SUM:STRIP_SUM + 1, :cols] = strip_sum[:1]
    out_ref[0, STRIP:STRIP + 1, :cols] = eta[:1]
    out_ref[0, STRIP_DEPTH:STRIP_DEPTH + 1, :cols] = depth[:1]
    out_ref[0, GAIN:GAIN + 1, :cols] = gains[pl.ds(level, 1), :]
    out_ref[0, INDEX:INDEX + 1, :cols] = indices[pl.ds(level, 1), :].astype(jnp.float32)

    eta, row, col, depth, mask = loaded(1)
    east = jnp.where(lane == cols - 1, 0.0, rolled(eta, -1, 1))
    row = mask * (row - courant * (east - eta))
    west = jnp.where(lane == 0, 0.0, rolled(row, 1, 1))
    flow = mask * (col + courant * eta)
    above = rolled(flow - courant * mask * rolled(eta, -1, 0), 1, 0)
    edge_sum = mask * eta - courant * depth * (row - west - above)
    out_ref[0, EDGE_FLOW:EDGE_FLOW + 1, :cols] = flow[TILE - 1:]
    out_ref[0, EDGE_DEPTH:EDGE_DEPTH + 1, :cols] = depth[TILE - 1:]
    out_ref[0, EDGE_SUM:EDGE_SUM + 1, :cols] = edge_sum[TILE - 1:]

    lane = iota((rows, LANES), 1)
    columns = jnp.zeros((rows, LANES), jnp.float32)
    depths = [sides[end, 3] * side_wet[end].astype(jnp.float32) for end in range(2)]
    for place, value, at in (
        (FIRST_ETA, sides[0, 0], 0), (SECOND_ETA, sides[0, 0], 1), (FIRST_ROW, sides[0, 1], 0),
        (FIRST_COL, sides[0, 2], 0), (FIRST_DEPTH, depths[0], 0),
        (NEXT_ETA, sides[1, 0], LANES - 2), (LAST_ETA, sides[1, 0], LANES - 1),
        (NEXT_ROW, sides[1, 1], LANES - 2), (LAST_ROW, sides[1, 1], LANES - 1),
        (LAST_COL, sides[1, 2], LANES - 1),
        (NEXT_DEPTH, depths[1], LANES - 2), (LAST_DEPTH, depths[1], LANES - 1),
    ):
        moved = value if place == at else rolled(value, place - at, 1)
        columns = jnp.where(lane == place, moved, columns)
    columns = columns.T
    out_ref[0, :, cols:cols + LANES] = columns[:TILE]
    out_ref[0, :, cols + LANES:] = columns[TILE:2 * TILE]
    packet = out_ref[0]
    for turn in range(1, count):
        out_ref[turn] = packet


def bulk_kernel(eta_ref, momenta_ref, depth_ref, wet_ref, eta_out, momenta_out,
                eta_after, momenta_after, wet_after, depth_after, eta_ends, row_ends, turned,
                eta_pad, col_pad, momenta_in, depth_in, wet_in, eta_left, row_right, sems, out_sems):
    rows, cols = eta_ref.shape[1:]
    parts = sems.shape[0]
    size = rows // parts
    loads = []
    for part in range(parts):
        here = pl.ds(part * size, size)
        loads.append(copied([
            (eta_ref.at[0, here, :], eta_pad.at[pl.ds(TILE + part * size, size), :]),
            (momenta_ref.at[:, 0, here, :], momenta_in.at[:, here, :]),
            (depth_ref.at[0, here, :], depth_in.at[here, :]),
            (wet_ref.at[0, here, :], wet_in.at[here, :]),
        ], sems.at[part]))
    lane = iota((TILE, cols), 1)
    eta_pad[TILE + rows:] = jnp.zeros((TILE, cols), jnp.float32)
    col_pad[:TILE] = jnp.zeros((TILE, cols), jnp.float32)

    def step(number, low):
        chunk, padded = slice(low, low + TILE), slice(TILE + low, 2 * TILE + low)
        eta = eta_pad[padded]
        if number == 0:
            mask = wet_in[chunk].astype(jnp.float32)
            depth = courant * mask * depth_in[chunk]
            wet_after[chunk] = mask
            depth_after[chunk] = depth
            row, col = momenta_in[0, chunk], momenta_in[1, chunk]
        else:
            mask, depth = wet_after[chunk], depth_after[chunk]
            row, col = momenta_after[0, chunk], col_pad[padded]
        east = jnp.where(lane == cols - 1, 0.0, rolled(eta, -1, 1))
        south = eta_pad[TILE + low + 1:2 * TILE + low + 1]
        row = mask * (row - courant * (east - eta))
        col = mask * (col - courant * (south - eta))
        momenta_after[0, chunk] = row
        col_pad[padded] = col
        if number:
            momenta_after[1, chunk] = col
        west = jnp.where(lane == 0, 0.0, rolled(row, 1, 1))
        north = col_pad[TILE + low - 1:2 * TILE + low - 1]
        eta = mask * eta - depth * (row - west + (col - north))
        if number:
            eta_after[chunk] = eta
            return
        eta_pad[padded] = eta
        eta_left[chunk] = eta[:, :LANES]
        row_right[chunk] = row[:, cols - LANES:]
        if low in (0, rows - TILE):
            end = int(low > 0)
            eta_ends[end] = eta
            row_ends[end] = row

    for copy in loads[0]:
        copy.wait()
    stores = []
    for part in range(parts + 1):
        if part + 1 < parts:
            for copy in loads[part + 1]:
                copy.wait()
        if part < parts:
            for low in range(part * size, (part + 1) * size, TILE):
                step(0, low)
        if part:
            for low in range((part - 1) * size, part * size, TILE):
                step(1, low)
            here = pl.ds((part - 1) * size, size)
            stores += copied([
                (eta_after.at[here, :], eta_out.at[0, here, :]),
                (momenta_after.at[:, here, :], momenta_out.at[:, 0, here, :]),
            ], out_sems.at[part - 1])
    right = cols - LANES
    turned[0] = wet_after[:, :LANES].T[:TILE]
    turned[1] = depth_after[:, :LANES].T[:TILE]
    turned[2] = wet_after[:, right:].T[LANES - TILE:]
    turned[3] = depth_after[:, right:].T[LANES - TILE:]
    turned[4] = eta_left[...].T[:TILE]
    turned[5] = row_right[...].T[LANES - TILE:]
    for copy in stores:
        copy.wait()


class Links:
    def __init__(self, links_ref, subs):
        self.links_ref, self.subs = links_ref, subs

    def across(self, segment, way):
        patch = self.links_ref[0, segment // self.subs, way]
        return jnp.maximum(patch, 0), jnp.where(patch >= 0, 1.0, 0.0)

    def north(self, segment):
        patch, there = self.across(segment, 0)
        inside = segment % self.subs > 0
        return jnp.where(inside, segment - 1, patch * self.subs + self.subs - 1), jnp.where(inside, 1.0, there)

    def south(self, segment):
        patch, there = self.across(segment, 1)
        inside = segment % self.subs < self.subs - 1
        return jnp.where(inside, segment + 1, patch * self.subs), jnp.where(inside, 1.0, there)

    def west(self, segment):
        patch, there = self.across(segment, 2)
        return patch * self.subs + segment % self.subs, there

    def east(self, segment):
        patch, there = self.across(segment, 3)
        return patch * self.subs + segment % self.subs, there


def nested(flux, index):
    segments, cols = index.shape
    rows = []
    for low in range(0, segments, TILE):
        tiles = []
        for left in range(0, cols, LANES):
            at = index[low:low + TILE, left:left + LANES]
            lane, tile = at % LANES, at // LANES
            taken = jnp.zeros(at.shape, jnp.float32)
            for source in range(cols // LANES):
                values = flux[low:low + TILE, source * LANES:(source + 1) * LANES]
                found = jnp.take_along_axis(values, lane, axis=1, mode="promise_in_bounds")
                taken = jnp.where(tile == source, found, taken)
            tiles.append(taken)
        rows.append(jnp.concatenate(tiles, axis=1))
    return jnp.concatenate(rows, axis=0) if len(rows) > 1 else rows[0]


def strips_of(links, got_ref, finer, picked_ref, narrow_ref):
    count, _, width = got_ref.shape
    cols = width - 2 * LANES
    lane = iota((count, LANES), 1)
    strip, depth = got_ref[:, STRIP, :cols], got_ref[:, STRIP_DEPTH, :cols]
    mask = wet(depth)
    if finer is None:
        inflow = jnp.zeros_like(strip)
    else:
        gain = got_ref[:, GAIN, :cols]
        index = got_ref[:, INDEX, :cols].astype(jnp.int32)
        inflow = gain * nested(finer[0], index)
    eta = strip + inflow

    narrow_ref[...] = eta[:, :LANES]
    for segment in range(count):
        east, there = links.east(segment)
        picked_ref[segment:segment + 1, :LANES] = narrow_ref[pl.ds(east, 1), :] * there
    east_eta = rolled(picked_ref[:, :LANES], -1, 1)
    after = rolled(inflow, -1, 1)
    after = jnp.concatenate(
        [after[:, :-LANES], jnp.where(lane == LANES - 1, east_eta, after[:, -LANES:])], axis=1)
    more_row = courant * mask * (inflow - after)

    last_eta = got_ref[:, LAST_ETA % TILE, cols:cols + LANES]
    last_row = got_ref[:, LAST_ROW % TILE, cols + LANES:]
    first_of_last = rolled(last_row + courant * last_eta, -1, 1)
    narrow_ref[...] = mask[:, -LANES:] * first_of_last + more_row[:, -LANES:]
    for segment in range(count):
        west, there = links.west(segment)
        picked_ref[segment:segment + 1, :LANES] = narrow_ref[pl.ds(west, 1), :] * there
    west_row = rolled(picked_ref[:, :LANES], 1, 1)
    before = rolled(more_row, 1, 1)
    before = jnp.concatenate([jnp.where(lane == 0, west_row, before[:, :LANES]), before[:, LANES:]], axis=1)

    for segment in range(count):
        north, there = links.north(segment)
        picked_ref[segment:segment + 1, :] = got_ref[pl.ds(north, 1), EDGE_FLOW, :cols] * there
    flow = picked_ref[...]
    for segment in range(count):
        north, there = links.north(segment)
        picked_ref[segment:segment + 1, :] = got_ref[pl.ds(north, 1), EDGE_DEPTH, :cols] * there
    north_col = flow - courant * wet(picked_ref[...]) * eta
    later = (got_ref[:, STRIP_SUM, :cols] + mask * inflow
             - courant * depth * (more_row - before + courant * mask * inflow - north_col))
    if finer is None:
        return eta, later
    return eta, later + gain * nested(finer[1], index)


def strips_kernel(subs, *refs):
    links_ref, got_ref = refs[:2]
    out_ref, rows_ref, picked_ref, narrow_ref = refs[-4:]
    finer = (refs[2][0], refs[2][1]) if len(refs) == 7 else None
    eta, later = strips_of(Links(links_ref, subs), got_ref, finer, picked_ref, narrow_ref)
    out_ref[0] = eta
    out_ref[1] = later
    for segment in range(out_ref.shape[1]):
        rows_ref[segment] = later[segment:segment + 1]


class Packets:
    def __init__(self, got_ref, rows, cols, inflow_ref=None):
        self.got_ref, self.rows, self.cols, self.inflow_ref = got_ref, rows, cols, inflow_ref

    def row(self, segment, row, left=0, size=None):
        size = self.cols if size is None else size
        return self.got_ref[pl.ds(segment, 1), row, left:left + size]

    def column(self, segment, column):
        left = self.cols + column // TILE * LANES
        return self.got_ref[pl.ds(segment, 1), column % TILE, left:left + LANES]

    def field_row(self, segment, row, left=0, size=None):
        return self.row(segment, row, left, size) if self.inflow_ref is None else 0.0

    def field_column(self, segment, column):
        return self.column(segment, column) if self.inflow_ref is None else 0.0

    def inflow(self, step, segment, left=0, size=None):
        size = self.cols if size is None else size
        count = self.got_ref.shape[0]
        return self.inflow_ref[step * count + segment, :, left:left + size]

    def strip_tile(self, segment, left):
        if self.inflow_ref is None:
            return self.row(segment, STRIP, left, LANES)
        return self.inflow(0, segment, left, LANES)

    def at_first(self, step, segment, left, turned):
        if self.inflow_ref is None:
            return 0.0
        tile = self.inflow(step, segment, left, LANES)
        return jnp.where(iota((1, LANES), 1) == 0, rolled(tile, turned, 1) if turned else tile, 0.0)


def beside(links, packets, own):
    lane = iota((1, LANES), 1)
    first, last = lane == 0, lane == LANES - 1
    end = packets.cols - LANES

    def corner_col(segment, eta, left, turned):
        north, beyond = links.north(segment)
        flow = packets.field_row(north, EDGE_FLOW, left, LANES)
        mask = wet(packets.row(north, EDGE_DEPTH, left, LANES))
        if turned:
            flow = rolled(flow, turned, 1) if packets.inflow_ref is None else flow
            mask = rolled(mask, turned, 1)
        return beyond * (flow - courant * mask * eta)

    west, there = links.west(own)
    eta = packets.field_column(west, LAST_ETA) + packets.at_first(0, west, end, 1)
    next_eta = packets.field_column(west, NEXT_ETA) + packets.at_first(0, west, end, 2)
    own_eta = packets.field_column(own, FIRST_ETA) + packets.at_first(0, own, 0, 0)
    depth = packets.column(west, LAST_DEPTH) * there
    mask = wet(depth)
    next_row = wet(packets.column(west, NEXT_DEPTH)) * (
        packets.field_column(west, NEXT_ROW) - courant * (eta - next_eta))
    below, beyond = links.south(west)
    south_eta = jnp.where(last, packets.strip_tile(below, end) * beyond, rolled(eta, -1, 1))
    col = mask * (packets.field_column(west, LAST_COL) - courant * (south_eta - eta))
    north_col = jnp.where(first, corner_col(west, eta, end, 1), rolled(col, 1, 1))
    west_row = mask * (packets.field_column(west, LAST_ROW) - courant * (own_eta - eta))
    west_eta = (mask * eta - courant * depth * (west_row - next_row + col - north_col)
                + packets.at_first(1, west, end, 1))
    west_mask = mask

    east, there = links.east(own)
    eta = there * (packets.field_column(east, FIRST_ETA) + packets.at_first(0, east, 0, 0))
    second_eta = packets.field_column(east, SECOND_ETA) + packets.at_first(0, east, 0, -1)
    depth = packets.column(east, FIRST_DEPTH) * there
    mask = wet(depth)
    row = mask * (packets.field_column(east, FIRST_ROW) - courant * (second_eta - eta))
    below, beyond = links.south(east)
    south_eta = jnp.where(last, rolled(packets.strip_tile(below, 0), -1, 1) * beyond, rolled(eta, -1, 1))
    col = mask * (packets.field_column(east, FIRST_COL) - courant * (south_eta - eta))
    north_col = jnp.where(first, corner_col(east, eta, 0, 0), rolled(col, 1, 1))
    east_sum = (mask * eta - courant * depth * (row + col - north_col)
                + there * packets.at_first(1, east, 0, 0))
    return west_row, west_mask, west_eta, eta, east_sum, courant * depth


def advanced(eta, row, col, mask, depth, east, south, west, north):
    row = mask * (row - courant * (east(eta) - eta))
    col = mask * (col - courant * (south(eta) - eta))
    return mask * eta - depth * (row - west(row) + col - north(col)), row, col


def two_steps(start, mask, depth, sides, base, north=None, south=None, second=None):
    lane, line = iota(mask.shape, 1), iota(mask.shape, 0)
    cols = mask.shape[1]
    west_row, west_mask, west_eta, east_eta, east_sum, east_depth = sides
    state = start, 0.0, 0.0
    flow, beyond = west_row, east_eta
    above = 0.0 if north is None else north[0]
    for number in range(2):
        below = 0.0 if south is None else south[number]
        state = advanced(
            *state, mask, depth,
            lambda eta: jnp.where(lane == cols - 1, beyond, rolled(eta, -1, 1)),
            lambda eta: jnp.where(line == TILE - 1, below, rolled(eta, -1, 0)),
            lambda row: jnp.where(lane == 0, flow, rolled(row, 1, 1)),
            lambda col: jnp.where(line == 0, above, rolled(col, 1, 0)))
        if number:
            return state
        eta, row, col = state
        if second is not None:
            eta = eta + jnp.where(line == 0, second, 0.0)
            state = eta, row, col
        whole_eta, whole_row = (eta, row) if base is None else (eta + base[0], row + base[1])
        flow = west_mask * (west_row - courant * (whole_eta[:, :1] - west_eta))
        beyond = east_sum + east_depth * whole_row[:, cols - 1:]
        if north is not None:
            above = north[1] * (north[0] - courant * (whole_eta[:1] - north[2]))


def north_of(links, packets, own, own_strip):
    cols = packets.cols
    lane = iota((1, LANES), 1)
    north, there = links.north(own)
    depth = packets.row(north, EDGE_DEPTH) * there
    mask = wet(depth)
    if packets.inflow_ref is not None:
        col = -courant * mask * own_strip
        return col, mask, -courant * depth * col
    col = packets.row(north, EDGE_FLOW) * there - courant * mask * own_strip
    north_east, beyond = links.east(north)
    right_eta = beyond * packets.column(north_east, FIRST_ETA)
    north_west, beyond = links.west(north)
    left_row = beyond * wet(packets.column(north_west, LAST_DEPTH)) * (
        packets.column(north_west, LAST_ROW)
        - courant * (packets.column(north, FIRST_ETA) - packets.column(north_west, LAST_ETA)))
    nothing = jnp.zeros((1, cols - LANES), jnp.float32)
    corners = (jnp.concatenate([jnp.where(lane == 0, rolled(left_row, 1, 1), 0.0), nothing], axis=1)
               + jnp.concatenate([nothing, jnp.where(lane == LANES - 1, courant * right_eta, 0.0)], axis=1))
    return col, mask, packets.row(north, EDGE_SUM) + courant * depth * (corners - col)


def as_sublanes(columns):
    rows = columns[0].shape[1]
    count = -len(columns) % TILE
    turned = jnp.concatenate(list(columns) + [jnp.zeros((count, rows), jnp.float32)], axis=0).T
    return [[turned[low:low + TILE, place:place + 1] for place in range(len(columns))]
            for low in (0, rows - TILE)]


def own_segment(subs):
    return lax.axis_index("patch") * subs + lax.axis_index("sub")


def halo_kernel(subs, links_ref, got_ref, later_ref, eta_after, momenta_after, wet_after, depth_after,
                eta_ends, row_ends, turned, eta_hbm, momenta_hbm, eta_out, momenta_out, ends_out,
                left_new, right_new, sems):
    del eta_hbm, momenta_hbm
    rows, cols = eta_after.shape
    right = cols - LANES
    links, own = Links(links_ref, subs), own_segment(subs)
    packets = Packets(got_ref, rows, cols)
    columns = beside(links, packets, own)
    west_row, west_mask, west_eta, east_eta, east_sum, east_depth = columns
    fields = eta_after, momenta_after.at[0], momenta_after.at[1]

    line = iota((TILE, rows), 0)
    lane = iota((TILE, rows), 1)
    nothing = jnp.zeros((TILE, rows), jnp.float32)

    def south(eta):
        return jnp.where(lane == rows - 1, 0.0, rolled(eta, -1, 1))

    def north(col):
        return jnp.where(lane == 0, 0.0, rolled(col, 1, 1))

    def column_steps(mask, depth, east, west):
        state = nothing, nothing, nothing
        for number in range(2):
            state = advanced(
                *state, mask, depth,
                lambda eta: jnp.where(line == TILE - 1, east(number, state), rolled(eta, -1, 0)), south,
                lambda row: jnp.where(line == 0, west(number, state), rolled(row, 1, 0)), north)
        return state

    def west_of(number, state):
        if number == 0:
            return west_row
        whole = state[0][:1] + turned[4, :1]
        return west_mask * (west_row - courant * (whole - west_eta))

    def east_of(number, state):
        if number == 0:
            return east_eta
        return east_sum + east_depth * (state[1][TILE - 1:] + turned[5, TILE - 1:])

    left = column_steps(turned[0], turned[1], lambda number, state: 0.0, west_of)
    last = column_steps(turned[2], turned[3], east_of, lambda number, state: 0.0)
    middle = jnp.zeros((LANES - 2 * TILE, rows), jnp.float32)
    lane = iota((rows, LANES), 1)
    body_rows = slice(TILE, rows - TILE)
    copies = []
    outs = eta_out.at[0], momenta_out.at[0, 0], momenta_out.at[1, 0]
    inner = pl.ds(TILE, rows - 2 * TILE)
    for place, field in enumerate(fields):
        more = jnp.concatenate([left[place], middle, last[place]], axis=0).T[body_rows]
        inside = iota(more.shape, 1)
        left_new[place] = field[body_rows, :LANES] + jnp.where(inside < TILE, more, 0.0)
        right_new[place] = field[body_rows, right:] + jnp.where(inside >= LANES - TILE, more, 0.0)
        copies += copied([
            (left_new.at[place], outs[place].at[inner, pl.ds(0, LANES)]),
            (right_new.at[place], outs[place].at[inner, pl.ds(right, LANES)]),
        ], sems.at[place])

    top_sides, low_sides = as_sublanes(columns)
    nothing = jnp.zeros((TILE, cols), jnp.float32)
    top = two_steps(
        nothing, wet_after[:TILE], depth_after[:TILE], top_sides, (eta_ends[0], row_ends[0]),
        north=north_of(links, packets, own, packets.row(own, STRIP)))
    below, there = links.south(own)
    low = two_steps(
        nothing, wet_after[rows - TILE:], depth_after[rows - TILE:], low_sides, (eta_ends[1], row_ends[1]),
        south=(packets.row(below, STRIP) * there, later_ref[below] * there))
    line, lane = iota((TILE, cols), 0), iota((TILE, cols), 1)
    for place, field in enumerate(fields):
        more = jnp.concatenate([left[place], middle, last[place]], axis=0).T
        gap = jnp.zeros((TILE, cols - 2 * LANES), jnp.float32)
        for end, (low_row, near, found) in enumerate(
                ((0, line < TILE // 2, top), (rows - TILE, line >= TILE // 2, low))):
            tile = more[low_row:low_row + TILE]
            inside = iota(tile.shape, 1)
            wide = jnp.concatenate(
                [jnp.where(inside < TILE, tile, 0.0), gap, jnp.where(inside >= LANES - TILE, tile, 0.0)], axis=1)
            ends_out[place, end] = field[low_row:low_row + TILE] + jnp.where(near, found[place], wide)
    for copy in copies:
        copy.wait()


def inflow_kernel(subs, links_ref, got_ref, finer_ref, wet_after, depth_after, ends_ref, eta_hbm, momenta_hbm,
                  eta_out, momenta_out, inflow_ref, new_ref, sems):
    del eta_hbm, momenta_hbm
    rows, cols = wet_after.shape
    count = got_ref.shape[0]
    links, own = Links(links_ref, subs), own_segment(subs)
    gain = got_ref[:, GAIN, :cols]
    index = got_ref[:, INDEX, :cols].astype(jnp.int32)
    for number in range(2):
        inflow = gain * nested(finer_ref[number], index)
        for segment in range(count):
            inflow_ref[number * count + segment] = inflow[segment:segment + 1]
    packets = Packets(got_ref, rows, cols, inflow_ref)
    columns = beside(links, packets, own)
    top_sides, low_sides = as_sublanes(columns)
    line = iota((TILE, cols), 0)
    strip = packets.inflow(0, own)
    top = two_steps(
        jnp.where(line == 0, strip, 0.0), wet_after[:TILE], depth_after[:TILE], top_sides, None,
        north=north_of(links, packets, own, strip), second=packets.inflow(1, own))

    below, there = links.south(own)
    strip = packets.inflow(0, below) * there
    lane = iota((1, cols), 1)
    depth = packets.row(below, STRIP_DEPTH)
    mask = wet(depth)
    east, beyond = links.east(below)
    last_eta = rolled(packets.inflow(0, east, 0, LANES) * beyond, -1, 1)[:, LANES - 1:]
    after = jnp.where(lane == cols - 1, last_eta, rolled(strip, -1, 1))
    row = courant * mask * (strip - after)
    west, beyond = links.west(below)
    end = cols - LANES
    first_row = rolled(courant * wet(packets.row(west, STRIP_DEPTH, end, LANES)) * beyond * (
        packets.inflow(0, west, end, LANES) - rolled(strip[:, :LANES], -1, 1)), 1, 1)[:, :1]
    before = jnp.where(lane == 0, first_row, rolled(row, 1, 1))
    north, beyond = links.north(below)
    north_col = -courant * wet(packets.row(north, EDGE_DEPTH)) * beyond * strip
    later = there * (mask * strip - courant * depth * (row - before + courant * mask * strip - north_col)
                     + packets.inflow(1, below))
    low = two_steps(
        jnp.zeros((TILE, cols), jnp.float32), wet_after[rows - TILE:], depth_after[rows - TILE:],
        low_sides, None, south=(strip, later))
    copies = []
    outs = eta_out.at[0], momenta_out.at[0, 0], momenta_out.at[1, 0]
    for place, out in enumerate(outs):
        for end, (low_row, near, found) in enumerate(
                ((0, line < TILE // 2, top), (rows - TILE, line >= TILE // 2, low))):
            new_ref[place, end] = ends_ref[place, end] + jnp.where(near, found[place], 0.0)
        copies += copied([
            (new_ref.at[place, end], out.at[pl.ds(end * (rows - TILE), TILE), :]) for end in range(2)
        ], sems.at[place])
    for copy in copies:
        copy.wait()


def body(adjoint_height, adjoint_momenta, depth, wet_mask, adjacency, nest_gain, nest_index):
    rows, cols = adjoint_height.shape[1:]
    levels = lax.axis_size("level")
    subs = lax.axis_size("sub")
    count = lax.axis_size("patch") * subs
    params = pltpu.CompilerParams(vmem_limit_bytes=VMEM_LIMIT)
    vmem = pl.BlockSpec(memory_space=pltpu.VMEM)
    smem = pl.BlockSpec(memory_space=pltpu.SMEM)
    hbm = pl.BlockSpec(memory_space=pltpu.HBM)

    def array(*shape):
        return jax.ShapeDtypeStruct(shape, jnp.float32)

    def scratch(*shape):
        return pltpu.VMEM(shape, jnp.float32)

    fields = [pltpu.with_memory_space_constraint(field, pltpu.HBM)
              for field in (adjoint_height, adjoint_momenta, depth, wet_mask, nest_gain, nest_index)]
    packed = pl.pallas_call(
        pack_kernel,
        out_shape=array(count, 8, cols + 2 * LANES),
        in_specs=[hbm] * 6,
        out_specs=vmem,
        scratch_shapes=[
            scratch(2, 4, TILE, cols), pltpu.VMEM((2, TILE, cols), jnp.int32),
            scratch(2, 4, rows, LANES), pltpu.VMEM((2, rows, LANES), jnp.int32),
            scratch(levels, cols), pltpu.VMEM((levels, cols), jnp.int32),
            pltpu.SemaphoreType.DMA((22,)),
        ],
        compiler_params=params,
        name="pack",
    )(*fields)
    got = lax.all_to_all(packed, ("patch", "sub"), 0, 0, tiled=True)

    parts = 4
    eta_new, momenta_new, *after = pl.pallas_call(
        bulk_kernel,
        out_shape=[
            array(*adjoint_height.shape), array(*adjoint_momenta.shape),
            array(rows, cols), array(2, rows, cols), array(rows, cols), array(rows, cols),
            array(2, TILE, cols), array(2, TILE, cols), array(6, TILE, rows),
        ],
        in_specs=[hbm] * 4,
        out_specs=[hbm] * 2 + [vmem] * 7,
        scratch_shapes=[
            scratch(rows + 2 * TILE, cols), scratch(rows + 2 * TILE, cols),
            scratch(2, rows, cols), scratch(rows, cols), pltpu.VMEM((rows, cols), jnp.int32),
            scratch(rows, LANES), scratch(rows, LANES),
            pltpu.SemaphoreType.DMA((parts, 4)), pltpu.SemaphoreType.DMA((parts, 2)),
        ],
        compiler_params=params,
        name="bulk",
    )(*fields[:4])

    flux = ()
    laters = []
    for turn in range(levels - 1):
        strips, later = pl.pallas_call(
            functools.partial(strips_kernel, subs),
            out_shape=[array(2, count, cols), array(count, 1, cols)],
            in_specs=[smem, vmem] + [vmem] * len(flux),
            out_specs=[vmem, vmem],
            scratch_shapes=[scratch(count, cols), scratch(count, LANES)],
            compiler_params=params,
            name="strips",
        )(adjacency, got, *flux)
        laters.append(later)
        flux = (lax.ppermute(strips, "level", [(source, source - 1) for source in range(1, levels)]),)

    eta_new, momenta_new, ends = pl.pallas_call(
        functools.partial(halo_kernel, subs),
        out_shape=[array(*adjoint_height.shape), array(*adjoint_momenta.shape), array(3, 2, TILE, cols)],
        in_specs=[smem] + [vmem] * 9 + [hbm] * 2,
        out_specs=[hbm, hbm, vmem],
        input_output_aliases={10: 0, 11: 1},
        scratch_shapes=[
            scratch(3, rows - 2 * TILE, LANES), scratch(3, rows - 2 * TILE, LANES), pltpu.SemaphoreType.DMA((3, 2)),
        ],
        compiler_params=params,
        name="halo",
    )(adjacency, got, laters[0], *after, eta_new, momenta_new)

    return pl.pallas_call(
        functools.partial(inflow_kernel, subs),
        out_shape=[array(*adjoint_height.shape), array(*adjoint_momenta.shape)],
        in_specs=[smem] + [vmem] * 5 + [hbm] * 2,
        out_specs=[hbm, hbm],
        input_output_aliases={6: 0, 7: 1},
        scratch_shapes=[
            scratch(2 * count, 1, cols), scratch(3, 2, TILE, cols), pltpu.SemaphoreType.DMA((3, 2)),
        ],
        compiler_params=params,
        name="inflow",
    )(adjacency, got, *flux, after[2], after[3], ends, eta_new, momenta_new)


def solution(mesh):
    in_specs = (
        P(("parts", "level"), ("patch", "sub"), None),
        P(None, ("parts", "level"), ("patch", "sub"), None),
        P("level", ("patch", "sub"), None),
        P("level", ("patch", "sub"), None),
        P("level", None, None),
        P(None, ("patch", "sub")),
        P(None, ("patch", "sub")),
    )
    out_specs = (
        P(("parts", "level"), ("patch", "sub"), None),
        P(None, ("parts", "level"), ("patch", "sub"), None),
    )
    return jax.shard_map(body, mesh=mesh, in_specs=in_specs, out_specs=out_specs, check_vma=False)
```

```python
import functools

import jax
import jax.numpy as jnp
from jax import lax
from jax.experimental import pallas as pl
from jax.experimental.pallas import tpu as pltpu
from jax.sharding import PartitionSpec as P

STEPS = 2
LANES = 128
TILE = 8
VMEM_LIMIT = 48 * 1024 * 1024

courant = 0.45

STRIP_SUM, STRIP, STRIP_DEPTH, GAIN, INDEX, EDGE_FLOW, EDGE_DEPTH, EDGE_SUM = range(8)
ROWS = 8
(FIRST_ETA, SECOND_ETA, FIRST_ROW, FIRST_COL, FIRST_DEPTH, NEXT_ETA, LAST_ETA, NEXT_ROW,
 LAST_ROW, LAST_COL, NEXT_DEPTH, LAST_DEPTH) = range(12)
COLUMNS = 12


def row_at(row, cols, left=0, size=None):
    return slice(row * cols + left, row * cols + left + (cols if size is None else size))


def column_at(column, cols):
    return slice(ROWS * cols + column * LANES, ROWS * cols + (column + 1) * LANES)


def iota(shape, axis):
    return lax.broadcasted_iota(jnp.int32, shape, axis)


def rolled(value, shift, axis):
    return pltpu.roll(value, shift % value.shape[axis], axis)


def wet(depth):
    return (depth > 0).astype(jnp.float32)


def copied(pairs, sems):
    copies = [pltpu.make_async_copy(source, target, sems.at[place]) for place, (source, target) in enumerate(pairs)]
    for copy in copies:
        copy.start()
    return copies


def pack_kernel(eta_ref, momenta_ref, depth_ref, wet_ref, gain_ref, index_ref, out_ref,
                ends, end_wet, sides, side_wet, gains, indices, sems):
    count = out_ref.shape[0]
    rows, cols = eta_ref.shape[1:]
    fields = eta_ref.at[0], momenta_ref.at[0, 0], momenta_ref.at[1, 0], depth_ref.at[0]
    pairs = []
    for end in range(2):
        tall = pl.ds(end * (rows - TILE), TILE)
        wide = pl.ds(end * (cols - LANES), LANES)
        for place, field in enumerate(fields):
            pairs.append((field.at[tall, :], ends.at[end, place]))
            pairs.append((field.at[:, wide], sides.at[end, place]))
        pairs.append((wet_ref.at[0, tall, :], end_wet.at[end]))
        pairs.append((wet_ref.at[0, :, wide], side_wet.at[end]))
    for copy in copied(pairs + [(gain_ref, gains), (index_ref, indices)], sems):
        copy.wait()
    level = lax.axis_index("level")
    lane = iota((TILE, cols), 1)

    def loaded(end):
        mask = end_wet[end].astype(jnp.float32)
        return ends[end, 0], ends[end, 1], ends[end, 2], mask * ends[end, 3], mask

    eta, row, col, depth, mask = loaded(0)
    east = jnp.where(lane == cols - 1, 0.0, rolled(eta, -1, 1))
    row = mask * (row - courant * (east - eta))
    west = jnp.where(lane == 0, 0.0, rolled(row, 1, 1))
    col = mask * (col - courant * (rolled(eta, -1, 0) - eta))
    strip_sum = mask * eta - courant * depth * (row - west + col)
    out_ref[0, :, row_at(STRIP_SUM, cols)] = strip_sum[:1]
    out_ref[0, :, row_at(STRIP, cols)] = eta[:1]
    out_ref[0, :, row_at(STRIP_DEPTH, cols)] = depth[:1]
    out_ref[0, :, row_at(GAIN, cols)] = gains[pl.ds(level, 1), :]
    out_ref[0, :, row_at(INDEX, cols)] = indices[pl.ds(level, 1), :].astype(jnp.float32)

    eta, row, col, depth, mask = loaded(1)
    east = jnp.where(lane == cols - 1, 0.0, rolled(eta, -1, 1))
    row = mask * (row - courant * (east - eta))
    west = jnp.where(lane == 0, 0.0, rolled(row, 1, 1))
    flow = mask * (col + courant * eta)
    above = rolled(flow - courant * mask * rolled(eta, -1, 0), 1, 0)
    edge_sum = mask * eta - courant * depth * (row - west - above)
    out_ref[0, :, row_at(EDGE_FLOW, cols)] = flow[TILE - 1:]
    out_ref[0, :, row_at(EDGE_DEPTH, cols)] = depth[TILE - 1:]
    out_ref[0, :, row_at(EDGE_SUM, cols)] = edge_sum[TILE - 1:]

    lane = iota((rows, LANES), 1)
    columns = jnp.zeros((rows, LANES), jnp.float32)
    depths = [sides[end, 3] * side_wet[end].astype(jnp.float32) for end in range(2)]
    for place, value, at in (
        (FIRST_ETA, sides[0, 0], 0), (SECOND_ETA, sides[0, 0], 1), (FIRST_ROW, sides[0, 1], 0),
        (FIRST_COL, sides[0, 2], 0), (FIRST_DEPTH, depths[0], 0),
        (NEXT_ETA, sides[1, 0], LANES - 2), (LAST_ETA, sides[1, 0], LANES - 1),
        (NEXT_ROW, sides[1, 1], LANES - 2), (LAST_ROW, sides[1, 1], LANES - 1),
        (LAST_COL, sides[1, 2], LANES - 1),
        (NEXT_DEPTH, depths[1], LANES - 2), (LAST_DEPTH, depths[1], LANES - 1),
    ):
        moved = value if place == at else rolled(value, place - at, 1)
        columns = jnp.where(lane == place, moved, columns)
    columns = columns.T
    for place in range(COLUMNS):
        out_ref[0, :, column_at(place, cols)] = columns[place:place + 1]
    packet = out_ref[0]
    for turn in range(1, count):
        out_ref[turn] = packet


def bulk_kernel(eta_ref, momenta_ref, depth_ref, wet_ref, eta_out, momenta_out,
                eta_after, momenta_after, wet_after, depth_after, eta_ends, row_ends, turned,
                eta_pad, col_pad, momenta_in, depth_in, wet_in, eta_left, row_right, sems, out_sems):
    rows, cols = eta_ref.shape[1:]
    parts = sems.shape[0]
    size = rows // parts
    loads = []
    for part in range(parts):
        here = pl.ds(part * size, size)
        loads.append(copied([
            (eta_ref.at[0, here, :], eta_pad.at[pl.ds(TILE + part * size, size), :]),
            (momenta_ref.at[:, 0, here, :], momenta_in.at[:, here, :]),
            (depth_ref.at[0, here, :], depth_in.at[here, :]),
            (wet_ref.at[0, here, :], wet_in.at[here, :]),
        ], sems.at[part]))
    lane = iota((TILE, cols), 1)
    eta_pad[TILE + rows:] = jnp.zeros((TILE, cols), jnp.float32)
    col_pad[:TILE] = jnp.zeros((TILE, cols), jnp.float32)

    def step(number, low):
        chunk, padded = slice(low, low + TILE), slice(TILE + low, 2 * TILE + low)
        eta = eta_pad[padded]
        if number == 0:
            mask = wet_in[chunk].astype(jnp.float32)
            depth = courant * mask * depth_in[chunk]
            wet_after[chunk] = mask
            depth_after[chunk] = depth
            row, col = momenta_in[0, chunk], momenta_in[1, chunk]
        else:
            mask, depth = wet_after[chunk], depth_after[chunk]
            row, col = momenta_after[0, chunk], col_pad[padded]
        east = jnp.where(lane == cols - 1, 0.0, rolled(eta, -1, 1))
        south = eta_pad[TILE + low + 1:2 * TILE + low + 1]
        row = mask * (row - courant * (east - eta))
        col = mask * (col - courant * (south - eta))
        momenta_after[0, chunk] = row
        col_pad[padded] = col
        if number:
            momenta_after[1, chunk] = col
        west = jnp.where(lane == 0, 0.0, rolled(row, 1, 1))
        north = col_pad[TILE + low - 1:2 * TILE + low - 1]
        eta = mask * eta - depth * (row - west + (col - north))
        if number:
            eta_after[chunk] = eta
            return
        eta_pad[padded] = eta
        eta_left[chunk] = eta[:, :LANES]
        row_right[chunk] = row[:, cols - LANES:]
        if low in (0, rows - TILE):
            end = int(low > 0)
            eta_ends[end] = eta
            row_ends[end] = row

    for copy in loads[0]:
        copy.wait()
    stores = []
    for part in range(parts + 1):
        if part + 1 < parts:
            for copy in loads[part + 1]:
                copy.wait()
        if part < parts:
            for low in range(part * size, (part + 1) * size, TILE):
                step(0, low)
        if part:
            for low in range((part - 1) * size, part * size, TILE):
                step(1, low)
            here = pl.ds((part - 1) * size, size)
            stores += copied([
                (eta_after.at[here, :], eta_out.at[0, here, :]),
                (momenta_after.at[:, here, :], momenta_out.at[:, 0, here, :]),
            ], out_sems.at[part - 1])
    right = cols - LANES
    turned[0] = wet_after[:, :LANES].T[:TILE]
    turned[1] = depth_after[:, :LANES].T[:TILE]
    turned[2] = wet_after[:, right:].T[LANES - TILE:]
    turned[3] = depth_after[:, right:].T[LANES - TILE:]
    turned[4] = eta_left[...].T[:TILE]
    turned[5] = row_right[...].T[LANES - TILE:]
    for copy in stores:
        copy.wait()


def stacked(got_ref, part):
    return jnp.concatenate([got_ref[segment, :, part] for segment in range(got_ref.shape[0])], axis=0)


class Links:
    def __init__(self, links_ref, subs):
        self.links_ref, self.subs = links_ref, subs

    def across(self, segment, way):
        patch = self.links_ref[0, segment // self.subs, way]
        return jnp.maximum(patch, 0), jnp.where(patch >= 0, 1.0, 0.0)

    def north(self, segment):
        patch, there = self.across(segment, 0)
        inside = segment % self.subs > 0
        return jnp.where(inside, segment - 1, patch * self.subs + self.subs - 1), jnp.where(inside, 1.0, there)

    def south(self, segment):
        patch, there = self.across(segment, 1)
        inside = segment % self.subs < self.subs - 1
        return jnp.where(inside, segment + 1, patch * self.subs), jnp.where(inside, 1.0, there)

    def west(self, segment):
        patch, there = self.across(segment, 2)
        return patch * self.subs + segment % self.subs, there

    def east(self, segment):
        patch, there = self.across(segment, 3)
        return patch * self.subs + segment % self.subs, there


def nested(flux, index):
    segments, cols = index.shape
    rows = []
    for low in range(0, segments, TILE):
        tiles = []
        for left in range(0, cols, LANES):
            at = index[low:low + TILE, left:left + LANES]
            lane, tile = at % LANES, at // LANES
            taken = jnp.zeros(at.shape, jnp.float32)
            for source in range(cols // LANES):
                values = flux[low:low + TILE, source * LANES:(source + 1) * LANES]
                found = jnp.take_along_axis(values, lane, axis=1, mode="promise_in_bounds")
                taken = jnp.where(tile == source, found, taken)
            tiles.append(taken)
        rows.append(jnp.concatenate(tiles, axis=1))
    return jnp.concatenate(rows, axis=0) if len(rows) > 1 else rows[0]


def strips_of(links, got_ref, finer, picked_ref, narrow_ref):
    count, cols = picked_ref.shape
    lane = iota((count, LANES), 1)
    strip, depth = stacked(got_ref, row_at(STRIP, cols)), stacked(got_ref, row_at(STRIP_DEPTH, cols))
    mask = wet(depth)
    if finer is None:
        inflow = jnp.zeros_like(strip)
    else:
        gain = stacked(got_ref, row_at(GAIN, cols))
        index = stacked(got_ref, row_at(INDEX, cols)).astype(jnp.int32)
        inflow = gain * nested(finer[0], index)
    eta = strip + inflow

    narrow_ref[...] = eta[:, :LANES]
    for segment in range(count):
        east, there = links.east(segment)
        picked_ref[segment:segment + 1, :LANES] = narrow_ref[pl.ds(east, 1), :] * there
    east_eta = rolled(picked_ref[:, :LANES], -1, 1)
    after = rolled(inflow, -1, 1)
    after = jnp.concatenate(
        [after[:, :-LANES], jnp.where(lane == LANES - 1, east_eta, after[:, -LANES:])], axis=1)
    more_row = courant * mask * (inflow - after)

    last_eta = stacked(got_ref, column_at(LAST_ETA, cols))
    last_row = stacked(got_ref, column_at(LAST_ROW, cols))
    first_of_last = rolled(last_row + courant * last_eta, -1, 1)
    narrow_ref[...] = mask[:, -LANES:] * first_of_last + more_row[:, -LANES:]
    for segment in range(count):
        west, there = links.west(segment)
        picked_ref[segment:segment + 1, :LANES] = narrow_ref[pl.ds(west, 1), :] * there
    west_row = rolled(picked_ref[:, :LANES], 1, 1)
    before = rolled(more_row, 1, 1)
    before = jnp.concatenate([jnp.where(lane == 0, west_row, before[:, :LANES]), before[:, LANES:]], axis=1)

    for segment in range(count):
        north, there = links.north(segment)
        picked_ref[segment:segment + 1, :] = got_ref[north, :, row_at(EDGE_FLOW, cols)] * there
    flow = picked_ref[...]
    for segment in range(count):
        north, there = links.north(segment)
        picked_ref[segment:segment + 1, :] = got_ref[north, :, row_at(EDGE_DEPTH, cols)] * there
    north_col = flow - courant * wet(picked_ref[...]) * eta
    later = (stacked(got_ref, row_at(STRIP_SUM, cols)) + mask * inflow
             - courant * depth * (more_row - before + courant * mask * inflow - north_col))
    if finer is None:
        return eta, later
    return eta, later + gain * nested(finer[1], index)


def strips_kernel(subs, *refs):
    links_ref, got_ref = refs[:2]
    out_ref, rows_ref, picked_ref, narrow_ref = refs[-4:]
    finer = (refs[2][0], refs[2][1]) if len(refs) == 7 else None
    eta, later = strips_of(Links(links_ref, subs), got_ref, finer, picked_ref, narrow_ref)
    out_ref[0] = eta
    out_ref[1] = later
    for segment in range(out_ref.shape[1]):
        rows_ref[segment] = later[segment:segment + 1]


class Packets:
    def __init__(self, got_ref, rows, cols, inflow_ref=None):
        self.got_ref, self.rows, self.cols, self.inflow_ref = got_ref, rows, cols, inflow_ref

    def row(self, segment, row, left=0, size=None):
        return self.got_ref[segment, :, row_at(row, self.cols, left, size)]

    def column(self, segment, column):
        return self.got_ref[segment, :, column_at(column, self.cols)]

    def field_row(self, segment, row, left=0, size=None):
        return self.row(segment, row, left, size) if self.inflow_ref is None else 0.0

    def field_column(self, segment, column):
        return self.column(segment, column) if self.inflow_ref is None else 0.0

    def inflow(self, step, segment, left=0, size=None):
        size = self.cols if size is None else size
        count = self.got_ref.shape[0]
        return self.inflow_ref[step * count + segment, :, left:left + size]

    def strip_tile(self, segment, left):
        if self.inflow_ref is None:
            return self.row(segment, STRIP, left, LANES)
        return self.inflow(0, segment, left, LANES)

    def at_first(self, step, segment, left, turned):
        if self.inflow_ref is None:
            return 0.0
        tile = self.inflow(step, segment, left, LANES)
        return jnp.where(iota((1, LANES), 1) == 0, rolled(tile, turned, 1) if turned else tile, 0.0)


def beside(links, packets, own):
    lane = iota((1, LANES), 1)
    first, last = lane == 0, lane == LANES - 1
    end = packets.cols - LANES

    def corner_col(segment, eta, left, turned):
        north, beyond = links.north(segment)
        flow = packets.field_row(north, EDGE_FLOW, left, LANES)
        mask = wet(packets.row(north, EDGE_DEPTH, left, LANES))
        if turned:
            flow = rolled(flow, turned, 1) if packets.inflow_ref is None else flow
            mask = rolled(mask, turned, 1)
        return beyond * (flow - courant * mask * eta)

    west, there = links.west(own)
    eta = packets.field_column(west, LAST_ETA) + packets.at_first(0, west, end, 1)
    next_eta = packets.field_column(west, NEXT_ETA) + packets.at_first(0, west, end, 2)
    own_eta = packets.field_column(own, FIRST_ETA) + packets.at_first(0, own, 0, 0)
    depth = packets.column(west, LAST_DEPTH) * there
    mask = wet(depth)
    next_row = wet(packets.column(west, NEXT_DEPTH)) * (
        packets.field_column(west, NEXT_ROW) - courant * (eta - next_eta))
    below, beyond = links.south(west)
    south_eta = jnp.where(last, packets.strip_tile(below, end) * beyond, rolled(eta, -1, 1))
    col = mask * (packets.field_column(west, LAST_COL) - courant * (south_eta - eta))
    north_col = jnp.where(first, corner_col(west, eta, end, 1), rolled(col, 1, 1))
    west_row = mask * (packets.field_column(west, LAST_ROW) - courant * (own_eta - eta))
    west_eta = (mask * eta - courant * depth * (west_row - next_row + col - north_col)
                + packets.at_first(1, west, end, 1))
    west_mask = mask

    east, there = links.east(own)
    eta = there * (packets.field_column(east, FIRST_ETA) + packets.at_first(0, east, 0, 0))
    second_eta = packets.field_column(east, SECOND_ETA) + packets.at_first(0, east, 0, -1)
    depth = packets.column(east, FIRST_DEPTH) * there
    mask = wet(depth)
    row = mask * (packets.field_column(east, FIRST_ROW) - courant * (second_eta - eta))
    below, beyond = links.south(east)
    south_eta = jnp.where(last, rolled(packets.strip_tile(below, 0), -1, 1) * beyond, rolled(eta, -1, 1))
    col = mask * (packets.field_column(east, FIRST_COL) - courant * (south_eta - eta))
    north_col = jnp.where(first, corner_col(east, eta, 0, 0), rolled(col, 1, 1))
    east_sum = (mask * eta - courant * depth * (row + col - north_col)
                + there * packets.at_first(1, east, 0, 0))
    return west_row, west_mask, west_eta, eta, east_sum, courant * depth


def advanced(eta, row, col, mask, depth, east, south, west, north):
    row = mask * (row - courant * (east(eta) - eta))
    col = mask * (col - courant * (south(eta) - eta))
    return mask * eta - depth * (row - west(row) + col - north(col)), row, col


def two_steps(start, mask, depth, sides, base, north=None, south=None, second=None):
    lane, line = iota(mask.shape, 1), iota(mask.shape, 0)
    cols = mask.shape[1]
    west_row, west_mask, west_eta, east_eta, east_sum, east_depth = sides
    state = start, 0.0, 0.0
    flow, beyond = west_row, east_eta
    above = 0.0 if north is None else north[0]
    for number in range(2):
        below = 0.0 if south is None else south[number]
        state = advanced(
            *state, mask, depth,
            lambda eta: jnp.where(lane == cols - 1, beyond, rolled(eta, -1, 1)),
            lambda eta: jnp.where(line == TILE - 1, below, rolled(eta, -1, 0)),
            lambda row: jnp.where(lane == 0, flow, rolled(row, 1, 1)),
            lambda col: jnp.where(line == 0, above, rolled(col, 1, 0)))
        if number:
            return state
        eta, row, col = state
        if second is not None:
            eta = eta + jnp.where(line == 0, second, 0.0)
            state = eta, row, col
        whole_eta, whole_row = (eta, row) if base is None else (eta + base[0], row + base[1])
        flow = west_mask * (west_row - courant * (whole_eta[:, :1] - west_eta))
        beyond = east_sum + east_depth * whole_row[:, cols - 1:]
        if north is not None:
            above = north[1] * (north[0] - courant * (whole_eta[:1] - north[2]))


def north_of(links, packets, own, own_strip):
    cols = packets.cols
    lane = iota((1, LANES), 1)
    north, there = links.north(own)
    depth = packets.row(north, EDGE_DEPTH) * there
    mask = wet(depth)
    if packets.inflow_ref is not None:
        col = -courant * mask * own_strip
        return col, mask, -courant * depth * col
    col = packets.row(north, EDGE_FLOW) * there - courant * mask * own_strip
    north_east, beyond = links.east(north)
    right_eta = beyond * packets.column(north_east, FIRST_ETA)
    north_west, beyond = links.west(north)
    left_row = beyond * wet(packets.column(north_west, LAST_DEPTH)) * (
        packets.column(north_west, LAST_ROW)
        - courant * (packets.column(north, FIRST_ETA) - packets.column(north_west, LAST_ETA)))
    nothing = jnp.zeros((1, cols - LANES), jnp.float32)
    corners = (jnp.concatenate([jnp.where(lane == 0, rolled(left_row, 1, 1), 0.0), nothing], axis=1)
               + jnp.concatenate([nothing, jnp.where(lane == LANES - 1, courant * right_eta, 0.0)], axis=1))
    return col, mask, packets.row(north, EDGE_SUM) + courant * depth * (corners - col)


def as_sublanes(columns):
    rows = columns[0].shape[1]
    count = -len(columns) % TILE
    turned = jnp.concatenate(list(columns) + [jnp.zeros((count, rows), jnp.float32)], axis=0).T
    return [[turned[low:low + TILE, place:place + 1] for place in range(len(columns))]
            for low in (0, rows - TILE)]


def own_segment(subs):
    return lax.axis_index("patch") * subs + lax.axis_index("sub")


def halo_kernel(subs, links_ref, got_ref, later_ref, eta_after, momenta_after, wet_after, depth_after,
                eta_ends, row_ends, turned, eta_hbm, momenta_hbm, eta_out, momenta_out, ends_out,
                left_new, right_new, sems):
    del eta_hbm, momenta_hbm
    rows, cols = eta_after.shape
    right = cols - LANES
    links, own = Links(links_ref, subs), own_segment(subs)
    packets = Packets(got_ref, rows, cols)
    columns = beside(links, packets, own)
    west_row, west_mask, west_eta, east_eta, east_sum, east_depth = columns
    fields = eta_after, momenta_after.at[0], momenta_after.at[1]

    line = iota((TILE, rows), 0)
    lane = iota((TILE, rows), 1)
    nothing = jnp.zeros((TILE, rows), jnp.float32)

    def south(eta):
        return jnp.where(lane == rows - 1, 0.0, rolled(eta, -1, 1))

    def north(col):
        return jnp.where(lane == 0, 0.0, rolled(col, 1, 1))

    def column_steps(mask, depth, east, west):
        state = nothing, nothing, nothing
        for number in range(2):
            state = advanced(
                *state, mask, depth,
                lambda eta: jnp.where(line == TILE - 1, east(number, state), rolled(eta, -1, 0)), south,
                lambda row: jnp.where(line == 0, west(number, state), rolled(row, 1, 0)), north)
        return state

    def west_of(number, state):
        if number == 0:
            return west_row
        whole = state[0][:1] + turned[4, :1]
        return west_mask * (west_row - courant * (whole - west_eta))

    def east_of(number, state):
        if number == 0:
            return east_eta
        return east_sum + east_depth * (state[1][TILE - 1:] + turned[5, TILE - 1:])

    left = column_steps(turned[0], turned[1], lambda number, state: 0.0, west_of)
    last = column_steps(turned[2], turned[3], east_of, lambda number, state: 0.0)
    middle = jnp.zeros((LANES - 2 * TILE, rows), jnp.float32)
    lane = iota((rows, LANES), 1)
    body_rows = slice(TILE, rows - TILE)
    copies = []
    outs = eta_out.at[0], momenta_out.at[0, 0], momenta_out.at[1, 0]
    inner = pl.ds(TILE, rows - 2 * TILE)
    for place, field in enumerate(fields):
        more = jnp.concatenate([left[place], middle, last[place]], axis=0).T[body_rows]
        inside = iota(more.shape, 1)
        left_new[place] = field[body_rows, :LANES] + jnp.where(inside < TILE, more, 0.0)
        right_new[place] = field[body_rows, right:] + jnp.where(inside >= LANES - TILE, more, 0.0)
        copies += copied([
            (left_new.at[place], outs[place].at[inner, pl.ds(0, LANES)]),
            (right_new.at[place], outs[place].at[inner, pl.ds(right, LANES)]),
        ], sems.at[place])

    top_sides, low_sides = as_sublanes(columns)
    nothing = jnp.zeros((TILE, cols), jnp.float32)
    top = two_steps(
        nothing, wet_after[:TILE], depth_after[:TILE], top_sides, (eta_ends[0], row_ends[0]),
        north=north_of(links, packets, own, packets.row(own, STRIP)))
    below, there = links.south(own)
    low = two_steps(
        nothing, wet_after[rows - TILE:], depth_after[rows - TILE:], low_sides, (eta_ends[1], row_ends[1]),
        south=(packets.row(below, STRIP) * there, later_ref[below] * there))
    line, lane = iota((TILE, cols), 0), iota((TILE, cols), 1)
    for place, field in enumerate(fields):
        more = jnp.concatenate([left[place], middle, last[place]], axis=0).T
        gap = jnp.zeros((TILE, cols - 2 * LANES), jnp.float32)
        for end, (low_row, near, found) in enumerate(
                ((0, line < TILE // 2, top), (rows - TILE, line >= TILE // 2, low))):
            tile = more[low_row:low_row + TILE]
            inside = iota(tile.shape, 1)
            wide = jnp.concatenate(
                [jnp.where(inside < TILE, tile, 0.0), gap, jnp.where(inside >= LANES - TILE, tile, 0.0)], axis=1)
            ends_out[place, end] = field[low_row:low_row + TILE] + jnp.where(near, found[place], wide)
    for copy in copies:
        copy.wait()


def inflow_kernel(subs, links_ref, got_ref, finer_ref, wet_after, depth_after, ends_ref, eta_hbm, momenta_hbm,
                  eta_out, momenta_out, inflow_ref, new_ref, sems):
    del eta_hbm, momenta_hbm
    rows, cols = wet_after.shape
    count = got_ref.shape[0]
    links, own = Links(links_ref, subs), own_segment(subs)
    gain = stacked(got_ref, row_at(GAIN, cols))
    index = stacked(got_ref, row_at(INDEX, cols)).astype(jnp.int32)
    for number in range(2):
        inflow = gain * nested(finer_ref[number], index)
        for segment in range(count):
            inflow_ref[number * count + segment] = inflow[segment:segment + 1]
    packets = Packets(got_ref, rows, cols, inflow_ref)
    columns = beside(links, packets, own)
    top_sides, low_sides = as_sublanes(columns)
    line = iota((TILE, cols), 0)
    strip = packets.inflow(0, own)
    top = two_steps(
        jnp.where(line == 0, strip, 0.0), wet_after[:TILE], depth_after[:TILE], top_sides, None,
        north=north_of(links, packets, own, strip), second=packets.inflow(1, own))

    below, there = links.south(own)
    strip = packets.inflow(0, below) * there
    lane = iota((1, cols), 1)
    depth = packets.row(below, STRIP_DEPTH)
    mask = wet(depth)
    east, beyond = links.east(below)
    last_eta = rolled(packets.inflow(0, east, 0, LANES) * beyond, -1, 1)[:, LANES - 1:]
    after = jnp.where(lane == cols - 1, last_eta, rolled(strip, -1, 1))
    row = courant * mask * (strip - after)
    west, beyond = links.west(below)
    end = cols - LANES
    first_row = rolled(courant * wet(packets.row(west, STRIP_DEPTH, end, LANES)) * beyond * (
        packets.inflow(0, west, end, LANES) - rolled(strip[:, :LANES], -1, 1)), 1, 1)[:, :1]
    before = jnp.where(lane == 0, first_row, rolled(row, 1, 1))
    north, beyond = links.north(below)
    north_col = -courant * wet(packets.row(north, EDGE_DEPTH)) * beyond * strip
    later = there * (mask * strip - courant * depth * (row - before + courant * mask * strip - north_col)
                     + packets.inflow(1, below))
    low = two_steps(
        jnp.zeros((TILE, cols), jnp.float32), wet_after[rows - TILE:], depth_after[rows - TILE:],
        low_sides, None, south=(strip, later))
    copies = []
    outs = eta_out.at[0], momenta_out.at[0, 0], momenta_out.at[1, 0]
    for place, out in enumerate(outs):
        for end, (low_row, near, found) in enumerate(
                ((0, line < TILE // 2, top), (rows - TILE, line >= TILE // 2, low))):
            new_ref[place, end] = ends_ref[place, end] + jnp.where(near, found[place], 0.0)
        copies += copied([
            (new_ref.at[place, end], out.at[pl.ds(end * (rows - TILE), TILE), :]) for end in range(2)
        ], sems.at[place])
    for copy in copies:
        copy.wait()


def body(adjoint_height, adjoint_momenta, depth, wet_mask, adjacency, nest_gain, nest_index):
    rows, cols = adjoint_height.shape[1:]
    levels = lax.axis_size("level")
    subs = lax.axis_size("sub")
    count = lax.axis_size("patch") * subs
    params = pltpu.CompilerParams(vmem_limit_bytes=VMEM_LIMIT)
    vmem = pl.BlockSpec(memory_space=pltpu.VMEM)
    smem = pl.BlockSpec(memory_space=pltpu.SMEM)
    hbm = pl.BlockSpec(memory_space=pltpu.HBM)

    def array(*shape):
        return jax.ShapeDtypeStruct(shape, jnp.float32)

    def scratch(*shape):
        return pltpu.VMEM(shape, jnp.float32)

    fields = [pltpu.with_memory_space_constraint(field, pltpu.HBM)
              for field in (adjoint_height, adjoint_momenta, depth, wet_mask, nest_gain, nest_index)]
    packed = pl.pallas_call(
        pack_kernel,
        out_shape=array(count, 1, ROWS * cols + COLUMNS * LANES),
        in_specs=[hbm] * 6,
        out_specs=vmem,
        scratch_shapes=[
            scratch(2, 4, TILE, cols), pltpu.VMEM((2, TILE, cols), jnp.int32),
            scratch(2, 4, rows, LANES), pltpu.VMEM((2, rows, LANES), jnp.int32),
            scratch(levels, cols), pltpu.VMEM((levels, cols), jnp.int32),
            pltpu.SemaphoreType.DMA((22,)),
        ],
        compiler_params=params,
        name="pack",
    )(*fields)
    got = lax.all_to_all(packed, ("patch", "sub"), 0, 0, tiled=True)

    parts = 4
    eta_new, momenta_new, *after = pl.pallas_call(
        bulk_kernel,
        out_shape=[
            array(*adjoint_height.shape), array(*adjoint_momenta.shape),
            array(rows, cols), array(2, rows, cols), array(rows, cols), array(rows, cols),
            array(2, TILE, cols), array(2, TILE, cols), array(6, TILE, rows),
        ],
        in_specs=[hbm] * 4,
        out_specs=[hbm] * 2 + [vmem] * 7,
        scratch_shapes=[
            scratch(rows + 2 * TILE, cols), scratch(rows + 2 * TILE, cols),
            scratch(2, rows, cols), scratch(rows, cols), pltpu.VMEM((rows, cols), jnp.int32),
            scratch(rows, LANES), scratch(rows, LANES),
            pltpu.SemaphoreType.DMA((parts, 4)), pltpu.SemaphoreType.DMA((parts, 2)),
        ],
        compiler_params=params,
        name="bulk",
    )(*fields[:4])

    flux = ()
    laters = []
    for turn in range(levels - 1):
        strips, later = pl.pallas_call(
            functools.partial(strips_kernel, subs),
            out_shape=[array(2, count, cols), array(count, 1, cols)],
            in_specs=[smem, vmem] + [vmem] * len(flux),
            out_specs=[vmem, vmem],
            scratch_shapes=[scratch(count, cols), scratch(count, LANES)],
            compiler_params=params,
            name="strips",
        )(adjacency, got, *flux)
        laters.append(later)
        flux = (lax.ppermute(strips, "level", [(source, source - 1) for source in range(1, levels)]),)

    eta_new, momenta_new, ends = pl.pallas_call(
        functools.partial(halo_kernel, subs),
        out_shape=[array(*adjoint_height.shape), array(*adjoint_momenta.shape), array(3, 2, TILE, cols)],
        in_specs=[smem] + [vmem] * 9 + [hbm] * 2,
        out_specs=[hbm, hbm, vmem],
        input_output_aliases={10: 0, 11: 1},
        scratch_shapes=[
            scratch(3, rows - 2 * TILE, LANES), scratch(3, rows - 2 * TILE, LANES), pltpu.SemaphoreType.DMA((3, 2)),
        ],
        compiler_params=params,
        name="halo",
    )(adjacency, got, laters[0], *after, eta_new, momenta_new)

    return pl.pallas_call(
        functools.partial(inflow_kernel, subs),
        out_shape=[array(*adjoint_height.shape), array(*adjoint_momenta.shape)],
        in_specs=[smem] + [vmem] * 5 + [hbm] * 2,
        out_specs=[hbm, hbm],
        input_output_aliases={6: 0, 7: 1},
        scratch_shapes=[
            scratch(2 * count, 1, cols), scratch(3, 2, TILE, cols), pltpu.SemaphoreType.DMA((3, 2)),
        ],
        compiler_params=params,
        name="inflow",
    )(adjacency, got, *flux, after[2], after[3], ends, eta_new, momenta_new)


def solution(mesh):
    in_specs = (
        P(("parts", "level"), ("patch", "sub"), None),
        P(None, ("parts", "level"), ("patch", "sub"), None),
        P("level", ("patch", "sub"), None),
        P("level", ("patch", "sub"), None),
        P("level", None, None),
        P(None, ("patch", "sub")),
        P(None, ("patch", "sub")),
    )
    out_specs = (
        P(("parts", "level"), ("patch", "sub"), None),
        P(None, ("parts", "level"), ("patch", "sub"), None),
    )
    return jax.shard_map(body, mesh=mesh, in_specs=in_specs, out_specs=out_specs, check_vma=False)
```

```python
import functools

import jax
import jax.numpy as jnp
from jax import lax
from jax.experimental import pallas as pl
from jax.experimental.pallas import tpu as pltpu
from jax.sharding import PartitionSpec as P

STEPS = 2
LANES = 128
TILE = 8
VMEM_LIMIT = 48 * 1024 * 1024

courant = 0.45

STRIP_SUM, STRIP, STRIP_DEPTH, GAIN, INDEX, EDGE_FLOW, EDGE_DEPTH, EDGE_SUM = range(8)
ROWS = 8
(FIRST_ETA, SECOND_ETA, FIRST_ROW, FIRST_COL, FIRST_DEPTH, NEXT_ETA, LAST_ETA, NEXT_ROW,
 LAST_ROW, LAST_COL, NEXT_DEPTH, LAST_DEPTH) = range(12)
COLUMNS = 12


def row_at(row, cols, left=0, size=None):
    return slice(row * cols + left, row * cols + left + (cols if size is None else size))


def column_at(column, cols):
    return slice(ROWS * cols + column * LANES, ROWS * cols + (column + 1) * LANES)


def iota(shape, axis):
    return lax.broadcasted_iota(jnp.int32, shape, axis)


def rolled(value, shift, axis):
    return pltpu.roll(value, shift % value.shape[axis], axis)


def wet(depth):
    return (depth > 0).astype(jnp.float32)


def copied(pairs, sems):
    copies = [pltpu.make_async_copy(source, target, sems.at[place]) for place, (source, target) in enumerate(pairs)]
    for copy in copies:
        copy.start()
    return copies


def pack_kernel(eta_ref, momenta_ref, depth_ref, wet_ref, gain_ref, index_ref, out_ref,
                ends, end_wet, sides, side_wet, gains, indices, sems):
    count = out_ref.shape[0]
    rows, cols = eta_ref.shape[1:]
    fields = eta_ref.at[0], momenta_ref.at[0, 0], momenta_ref.at[1, 0], depth_ref.at[0]
    pairs = []
    for end in range(2):
        tall = pl.ds(end * (rows - TILE), TILE)
        wide = pl.ds(end * (cols - LANES), LANES)
        for place, field in enumerate(fields):
            pairs.append((field.at[tall, :], ends.at[end, place]))
            pairs.append((field.at[:, wide], sides.at[end, place]))
        pairs.append((wet_ref.at[0, tall, :], end_wet.at[end]))
        pairs.append((wet_ref.at[0, :, wide], side_wet.at[end]))
    for copy in copied(pairs + [(gain_ref, gains), (index_ref, indices)], sems):
        copy.wait()
    level = lax.axis_index("level")
    lane = iota((TILE, cols), 1)

    def loaded(end):
        mask = end_wet[end].astype(jnp.float32)
        return ends[end, 0], ends[end, 1], ends[end, 2], mask * ends[end, 3], mask

    eta, row, col, depth, mask = loaded(0)
    east = jnp.where(lane == cols - 1, 0.0, rolled(eta, -1, 1))
    row = mask * (row - courant * (east - eta))
    west = jnp.where(lane == 0, 0.0, rolled(row, 1, 1))
    col = mask * (col - courant * (rolled(eta, -1, 0) - eta))
    strip_sum = mask * eta - courant * depth * (row - west + col)
    out_ref[0, :, row_at(STRIP_SUM, cols)] = strip_sum[:1]
    out_ref[0, :, row_at(STRIP, cols)] = eta[:1]
    out_ref[0, :, row_at(STRIP_DEPTH, cols)] = depth[:1]
    out_ref[0, :, row_at(GAIN, cols)] = gains[pl.ds(level, 1), :]
    out_ref[0, :, row_at(INDEX, cols)] = indices[pl.ds(level, 1), :].astype(jnp.float32)

    eta, row, col, depth, mask = loaded(1)
    east = jnp.where(lane == cols - 1, 0.0, rolled(eta, -1, 1))
    row = mask * (row - courant * (east - eta))
    west = jnp.where(lane == 0, 0.0, rolled(row, 1, 1))
    flow = mask * (col + courant * eta)
    above = rolled(flow - courant * mask * rolled(eta, -1, 0), 1, 0)
    edge_sum = mask * eta - courant * depth * (row - west - above)
    out_ref[0, :, row_at(EDGE_FLOW, cols)] = flow[TILE - 1:]
    out_ref[0, :, row_at(EDGE_DEPTH, cols)] = depth[TILE - 1:]
    out_ref[0, :, row_at(EDGE_SUM, cols)] = edge_sum[TILE - 1:]

    lane = iota((rows, LANES), 1)
    columns = jnp.zeros((rows, LANES), jnp.float32)
    depths = [sides[end, 3] * side_wet[end].astype(jnp.float32) for end in range(2)]
    for place, value, at in (
        (FIRST_ETA, sides[0, 0], 0), (SECOND_ETA, sides[0, 0], 1), (FIRST_ROW, sides[0, 1], 0),
        (FIRST_COL, sides[0, 2], 0), (FIRST_DEPTH, depths[0], 0),
        (NEXT_ETA, sides[1, 0], LANES - 2), (LAST_ETA, sides[1, 0], LANES - 1),
        (NEXT_ROW, sides[1, 1], LANES - 2), (LAST_ROW, sides[1, 1], LANES - 1),
        (LAST_COL, sides[1, 2], LANES - 1),
        (NEXT_DEPTH, depths[1], LANES - 2), (LAST_DEPTH, depths[1], LANES - 1),
    ):
        moved = value if place == at else rolled(value, place - at, 1)
        columns = jnp.where(lane == place, moved, columns)
    columns = columns.T
    for place in range(COLUMNS):
        out_ref[0, :, column_at(place, cols)] = columns[place:place + 1]
    packet = out_ref[0]
    for turn in range(1, count):
        out_ref[turn] = packet


def bulk_kernel(eta_ref, momenta_ref, depth_ref, wet_ref, eta_out, momenta_out,
                eta_after, momenta_after, wet_after, depth_after, eta_ends, row_ends, turned,
                eta_pad, col_pad, momenta_in, depth_in, wet_in, eta_left, row_right, sems, out_sems):
    rows, cols = eta_ref.shape[1:]
    parts = sems.shape[0]
    size = rows // parts
    loads = []
    for part in range(parts):
        here = pl.ds(part * size, size)
        loads.append(copied([
            (eta_ref.at[0, here, :], eta_pad.at[pl.ds(TILE + part * size, size), :]),
            (momenta_ref.at[:, 0, here, :], momenta_in.at[:, here, :]),
            (depth_ref.at[0, here, :], depth_in.at[here, :]),
            (wet_ref.at[0, here, :], wet_in.at[here, :]),
        ], sems.at[part]))
    lane = iota((TILE, cols), 1)
    eta_pad[TILE + rows:] = jnp.zeros((TILE, cols), jnp.float32)
    col_pad[:TILE] = jnp.zeros((TILE, cols), jnp.float32)

    def step(number, low):
        chunk, padded = slice(low, low + TILE), slice(TILE + low, 2 * TILE + low)
        eta = eta_pad[padded]
        if number == 0:
            mask = wet_in[chunk].astype(jnp.float32)
            depth = courant * mask * depth_in[chunk]
            wet_after[chunk] = mask
            depth_after[chunk] = depth
            row, col = momenta_in[0, chunk], momenta_in[1, chunk]
        else:
            mask, depth = wet_after[chunk], depth_after[chunk]
            row, col = momenta_after[0, chunk], col_pad[padded]
        east = jnp.where(lane == cols - 1, 0.0, rolled(eta, -1, 1))
        south = eta_pad[TILE + low + 1:2 * TILE + low + 1]
        row = mask * (row - courant * (east - eta))
        col = mask * (col - courant * (south - eta))
        momenta_after[0, chunk] = row
        col_pad[padded] = col
        if number:
            momenta_after[1, chunk] = col
        west = jnp.where(lane == 0, 0.0, rolled(row, 1, 1))
        north = col_pad[TILE + low - 1:2 * TILE + low - 1]
        eta = mask * eta - depth * (row - west + (col - north))
        if number:
            eta_after[chunk] = eta
            return
        eta_pad[padded] = eta
        eta_left[chunk] = eta[:, :LANES]
        row_right[chunk] = row[:, cols - LANES:]
        if low in (0, rows - TILE):
            end = int(low > 0)
            eta_ends[end] = eta
            row_ends[end] = row

    for copy in loads[0]:
        copy.wait()
    stores = []
    for part in range(parts + 1):
        if part + 1 < parts:
            for copy in loads[part + 1]:
                copy.wait()
        if part < parts:
            for low in range(part * size, (part + 1) * size, TILE):
                step(0, low)
        if part:
            for low in range((part - 1) * size, part * size, TILE):
                step(1, low)
            here = pl.ds((part - 1) * size, size)
            stores += copied([
                (eta_after.at[here, :], eta_out.at[0, here, :]),
                (momenta_after.at[:, here, :], momenta_out.at[:, 0, here, :]),
            ], out_sems.at[part - 1])
    right = cols - LANES
    turned[0] = wet_after[:, :LANES].T[:TILE]
    turned[1] = depth_after[:, :LANES].T[:TILE]
    turned[2] = wet_after[:, right:].T[LANES - TILE:]
    turned[3] = depth_after[:, right:].T[LANES - TILE:]
    turned[4] = eta_left[...].T[:TILE]
    turned[5] = row_right[...].T[LANES - TILE:]
    for copy in stores:
        copy.wait()


def stacked(got_ref, part):
    return jnp.concatenate([got_ref[segment, :, part] for segment in range(got_ref.shape[0])], axis=0)


class Links:
    def __init__(self, links_ref, subs):
        self.links_ref, self.subs = links_ref, subs

    def across(self, segment, way):
        patch = self.links_ref[0, segment // self.subs, way]
        return jnp.maximum(patch, 0), jnp.where(patch >= 0, 1.0, 0.0)

    def north(self, segment):
        patch, there = self.across(segment, 0)
        inside = segment % self.subs > 0
        return jnp.where(inside, segment - 1, patch * self.subs + self.subs - 1), jnp.where(inside, 1.0, there)

    def south(self, segment):
        patch, there = self.across(segment, 1)
        inside = segment % self.subs < self.subs - 1
        return jnp.where(inside, segment + 1, patch * self.subs), jnp.where(inside, 1.0, there)

    def west(self, segment):
        patch, there = self.across(segment, 2)
        return patch * self.subs + segment % self.subs, there

    def east(self, segment):
        patch, there = self.across(segment, 3)
        return patch * self.subs + segment % self.subs, there


def nested(flux, index):
    segments, cols = index.shape
    rows = []
    for low in range(0, segments, TILE):
        tiles = []
        for left in range(0, cols, LANES):
            at = index[low:low + TILE, left:left + LANES]
            lane, tile = at % LANES, at // LANES
            taken = jnp.zeros(at.shape, jnp.float32)
            for source in range(cols // LANES):
                values = flux[low:low + TILE, source * LANES:(source + 1) * LANES]
                found = jnp.take_along_axis(values, lane, axis=1, mode="promise_in_bounds")
                taken = jnp.where(tile == source, found, taken)
            tiles.append(taken)
        rows.append(jnp.concatenate(tiles, axis=1))
    return jnp.concatenate(rows, axis=0) if len(rows) > 1 else rows[0]


def strips_of(links, got_ref, finer, picked_ref, narrow_ref):
    count, cols = picked_ref.shape
    lane = iota((count, LANES), 1)
    strip, depth = stacked(got_ref, row_at(STRIP, cols)), stacked(got_ref, row_at(STRIP_DEPTH, cols))
    mask = wet(depth)
    if finer is None:
        inflow = jnp.zeros_like(strip)
    else:
        gain = stacked(got_ref, row_at(GAIN, cols))
        index = stacked(got_ref, row_at(INDEX, cols)).astype(jnp.int32)
        inflow = gain * nested(finer[0], index)
    eta = strip + inflow

    narrow_ref[...] = eta[:, :LANES]
    for segment in range(count):
        east, there = links.east(segment)
        picked_ref[segment:segment + 1, :LANES] = narrow_ref[pl.ds(east, 1), :] * there
    east_eta = rolled(picked_ref[:, :LANES], -1, 1)
    after = rolled(inflow, -1, 1)
    after = jnp.concatenate(
        [after[:, :-LANES], jnp.where(lane == LANES - 1, east_eta, after[:, -LANES:])], axis=1)
    more_row = courant * mask * (inflow - after)

    last_eta = stacked(got_ref, column_at(LAST_ETA, cols))
    last_row = stacked(got_ref, column_at(LAST_ROW, cols))
    first_of_last = rolled(last_row + courant * last_eta, -1, 1)
    narrow_ref[...] = mask[:, -LANES:] * first_of_last + more_row[:, -LANES:]
    for segment in range(count):
        west, there = links.west(segment)
        picked_ref[segment:segment + 1, :LANES] = narrow_ref[pl.ds(west, 1), :] * there
    west_row = rolled(picked_ref[:, :LANES], 1, 1)
    before = rolled(more_row, 1, 1)
    before = jnp.concatenate([jnp.where(lane == 0, west_row, before[:, :LANES]), before[:, LANES:]], axis=1)

    for segment in range(count):
        north, there = links.north(segment)
        picked_ref[segment:segment + 1, :] = got_ref[north, :, row_at(EDGE_FLOW, cols)] * there
    flow = picked_ref[...]
    for segment in range(count):
        north, there = links.north(segment)
        picked_ref[segment:segment + 1, :] = got_ref[north, :, row_at(EDGE_DEPTH, cols)] * there
    north_col = flow - courant * wet(picked_ref[...]) * eta
    later = (stacked(got_ref, row_at(STRIP_SUM, cols)) + mask * inflow
             - courant * depth * (more_row - before + courant * mask * inflow - north_col))
    if finer is None:
        return eta, later
    return eta, later + gain * nested(finer[1], index)


def strips_kernel(subs, *refs):
    links_ref, got_ref, _ = refs[:3]
    out_ref, rows_ref, picked_ref, narrow_ref = refs[-4:]
    finer = (refs[3][0], refs[3][1]) if len(refs) == 8 else None
    eta, later = strips_of(Links(links_ref, subs), got_ref, finer, picked_ref, narrow_ref)
    out_ref[0] = eta
    out_ref[1] = later
    for segment in range(out_ref.shape[1]):
        rows_ref[segment] = later[segment:segment + 1]


class Packets:
    def __init__(self, got_ref, rows, cols, inflow_ref=None):
        self.got_ref, self.rows, self.cols, self.inflow_ref = got_ref, rows, cols, inflow_ref

    def row(self, segment, row, left=0, size=None):
        return self.got_ref[segment, :, row_at(row, self.cols, left, size)]

    def column(self, segment, column):
        return self.got_ref[segment, :, column_at(column, self.cols)]

    def field_row(self, segment, row, left=0, size=None):
        return self.row(segment, row, left, size) if self.inflow_ref is None else 0.0

    def field_column(self, segment, column):
        return self.column(segment, column) if self.inflow_ref is None else 0.0

    def inflow(self, step, segment, left=0, size=None):
        size = self.cols if size is None else size
        count = self.got_ref.shape[0]
        return self.inflow_ref[step * count + segment, :, left:left + size]

    def strip_tile(self, segment, left):
        if self.inflow_ref is None:
            return self.row(segment, STRIP, left, LANES)
        return self.inflow(0, segment, left, LANES)

    def at_first(self, step, segment, left, turned):
        if self.inflow_ref is None:
            return 0.0
        tile = self.inflow(step, segment, left, LANES)
        return jnp.where(iota((1, LANES), 1) == 0, rolled(tile, turned, 1) if turned else tile, 0.0)


def beside(links, packets, own):
    lane = iota((1, LANES), 1)
    first, last = lane == 0, lane == LANES - 1
    end = packets.cols - LANES

    def corner_col(segment, eta, left, turned):
        north, beyond = links.north(segment)
        flow = packets.field_row(north, EDGE_FLOW, left, LANES)
        mask = wet(packets.row(north, EDGE_DEPTH, left, LANES))
        if turned:
            flow = rolled(flow, turned, 1) if packets.inflow_ref is None else flow
            mask = rolled(mask, turned, 1)
        return beyond * (flow - courant * mask * eta)

    west, there = links.west(own)
    eta = packets.field_column(west, LAST_ETA) + packets.at_first(0, west, end, 1)
    next_eta = packets.field_column(west, NEXT_ETA) + packets.at_first(0, west, end, 2)
    own_eta = packets.field_column(own, FIRST_ETA) + packets.at_first(0, own, 0, 0)
    depth = packets.column(west, LAST_DEPTH) * there
    mask = wet(depth)
    next_row = wet(packets.column(west, NEXT_DEPTH)) * (
        packets.field_column(west, NEXT_ROW) - courant * (eta - next_eta))
    below, beyond = links.south(west)
    south_eta = jnp.where(last, packets.strip_tile(below, end) * beyond, rolled(eta, -1, 1))
    col = mask * (packets.field_column(west, LAST_COL) - courant * (south_eta - eta))
    north_col = jnp.where(first, corner_col(west, eta, end, 1), rolled(col, 1, 1))
    west_row = mask * (packets.field_column(west, LAST_ROW) - courant * (own_eta - eta))
    west_eta = (mask * eta - courant * depth * (west_row - next_row + col - north_col)
                + packets.at_first(1, west, end, 1))
    west_mask = mask

    east, there = links.east(own)
    eta = there * (packets.field_column(east, FIRST_ETA) + packets.at_first(0, east, 0, 0))
    second_eta = packets.field_column(east, SECOND_ETA) + packets.at_first(0, east, 0, -1)
    depth = packets.column(east, FIRST_DEPTH) * there
    mask = wet(depth)
    row = mask * (packets.field_column(east, FIRST_ROW) - courant * (second_eta - eta))
    below, beyond = links.south(east)
    south_eta = jnp.where(last, rolled(packets.strip_tile(below, 0), -1, 1) * beyond, rolled(eta, -1, 1))
    col = mask * (packets.field_column(east, FIRST_COL) - courant * (south_eta - eta))
    north_col = jnp.where(first, corner_col(east, eta, 0, 0), rolled(col, 1, 1))
    east_sum = (mask * eta - courant * depth * (row + col - north_col)
                + there * packets.at_first(1, east, 0, 0))
    return west_row, west_mask, west_eta, eta, east_sum, courant * depth


def advanced(eta, row, col, mask, depth, east, south, west, north):
    row = mask * (row - courant * (east(eta) - eta))
    col = mask * (col - courant * (south(eta) - eta))
    return mask * eta - depth * (row - west(row) + col - north(col)), row, col


def two_steps(start, mask, depth, sides, base, north=None, south=None, second=None):
    lane, line = iota(mask.shape, 1), iota(mask.shape, 0)
    cols = mask.shape[1]
    west_row, west_mask, west_eta, east_eta, east_sum, east_depth = sides
    state = start, 0.0, 0.0
    flow, beyond = west_row, east_eta
    above = 0.0 if north is None else north[0]
    for number in range(2):
        below = 0.0 if south is None else south[number]
        state = advanced(
            *state, mask, depth,
            lambda eta: jnp.where(lane == cols - 1, beyond, rolled(eta, -1, 1)),
            lambda eta: jnp.where(line == TILE - 1, below, rolled(eta, -1, 0)),
            lambda row: jnp.where(lane == 0, flow, rolled(row, 1, 1)),
            lambda col: jnp.where(line == 0, above, rolled(col, 1, 0)))
        if number:
            return state
        eta, row, col = state
        if second is not None:
            eta = eta + jnp.where(line == 0, second, 0.0)
            state = eta, row, col
        whole_eta, whole_row = (eta, row) if base is None else (eta + base[0], row + base[1])
        flow = west_mask * (west_row - courant * (whole_eta[:, :1] - west_eta))
        beyond = east_sum + east_depth * whole_row[:, cols - 1:]
        if north is not None:
            above = north[1] * (north[0] - courant * (whole_eta[:1] - north[2]))


def north_of(links, packets, own, own_strip):
    cols = packets.cols
    lane = iota((1, LANES), 1)
    north, there = links.north(own)
    depth = packets.row(north, EDGE_DEPTH) * there
    mask = wet(depth)
    if packets.inflow_ref is not None:
        col = -courant * mask * own_strip
        return col, mask, -courant * depth * col
    col = packets.row(north, EDGE_FLOW) * there - courant * mask * own_strip
    north_east, beyond = links.east(north)
    right_eta = beyond * packets.column(north_east, FIRST_ETA)
    north_west, beyond = links.west(north)
    left_row = beyond * wet(packets.column(north_west, LAST_DEPTH)) * (
        packets.column(north_west, LAST_ROW)
        - courant * (packets.column(north, FIRST_ETA) - packets.column(north_west, LAST_ETA)))
    nothing = jnp.zeros((1, cols - LANES), jnp.float32)
    corners = (jnp.concatenate([jnp.where(lane == 0, rolled(left_row, 1, 1), 0.0), nothing], axis=1)
               + jnp.concatenate([nothing, jnp.where(lane == LANES - 1, courant * right_eta, 0.0)], axis=1))
    return col, mask, packets.row(north, EDGE_SUM) + courant * depth * (corners - col)


def as_sublanes(columns):
    rows = columns[0].shape[1]
    count = -len(columns) % TILE
    turned = jnp.concatenate(list(columns) + [jnp.zeros((count, rows), jnp.float32)], axis=0).T
    return [[turned[low:low + TILE, place:place + 1] for place in range(len(columns))]
            for low in (0, rows - TILE)]


def own_segment(subs):
    return lax.axis_index("patch") * subs + lax.axis_index("sub")


def halo_kernel(subs, links_ref, got_ref, later_ref, eta_after, momenta_after, wet_after, depth_after,
                eta_ends, row_ends, turned, eta_hbm, momenta_hbm, eta_out, momenta_out, ends_out,
                left_new, right_new, sems):
    del eta_hbm, momenta_hbm
    rows, cols = eta_after.shape
    right = cols - LANES
    links, own = Links(links_ref, subs), own_segment(subs)
    packets = Packets(got_ref, rows, cols)
    columns = beside(links, packets, own)
    west_row, west_mask, west_eta, east_eta, east_sum, east_depth = columns
    fields = eta_after, momenta_after.at[0], momenta_after.at[1]

    line = iota((TILE, rows), 0)
    lane = iota((TILE, rows), 1)
    nothing = jnp.zeros((TILE, rows), jnp.float32)

    def south(eta):
        return jnp.where(lane == rows - 1, 0.0, rolled(eta, -1, 1))

    def north(col):
        return jnp.where(lane == 0, 0.0, rolled(col, 1, 1))

    def column_steps(mask, depth, east, west):
        state = nothing, nothing, nothing
        for number in range(2):
            state = advanced(
                *state, mask, depth,
                lambda eta: jnp.where(line == TILE - 1, east(number, state), rolled(eta, -1, 0)), south,
                lambda row: jnp.where(line == 0, west(number, state), rolled(row, 1, 0)), north)
        return state

    def west_of(number, state):
        if number == 0:
            return west_row
        whole = state[0][:1] + turned[4, :1]
        return west_mask * (west_row - courant * (whole - west_eta))

    def east_of(number, state):
        if number == 0:
            return east_eta
        return east_sum + east_depth * (state[1][TILE - 1:] + turned[5, TILE - 1:])

    left = column_steps(turned[0], turned[1], lambda number, state: 0.0, west_of)
    last = column_steps(turned[2], turned[3], east_of, lambda number, state: 0.0)
    middle = jnp.zeros((LANES - 2 * TILE, rows), jnp.float32)
    lane = iota((rows, LANES), 1)
    body_rows = slice(TILE, rows - TILE)
    copies = []
    outs = eta_out.at[0], momenta_out.at[0, 0], momenta_out.at[1, 0]
    inner = pl.ds(TILE, rows - 2 * TILE)
    for place, field in enumerate(fields):
        more = jnp.concatenate([left[place], middle, last[place]], axis=0).T[body_rows]
        inside = iota(more.shape, 1)
        left_new[place] = field[body_rows, :LANES] + jnp.where(inside < TILE, more, 0.0)
        right_new[place] = field[body_rows, right:] + jnp.where(inside >= LANES - TILE, more, 0.0)
        copies += copied([
            (left_new.at[place], outs[place].at[inner, pl.ds(0, LANES)]),
            (right_new.at[place], outs[place].at[inner, pl.ds(right, LANES)]),
        ], sems.at[place])

    top_sides, low_sides = as_sublanes(columns)
    nothing = jnp.zeros((TILE, cols), jnp.float32)
    top = two_steps(
        nothing, wet_after[:TILE], depth_after[:TILE], top_sides, (eta_ends[0], row_ends[0]),
        north=north_of(links, packets, own, packets.row(own, STRIP)))
    below, there = links.south(own)
    low = two_steps(
        nothing, wet_after[rows - TILE:], depth_after[rows - TILE:], low_sides, (eta_ends[1], row_ends[1]),
        south=(packets.row(below, STRIP) * there, later_ref[below] * there))
    line, lane = iota((TILE, cols), 0), iota((TILE, cols), 1)
    for place, field in enumerate(fields):
        more = jnp.concatenate([left[place], middle, last[place]], axis=0).T
        gap = jnp.zeros((TILE, cols - 2 * LANES), jnp.float32)
        for end, (low_row, near, found) in enumerate(
                ((0, line < TILE // 2, top), (rows - TILE, line >= TILE // 2, low))):
            tile = more[low_row:low_row + TILE]
            inside = iota(tile.shape, 1)
            wide = jnp.concatenate(
                [jnp.where(inside < TILE, tile, 0.0), gap, jnp.where(inside >= LANES - TILE, tile, 0.0)], axis=1)
            ends_out[place, end] = field[low_row:low_row + TILE] + jnp.where(near, found[place], wide)
    for copy in copies:
        copy.wait()


def inflow_kernel(subs, links_ref, got_ref, finer_ref, wet_after, depth_after, ends_ref, eta_hbm, momenta_hbm,
                  eta_out, momenta_out, inflow_ref, new_ref, sems):
    del eta_hbm, momenta_hbm
    rows, cols = wet_after.shape
    count = got_ref.shape[0]
    links, own = Links(links_ref, subs), own_segment(subs)
    gain = stacked(got_ref, row_at(GAIN, cols))
    index = stacked(got_ref, row_at(INDEX, cols)).astype(jnp.int32)
    for number in range(2):
        inflow = gain * nested(finer_ref[number], index)
        for segment in range(count):
            inflow_ref[number * count + segment] = inflow[segment:segment + 1]
    packets = Packets(got_ref, rows, cols, inflow_ref)
    columns = beside(links, packets, own)
    top_sides, low_sides = as_sublanes(columns)
    line = iota((TILE, cols), 0)
    strip = packets.inflow(0, own)
    top = two_steps(
        jnp.where(line == 0, strip, 0.0), wet_after[:TILE], depth_after[:TILE], top_sides, None,
        north=north_of(links, packets, own, strip), second=packets.inflow(1, own))

    below, there = links.south(own)
    strip = packets.inflow(0, below) * there
    lane = iota((1, cols), 1)
    depth = packets.row(below, STRIP_DEPTH)
    mask = wet(depth)
    east, beyond = links.east(below)
    last_eta = rolled(packets.inflow(0, east, 0, LANES) * beyond, -1, 1)[:, LANES - 1:]
    after = jnp.where(lane == cols - 1, last_eta, rolled(strip, -1, 1))
    row = courant * mask * (strip - after)
    west, beyond = links.west(below)
    end = cols - LANES
    first_row = rolled(courant * wet(packets.row(west, STRIP_DEPTH, end, LANES)) * beyond * (
        packets.inflow(0, west, end, LANES) - rolled(strip[:, :LANES], -1, 1)), 1, 1)[:, :1]
    before = jnp.where(lane == 0, first_row, rolled(row, 1, 1))
    north, beyond = links.north(below)
    north_col = -courant * wet(packets.row(north, EDGE_DEPTH)) * beyond * strip
    later = there * (mask * strip - courant * depth * (row - before + courant * mask * strip - north_col)
                     + packets.inflow(1, below))
    low = two_steps(
        jnp.zeros((TILE, cols), jnp.float32), wet_after[rows - TILE:], depth_after[rows - TILE:],
        low_sides, None, south=(strip, later))
    copies = []
    outs = eta_out.at[0], momenta_out.at[0, 0], momenta_out.at[1, 0]
    for place, out in enumerate(outs):
        for end, (low_row, near, found) in enumerate(
                ((0, line < TILE // 2, top), (rows - TILE, line >= TILE // 2, low))):
            new_ref[place, end] = ends_ref[place, end] + jnp.where(near, found[place], 0.0)
        copies += copied([
            (new_ref.at[place, end], out.at[pl.ds(end * (rows - TILE), TILE), :]) for end in range(2)
        ], sems.at[place])
    for copy in copies:
        copy.wait()


def body(adjoint_height, adjoint_momenta, depth, wet_mask, adjacency, nest_gain, nest_index):
    rows, cols = adjoint_height.shape[1:]
    levels = lax.axis_size("level")
    subs = lax.axis_size("sub")
    count = lax.axis_size("patch") * subs
    params = pltpu.CompilerParams(vmem_limit_bytes=VMEM_LIMIT)
    vmem = pl.BlockSpec(memory_space=pltpu.VMEM)
    smem = pl.BlockSpec(memory_space=pltpu.SMEM)
    hbm = pl.BlockSpec(memory_space=pltpu.HBM)

    def array(*shape):
        return jax.ShapeDtypeStruct(shape, jnp.float32)

    def scratch(*shape):
        return pltpu.VMEM(shape, jnp.float32)

    fields = [pltpu.with_memory_space_constraint(field, pltpu.HBM)
              for field in (adjoint_height, adjoint_momenta, depth, wet_mask, nest_gain, nest_index)]
    packed = pl.pallas_call(
        pack_kernel,
        out_shape=array(count, 1, ROWS * cols + COLUMNS * LANES),
        in_specs=[hbm] * 6,
        out_specs=vmem,
        scratch_shapes=[
            scratch(2, 4, TILE, cols), pltpu.VMEM((2, TILE, cols), jnp.int32),
            scratch(2, 4, rows, LANES), pltpu.VMEM((2, rows, LANES), jnp.int32),
            scratch(levels, cols), pltpu.VMEM((levels, cols), jnp.int32),
            pltpu.SemaphoreType.DMA((22,)),
        ],
        compiler_params=params,
        name="pack",
    )(*fields)
    got = lax.all_to_all(packed, ("patch", "sub"), 0, 0, tiled=True)

    parts = 4
    eta_new, momenta_new, *after = pl.pallas_call(
        bulk_kernel,
        out_shape=[
            array(*adjoint_height.shape), array(*adjoint_momenta.shape),
            array(rows, cols), array(2, rows, cols), array(rows, cols), array(rows, cols),
            array(2, TILE, cols), array(2, TILE, cols), array(6, TILE, rows),
        ],
        in_specs=[hbm] * 4,
        out_specs=[hbm] * 2 + [vmem] * 7,
        scratch_shapes=[
            scratch(rows + 2 * TILE, cols), scratch(rows + 2 * TILE, cols),
            scratch(2, rows, cols), scratch(rows, cols), pltpu.VMEM((rows, cols), jnp.int32),
            scratch(rows, LANES), scratch(rows, LANES),
            pltpu.SemaphoreType.DMA((parts, 4)), pltpu.SemaphoreType.DMA((parts, 2)),
        ],
        compiler_params=params,
        name="bulk",
    )(*fields[:4])

    flux = ()
    laters = []
    for turn in range(levels - 1):
        strips, later = pl.pallas_call(
            functools.partial(strips_kernel, subs),
            out_shape=[array(2, count, cols), array(count, 1, cols)],
            in_specs=[smem, vmem, vmem] + [vmem] * len(flux),
            out_specs=[vmem, vmem],
            scratch_shapes=[scratch(count, cols), scratch(count, LANES)],
            compiler_params=params,
            name="strips",
        )(adjacency, got, after[-1], *flux)
        laters.append(later)
        flux = (lax.ppermute(strips, "level", [(source, source - 1) for source in range(1, levels)]),)

    eta_new, momenta_new, ends = pl.pallas_call(
        functools.partial(halo_kernel, subs),
        out_shape=[array(*adjoint_height.shape), array(*adjoint_momenta.shape), array(3, 2, TILE, cols)],
        in_specs=[smem] + [vmem] * 9 + [hbm] * 2,
        out_specs=[hbm, hbm, vmem],
        input_output_aliases={10: 0, 11: 1},
        scratch_shapes=[
            scratch(3, rows - 2 * TILE, LANES), scratch(3, rows - 2 * TILE, LANES), pltpu.SemaphoreType.DMA((3, 2)),
        ],
        compiler_params=params,
        name="halo",
    )(adjacency, got, laters[0], *after, eta_new, momenta_new)

    return pl.pallas_call(
        functools.partial(inflow_kernel, subs),
        out_shape=[array(*adjoint_height.shape), array(*adjoint_momenta.shape)],
        in_specs=[smem] + [vmem] * 5 + [hbm] * 2,
        out_specs=[hbm, hbm],
        input_output_aliases={6: 0, 7: 1},
        scratch_shapes=[
            scratch(2 * count, 1, cols), scratch(3, 2, TILE, cols), pltpu.SemaphoreType.DMA((3, 2)),
        ],
        compiler_params=params,
        name="inflow",
    )(adjacency, got, *flux, after[2], after[3], ends, eta_new, momenta_new)


def solution(mesh):
    in_specs = (
        P(("parts", "level"), ("patch", "sub"), None),
        P(None, ("parts", "level"), ("patch", "sub"), None),
        P("level", ("patch", "sub"), None),
        P("level", ("patch", "sub"), None),
        P("level", None, None),
        P(None, ("patch", "sub")),
        P(None, ("patch", "sub")),
    )
    out_specs = (
        P(("parts", "level"), ("patch", "sub"), None),
        P(None, ("parts", "level"), ("patch", "sub"), None),
    )
    return jax.shard_map(body, mesh=mesh, in_specs=in_specs, out_specs=out_specs, check_vma=False)
```

```python
import jax
import jax.numpy as jnp
from jax import lax
from jax.experimental import pallas as pl
from jax.experimental.pallas import tpu as pltpu
from jax.sharding import PartitionSpec as P

STEPS = 2
LANES = 128
TILE = 8
VMEM_LIMIT = 48 * 1024 * 1024

courant = 0.45

STRIP_SUM, STRIP, STRIP_DEPTH, GAIN, INDEX, EDGE_FLOW, EDGE_DEPTH, EDGE_SUM = range(8)
ROWS = 8
(FIRST_ETA, SECOND_ETA, FIRST_ROW, FIRST_COL, FIRST_DEPTH, NEXT_ETA, LAST_ETA, NEXT_ROW,
 LAST_ROW, LAST_COL, NEXT_DEPTH, LAST_DEPTH) = range(12)
COLUMNS = 12


def row_at(row, cols, left=0, size=None):
    return slice(row * cols + left, row * cols + left + (cols if size is None else size))


def column_at(column, cols):
    return slice(ROWS * cols + column * LANES, ROWS * cols + (column + 1) * LANES)


def iota(shape, axis):
    return lax.broadcasted_iota(jnp.int32, shape, axis)


def rolled(value, shift, axis):
    return pltpu.roll(value, shift % value.shape[axis], axis)


def wet(depth):
    return (depth > 0).astype(jnp.float32)


def copied(pairs, sems):
    copies = [pltpu.make_async_copy(source, target, sems.at[place]) for place, (source, target) in enumerate(pairs)]
    for copy in copies:
        copy.start()
    return copies


def pack_kernel(eta_ref, momenta_ref, depth_ref, wet_ref, gain_ref, index_ref, out_ref,
                ends, end_wet, sides, side_wet, gains, indices, sems):
    count = out_ref.shape[0]
    rows, cols = eta_ref.shape[1:]
    fields = eta_ref.at[0], momenta_ref.at[0, 0], momenta_ref.at[1, 0], depth_ref.at[0]
    pairs = []
    for end in range(2):
        tall = pl.ds(end * (rows - TILE), TILE)
        wide = pl.ds(end * (cols - LANES), LANES)
        for place, field in enumerate(fields):
            pairs.append((field.at[tall, :], ends.at[end, place]))
            pairs.append((field.at[:, wide], sides.at[end, place]))
        pairs.append((wet_ref.at[0, tall, :], end_wet.at[end]))
        pairs.append((wet_ref.at[0, :, wide], side_wet.at[end]))
    for copy in copied(pairs + [(gain_ref, gains), (index_ref, indices)], sems):
        copy.wait()
    level = lax.axis_index("level")
    lane = iota((TILE, cols), 1)

    def loaded(end):
        mask = end_wet[end].astype(jnp.float32)
        return ends[end, 0], ends[end, 1], ends[end, 2], mask * ends[end, 3], mask

    eta, row, col, depth, mask = loaded(0)
    east = jnp.where(lane == cols - 1, 0.0, rolled(eta, -1, 1))
    row = mask * (row - courant * (east - eta))
    west = jnp.where(lane == 0, 0.0, rolled(row, 1, 1))
    col = mask * (col - courant * (rolled(eta, -1, 0) - eta))
    strip_sum = mask * eta - courant * depth * (row - west + col)
    out_ref[0, :, row_at(STRIP_SUM, cols)] = strip_sum[:1]
    out_ref[0, :, row_at(STRIP, cols)] = eta[:1]
    out_ref[0, :, row_at(STRIP_DEPTH, cols)] = depth[:1]
    out_ref[0, :, row_at(GAIN, cols)] = gains[pl.ds(level, 1), :]
    out_ref[0, :, row_at(INDEX, cols)] = indices[pl.ds(level, 1), :].astype(jnp.float32)

    eta, row, col, depth, mask = loaded(1)
    east = jnp.where(lane == cols - 1, 0.0, rolled(eta, -1, 1))
    row = mask * (row - courant * (east - eta))
    west = jnp.where(lane == 0, 0.0, rolled(row, 1, 1))
    flow = mask * (col + courant * eta)
    above = rolled(flow - courant * mask * rolled(eta, -1, 0), 1, 0)
    edge_sum = mask * eta - courant * depth * (row - west - above)
    out_ref[0, :, row_at(EDGE_FLOW, cols)] = flow[TILE - 1:]
    out_ref[0, :, row_at(EDGE_DEPTH, cols)] = depth[TILE - 1:]
    out_ref[0, :, row_at(EDGE_SUM, cols)] = edge_sum[TILE - 1:]

    lane = iota((rows, LANES), 1)
    columns = jnp.zeros((rows, LANES), jnp.float32)
    depths = [sides[end, 3] * side_wet[end].astype(jnp.float32) for end in range(2)]
    for place, value, at in (
        (FIRST_ETA, sides[0, 0], 0), (SECOND_ETA, sides[0, 0], 1), (FIRST_ROW, sides[0, 1], 0),
        (FIRST_COL, sides[0, 2], 0), (FIRST_DEPTH, depths[0], 0),
        (NEXT_ETA, sides[1, 0], LANES - 2), (LAST_ETA, sides[1, 0], LANES - 1),
        (NEXT_ROW, sides[1, 1], LANES - 2), (LAST_ROW, sides[1, 1], LANES - 1),
        (LAST_COL, sides[1, 2], LANES - 1),
        (NEXT_DEPTH, depths[1], LANES - 2), (LAST_DEPTH, depths[1], LANES - 1),
    ):
        moved = value if place == at else rolled(value, place - at, 1)
        columns = jnp.where(lane == place, moved, columns)
    columns = columns.T
    for place in range(COLUMNS):
        out_ref[0, :, column_at(place, cols)] = columns[place:place + 1]
    packet = out_ref[0]
    for turn in range(1, count):
        out_ref[turn] = packet


def bulk_kernel(eta_ref, momenta_ref, depth_ref, wet_ref, eta_out, momenta_out,
                eta_after, momenta_after, wet_after, depth_after, eta_ends, row_ends, turned,
                eta_pad, col_pad, momenta_in, depth_in, wet_in, eta_left, row_right, sems, out_sems):
    rows, cols = eta_ref.shape[1:]
    parts = sems.shape[0]
    size = rows // parts
    loads = []
    for part in range(parts):
        here = pl.ds(part * size, size)
        loads.append(copied([
            (eta_ref.at[0, here, :], eta_pad.at[pl.ds(TILE + part * size, size), :]),
            (momenta_ref.at[:, 0, here, :], momenta_in.at[:, here, :]),
            (depth_ref.at[0, here, :], depth_in.at[here, :]),
            (wet_ref.at[0, here, :], wet_in.at[here, :]),
        ], sems.at[part]))
    lane = iota((TILE, cols), 1)
    eta_pad[TILE + rows:] = jnp.zeros((TILE, cols), jnp.float32)
    col_pad[:TILE] = jnp.zeros((TILE, cols), jnp.float32)

    def step(number, low):
        chunk, padded = slice(low, low + TILE), slice(TILE + low, 2 * TILE + low)
        eta = eta_pad[padded]
        if number == 0:
            mask = wet_in[chunk].astype(jnp.float32)
            depth = courant * mask * depth_in[chunk]
            wet_after[chunk] = mask
            depth_after[chunk] = depth
            row, col = momenta_in[0, chunk], momenta_in[1, chunk]
        else:
            mask, depth = wet_after[chunk], depth_after[chunk]
            row, col = momenta_after[0, chunk], col_pad[padded]
        east = jnp.where(lane == cols - 1, 0.0, rolled(eta, -1, 1))
        south = eta_pad[TILE + low + 1:2 * TILE + low + 1]
        row = mask * (row - courant * (east - eta))
        col = mask * (col - courant * (south - eta))
        momenta_after[0, chunk] = row
        col_pad[padded] = col
        if number:
            momenta_after[1, chunk] = col
        west = jnp.where(lane == 0, 0.0, rolled(row, 1, 1))
        north = col_pad[TILE + low - 1:2 * TILE + low - 1]
        eta = mask * eta - depth * (row - west + (col - north))
        if number:
            eta_after[chunk] = eta
            return
        eta_pad[padded] = eta
        eta_left[chunk] = eta[:, :LANES]
        row_right[chunk] = row[:, cols - LANES:]
        if low in (0, rows - TILE):
            end = int(low > 0)
            eta_ends[end] = eta
            row_ends[end] = row

    for copy in loads[0]:
        copy.wait()
    stores = []
    for part in range(parts + 1):
        if part + 1 < parts:
            for copy in loads[part + 1]:
                copy.wait()
        if part < parts:
            for low in range(part * size, (part + 1) * size, TILE):
                step(0, low)
        if part:
            for low in range((part - 1) * size, part * size, TILE):
                step(1, low)
            here = pl.ds((part - 1) * size, size)
            stores += copied([
                (eta_after.at[here, :], eta_out.at[0, here, :]),
                (momenta_after.at[:, here, :], momenta_out.at[:, 0, here, :]),
            ], out_sems.at[part - 1])
    right = cols - LANES
    turned[0] = wet_after[:, :LANES].T[:TILE]
    turned[1] = depth_after[:, :LANES].T[:TILE]
    turned[2] = wet_after[:, right:].T[LANES - TILE:]
    turned[3] = depth_after[:, right:].T[LANES - TILE:]
    turned[4] = eta_left[...].T[:TILE]
    turned[5] = row_right[...].T[LANES - TILE:]
    for copy in stores:
        copy.wait()


def after_kernel(value_ref, other_ref, out_ref):
    del value_ref, other_ref, out_ref


class Segment:
    def __init__(self, patch, flipped):
        self.patch, self.flipped = patch, flipped

    def place(self, patches):
        return self.flipped * patches + self.patch


class Links:
    def __init__(self, links_ref, patches):
        self.links_ref, self.patches = links_ref, patches
        self.half = lax.axis_index("sub")

    def own(self):
        return Segment(lax.axis_index("patch"), 0)

    def all(self):
        return [Segment(patch, flipped) for flipped in range(2) for patch in range(self.patches)]

    def across(self, segment, way):
        patch = self.links_ref[0, segment.patch, way]
        return jnp.maximum(patch, 0), jnp.where(patch >= 0, 1.0, 0.0)

    def other_half(self, segment, way, inner):
        patch, there = self.across(segment, way)
        inside = self.half == (inner ^ segment.flipped)
        return Segment(jnp.where(inside, segment.patch, patch), 1 - segment.flipped), jnp.where(inside, 1.0, there)

    def north(self, segment):
        return self.other_half(segment, 0, 1)

    def south(self, segment):
        return self.other_half(segment, 1, 0)

    def west(self, segment):
        patch, there = self.across(segment, 2)
        return Segment(patch, segment.flipped), there

    def east(self, segment):
        patch, there = self.across(segment, 3)
        return Segment(patch, segment.flipped), there


class Packets:
    def __init__(self, got_refs, rows, cols, inflow_ref=None):
        self.got_refs, self.rows, self.cols, self.inflow_ref = got_refs, rows, cols, inflow_ref
        self.patches = got_refs[0].shape[0]

    def row(self, segment, row, left=0, size=None):
        return self.got_refs[segment.flipped][segment.patch, :, row_at(row, self.cols, left, size)]

    def column(self, segment, column):
        return self.got_refs[segment.flipped][segment.patch, :, column_at(column, self.cols)]

    def rows_of(self, segments, row):
        return jnp.concatenate([self.row(segment, row) for segment in segments], axis=0)

    def columns_of(self, segments, column):
        return jnp.concatenate([self.column(segment, column) for segment in segments], axis=0)

    def field_row(self, segment, row, left=0, size=None):
        return self.row(segment, row, left, size) if self.inflow_ref is None else 0.0

    def field_column(self, segment, column):
        return self.column(segment, column) if self.inflow_ref is None else 0.0

    def inflow(self, step, segment, left=0, size=None):
        size = self.cols if size is None else size
        place = 2 * self.patches * step + segment.place(self.patches)
        return self.inflow_ref[place, :, left:left + size]

    def strip_tile(self, segment, left):
        if self.inflow_ref is None:
            return self.row(segment, STRIP, left, LANES)
        return self.inflow(0, segment, left, LANES)

    def at_first(self, step, segment, left, turned):
        if self.inflow_ref is None:
            return 0.0
        tile = self.inflow(step, segment, left, LANES)
        return jnp.where(iota((1, LANES), 1) == 0, rolled(tile, turned, 1) if turned else tile, 0.0)


def nested(flux, index):
    segments, cols = index.shape
    rows = []
    for low in range(0, segments, TILE):
        tiles = []
        for left in range(0, cols, LANES):
            at = index[low:low + TILE, left:left + LANES]
            lane, tile = at % LANES, at // LANES
            taken = jnp.zeros(at.shape, jnp.float32)
            for source in range(cols // LANES):
                values = flux[low:low + TILE, source * LANES:(source + 1) * LANES]
                found = jnp.take_along_axis(values, lane, axis=1, mode="promise_in_bounds")
                taken = jnp.where(tile == source, found, taken)
            tiles.append(taken)
        rows.append(jnp.concatenate(tiles, axis=1))
    return jnp.concatenate(rows, axis=0) if len(rows) > 1 else rows[0]


def strips_of(links, packets, finer, picked_ref, narrow_ref):
    count, cols = picked_ref.shape
    patches = packets.patches
    lane = iota((count, LANES), 1)
    every = links.all()
    strip, depth = packets.rows_of(every, STRIP), packets.rows_of(every, STRIP_DEPTH)
    mask = wet(depth)
    if finer is None:
        inflow = jnp.zeros_like(strip)
    else:
        gain = packets.rows_of(every, GAIN)
        index = packets.rows_of(every, INDEX).astype(jnp.int32)
        inflow = gain * nested(finer[0], index)
    eta = strip + inflow

    narrow_ref[...] = eta[:, :LANES]
    for place, segment in enumerate(every):
        east, there = links.east(segment)
        picked_ref[place:place + 1, :LANES] = narrow_ref[pl.ds(east.place(patches), 1), :] * there
    east_eta = rolled(picked_ref[:, :LANES], -1, 1)
    after = rolled(inflow, -1, 1)
    after = jnp.concatenate(
        [after[:, :-LANES], jnp.where(lane == LANES - 1, east_eta, after[:, -LANES:])], axis=1)
    more_row = courant * mask * (inflow - after)

    last_eta = packets.columns_of(every, LAST_ETA)
    last_row = packets.columns_of(every, LAST_ROW)
    first_of_last = rolled(last_row + courant * last_eta, -1, 1)
    narrow_ref[...] = mask[:, -LANES:] * first_of_last + more_row[:, -LANES:]
    for place, segment in enumerate(every):
        west, there = links.west(segment)
        picked_ref[place:place + 1, :LANES] = narrow_ref[pl.ds(west.place(patches), 1), :] * there
    west_row = rolled(picked_ref[:, :LANES], 1, 1)
    before = rolled(more_row, 1, 1)
    before = jnp.concatenate([jnp.where(lane == 0, west_row, before[:, :LANES]), before[:, LANES:]], axis=1)

    for place, segment in enumerate(every):
        north, there = links.north(segment)
        picked_ref[place:place + 1, :] = packets.row(north, EDGE_FLOW) * there
    flow = picked_ref[...]
    for place, segment in enumerate(every):
        north, there = links.north(segment)
        picked_ref[place:place + 1, :] = packets.row(north, EDGE_DEPTH) * there
    north_col = flow - courant * wet(picked_ref[...]) * eta
    later = (packets.rows_of(every, STRIP_SUM) + mask * inflow
             - courant * depth * (more_row - before + courant * mask * inflow - north_col))
    if finer is None:
        return eta, later
    return eta, later + gain * nested(finer[1], index)


def strips_kernel(*refs):
    links_ref, mine_ref, other_ref = refs[:3]
    out_ref, rows_ref, picked_ref, narrow_ref = refs[-4:]
    finer = (refs[3][0], refs[3][1]) if len(refs) == 8 else None
    links = Links(links_ref, mine_ref.shape[0])
    packets = Packets((mine_ref, other_ref), None, out_ref.shape[2])
    eta, later = strips_of(links, packets, finer, picked_ref, narrow_ref)
    out_ref[0] = eta
    out_ref[1] = later
    for place in range(out_ref.shape[1]):
        rows_ref[place] = later[place:place + 1]


def beside(links, packets, own):
    lane = iota((1, LANES), 1)
    first, last = lane == 0, lane == LANES - 1
    end = packets.cols - LANES

    def corner_col(segment, eta, left, turned):
        north, beyond = links.north(segment)
        flow = packets.field_row(north, EDGE_FLOW, left, LANES)
        mask = wet(packets.row(north, EDGE_DEPTH, left, LANES))
        if turned:
            flow = rolled(flow, turned, 1) if packets.inflow_ref is None else flow
            mask = rolled(mask, turned, 1)
        return beyond * (flow - courant * mask * eta)

    west, there = links.west(own)
    eta = packets.field_column(west, LAST_ETA) + packets.at_first(0, west, end, 1)
    next_eta = packets.field_column(west, NEXT_ETA) + packets.at_first(0, west, end, 2)
    own_eta = packets.field_column(own, FIRST_ETA) + packets.at_first(0, own, 0, 0)
    depth = packets.column(west, LAST_DEPTH) * there
    mask = wet(depth)
    next_row = wet(packets.column(west, NEXT_DEPTH)) * (
        packets.field_column(west, NEXT_ROW) - courant * (eta - next_eta))
    below, beyond = links.south(west)
    south_eta = jnp.where(last, packets.strip_tile(below, end) * beyond, rolled(eta, -1, 1))
    col = mask * (packets.field_column(west, LAST_COL) - courant * (south_eta - eta))
    north_col = jnp.where(first, corner_col(west, eta, end, 1), rolled(col, 1, 1))
    west_row = mask * (packets.field_column(west, LAST_ROW) - courant * (own_eta - eta))
    west_eta = (mask * eta - courant * depth * (west_row - next_row + col - north_col)
                + packets.at_first(1, west, end, 1))
    west_mask = mask

    east, there = links.east(own)
    eta = there * (packets.field_column(east, FIRST_ETA) + packets.at_first(0, east, 0, 0))
    second_eta = packets.field_column(east, SECOND_ETA) + packets.at_first(0, east, 0, -1)
    depth = packets.column(east, FIRST_DEPTH) * there
    mask = wet(depth)
    row = mask * (packets.field_column(east, FIRST_ROW) - courant * (second_eta - eta))
    below, beyond = links.south(east)
    south_eta = jnp.where(last, rolled(packets.strip_tile(below, 0), -1, 1) * beyond, rolled(eta, -1, 1))
    col = mask * (packets.field_column(east, FIRST_COL) - courant * (south_eta - eta))
    north_col = jnp.where(first, corner_col(east, eta, 0, 0), rolled(col, 1, 1))
    east_sum = (mask * eta - courant * depth * (row + col - north_col)
                + there * packets.at_first(1, east, 0, 0))
    return west_row, west_mask, west_eta, eta, east_sum, courant * depth


def advanced(eta, row, col, mask, depth, east, south, west, north):
    row = mask * (row - courant * (east(eta) - eta))
    col = mask * (col - courant * (south(eta) - eta))
    return mask * eta - depth * (row - west(row) + col - north(col)), row, col


def two_steps(start, mask, depth, sides, base, north=None, south=None, second=None):
    lane, line = iota(mask.shape, 1), iota(mask.shape, 0)
    cols = mask.shape[1]
    west_row, west_mask, west_eta, east_eta, east_sum, east_depth = sides
    state = start, 0.0, 0.0
    flow, beyond = west_row, east_eta
    above = 0.0 if north is None else north[0]
    for number in range(2):
        below = 0.0 if south is None else south[number]
        state = advanced(
            *state, mask, depth,
            lambda eta: jnp.where(lane == cols - 1, beyond, rolled(eta, -1, 1)),
            lambda eta: jnp.where(line == TILE - 1, below, rolled(eta, -1, 0)),
            lambda row: jnp.where(lane == 0, flow, rolled(row, 1, 1)),
            lambda col: jnp.where(line == 0, above, rolled(col, 1, 0)))
        if number:
            return state
        eta, row, col = state
        if second is not None:
            eta = eta + jnp.where(line == 0, second, 0.0)
            state = eta, row, col
        whole_eta, whole_row = (eta, row) if base is None else (eta + base[0], row + base[1])
        flow = west_mask * (west_row - courant * (whole_eta[:, :1] - west_eta))
        beyond = east_sum + east_depth * whole_row[:, cols - 1:]
        if north is not None:
            above = north[1] * (north[0] - courant * (whole_eta[:1] - north[2]))


def north_of(links, packets, own, own_strip):
    cols = packets.cols
    lane = iota((1, LANES), 1)
    north, there = links.north(own)
    depth = packets.row(north, EDGE_DEPTH) * there
    mask = wet(depth)
    if packets.inflow_ref is not None:
        col = -courant * mask * own_strip
        return col, mask, -courant * depth * col
    col = packets.row(north, EDGE_FLOW) * there - courant * mask * own_strip
    north_east, beyond = links.east(north)
    right_eta = beyond * packets.column(north_east, FIRST_ETA)
    north_west, beyond = links.west(north)
    left_row = beyond * wet(packets.column(north_west, LAST_DEPTH)) * (
        packets.column(north_west, LAST_ROW)
        - courant * (packets.column(north, FIRST_ETA) - packets.column(north_west, LAST_ETA)))
    nothing = jnp.zeros((1, cols - LANES), jnp.float32)
    corners = (jnp.concatenate([jnp.where(lane == 0, rolled(left_row, 1, 1), 0.0), nothing], axis=1)
               + jnp.concatenate([nothing, jnp.where(lane == LANES - 1, courant * right_eta, 0.0)], axis=1))
    return col, mask, packets.row(north, EDGE_SUM) + courant * depth * (corners - col)


def as_sublanes(columns):
    rows = columns[0].shape[1]
    count = -len(columns) % TILE
    turned = jnp.concatenate(list(columns) + [jnp.zeros((count, rows), jnp.float32)], axis=0).T
    return [[turned[low:low + TILE, place:place + 1] for place in range(len(columns))]
            for low in (0, rows - TILE)]


def halo_kernel(links_ref, mine_ref, other_ref, later_ref, eta_after, momenta_after, wet_after, depth_after,
                eta_ends, row_ends, turned, eta_hbm, momenta_hbm, eta_out, momenta_out, ends_out,
                left_new, right_new, sems):
    del eta_hbm, momenta_hbm
    rows, cols = eta_after.shape
    right = cols - LANES
    links = Links(links_ref, mine_ref.shape[0])
    own = links.own()
    packets = Packets((mine_ref, other_ref), rows, cols)
    columns = beside(links, packets, own)
    west_row, west_mask, west_eta, east_eta, east_sum, east_depth = columns
    fields = eta_after, momenta_after.at[0], momenta_after.at[1]

    line = iota((TILE, rows), 0)
    lane = iota((TILE, rows), 1)
    nothing = jnp.zeros((TILE, rows), jnp.float32)

    def south(eta):
        return jnp.where(lane == rows - 1, 0.0, rolled(eta, -1, 1))

    def north(col):
        return jnp.where(lane == 0, 0.0, rolled(col, 1, 1))

    def column_steps(mask, depth, east, west):
        state = nothing, nothing, nothing
        for number in range(2):
            state = advanced(
                *state, mask, depth,
                lambda eta: jnp.where(line == TILE - 1, east(number, state), rolled(eta, -1, 0)), south,
                lambda row: jnp.where(line == 0, west(number, state), rolled(row, 1, 0)), north)
        return state

    def west_of(number, state):
        if number == 0:
            return west_row
        whole = state[0][:1] + turned[4, :1]
        return west_mask * (west_row - courant * (whole - west_eta))

    def east_of(number, state):
        if number == 0:
            return east_eta
        return east_sum + east_depth * (state[1][TILE - 1:] + turned[5, TILE - 1:])

    left = column_steps(turned[0], turned[1], lambda number, state: 0.0, west_of)
    last = column_steps(turned[2], turned[3], east_of, lambda number, state: 0.0)
    middle = jnp.zeros((LANES - 2 * TILE, rows), jnp.float32)
    lane = iota((rows, LANES), 1)
    body_rows = slice(TILE, rows - TILE)
    copies = []
    outs = eta_out.at[0], momenta_out.at[0, 0], momenta_out.at[1, 0]
    inner = pl.ds(TILE, rows - 2 * TILE)
    for place, field in enumerate(fields):
        more = jnp.concatenate([left[place], middle, last[place]], axis=0).T[body_rows]
        inside = iota(more.shape, 1)
        left_new[place] = field[body_rows, :LANES] + jnp.where(inside < TILE, more, 0.0)
        right_new[place] = field[body_rows, right:] + jnp.where(inside >= LANES - TILE, more, 0.0)
        copies += copied([
            (left_new.at[place], outs[place].at[inner, pl.ds(0, LANES)]),
            (right_new.at[place], outs[place].at[inner, pl.ds(right, LANES)]),
        ], sems.at[place])

    top_sides, low_sides = as_sublanes(columns)
    nothing = jnp.zeros((TILE, cols), jnp.float32)
    top = two_steps(
        nothing, wet_after[:TILE], depth_after[:TILE], top_sides, (eta_ends[0], row_ends[0]),
        north=north_of(links, packets, own, packets.row(own, STRIP)))
    below, there = links.south(own)
    low = two_steps(
        nothing, wet_after[rows - TILE:], depth_after[rows - TILE:], low_sides, (eta_ends[1], row_ends[1]),
        south=(packets.row(below, STRIP) * there, later_ref[below.place(packets.patches)] * there))
    line, lane = iota((TILE, cols), 0), iota((TILE, cols), 1)
    for place, field in enumerate(fields):
        more = jnp.concatenate([left[place], middle, last[place]], axis=0).T
        gap = jnp.zeros((TILE, cols - 2 * LANES), jnp.float32)
        for end, (low_row, near, found) in enumerate(
                ((0, line < TILE // 2, top), (rows - TILE, line >= TILE // 2, low))):
            tile = more[low_row:low_row + TILE]
            inside = iota(tile.shape, 1)
            wide = jnp.concatenate(
                [jnp.where(inside < TILE, tile, 0.0), gap, jnp.where(inside >= LANES - TILE, tile, 0.0)], axis=1)
            ends_out[place, end] = field[low_row:low_row + TILE] + jnp.where(near, found[place], wide)
    for copy in copies:
        copy.wait()


def inflow_kernel(links_ref, mine_ref, other_ref, finer_ref, wet_after, depth_after, ends_ref, eta_hbm, momenta_hbm,
                  eta_out, momenta_out, inflow_ref, new_ref, sems):
    del eta_hbm, momenta_hbm
    rows, cols = wet_after.shape
    links = Links(links_ref, mine_ref.shape[0])
    own, every = links.own(), links.all()
    packets = Packets((mine_ref, other_ref), rows, cols, inflow_ref)
    gain = packets.rows_of(every, GAIN)
    index = packets.rows_of(every, INDEX).astype(jnp.int32)
    for number in range(2):
        inflow = gain * nested(finer_ref[number], index)
        for place in range(len(every)):
            inflow_ref[number * len(every) + place] = inflow[place:place + 1]
    columns = beside(links, packets, own)
    top_sides, low_sides = as_sublanes(columns)
    line = iota((TILE, cols), 0)
    strip = packets.inflow(0, own)
    top = two_steps(
        jnp.where(line == 0, strip, 0.0), wet_after[:TILE], depth_after[:TILE], top_sides, None,
        north=north_of(links, packets, own, strip), second=packets.inflow(1, own))

    below, there = links.south(own)
    strip = packets.inflow(0, below) * there
    lane = iota((1, cols), 1)
    depth = packets.row(below, STRIP_DEPTH)
    mask = wet(depth)
    east, beyond = links.east(below)
    last_eta = rolled(packets.inflow(0, east, 0, LANES) * beyond, -1, 1)[:, LANES - 1:]
    after = jnp.where(lane == cols - 1, last_eta, rolled(strip, -1, 1))
    row = courant * mask * (strip - after)
    west, beyond = links.west(below)
    end = cols - LANES
    first_row = rolled(courant * wet(packets.row(west, STRIP_DEPTH, end, LANES)) * beyond * (
        packets.inflow(0, west, end, LANES) - rolled(strip[:, :LANES], -1, 1)), 1, 1)[:, :1]
    before = jnp.where(lane == 0, first_row, rolled(row, 1, 1))
    north, beyond = links.north(below)
    north_col = -courant * wet(packets.row(north, EDGE_DEPTH)) * beyond * strip
    later = there * (mask * strip - courant * depth * (row - before + courant * mask * strip - north_col)
                     + packets.inflow(1, below))
    low = two_steps(
        jnp.zeros((TILE, cols), jnp.float32), wet_after[rows - TILE:], depth_after[rows - TILE:],
        low_sides, None, south=(strip, later))
    copies = []
    outs = eta_out.at[0], momenta_out.at[0, 0], momenta_out.at[1, 0]
    for place, out in enumerate(outs):
        for end, (low_row, near, found) in enumerate(
                ((0, line < TILE // 2, top), (rows - TILE, line >= TILE // 2, low))):
            new_ref[place, end] = ends_ref[place, end] + jnp.where(near, found[place], 0.0)
        copies += copied([
            (new_ref.at[place, end], out.at[pl.ds(end * (rows - TILE), TILE), :]) for end in range(2)
        ], sems.at[place])
    for copy in copies:
        copy.wait()


def body(adjoint_height, adjoint_momenta, depth, wet_mask, adjacency, nest_gain, nest_index):
    rows, cols = adjoint_height.shape[1:]
    levels = lax.axis_size("level")
    patches = lax.axis_size("patch")
    count = 2 * patches
    params = pltpu.CompilerParams(vmem_limit_bytes=VMEM_LIMIT)
    vmem = pl.BlockSpec(memory_space=pltpu.VMEM)
    smem = pl.BlockSpec(memory_space=pltpu.SMEM)
    hbm = pl.BlockSpec(memory_space=pltpu.HBM)

    def array(*shape):
        return jax.ShapeDtypeStruct(shape, jnp.float32)

    def scratch(*shape):
        return pltpu.VMEM(shape, jnp.float32)

    fields = [pltpu.with_memory_space_constraint(field, pltpu.HBM)
              for field in (adjoint_height, adjoint_momenta, depth, wet_mask, nest_gain, nest_index)]
    packed = pl.pallas_call(
        pack_kernel,
        out_shape=pltpu.VMEM((patches, 1, ROWS * cols + COLUMNS * LANES), jnp.float32),
        in_specs=[hbm] * 6,
        out_specs=vmem,
        scratch_shapes=[
            scratch(2, 4, TILE, cols), pltpu.VMEM((2, TILE, cols), jnp.int32),
            scratch(2, 4, rows, LANES), pltpu.VMEM((2, rows, LANES), jnp.int32),
            scratch(levels, cols), pltpu.VMEM((levels, cols), jnp.int32),
            pltpu.SemaphoreType.DMA((22,)),
        ],
        compiler_params=params,
        name="pack",
    )(*fields)
    parts = 4
    eta_new, momenta_new, *after = pl.pallas_call(
        bulk_kernel,
        out_shape=[
            array(*adjoint_height.shape), array(*adjoint_momenta.shape),
            array(rows, cols), array(2, rows, cols), array(rows, cols), array(rows, cols),
            array(2, TILE, cols), array(2, TILE, cols), array(6, TILE, rows),
        ],
        in_specs=[hbm] * 4,
        out_specs=[hbm] * 2 + [vmem] * 7,
        scratch_shapes=[
            scratch(rows + 2 * TILE, cols), scratch(rows + 2 * TILE, cols),
            scratch(2, rows, cols), scratch(rows, cols), pltpu.VMEM((rows, cols), jnp.int32),
            scratch(rows, LANES), scratch(rows, LANES),
            pltpu.SemaphoreType.DMA((parts, 4)), pltpu.SemaphoreType.DMA((parts, 2)),
        ],
        compiler_params=params,
        name="bulk",
    )(*fields[:4])

    mine = pl.pallas_call(
        after_kernel,
        out_shape=array(*packed.shape),
        in_specs=[vmem, vmem],
        out_specs=vmem,
        input_output_aliases={0: 0},
        compiler_params=params,
        name="after",
    )(lax.all_to_all(packed, "patch", 0, 0, tiled=True), after[-1])
    other = lax.ppermute(mine, "sub", [(0, 1), (1, 0)])

    flux = ()
    laters = []
    for turn in range(levels - 1):
        strips, later = pl.pallas_call(
            strips_kernel,
            out_shape=[array(2, count, cols), array(count, 1, cols)],
            in_specs=[smem] + [vmem] * (2 + len(flux)),
            out_specs=[vmem, vmem],
            scratch_shapes=[scratch(count, cols), scratch(count, LANES)],
            compiler_params=params,
            name="strips",
        )(adjacency, mine, other, *flux)
        laters.append(later)
        flux = (lax.ppermute(strips, "level", [(source, source - 1) for source in range(1, levels)]),)

    eta_new, momenta_new, ends = pl.pallas_call(
        halo_kernel,
        out_shape=[array(*adjoint_height.shape), array(*adjoint_momenta.shape), array(3, 2, TILE, cols)],
        in_specs=[smem] + [vmem] * 10 + [hbm] * 2,
        out_specs=[hbm, hbm, vmem],
        input_output_aliases={11: 0, 12: 1},
        scratch_shapes=[
            scratch(3, rows - 2 * TILE, LANES), scratch(3, rows - 2 * TILE, LANES), pltpu.SemaphoreType.DMA((3, 2)),
        ],
        compiler_params=params,
        name="halo",
    )(adjacency, mine, other, laters[0], *after, eta_new, momenta_new)

    return pl.pallas_call(
        inflow_kernel,
        out_shape=[array(*adjoint_height.shape), array(*adjoint_momenta.shape)],
        in_specs=[smem] + [vmem] * 6 + [hbm] * 2,
        out_specs=[hbm, hbm],
        input_output_aliases={7: 0, 8: 1},
        scratch_shapes=[
            scratch(2 * count, 1, cols), scratch(3, 2, TILE, cols), pltpu.SemaphoreType.DMA((3, 2)),
        ],
        compiler_params=params,
        name="inflow",
    )(adjacency, mine, other, *flux, after[2], after[3], ends, eta_new, momenta_new)


def solution(mesh):
    in_specs = (
        P(("parts", "level"), ("patch", "sub"), None),
        P(None, ("parts", "level"), ("patch", "sub"), None),
        P("level", ("patch", "sub"), None),
        P("level", ("patch", "sub"), None),
        P("level", None, None),
        P(None, ("patch", "sub")),
        P(None, ("patch", "sub")),
    )
    out_specs = (
        P(("parts", "level"), ("patch", "sub"), None),
        P(None, ("parts", "level"), ("patch", "sub"), None),
    )
    return jax.shard_map(body, mesh=mesh, in_specs=in_specs, out_specs=out_specs, check_vma=False)
```

```python
import jax
import jax.numpy as jnp
from jax import lax
from jax.experimental import pallas as pl
from jax.experimental.pallas import tpu as pltpu
from jax.sharding import PartitionSpec as P

STEPS = 2
LANES = 128
TILE = 8
VMEM_LIMIT = 48 * 1024 * 1024

courant = 0.45

STRIP_SUM, STRIP, STRIP_DEPTH, GAIN, INDEX, EDGE_FLOW, EDGE_DEPTH, EDGE_SUM = range(8)
(FIRST_ETA, SECOND_ETA, FIRST_ROW, FIRST_COL, FIRST_DEPTH, NEXT_ETA, LAST_ETA, NEXT_ROW,
 LAST_ROW, LAST_COL, NEXT_DEPTH, LAST_DEPTH) = range(12)
ROWS, COLUMNS = 8, 16
LINES = ROWS * TILE + COLUMNS


def iota(shape, axis):
    return lax.broadcasted_iota(jnp.int32, shape, axis)


def rolled(value, shift, axis):
    if shift == 0:
        return value
    return pltpu.roll(value, shift % value.shape[axis], axis)


def wet(depth):
    return (depth > 0).astype(jnp.float32)


def copied(pairs, sems):
    copies = [pltpu.make_async_copy(source, target, sems.at[place]) for place, (source, target) in enumerate(pairs)]
    for copy in copies:
        copy.start()
    return copies


def pack_kernel(eta_ref, momenta_ref, depth_ref, wet_ref, gain_ref, index_ref, out_ref,
                ends, end_wet, sides, side_wet, gains, indices, packet, sems, out_sems):
    rows, cols = eta_ref.shape[1:]
    fields = eta_ref.at[0], momenta_ref.at[0, 0], momenta_ref.at[1, 0], depth_ref.at[0]
    tall, wide = [], []
    for end in range(2):
        here = pl.ds(end * (rows - TILE), TILE)
        tall += [(field.at[here, :], ends.at[end, place]) for place, field in enumerate(fields)]
        tall.append((wet_ref.at[0, here, :], end_wet.at[end]))
        here = pl.ds(end * (cols - LANES), LANES)
        wide += [(field.at[:, here], sides.at[end, place]) for place, field in enumerate(fields)]
        wide.append((wet_ref.at[0, :, here], side_wet.at[end]))
    tall += [(gain_ref, gains), (index_ref, indices)]
    copies = copied(tall + wide, sems)
    for copy in copies[:len(tall)]:
        copy.wait()
    level = lax.axis_index("level")
    lane = iota((TILE, cols), 1)

    def loaded(end):
        mask = end_wet[end].astype(jnp.float32)
        return ends[end, 0], ends[end, 1], ends[end, 2], mask * ends[end, 3], mask

    def put(row, value):
        for tile in range(TILE):
            packet[row * TILE + tile:row * TILE + tile + 1] = value[:, tile * LANES:(tile + 1) * LANES]

    eta, row, col, depth, mask = loaded(0)
    east = jnp.where(lane == cols - 1, 0.0, rolled(eta, -1, 1))
    row = mask * (row - courant * (east - eta))
    west = jnp.where(lane == 0, 0.0, rolled(row, 1, 1))
    col = mask * (col - courant * (rolled(eta, -1, 0) - eta))
    strip_sum = mask * eta - courant * depth * (row - west + col)
    put(STRIP_SUM, strip_sum[:1])
    put(STRIP, eta[:1])
    put(STRIP_DEPTH, depth[:1])
    put(GAIN, gains[pl.ds(level, 1), :])
    put(INDEX, indices[pl.ds(level, 1), :].astype(jnp.float32))

    eta, row, col, depth, mask = loaded(1)
    east = jnp.where(lane == cols - 1, 0.0, rolled(eta, -1, 1))
    row = mask * (row - courant * (east - eta))
    west = jnp.where(lane == 0, 0.0, rolled(row, 1, 1))
    flow = mask * (col + courant * eta)
    above = rolled(flow - courant * mask * rolled(eta, -1, 0), 1, 0)
    edge_sum = mask * eta - courant * depth * (row - west - above)
    put(EDGE_FLOW, flow[TILE - 1:])
    put(EDGE_DEPTH, depth[TILE - 1:])
    put(EDGE_SUM, edge_sum[TILE - 1:])
    lines = pl.ds(0, ROWS * TILE)
    out_copies = copied(
        [(packet.at[lines], out_ref.at[turn, lines]) for turn in range(out_ref.shape[0])], out_sems.at[0])

    for copy in copies[len(tall):]:
        copy.wait()
    lane = iota((rows, LANES), 1)
    columns = jnp.zeros((rows, LANES), jnp.float32)
    depths = [sides[end, 3] * side_wet[end].astype(jnp.float32) for end in range(2)]
    for place, value, at in (
        (FIRST_ETA, sides[0, 0], 0), (SECOND_ETA, sides[0, 0], 1), (FIRST_ROW, sides[0, 1], 0),
        (FIRST_COL, sides[0, 2], 0), (FIRST_DEPTH, depths[0], 0),
        (NEXT_ETA, sides[1, 0], LANES - 2), (LAST_ETA, sides[1, 0], LANES - 1),
        (NEXT_ROW, sides[1, 1], LANES - 2), (LAST_ROW, sides[1, 1], LANES - 1),
        (LAST_COL, sides[1, 2], LANES - 1),
        (NEXT_DEPTH, depths[1], LANES - 2), (LAST_DEPTH, depths[1], LANES - 1),
    ):
        moved = value if place == at else rolled(value, place - at, 1)
        columns = jnp.where(lane == place, moved, columns)
    packet[ROWS * TILE:] = columns.T[:COLUMNS]
    lines = pl.ds(ROWS * TILE, COLUMNS)
    out_copies += copied(
        [(packet.at[lines], out_ref.at[turn, lines]) for turn in range(out_ref.shape[0])], out_sems.at[1])
    for copy in out_copies:
        copy.wait()


def bulk_kernel(eta_ref, momenta_ref, depth_ref, wet_ref, eta_out, momenta_out,
                eta_after, momenta_after, wet_after, depth_after, eta_ends, row_ends, turned,
                eta_pad, col_pad, momenta_in, depth_in, wet_in, eta_left, row_right, sems, out_sems):
    rows, cols = eta_ref.shape[1:]
    parts = sems.shape[0]
    size = rows // parts
    loads = []
    for part in range(parts):
        here = pl.ds(part * size, size)
        loads.append(copied([
            (eta_ref.at[0, here, :], eta_pad.at[pl.ds(TILE + part * size, size), :]),
            (momenta_ref.at[:, 0, here, :], momenta_in.at[:, here, :]),
            (depth_ref.at[0, here, :], depth_in.at[here, :]),
            (wet_ref.at[0, here, :], wet_in.at[here, :]),
        ], sems.at[part]))
    lane = iota((TILE, cols), 1)
    eta_pad[TILE + rows:] = jnp.zeros((TILE, cols), jnp.float32)
    col_pad[:TILE] = jnp.zeros((TILE, cols), jnp.float32)

    def step(number, low):
        chunk, padded = slice(low, low + TILE), slice(TILE + low, 2 * TILE + low)
        eta = eta_pad[padded]
        if number == 0:
            mask = wet_in[chunk].astype(jnp.float32)
            depth = courant * mask * depth_in[chunk]
            wet_after[chunk] = mask
            depth_after[chunk] = depth
            row, col = momenta_in[0, chunk], momenta_in[1, chunk]
        else:
            mask, depth = wet_after[chunk], depth_after[chunk]
            row, col = momenta_after[0, chunk], col_pad[padded]
        east = jnp.where(lane == cols - 1, 0.0, rolled(eta, -1, 1))
        south = eta_pad[TILE + low + 1:2 * TILE + low + 1]
        row = mask * (row - courant * (east - eta))
        col = mask * (col - courant * (south - eta))
        momenta_after[0, chunk] = row
        col_pad[padded] = col
        if number:
            momenta_after[1, chunk] = col
        west = jnp.where(lane == 0, 0.0, rolled(row, 1, 1))
        north = col_pad[TILE + low - 1:2 * TILE + low - 1]
        eta = mask * eta - depth * (row - west + (col - north))
        if number:
            eta_after[chunk] = eta
            return
        eta_pad[padded] = eta
        eta_left[chunk] = eta[:, :LANES]
        row_right[chunk] = row[:, cols - LANES:]
        if low in (0, rows - TILE):
            end = int(low > 0)
            eta_ends[end] = eta
            row_ends[end] = row

    for copy in loads[0]:
        copy.wait()
    stores = []
    for part in range(parts + 1):
        if part + 1 < parts:
            for copy in loads[part + 1]:
                copy.wait()
        if part < parts:
            for low in range(part * size, (part + 1) * size, TILE):
                step(0, low)
        if part:
            for low in range((part - 1) * size, part * size, TILE):
                step(1, low)
            here = pl.ds((part - 1) * size, size)
            stores += copied([
                (eta_after.at[here, :], eta_out.at[0, here, :]),
                (momenta_after.at[:, here, :], momenta_out.at[:, 0, here, :]),
            ], out_sems.at[part - 1])
    right = cols - LANES
    turned[0] = wet_after[:, :LANES].T[:TILE]
    turned[1] = depth_after[:, :LANES].T[:TILE]
    turned[2] = wet_after[:, right:].T[LANES - TILE:]
    turned[3] = depth_after[:, right:].T[LANES - TILE:]
    turned[4] = eta_left[...].T[:TILE]
    turned[5] = row_right[...].T[LANES - TILE:]
    for copy in stores:
        copy.wait()


def after_kernel(value_ref, other_ref, out_ref):
    del value_ref, other_ref, out_ref


class Segment:
    def __init__(self, patch, flipped):
        self.patch, self.flipped = patch, flipped

    def place(self, patches):
        return self.flipped * patches + self.patch


class Links:
    def __init__(self, links_ref, patches):
        self.links_ref, self.patches = links_ref, patches
        self.half = lax.axis_index("sub")

    def own(self):
        return Segment(lax.axis_index("patch"), 0)

    def all(self):
        return [Segment(patch, flipped) for flipped in range(2) for patch in range(self.patches)]

    def across(self, segment, way):
        patch = self.links_ref[0, segment.patch, way]
        return jnp.maximum(patch, 0), jnp.where(patch >= 0, 1.0, 0.0)

    def other_half(self, segment, way, inner):
        patch, there = self.across(segment, way)
        inside = self.half == (inner ^ segment.flipped)
        return Segment(jnp.where(inside, segment.patch, patch), 1 - segment.flipped), jnp.where(inside, 1.0, there)

    def north(self, segment):
        return self.other_half(segment, 0, 1)

    def south(self, segment):
        return self.other_half(segment, 1, 0)

    def west(self, segment):
        patch, there = self.across(segment, 2)
        return Segment(patch, segment.flipped), there

    def east(self, segment):
        patch, there = self.across(segment, 3)
        return Segment(patch, segment.flipped), there


class Packets:
    def __init__(self, got_refs):
        self.got_refs = got_refs

    def tile(self, segment, row):
        return self.got_refs[segment.flipped][segment.patch, row * TILE:(row + 1) * TILE]

    def line(self, segment, row, line):
        return self.got_refs[segment.flipped][segment.patch, row * TILE + line:row * TILE + line + 1]

    def row(self, segment, row):
        return jnp.concatenate([self.line(segment, row, line) for line in range(TILE)], axis=1)

    def column(self, segment, column):
        return self.line(segment, ROWS, column)


def is_first(shape=(TILE, LANES)):
    return (iota(shape, 0) == 0) & (iota(shape, 1) == 0)


def is_last(shape=(TILE, LANES)):
    return (iota(shape, 0) == shape[0] - 1) & (iota(shape, 1) == shape[1] - 1)


def next_cells(tile, edge):
    lane = iota(tile.shape, 1)
    moved = rolled(tile, -1, 1)
    moved = jnp.where(lane == LANES - 1, rolled(moved, -1, 0), moved)
    return jnp.where(is_last(), edge, moved)


def last_cells(tile, edge):
    lane = iota(tile.shape, 1)
    moved = rolled(tile, 1, 1)
    moved = jnp.where(lane == 0, rolled(moved, 1, 0), moved)
    return jnp.where(is_first(), edge, moved)


def row_of(ref, place):
    return jnp.concatenate([ref[place, line:line + 1] for line in range(TILE)], axis=1)


def nested(flux, index):
    lane, line = index % LANES, index // LANES
    taken = jnp.zeros(index.shape, jnp.float32)
    for source in range(TILE):
        values = jnp.broadcast_to(flux[source:source + 1], index.shape)
        found = jnp.take_along_axis(values, lane, axis=1, mode="promise_in_bounds")
        taken = jnp.where(line == source, found, taken)
    return taken


def strips_kernel(*refs):
    links_ref, mine_ref, other_ref = refs[:3]
    out_ref = refs[-1]
    finer_ref = refs[3] if len(refs) == 5 else None
    links = Links(links_ref, mine_ref.shape[0])
    patches, count = links.patches, 2 * links.patches
    packets = Packets((mine_ref, other_ref))
    inflows = []
    for segment in links.all():
        eta = packets.tile(segment, STRIP)
        if finer_ref is not None:
            place = segment.place(patches)
            gain, index = packets.tile(segment, GAIN), packets.tile(segment, INDEX).astype(jnp.int32)
            inflow, later = [gain * nested(finer_ref[step * count + place], index) for step in range(2)]
            inflows.append((inflow, later))
            eta = eta + inflow
        out_ref[segment.place(patches)] = eta
    for segment in links.all():
        place = segment.place(patches)
        eta, depth = out_ref[place], packets.tile(segment, STRIP_DEPTH)
        mask = wet(depth)
        east, there = links.east(segment)
        edge = there * rolled(rolled(out_ref[east.place(patches)], -1, 1), -1, 0)
        if finer_ref is None:
            row = jnp.where(is_last(), -courant * mask * edge, 0.0)
        else:
            inflow, later = inflows[place]
            row = courant * mask * (inflow - next_cells(inflow, edge))
        west, there = links.west(segment)
        west_eta = rolled(rolled(out_ref[west.place(patches)], 1, 1), 1, 0)
        west_mask = rolled(rolled(wet(packets.tile(west, STRIP_DEPTH)), 1, 1), 1, 0)
        edge = there * west_mask * (packets.column(west, LAST_ROW) - courant * (eta - west_eta))
        north, there = links.north(segment)
        col = there * (packets.tile(north, EDGE_FLOW) - courant * wet(packets.tile(north, EDGE_DEPTH)) * eta)
        total = packets.tile(segment, STRIP_SUM)
        if finer_ref is None:
            total = total - courant * depth * (row - jnp.where(is_first(), edge, 0.0) - col)
        else:
            total = (total + mask * inflow + later
                     - courant * depth * (row - last_cells(row, edge) + courant * mask * inflow - col))
        out_ref[count + place] = total


def beside(links, packets, own, inflow=None):
    lane = iota((1, LANES), 1)
    first, last = lane == 0, lane == LANES - 1

    def field(segment, column):
        return packets.column(segment, column) if inflow is None else 0.0

    def strip(name, turned):
        return 0.0 if inflow is None else jnp.where(first, rolled(inflow[name], turned, 1), 0.0)

    def corner_col(segment, eta, line, turned):
        north, beyond = links.north(segment)
        mask = rolled(wet(packets.line(north, EDGE_DEPTH, line)), turned, 1)
        flow = rolled(packets.line(north, EDGE_FLOW, line), turned, 1) if inflow is None else 0.0
        return beyond * (flow - courant * mask * eta)

    west, there = links.west(own)
    eta = field(west, LAST_ETA) + strip("west", 1)
    next_eta = field(west, NEXT_ETA) + strip("west", 2)
    own_eta = field(own, FIRST_ETA) + strip("own", 0)
    depth = packets.column(west, LAST_DEPTH) * there
    mask = wet(depth)
    next_row = wet(packets.column(west, NEXT_DEPTH)) * (field(west, NEXT_ROW) - courant * (eta - next_eta))
    below, beyond = links.south(west)
    corner = packets.line(below, STRIP, TILE - 1) if inflow is None else inflow["south west"]
    south_eta = jnp.where(last, corner * beyond, rolled(eta, -1, 1))
    col = mask * (field(west, LAST_COL) - courant * (south_eta - eta))
    north_col = jnp.where(first, corner_col(west, eta, TILE - 1, 1), rolled(col, 1, 1))
    west_row = mask * (field(west, LAST_ROW) - courant * (own_eta - eta))
    west_eta = (mask * eta - courant * depth * (west_row - next_row + col - north_col) + strip("west later", 1))
    west_mask = mask

    east, there = links.east(own)
    eta = there * (field(east, FIRST_ETA) + strip("east", 0))
    second_eta = field(east, SECOND_ETA) + strip("east", -1)
    depth = packets.column(east, FIRST_DEPTH) * there
    mask = wet(depth)
    row = mask * (field(east, FIRST_ROW) - courant * (second_eta - eta))
    below, beyond = links.south(east)
    corner = packets.line(below, STRIP, 0) if inflow is None else inflow["south east"]
    south_eta = jnp.where(last, rolled(corner, -1, 1) * beyond, rolled(eta, -1, 1))
    col = mask * (field(east, FIRST_COL) - courant * (south_eta - eta))
    north_col = jnp.where(first, corner_col(east, eta, 0, 0), rolled(col, 1, 1))
    east_sum = mask * eta - courant * depth * (row + col - north_col) + there * strip("east later", 0)
    return west_row, west_mask, west_eta, eta, east_sum, courant * depth


def advanced(eta, row, col, mask, depth, east, south, west, north):
    row = mask * (row - courant * (east(eta) - eta))
    col = mask * (col - courant * (south(eta) - eta))
    return mask * eta - depth * (row - west(row) + col - north(col)), row, col


def two_steps(start, mask, depth, sides, base, north=None, south=None, second=None):
    lane, line = iota(mask.shape, 1), iota(mask.shape, 0)
    cols = mask.shape[1]
    west_row, west_mask, west_eta, east_eta, east_sum, east_depth = sides
    state = start, 0.0, 0.0
    flow, beyond = west_row, east_eta
    above = 0.0 if north is None else north[0]
    for number in range(2):
        below = 0.0 if south is None else south[number]
        state = advanced(
            *state, mask, depth,
            lambda eta: jnp.where(lane == cols - 1, beyond, rolled(eta, -1, 1)),
            lambda eta: jnp.where(line == TILE - 1, below, rolled(eta, -1, 0)),
            lambda row: jnp.where(lane == 0, flow, rolled(row, 1, 1)),
            lambda col: jnp.where(line == 0, above, rolled(col, 1, 0)))
        if number:
            return state
        eta, row, col = state
        if second is not None:
            eta = eta + jnp.where(line == 0, second, 0.0)
            state = eta, row, col
        whole_eta, whole_row = (eta, row) if base is None else (eta + base[0], row + base[1])
        flow = west_mask * (west_row - courant * (whole_eta[:, :1] - west_eta))
        beyond = east_sum + east_depth * whole_row[:, cols - 1:]
        if north is not None:
            above = north[1] * (north[0] - courant * (whole_eta[:1] - north[2]))


def north_of(links, packets, own, own_strip, inflow=None):
    cols = own_strip.shape[1]
    lane = iota((1, LANES), 1)
    north, there = links.north(own)
    depth = packets.row(north, EDGE_DEPTH) * there
    mask = wet(depth)
    if inflow is not None:
        col = -courant * mask * own_strip
        return col, mask, -courant * depth * col
    col = packets.row(north, EDGE_FLOW) * there - courant * mask * own_strip
    north_east, beyond = links.east(north)
    right_eta = beyond * packets.column(north_east, FIRST_ETA)
    north_west, beyond = links.west(north)
    left_row = beyond * wet(packets.column(north_west, LAST_DEPTH)) * (
        packets.column(north_west, LAST_ROW)
        - courant * (packets.column(north, FIRST_ETA) - packets.column(north_west, LAST_ETA)))
    nothing = jnp.zeros((1, cols - LANES), jnp.float32)
    corners = (jnp.concatenate([jnp.where(lane == 0, rolled(left_row, 1, 1), 0.0), nothing], axis=1)
               + jnp.concatenate([nothing, jnp.where(lane == LANES - 1, courant * right_eta, 0.0)], axis=1))
    return col, mask, packets.row(north, EDGE_SUM) + courant * depth * (corners - col)


def as_sublanes(columns):
    rows = columns[0].shape[1]
    count = -len(columns) % TILE
    turned = jnp.concatenate(list(columns) + [jnp.zeros((count, rows), jnp.float32)], axis=0).T
    return [[turned[low:low + TILE, place:place + 1] for place in range(len(columns))]
            for low in (0, rows - TILE)]


def halo_kernel(links_ref, mine_ref, other_ref, strips_ref, eta_after, momenta_after, wet_after, depth_after,
                eta_ends, row_ends, turned, eta_hbm, momenta_hbm, eta_out, momenta_out, ends_out,
                left_new, right_new, sems):
    del eta_hbm, momenta_hbm
    rows, cols = eta_after.shape
    right = cols - LANES
    links = Links(links_ref, mine_ref.shape[0])
    own = links.own()
    packets = Packets((mine_ref, other_ref))
    columns = beside(links, packets, own)
    west_row, west_mask, west_eta, east_eta, east_sum, east_depth = columns
    fields = eta_after, momenta_after.at[0], momenta_after.at[1]

    line = iota((TILE, rows), 0)
    lane = iota((TILE, rows), 1)
    nothing = jnp.zeros((TILE, rows), jnp.float32)

    def south(eta):
        return jnp.where(lane == rows - 1, 0.0, rolled(eta, -1, 1))

    def north(col):
        return jnp.where(lane == 0, 0.0, rolled(col, 1, 1))

    def column_steps(mask, depth, east, west):
        state = nothing, nothing, nothing
        for number in range(2):
            state = advanced(
                *state, mask, depth,
                lambda eta: jnp.where(line == TILE - 1, east(number, state), rolled(eta, -1, 0)), south,
                lambda row: jnp.where(line == 0, west(number, state), rolled(row, 1, 0)), north)
        return state

    def west_of(number, state):
        if number == 0:
            return west_row
        whole = state[0][:1] + turned[4, :1]
        return west_mask * (west_row - courant * (whole - west_eta))

    def east_of(number, state):
        if number == 0:
            return east_eta
        return east_sum + east_depth * (state[1][TILE - 1:] + turned[5, TILE - 1:])

    left = column_steps(turned[0], turned[1], lambda number, state: 0.0, west_of)
    last = column_steps(turned[2], turned[3], east_of, lambda number, state: 0.0)
    middle = jnp.zeros((LANES - 2 * TILE, rows), jnp.float32)
    lane = iota((rows, LANES), 1)
    body_rows = slice(TILE, rows - TILE)
    copies = []
    outs = eta_out.at[0], momenta_out.at[0, 0], momenta_out.at[1, 0]
    inner = pl.ds(TILE, rows - 2 * TILE)
    for place, field in enumerate(fields):
        more = jnp.concatenate([left[place], middle, last[place]], axis=0).T[body_rows]
        inside = iota(more.shape, 1)
        left_new[place] = field[body_rows, :LANES] + jnp.where(inside < TILE, more, 0.0)
        right_new[place] = field[body_rows, right:] + jnp.where(inside >= LANES - TILE, more, 0.0)
        copies += copied([
            (left_new.at[place], outs[place].at[inner, pl.ds(0, LANES)]),
            (right_new.at[place], outs[place].at[inner, pl.ds(right, LANES)]),
        ], sems.at[place])

    top_sides, low_sides = as_sublanes(columns)
    nothing = jnp.zeros((TILE, cols), jnp.float32)
    top = two_steps(
        nothing, wet_after[:TILE], depth_after[:TILE], top_sides, (eta_ends[0], row_ends[0]),
        north=north_of(links, packets, own, packets.row(own, STRIP)))
    below, there = links.south(own)
    low = two_steps(
        nothing, wet_after[rows - TILE:], depth_after[rows - TILE:], low_sides, (eta_ends[1], row_ends[1]),
        south=(packets.row(below, STRIP) * there, row_of(strips_ref, 2 * links.patches + below.place(links.patches)) * there))
    line, lane = iota((TILE, cols), 0), iota((TILE, cols), 1)
    for place, field in enumerate(fields):
        more = jnp.concatenate([left[place], middle, last[place]], axis=0).T
        gap = jnp.zeros((TILE, cols - 2 * LANES), jnp.float32)
        for end, (low_row, near, found) in enumerate(
                ((0, line < TILE // 2, top), (rows - TILE, line >= TILE // 2, low))):
            tile = more[low_row:low_row + TILE]
            inside = iota(tile.shape, 1)
            wide = jnp.concatenate(
                [jnp.where(inside < TILE, tile, 0.0), gap, jnp.where(inside >= LANES - TILE, tile, 0.0)], axis=1)
            ends_out[place, end] = field[low_row:low_row + TILE] + jnp.where(near, found[place], wide)
    for copy in copies:
        copy.wait()


def inflow_kernel(links_ref, mine_ref, other_ref, finer_ref, wet_after, depth_after, ends_ref, eta_hbm, momenta_hbm,
                  eta_out, momenta_out, rows_ref, new_ref, sems):
    del eta_hbm, momenta_hbm
    rows, cols = wet_after.shape
    links = Links(links_ref, mine_ref.shape[0])
    patches = links.patches
    own = links.own()
    packets = Packets((mine_ref, other_ref))

    def flux_place(step, segment):
        return step * 2 * patches + segment.place(patches)

    def inflows(segment):
        gain, index = packets.tile(segment, GAIN), packets.tile(segment, INDEX).astype(jnp.int32)
        return [gain * nested(finer_ref[flux_place(step, segment)], index) for step in range(2)]

    below, there = links.south(own)
    west, east = links.west(own)[0], links.east(own)[0]
    below_west, beyond_west = links.west(below)
    below_east, beyond_east = links.east(below)
    wanted = (
        ("west", 0, west, TILE - 1), ("west later", 1, west, TILE - 1), ("east", 0, east, 0),
        ("east later", 1, east, 0), ("south west", 0, links.south(west)[0], TILE - 1),
        ("south east", 0, links.south(east)[0], 0), ("below west", 0, below_west, TILE - 1),
        ("below east", 0, below_east, 0))
    gain = jnp.concatenate([packets.line(segment, GAIN, line) for _, _, segment, line in wanted], axis=0)
    index = jnp.concatenate([packets.line(segment, INDEX, line) for _, _, segment, line in wanted], axis=0)
    index = index.astype(jnp.int32)
    lane, line = index % LANES, index // LANES
    taken = jnp.zeros((TILE, LANES), jnp.float32)
    for source in range(TILE):
        values = jnp.concatenate(
            [finer_ref[flux_place(step, segment), source:source + 1] for _, step, segment, _ in wanted], axis=0)
        found = jnp.take_along_axis(values, lane, axis=1, mode="promise_in_bounds")
        taken = jnp.where(line == source, found, taken)
    taken = gain * taken
    inflow = {name: taken[place:place + 1] for place, (name, _, _, _) in enumerate(wanted)}

    rows_ref[0], rows_ref[1] = inflows(own)
    strip, later = inflows(below)
    strip, later = strip * there, later * there
    inflow["own"] = rows_ref[0, :1]

    depth = packets.tile(below, STRIP_DEPTH)
    mask = wet(depth)
    edge = jnp.broadcast_to(rolled(inflow["below east"] * beyond_east, -1, 1), (TILE, LANES))
    row = courant * mask * (strip - next_cells(strip, edge))
    west_mask = rolled(wet(packets.line(below_west, STRIP_DEPTH, TILE - 1)), 1, 1)
    edge = beyond_west * courant * west_mask * (rolled(inflow["below west"], 1, 1) - strip[:1])
    edge = jnp.broadcast_to(edge, (TILE, LANES))
    north, beyond = links.north(below)
    col = -courant * wet(packets.tile(north, EDGE_DEPTH)) * beyond * strip
    rows_ref[2] = strip
    rows_ref[3] = there * (
        mask * strip - courant * depth * (row - last_cells(row, edge) + courant * mask * strip - col) + later)

    columns = beside(links, packets, own, inflow)
    top_sides, low_sides = as_sublanes(columns)
    line = iota((TILE, cols), 0)
    strip = row_of(rows_ref, 0)
    top = two_steps(
        jnp.where(line == 0, strip, 0.0), wet_after[:TILE], depth_after[:TILE], top_sides, None,
        north=north_of(links, packets, own, strip, inflow), second=row_of(rows_ref, 1))
    low = two_steps(
        jnp.zeros((TILE, cols), jnp.float32), wet_after[rows - TILE:], depth_after[rows - TILE:],
        low_sides, None, south=(row_of(rows_ref, 2), row_of(rows_ref, 3)))
    copies = []
    outs = eta_out.at[0], momenta_out.at[0, 0], momenta_out.at[1, 0]
    for end, (near, found) in enumerate(((line < TILE // 2, top), (line >= TILE // 2, low))):
        for place in range(3):
            new_ref[place, end] = ends_ref[place, end] + jnp.where(near, found[place], 0.0)
        copies += copied([
            (new_ref.at[place, end], out.at[pl.ds(end * (rows - TILE), TILE), :]) for place, out in enumerate(outs)
        ], sems.at[end])
    for copy in copies:
        copy.wait()


def body(adjoint_height, adjoint_momenta, depth, wet_mask, adjacency, nest_gain, nest_index):
    rows, cols = adjoint_height.shape[1:]
    levels = lax.axis_size("level")
    patches = lax.axis_size("patch")
    count = 2 * patches
    params = pltpu.CompilerParams(vmem_limit_bytes=VMEM_LIMIT)
    vmem = pl.BlockSpec(memory_space=pltpu.VMEM)
    smem = pl.BlockSpec(memory_space=pltpu.SMEM)
    hbm = pl.BlockSpec(memory_space=pltpu.HBM)

    def array(*shape):
        return jax.ShapeDtypeStruct(shape, jnp.float32)

    def scratch(*shape):
        return pltpu.VMEM(shape, jnp.float32)

    fields = [pltpu.with_memory_space_constraint(field, pltpu.HBM)
              for field in (adjoint_height, adjoint_momenta, depth, wet_mask, nest_gain, nest_index)]
    packed = pl.pallas_call(
        pack_kernel,
        out_shape=array(patches, LINES, LANES),
        in_specs=[hbm] * 6,
        out_specs=hbm,
        scratch_shapes=[
            scratch(2, 4, TILE, cols), pltpu.VMEM((2, TILE, cols), jnp.int32),
            scratch(2, 4, rows, LANES), pltpu.VMEM((2, rows, LANES), jnp.int32),
            scratch(levels, cols), pltpu.VMEM((levels, cols), jnp.int32),
            scratch(LINES, LANES), pltpu.SemaphoreType.DMA((22,)), pltpu.SemaphoreType.DMA((2, patches)),
        ],
        compiler_params=params,
        name="pack",
    )(*fields)
    parts = 4
    eta_new, momenta_new, *after = pl.pallas_call(
        bulk_kernel,
        out_shape=[
            array(*adjoint_height.shape), array(*adjoint_momenta.shape),
            array(rows, cols), array(2, rows, cols), array(rows, cols), array(rows, cols),
            array(2, TILE, cols), array(2, TILE, cols), array(6, TILE, rows),
        ],
        in_specs=[hbm] * 4,
        out_specs=[hbm] * 2 + [vmem] * 7,
        scratch_shapes=[
            scratch(rows + 2 * TILE, cols), scratch(rows + 2 * TILE, cols),
            scratch(2, rows, cols), scratch(rows, cols), pltpu.VMEM((rows, cols), jnp.int32),
            scratch(rows, LANES), scratch(rows, LANES),
            pltpu.SemaphoreType.DMA((parts, 4)), pltpu.SemaphoreType.DMA((parts, 2)),
        ],
        compiler_params=params,
        name="bulk",
    )(*fields[:4])

    mine = pl.pallas_call(
        after_kernel,
        out_shape=array(*packed.shape),
        in_specs=[vmem, vmem],
        out_specs=vmem,
        input_output_aliases={0: 0},
        compiler_params=params,
        name="after",
    )(lax.all_to_all(packed, "patch", 0, 0, tiled=True), after[-1])
    other = lax.ppermute(mine, "sub", [(0, 1), (1, 0)])

    flux = ()
    strips = []
    for turn in range(levels - 1):
        strips.append(pl.pallas_call(
            strips_kernel,
            out_shape=array(2 * count, TILE, LANES),
            in_specs=[smem] + [vmem] * (2 + len(flux)),
            out_specs=vmem,
            compiler_params=params,
            name="strips",
        )(adjacency, mine, other, *flux))
        flux = (lax.ppermute(strips[-1], "level", [(source, source - 1) for source in range(1, levels)]),)

    eta_new, momenta_new, ends = pl.pallas_call(
        halo_kernel,
        out_shape=[array(*adjoint_height.shape), array(*adjoint_momenta.shape), array(3, 2, TILE, cols)],
        in_specs=[smem] + [vmem] * 10 + [hbm] * 2,
        out_specs=[hbm, hbm, vmem],
        input_output_aliases={11: 0, 12: 1},
        scratch_shapes=[
            scratch(3, rows - 2 * TILE, LANES), scratch(3, rows - 2 * TILE, LANES), pltpu.SemaphoreType.DMA((3, 2)),
        ],
        compiler_params=params,
        name="halo",
    )(adjacency, mine, other, strips[0], *after, eta_new, momenta_new)

    return pl.pallas_call(
        inflow_kernel,
        out_shape=[array(*adjoint_height.shape), array(*adjoint_momenta.shape)],
        in_specs=[smem] + [vmem] * 6 + [hbm] * 2,
        out_specs=[hbm, hbm],
        input_output_aliases={7: 0, 8: 1},
        scratch_shapes=[
            scratch(4, TILE, LANES), scratch(3, 2, TILE, cols), pltpu.SemaphoreType.DMA((2, 3)),
        ],
        compiler_params=params,
        name="inflow",
    )(adjacency, mine, other, *flux, after[2], after[3], ends, eta_new, momenta_new)


def solution(mesh):
    in_specs = (
        P(("parts", "level"), ("patch", "sub"), None),
        P(None, ("parts", "level"), ("patch", "sub"), None),
        P("level", ("patch", "sub"), None),
        P("level", ("patch", "sub"), None),
        P("level", None, None),
        P(None, ("patch", "sub")),
        P(None, ("patch", "sub")),
    )
    out_specs = (
        P(("parts", "level"), ("patch", "sub"), None),
        P(None, ("parts", "level"), ("patch", "sub"), None),
    )
    return jax.shard_map(body, mesh=mesh, in_specs=in_specs, out_specs=out_specs, check_vma=False)
```

```python
import jax
import jax.numpy as jnp
from jax import lax
from jax.experimental import pallas as pl
from jax.experimental.pallas import tpu as pltpu
from jax.sharding import PartitionSpec as P

STEPS = 2
LANES = 128
TILE = 8
VMEM_LIMIT = 48 * 1024 * 1024

courant = 0.45

STRIP_SUM, STRIP, STRIP_DEPTH, GAIN, INDEX, EDGE_FLOW, EDGE_DEPTH, EDGE_SUM = range(8)
(FIRST_ETA, SECOND_ETA, FIRST_ROW, FIRST_COL, FIRST_DEPTH, NEXT_ETA, LAST_ETA, NEXT_ROW,
 LAST_ROW, LAST_COL, NEXT_DEPTH, LAST_DEPTH) = range(12)
ROWS, COLUMNS = 8, 16
LINES = ROWS * TILE + COLUMNS


def iota(shape, axis):
    return lax.broadcasted_iota(jnp.int32, shape, axis)


def rolled(value, shift, axis):
    if shift == 0:
        return value
    return pltpu.roll(value, shift % value.shape[axis], axis)


def wet(depth):
    return (depth > 0).astype(jnp.float32)


def copied(pairs, sems):
    copies = [pltpu.make_async_copy(source, target, sems.at[place]) for place, (source, target) in enumerate(pairs)]
    for copy in copies:
        copy.start()
    return copies


def pack_kernel(eta_ref, momenta_ref, depth_ref, wet_ref, gain_ref, index_ref, out_ref,
                ends, end_wet, sides, side_wet, gains, indices, sems):
    rows, cols = eta_ref.shape[1:]
    fields = eta_ref.at[0], momenta_ref.at[0, 0], momenta_ref.at[1, 0], depth_ref.at[0]
    tall, wide = [], []
    for end in range(2):
        here = pl.ds(end * (rows - TILE), TILE)
        tall += [(field.at[here, :], ends.at[end, place]) for place, field in enumerate(fields)]
        tall.append((wet_ref.at[0, here, :], end_wet.at[end]))
        here = pl.ds(end * (cols - LANES), LANES)
        wide += [(field.at[:, here], sides.at[end, place]) for place, field in enumerate(fields)]
        wide.append((wet_ref.at[0, :, here], side_wet.at[end]))
    tall += [(gain_ref, gains), (index_ref, indices)]
    copies = copied(tall + wide, sems)
    for copy in copies[:len(tall)]:
        copy.wait()
    level = lax.axis_index("level")
    lane = iota((TILE, cols), 1)

    def loaded(end):
        mask = end_wet[end].astype(jnp.float32)
        return ends[end, 0], ends[end, 1], ends[end, 2], mask * ends[end, 3], mask

    def put(row, value):
        for tile in range(TILE):
            out_ref[row * TILE + tile:row * TILE + tile + 1] = value[:, tile * LANES:(tile + 1) * LANES]

    eta, row, col, depth, mask = loaded(0)
    east = jnp.where(lane == cols - 1, 0.0, rolled(eta, -1, 1))
    row = mask * (row - courant * (east - eta))
    west = jnp.where(lane == 0, 0.0, rolled(row, 1, 1))
    col = mask * (col - courant * (rolled(eta, -1, 0) - eta))
    strip_sum = mask * eta - courant * depth * (row - west + col)
    put(STRIP_SUM, strip_sum[:1])
    put(STRIP, eta[:1])
    put(STRIP_DEPTH, depth[:1])
    put(GAIN, gains[pl.ds(level, 1), :])
    put(INDEX, indices[pl.ds(level, 1), :].astype(jnp.float32))

    eta, row, col, depth, mask = loaded(1)
    east = jnp.where(lane == cols - 1, 0.0, rolled(eta, -1, 1))
    row = mask * (row - courant * (east - eta))
    west = jnp.where(lane == 0, 0.0, rolled(row, 1, 1))
    flow = mask * (col + courant * eta)
    above = rolled(flow - courant * mask * rolled(eta, -1, 0), 1, 0)
    edge_sum = mask * eta - courant * depth * (row - west - above)
    put(EDGE_FLOW, flow[TILE - 1:])
    put(EDGE_DEPTH, depth[TILE - 1:])
    put(EDGE_SUM, edge_sum[TILE - 1:])

    for copy in copies[len(tall):]:
        copy.wait()
    lane = iota((rows, LANES), 1)
    columns = jnp.zeros((rows, LANES), jnp.float32)
    depths = [sides[end, 3] * side_wet[end].astype(jnp.float32) for end in range(2)]
    for place, value, at in (
        (FIRST_ETA, sides[0, 0], 0), (SECOND_ETA, sides[0, 0], 1), (FIRST_ROW, sides[0, 1], 0),
        (FIRST_COL, sides[0, 2], 0), (FIRST_DEPTH, depths[0], 0),
        (NEXT_ETA, sides[1, 0], LANES - 2), (LAST_ETA, sides[1, 0], LANES - 1),
        (NEXT_ROW, sides[1, 1], LANES - 2), (LAST_ROW, sides[1, 1], LANES - 1),
        (LAST_COL, sides[1, 2], LANES - 1),
        (NEXT_DEPTH, depths[1], LANES - 2), (LAST_DEPTH, depths[1], LANES - 1),
    ):
        moved = value if place == at else rolled(value, place - at, 1)
        columns = jnp.where(lane == place, moved, columns)
    out_ref[ROWS * TILE:] = columns.T[:COLUMNS]


def bulk_kernel(eta_ref, momenta_ref, depth_ref, wet_ref, eta_out, momenta_out,
                eta_after, momenta_after, wet_after, depth_after, eta_ends, row_ends, turned,
                eta_pad, col_pad, momenta_in, depth_in, wet_in, eta_left, row_right, sems, out_sems):
    rows, cols = eta_ref.shape[1:]
    parts = sems.shape[0]
    size = rows // parts
    loads = []
    for part in range(parts):
        here = pl.ds(part * size, size)
        loads.append(copied([
            (eta_ref.at[0, here, :], eta_pad.at[pl.ds(TILE + part * size, size), :]),
            (momenta_ref.at[:, 0, here, :], momenta_in.at[:, here, :]),
            (depth_ref.at[0, here, :], depth_in.at[here, :]),
            (wet_ref.at[0, here, :], wet_in.at[here, :]),
        ], sems.at[part]))
    lane = iota((TILE, cols), 1)
    eta_pad[TILE + rows:] = jnp.zeros((TILE, cols), jnp.float32)
    col_pad[:TILE] = jnp.zeros((TILE, cols), jnp.float32)

    def step(number, low):
        chunk, padded = slice(low, low + TILE), slice(TILE + low, 2 * TILE + low)
        eta = eta_pad[padded]
        if number == 0:
            mask = wet_in[chunk].astype(jnp.float32)
            depth = courant * mask * depth_in[chunk]
            wet_after[chunk] = mask
            depth_after[chunk] = depth
            row, col = momenta_in[0, chunk], momenta_in[1, chunk]
        else:
            mask, depth = wet_after[chunk], depth_after[chunk]
            row, col = momenta_after[0, chunk], col_pad[padded]
        east = jnp.where(lane == cols - 1, 0.0, rolled(eta, -1, 1))
        south = eta_pad[TILE + low + 1:2 * TILE + low + 1]
        row = mask * (row - courant * (east - eta))
        col = mask * (col - courant * (south - eta))
        momenta_after[0, chunk] = row
        col_pad[padded] = col
        if number:
            momenta_after[1, chunk] = col
        west = jnp.where(lane == 0, 0.0, rolled(row, 1, 1))
        north = col_pad[TILE + low - 1:2 * TILE + low - 1]
        eta = mask * eta - depth * (row - west + (col - north))
        if number:
            eta_after[chunk] = eta
            return
        eta_pad[padded] = eta
        eta_left[chunk] = eta[:, :LANES]
        row_right[chunk] = row[:, cols - LANES:]
        if low in (0, rows - TILE):
            end = int(low > 0)
            eta_ends[end] = eta
            row_ends[end] = row

    for copy in loads[0]:
        copy.wait()
    stores = []
    for part in range(parts + 1):
        if part + 1 < parts:
            for copy in loads[part + 1]:
                copy.wait()
        if part < parts:
            for low in range(part * size, (part + 1) * size, TILE):
                step(0, low)
        if part:
            for low in range((part - 1) * size, part * size, TILE):
                step(1, low)
            here = pl.ds((part - 1) * size, size)
            stores += copied([
                (eta_after.at[here, :], eta_out.at[0, here, :]),
                (momenta_after.at[:, here, :], momenta_out.at[:, 0, here, :]),
            ], out_sems.at[part - 1])
    right = cols - LANES
    turned[0] = wet_after[:, :LANES].T[:TILE]
    turned[1] = depth_after[:, :LANES].T[:TILE]
    turned[2] = wet_after[:, right:].T[LANES - TILE:]
    turned[3] = depth_after[:, right:].T[LANES - TILE:]
    turned[4] = eta_left[...].T[:TILE]
    turned[5] = row_right[...].T[LANES - TILE:]
    for copy in stores:
        copy.wait()


def gather_kernel(*refs):
    packets, out_ref = refs[:-2], refs[-1]
    own = lax.axis_index("patch")
    for turn, packet in enumerate(packets):
        out_ref[own ^ turn] = packet[...]


class Segment:
    def __init__(self, patch, flipped):
        self.patch, self.flipped = patch, flipped

    def place(self, patches):
        return self.flipped * patches + self.patch


class Links:
    def __init__(self, links_ref, patches):
        self.links_ref, self.patches = links_ref, patches
        self.half = lax.axis_index("sub")

    def own(self):
        return Segment(lax.axis_index("patch"), 0)

    def all(self):
        return [Segment(patch, flipped) for flipped in range(2) for patch in range(self.patches)]

    def across(self, segment, way):
        patch = self.links_ref[0, segment.patch, way]
        return jnp.maximum(patch, 0), jnp.where(patch >= 0, 1.0, 0.0)

    def other_half(self, segment, way, inner):
        patch, there = self.across(segment, way)
        inside = self.half == (inner ^ segment.flipped)
        return Segment(jnp.where(inside, segment.patch, patch), 1 - segment.flipped), jnp.where(inside, 1.0, there)

    def north(self, segment):
        return self.other_half(segment, 0, 1)

    def south(self, segment):
        return self.other_half(segment, 1, 0)

    def west(self, segment):
        patch, there = self.across(segment, 2)
        return Segment(patch, segment.flipped), there

    def east(self, segment):
        patch, there = self.across(segment, 3)
        return Segment(patch, segment.flipped), there


class Packets:
    def __init__(self, got_refs):
        self.got_refs = got_refs

    def tile(self, segment, row):
        return self.got_refs[segment.flipped][segment.patch, row * TILE:(row + 1) * TILE]

    def line(self, segment, row, line):
        return self.got_refs[segment.flipped][segment.patch, row * TILE + line:row * TILE + line + 1]

    def row(self, segment, row):
        return jnp.concatenate([self.line(segment, row, line) for line in range(TILE)], axis=1)

    def column(self, segment, column):
        return self.line(segment, ROWS, column)


def is_first(shape=(TILE, LANES)):
    return (iota(shape, 0) == 0) & (iota(shape, 1) == 0)


def is_last(shape=(TILE, LANES)):
    return (iota(shape, 0) == shape[0] - 1) & (iota(shape, 1) == shape[1] - 1)


def next_cells(tile, edge):
    lane = iota(tile.shape, 1)
    moved = rolled(tile, -1, 1)
    moved = jnp.where(lane == LANES - 1, rolled(moved, -1, 0), moved)
    return jnp.where(is_last(), edge, moved)


def last_cells(tile, edge):
    lane = iota(tile.shape, 1)
    moved = rolled(tile, 1, 1)
    moved = jnp.where(lane == 0, rolled(moved, 1, 0), moved)
    return jnp.where(is_first(), edge, moved)


def row_of(ref, place):
    return jnp.concatenate([ref[place, line:line + 1] for line in range(TILE)], axis=1)


def nested(flux, index):
    lane, line = index % LANES, index // LANES
    taken = jnp.zeros(index.shape, jnp.float32)
    for source in range(TILE):
        values = jnp.broadcast_to(flux[source:source + 1], index.shape)
        found = jnp.take_along_axis(values, lane, axis=1, mode="promise_in_bounds")
        taken = jnp.where(line == source, found, taken)
    return taken


def strips_kernel(*refs):
    links_ref, mine_ref, other_ref = refs[:3]
    out_ref, strips_ref = refs[-2:]
    finer_ref = refs[3] if len(refs) == 6 else None
    links = Links(links_ref, mine_ref.shape[0])
    patches, count = links.patches, 2 * links.patches
    packets = Packets((mine_ref, other_ref))
    every = links.all()
    strips, inflows = [], []
    for segment in every:
        strip = packets.tile(segment, STRIP)
        if finer_ref is not None:
            place = segment.place(patches)
            gain, index = packets.tile(segment, GAIN), packets.tile(segment, INDEX).astype(jnp.int32)
            inflow, later = [gain * nested(finer_ref[step * count + place], index) for step in range(2)]
            inflows.append((inflow, later))
            strip = strip + inflow
            strips_ref[place] = strip
        strips.append(strip)

    def strip_at(segment):
        return packets.tile(segment, STRIP) if finer_ref is None else strips_ref[segment.place(patches)]

    totals = []
    for place, segment in enumerate(every):
        eta, depth = strips[place], packets.tile(segment, STRIP_DEPTH)
        mask = wet(depth)
        east, there = links.east(segment)
        edge = there * rolled(rolled(strip_at(east), -1, 1), -1, 0)
        if finer_ref is None:
            row = jnp.where(is_last(), -courant * mask * edge, 0.0)
        else:
            inflow, later = inflows[place]
            row = courant * mask * (inflow - next_cells(inflow, edge))
        west, there = links.west(segment)
        west_eta = rolled(rolled(strip_at(west), 1, 1), 1, 0)
        west_mask = rolled(rolled(wet(packets.tile(west, STRIP_DEPTH)), 1, 1), 1, 0)
        edge = there * west_mask * (packets.column(west, LAST_ROW) - courant * (eta - west_eta))
        north, there = links.north(segment)
        col = there * (packets.tile(north, EDGE_FLOW) - courant * wet(packets.tile(north, EDGE_DEPTH)) * eta)
        total = packets.tile(segment, STRIP_SUM)
        if finer_ref is None:
            total = total - courant * depth * (row - jnp.where(is_first(), edge, 0.0) - col)
        else:
            total = (total + mask * inflow + later
                     - courant * depth * (row - last_cells(row, edge) + courant * mask * inflow - col))
        totals.append(total)
    for place, (strip, total) in enumerate(zip(strips, totals)):
        out_ref[place] = strip
        out_ref[count + place] = total


def beside(links, packets, own, inflow=None):
    lane = iota((1, LANES), 1)
    first, last = lane == 0, lane == LANES - 1

    def field(segment, column):
        return packets.column(segment, column) if inflow is None else 0.0

    def strip(name, turned):
        return 0.0 if inflow is None else jnp.where(first, rolled(inflow[name], turned, 1), 0.0)

    def corner_col(segment, eta, line, turned):
        north, beyond = links.north(segment)
        mask = rolled(wet(packets.line(north, EDGE_DEPTH, line)), turned, 1)
        flow = rolled(packets.line(north, EDGE_FLOW, line), turned, 1) if inflow is None else 0.0
        return beyond * (flow - courant * mask * eta)

    west, there = links.west(own)
    eta = field(west, LAST_ETA) + strip("west", 1)
    next_eta = field(west, NEXT_ETA) + strip("west", 2)
    own_eta = field(own, FIRST_ETA) + strip("own", 0)
    depth = packets.column(west, LAST_DEPTH) * there
    mask = wet(depth)
    next_row = wet(packets.column(west, NEXT_DEPTH)) * (field(west, NEXT_ROW) - courant * (eta - next_eta))
    below, beyond = links.south(west)
    corner = packets.line(below, STRIP, TILE - 1) if inflow is None else inflow["south west"]
    south_eta = jnp.where(last, corner * beyond, rolled(eta, -1, 1))
    col = mask * (field(west, LAST_COL) - courant * (south_eta - eta))
    north_col = jnp.where(first, corner_col(west, eta, TILE - 1, 1), rolled(col, 1, 1))
    west_row = mask * (field(west, LAST_ROW) - courant * (own_eta - eta))
    west_eta = (mask * eta - courant * depth * (west_row - next_row + col - north_col) + strip("west later", 1))
    west_mask = mask

    east, there = links.east(own)
    eta = there * (field(east, FIRST_ETA) + strip("east", 0))
    second_eta = field(east, SECOND_ETA) + strip("east", -1)
    depth = packets.column(east, FIRST_DEPTH) * there
    mask = wet(depth)
    row = mask * (field(east, FIRST_ROW) - courant * (second_eta - eta))
    below, beyond = links.south(east)
    corner = packets.line(below, STRIP, 0) if inflow is None else inflow["south east"]
    south_eta = jnp.where(last, rolled(corner, -1, 1) * beyond, rolled(eta, -1, 1))
    col = mask * (field(east, FIRST_COL) - courant * (south_eta - eta))
    north_col = jnp.where(first, corner_col(east, eta, 0, 0), rolled(col, 1, 1))
    east_sum = mask * eta - courant * depth * (row + col - north_col) + there * strip("east later", 0)
    return west_row, west_mask, west_eta, eta, east_sum, courant * depth


def advanced(eta, row, col, mask, depth, east, south, west, north):
    row = mask * (row - courant * (east(eta) - eta))
    col = mask * (col - courant * (south(eta) - eta))
    return mask * eta - depth * (row - west(row) + col - north(col)), row, col


def two_steps(start, mask, depth, sides, base, north=None, south=None, second=None):
    lane, line = iota(mask.shape, 1), iota(mask.shape, 0)
    cols = mask.shape[1]
    west_row, west_mask, west_eta, east_eta, east_sum, east_depth = sides
    state = start, 0.0, 0.0
    flow, beyond = west_row, east_eta
    above = 0.0 if north is None else north[0]
    for number in range(2):
        below = 0.0 if south is None else south[number]
        state = advanced(
            *state, mask, depth,
            lambda eta: jnp.where(lane == cols - 1, beyond, rolled(eta, -1, 1)),
            lambda eta: jnp.where(line == TILE - 1, below, rolled(eta, -1, 0)),
            lambda row: jnp.where(lane == 0, flow, rolled(row, 1, 1)),
            lambda col: jnp.where(line == 0, above, rolled(col, 1, 0)))
        if number:
            return state
        eta, row, col = state
        if second is not None:
            eta = eta + jnp.where(line == 0, second, 0.0)
            state = eta, row, col
        whole_eta, whole_row = (eta, row) if base is None else (eta + base[0], row + base[1])
        flow = west_mask * (west_row - courant * (whole_eta[:, :1] - west_eta))
        beyond = east_sum + east_depth * whole_row[:, cols - 1:]
        if north is not None:
            above = north[1] * (north[0] - courant * (whole_eta[:1] - north[2]))


def north_of(links, packets, own, own_strip, inflow=None):
    cols = own_strip.shape[1]
    lane = iota((1, LANES), 1)
    north, there = links.north(own)
    depth = packets.row(north, EDGE_DEPTH) * there
    mask = wet(depth)
    if inflow is not None:
        col = -courant * mask * own_strip
        return col, mask, -courant * depth * col
    col = packets.row(north, EDGE_FLOW) * there - courant * mask * own_strip
    north_east, beyond = links.east(north)
    right_eta = beyond * packets.column(north_east, FIRST_ETA)
    north_west, beyond = links.west(north)
    left_row = beyond * wet(packets.column(north_west, LAST_DEPTH)) * (
        packets.column(north_west, LAST_ROW)
        - courant * (packets.column(north, FIRST_ETA) - packets.column(north_west, LAST_ETA)))
    nothing = jnp.zeros((1, cols - LANES), jnp.float32)
    corners = (jnp.concatenate([jnp.where(lane == 0, rolled(left_row, 1, 1), 0.0), nothing], axis=1)
               + jnp.concatenate([nothing, jnp.where(lane == LANES - 1, courant * right_eta, 0.0)], axis=1))
    return col, mask, packets.row(north, EDGE_SUM) + courant * depth * (corners - col)


def as_sublanes(columns):
    rows = columns[0].shape[1]
    count = -len(columns) % TILE
    turned = jnp.concatenate(list(columns) + [jnp.zeros((count, rows), jnp.float32)], axis=0).T
    return [[turned[low:low + TILE, place:place + 1] for place in range(len(columns))]
            for low in (0, rows - TILE)]


def halo_kernel(links_ref, mine_ref, other_ref, strips_ref, eta_after, momenta_after, wet_after, depth_after,
                eta_ends, row_ends, turned, eta_hbm, momenta_hbm, eta_out, momenta_out, ends_out,
                left_new, right_new, sems):
    del eta_hbm, momenta_hbm
    rows, cols = eta_after.shape
    right = cols - LANES
    links = Links(links_ref, mine_ref.shape[0])
    own = links.own()
    packets = Packets((mine_ref, other_ref))
    columns = beside(links, packets, own)
    west_row, west_mask, west_eta, east_eta, east_sum, east_depth = columns
    fields = eta_after, momenta_after.at[0], momenta_after.at[1]

    line = iota((TILE, rows), 0)
    lane = iota((TILE, rows), 1)
    nothing = jnp.zeros((TILE, rows), jnp.float32)

    def south(eta):
        return jnp.where(lane == rows - 1, 0.0, rolled(eta, -1, 1))

    def north(col):
        return jnp.where(lane == 0, 0.0, rolled(col, 1, 1))

    def column_steps(mask, depth, east, west):
        state = nothing, nothing, nothing
        for number in range(2):
            state = advanced(
                *state, mask, depth,
                lambda eta: jnp.where(line == TILE - 1, east(number, state), rolled(eta, -1, 0)), south,
                lambda row: jnp.where(line == 0, west(number, state), rolled(row, 1, 0)), north)
        return state

    def west_of(number, state):
        if number == 0:
            return west_row
        whole = state[0][:1] + turned[4, :1]
        return west_mask * (west_row - courant * (whole - west_eta))

    def east_of(number, state):
        if number == 0:
            return east_eta
        return east_sum + east_depth * (state[1][TILE - 1:] + turned[5, TILE - 1:])

    left = column_steps(turned[0], turned[1], lambda number, state: 0.0, west_of)
    last = column_steps(turned[2], turned[3], east_of, lambda number, state: 0.0)
    middle = jnp.zeros((LANES - 2 * TILE, rows), jnp.float32)
    lane = iota((rows, LANES), 1)
    body_rows = slice(TILE, rows - TILE)
    copies = []
    outs = eta_out.at[0], momenta_out.at[0, 0], momenta_out.at[1, 0]
    inner = pl.ds(TILE, rows - 2 * TILE)
    for place, field in enumerate(fields):
        more = jnp.concatenate([left[place], middle, last[place]], axis=0).T[body_rows]
        inside = iota(more.shape, 1)
        left_new[place] = field[body_rows, :LANES] + jnp.where(inside < TILE, more, 0.0)
        right_new[place] = field[body_rows, right:] + jnp.where(inside >= LANES - TILE, more, 0.0)
        copies += copied([
            (left_new.at[place], outs[place].at[inner, pl.ds(0, LANES)]),
            (right_new.at[place], outs[place].at[inner, pl.ds(right, LANES)]),
        ], sems.at[place])

    top_sides, low_sides = as_sublanes(columns)
    nothing = jnp.zeros((TILE, cols), jnp.float32)
    top = two_steps(
        nothing, wet_after[:TILE], depth_after[:TILE], top_sides, (eta_ends[0], row_ends[0]),
        north=north_of(links, packets, own, packets.row(own, STRIP)))
    below, there = links.south(own)
    low = two_steps(
        nothing, wet_after[rows - TILE:], depth_after[rows - TILE:], low_sides, (eta_ends[1], row_ends[1]),
        south=(packets.row(below, STRIP) * there, row_of(strips_ref, 2 * links.patches + below.place(links.patches)) * there))
    line, lane = iota((TILE, cols), 0), iota((TILE, cols), 1)
    for place, field in enumerate(fields):
        more = jnp.concatenate([left[place], middle, last[place]], axis=0).T
        gap = jnp.zeros((TILE, cols - 2 * LANES), jnp.float32)
        for end, (low_row, near, found) in enumerate(
                ((0, line < TILE // 2, top), (rows - TILE, line >= TILE // 2, low))):
            tile = more[low_row:low_row + TILE]
            inside = iota(tile.shape, 1)
            wide = jnp.concatenate(
                [jnp.where(inside < TILE, tile, 0.0), gap, jnp.where(inside >= LANES - TILE, tile, 0.0)], axis=1)
            ends_out[place, end] = field[low_row:low_row + TILE] + jnp.where(near, found[place], wide)
    for copy in copies:
        copy.wait()


def inflow_kernel(links_ref, mine_ref, other_ref, finer_ref, wet_after, depth_after, ends_ref, eta_hbm, momenta_hbm,
                  eta_out, momenta_out, rows_ref, new_ref, sems):
    del eta_hbm, momenta_hbm
    rows, cols = wet_after.shape
    links = Links(links_ref, mine_ref.shape[0])
    patches = links.patches
    own = links.own()
    packets = Packets((mine_ref, other_ref))

    def flux_place(step, segment):
        return step * 2 * patches + segment.place(patches)

    def inflows(segment):
        gain, index = packets.tile(segment, GAIN), packets.tile(segment, INDEX).astype(jnp.int32)
        return [gain * nested(finer_ref[flux_place(step, segment)], index) for step in range(2)]

    below, there = links.south(own)
    west, east = links.west(own)[0], links.east(own)[0]
    below_west, beyond_west = links.west(below)
    below_east, beyond_east = links.east(below)
    wanted = (
        ("west", 0, west, TILE - 1), ("west later", 1, west, TILE - 1), ("east", 0, east, 0),
        ("east later", 1, east, 0), ("south west", 0, links.south(west)[0], TILE - 1),
        ("south east", 0, links.south(east)[0], 0), ("below west", 0, below_west, TILE - 1),
        ("below east", 0, below_east, 0))
    gain = jnp.concatenate([packets.line(segment, GAIN, line) for _, _, segment, line in wanted], axis=0)
    index = jnp.concatenate([packets.line(segment, INDEX, line) for _, _, segment, line in wanted], axis=0)
    index = index.astype(jnp.int32)
    lane, line = index % LANES, index // LANES
    taken = jnp.zeros((TILE, LANES), jnp.float32)
    for source in range(TILE):
        values = jnp.concatenate(
            [finer_ref[flux_place(step, segment), source:source + 1] for _, step, segment, _ in wanted], axis=0)
        found = jnp.take_along_axis(values, lane, axis=1, mode="promise_in_bounds")
        taken = jnp.where(line == source, found, taken)
    taken = gain * taken
    inflow = {name: taken[place:place + 1] for place, (name, _, _, _) in enumerate(wanted)}

    rows_ref[0], rows_ref[1] = inflows(own)
    strip, later = inflows(below)
    strip, later = strip * there, later * there
    inflow["own"] = rows_ref[0, :1]

    depth = packets.tile(below, STRIP_DEPTH)
    mask = wet(depth)
    edge = jnp.broadcast_to(rolled(inflow["below east"] * beyond_east, -1, 1), (TILE, LANES))
    row = courant * mask * (strip - next_cells(strip, edge))
    west_mask = rolled(wet(packets.line(below_west, STRIP_DEPTH, TILE - 1)), 1, 1)
    edge = beyond_west * courant * west_mask * (rolled(inflow["below west"], 1, 1) - strip[:1])
    edge = jnp.broadcast_to(edge, (TILE, LANES))
    north, beyond = links.north(below)
    col = -courant * wet(packets.tile(north, EDGE_DEPTH)) * beyond * strip
    rows_ref[2] = strip
    rows_ref[3] = there * (
        mask * strip - courant * depth * (row - last_cells(row, edge) + courant * mask * strip - col) + later)

    columns = beside(links, packets, own, inflow)
    top_sides, low_sides = as_sublanes(columns)
    line = iota((TILE, cols), 0)
    strip = row_of(rows_ref, 0)
    top = two_steps(
        jnp.where(line == 0, strip, 0.0), wet_after[:TILE], depth_after[:TILE], top_sides, None,
        north=north_of(links, packets, own, strip, inflow), second=row_of(rows_ref, 1))
    low = two_steps(
        jnp.zeros((TILE, cols), jnp.float32), wet_after[rows - TILE:], depth_after[rows - TILE:],
        low_sides, None, south=(row_of(rows_ref, 2), row_of(rows_ref, 3)))
    copies = []
    outs = eta_out.at[0], momenta_out.at[0, 0], momenta_out.at[1, 0]
    for end, (near, found) in enumerate(((line < TILE // 2, top), (line >= TILE // 2, low))):
        for place in range(3):
            new_ref[place, end] = ends_ref[place, end] + jnp.where(near, found[place], 0.0)
        copies += copied([
            (new_ref.at[place, end], out.at[pl.ds(end * (rows - TILE), TILE), :]) for place, out in enumerate(outs)
        ], sems.at[end])
    for copy in copies:
        copy.wait()


def body(adjoint_height, adjoint_momenta, depth, wet_mask, adjacency, nest_gain, nest_index):
    rows, cols = adjoint_height.shape[1:]
    levels = lax.axis_size("level")
    patches = lax.axis_size("patch")
    count = 2 * patches
    params = pltpu.CompilerParams(vmem_limit_bytes=VMEM_LIMIT)
    vmem = pl.BlockSpec(memory_space=pltpu.VMEM)
    smem = pl.BlockSpec(memory_space=pltpu.SMEM)
    hbm = pl.BlockSpec(memory_space=pltpu.HBM)

    def array(*shape):
        return jax.ShapeDtypeStruct(shape, jnp.float32)

    def scratch(*shape):
        return pltpu.VMEM(shape, jnp.float32)

    fields = [pltpu.with_memory_space_constraint(field, pltpu.HBM)
              for field in (adjoint_height, adjoint_momenta, depth, wet_mask, nest_gain, nest_index)]
    packed = pl.pallas_call(
        pack_kernel,
        out_shape=array(LINES, LANES),
        in_specs=[hbm] * 6,
        out_specs=vmem,
        scratch_shapes=[
            scratch(2, 4, TILE, cols), pltpu.VMEM((2, TILE, cols), jnp.int32),
            scratch(2, 4, rows, LANES), pltpu.VMEM((2, rows, LANES), jnp.int32),
            scratch(levels, cols), pltpu.VMEM((levels, cols), jnp.int32),
            pltpu.SemaphoreType.DMA((22,)),
        ],
        compiler_params=params,
        name="pack",
    )(*fields)
    parts = 4
    eta_new, momenta_new, *after = pl.pallas_call(
        bulk_kernel,
        out_shape=[
            array(*adjoint_height.shape), array(*adjoint_momenta.shape),
            array(rows, cols), array(2, rows, cols), array(rows, cols), array(rows, cols),
            array(2, TILE, cols), array(2, TILE, cols), array(6, TILE, rows),
        ],
        in_specs=[hbm] * 4,
        out_specs=[hbm] * 2 + [vmem] * 7,
        scratch_shapes=[
            scratch(rows + 2 * TILE, cols), scratch(rows + 2 * TILE, cols),
            scratch(2, rows, cols), scratch(rows, cols), pltpu.VMEM((rows, cols), jnp.int32),
            scratch(rows, LANES), scratch(rows, LANES),
            pltpu.SemaphoreType.DMA((parts, 4)), pltpu.SemaphoreType.DMA((parts, 2)),
        ],
        compiler_params=params,
        name="bulk",
    )(*fields[:4])

    sent = [packed] + [
        lax.ppermute(packed, "patch", [(source, source ^ turn) for source in range(patches)])
        for turn in range(1, patches)
    ]
    mine = pl.pallas_call(
        gather_kernel,
        out_shape=array(patches, LINES, LANES),
        in_specs=[vmem] * (patches + 1),
        out_specs=vmem,
        compiler_params=params,
        name="gather",
    )(*sent, after[-1])
    other = lax.ppermute(mine, "sub", [(0, 1), (1, 0)])

    flux = ()
    strips = []
    for turn in range(levels - 1):
        strips.append(pl.pallas_call(
            strips_kernel,
            out_shape=array(2 * count, TILE, LANES),
            in_specs=[smem] + [vmem] * (2 + len(flux)),
            out_specs=vmem,
            scratch_shapes=[scratch(count, TILE, LANES)],
            compiler_params=params,
            name="strips",
        )(adjacency, mine, other, *flux))
        flux = (lax.ppermute(strips[-1], "level", [(source, source - 1) for source in range(1, levels)]),)

    eta_new, momenta_new, ends = pl.pallas_call(
        halo_kernel,
        out_shape=[array(*adjoint_height.shape), array(*adjoint_momenta.shape), array(3, 2, TILE, cols)],
        in_specs=[smem] + [vmem] * 10 + [hbm] * 2,
        out_specs=[hbm, hbm, vmem],
        input_output_aliases={11: 0, 12: 1},
        scratch_shapes=[
            scratch(3, rows - 2 * TILE, LANES), scratch(3, rows - 2 * TILE, LANES), pltpu.SemaphoreType.DMA((3, 2)),
        ],
        compiler_params=params,
        name="halo",
    )(adjacency, mine, other, strips[0], *after, eta_new, momenta_new)

    return pl.pallas_call(
        inflow_kernel,
        out_shape=[array(*adjoint_height.shape), array(*adjoint_momenta.shape)],
        in_specs=[smem] + [vmem] * 6 + [hbm] * 2,
        out_specs=[hbm, hbm],
        input_output_aliases={7: 0, 8: 1},
        scratch_shapes=[
            scratch(4, TILE, LANES), scratch(3, 2, TILE, cols), pltpu.SemaphoreType.DMA((2, 3)),
        ],
        compiler_params=params,
        name="inflow",
    )(adjacency, mine, other, *flux, after[2], after[3], ends, eta_new, momenta_new)


def solution(mesh):
    in_specs = (
        P(("parts", "level"), ("patch", "sub"), None),
        P(None, ("parts", "level"), ("patch", "sub"), None),
        P("level", ("patch", "sub"), None),
        P("level", ("patch", "sub"), None),
        P("level", None, None),
        P(None, ("patch", "sub")),
        P(None, ("patch", "sub")),
    )
    out_specs = (
        P(("parts", "level"), ("patch", "sub"), None),
        P(None, ("parts", "level"), ("patch", "sub"), None),
    )
    return jax.shard_map(body, mesh=mesh, in_specs=in_specs, out_specs=out_specs, check_vma=False)
```

```python
import jax
import jax.numpy as jnp
from jax import lax
from jax.experimental import pallas as pl
from jax.experimental.pallas import tpu as pltpu
from jax.sharding import PartitionSpec as P

STEPS = 2
LANES = 128
TILE = 8
VMEM_LIMIT = 48 * 1024 * 1024

courant = 0.45

STRIP_SUM, STRIP, STRIP_DEPTH, GAIN, INDEX, EDGE_FLOW, EDGE_DEPTH, EDGE_SUM = range(8)
(FIRST_ETA, SECOND_ETA, FIRST_ROW, FIRST_COL, FIRST_DEPTH, NEXT_ETA, LAST_ETA, NEXT_ROW,
 LAST_ROW, LAST_COL, NEXT_DEPTH, LAST_DEPTH) = range(12)
ROWS, COLUMNS = 8, 16
LINES = ROWS * TILE + COLUMNS


def iota(shape, axis):
    return lax.broadcasted_iota(jnp.int32, shape, axis)


def rolled(value, shift, axis):
    if shift == 0:
        return value
    return pltpu.roll(value, shift % value.shape[axis], axis)


def wet(depth):
    return (depth > 0).astype(jnp.float32)


def copied(pairs, sems):
    copies = [pltpu.make_async_copy(source, target, sems.at[place]) for place, (source, target) in enumerate(pairs)]
    for copy in copies:
        copy.start()
    return copies


def pack_kernel(eta_ref, momenta_ref, depth_ref, wet_ref, gain_ref, index_ref, out_ref,
                ends, end_wet, sides, side_wet, gains, indices, sems):
    rows, cols = eta_ref.shape[1:]
    fields = eta_ref.at[0], momenta_ref.at[0, 0], momenta_ref.at[1, 0], depth_ref.at[0]
    tall, wide = [], []
    for end in range(2):
        here = pl.ds(end * (rows - TILE), TILE)
        tall += [(field.at[here, :], ends.at[end, place]) for place, field in enumerate(fields)]
        tall.append((wet_ref.at[0, here, :], end_wet.at[end]))
        here = pl.ds(end * (cols - LANES), LANES)
        wide += [(field.at[:, here], sides.at[end, place]) for place, field in enumerate(fields)]
        wide.append((wet_ref.at[0, :, here], side_wet.at[end]))
    tall += [(gain_ref, gains), (index_ref, indices)]
    copies = copied(tall + wide, sems)
    for copy in copies[:len(tall)]:
        copy.wait()
    level = lax.axis_index("level")
    lane = iota((TILE, cols), 1)

    def loaded(end):
        mask = end_wet[end].astype(jnp.float32)
        return ends[end, 0], ends[end, 1], ends[end, 2], mask * ends[end, 3], mask

    def put(row, value):
        for tile in range(TILE):
            out_ref[row * TILE + tile:row * TILE + tile + 1] = value[:, tile * LANES:(tile + 1) * LANES]

    eta, row, col, depth, mask = loaded(0)
    east = jnp.where(lane == cols - 1, 0.0, rolled(eta, -1, 1))
    row = mask * (row - courant * (east - eta))
    west = jnp.where(lane == 0, 0.0, rolled(row, 1, 1))
    col = mask * (col - courant * (rolled(eta, -1, 0) - eta))
    strip_sum = mask * eta - courant * depth * (row - west + col)
    put(STRIP_SUM, strip_sum[:1])
    put(STRIP, eta[:1])
    put(STRIP_DEPTH, depth[:1])
    put(GAIN, gains[pl.ds(level, 1), :])
    put(INDEX, indices[pl.ds(level, 1), :].astype(jnp.float32))

    eta, row, col, depth, mask = loaded(1)
    east = jnp.where(lane == cols - 1, 0.0, rolled(eta, -1, 1))
    row = mask * (row - courant * (east - eta))
    west = jnp.where(lane == 0, 0.0, rolled(row, 1, 1))
    flow = mask * (col + courant * eta)
    above = rolled(flow - courant * mask * rolled(eta, -1, 0), 1, 0)
    edge_sum = mask * eta - courant * depth * (row - west - above)
    put(EDGE_FLOW, flow[TILE - 1:])
    put(EDGE_DEPTH, depth[TILE - 1:])
    put(EDGE_SUM, edge_sum[TILE - 1:])

    for copy in copies[len(tall):]:
        copy.wait()
    lane = iota((rows, LANES), 1)
    columns = jnp.zeros((rows, LANES), jnp.float32)
    depths = [sides[end, 3] * side_wet[end].astype(jnp.float32) for end in range(2)]
    for place, value, at in (
        (FIRST_ETA, sides[0, 0], 0), (SECOND_ETA, sides[0, 0], 1), (FIRST_ROW, sides[0, 1], 0),
        (FIRST_COL, sides[0, 2], 0), (FIRST_DEPTH, depths[0], 0),
        (NEXT_ETA, sides[1, 0], LANES - 2), (LAST_ETA, sides[1, 0], LANES - 1),
        (NEXT_ROW, sides[1, 1], LANES - 2), (LAST_ROW, sides[1, 1], LANES - 1),
        (LAST_COL, sides[1, 2], LANES - 1),
        (NEXT_DEPTH, depths[1], LANES - 2), (LAST_DEPTH, depths[1], LANES - 1),
    ):
        moved = value if place == at else rolled(value, place - at, 1)
        columns = jnp.where(lane == place, moved, columns)
    out_ref[ROWS * TILE:] = columns.T[:COLUMNS]


def first_kernel(eta_ref, momenta_ref, depth_ref, wet_ref, eta_after, row_after, col_after, wet_after, depth_after,
                 turned, eta_pad, momenta_in, depth_in, wet_in, sems):
    rows, cols = row_after.shape
    parts = sems.shape[0]
    size = rows // parts
    loads = []
    for part in range(parts):
        here = pl.ds(part * size, size)
        loads.append(copied([
            (eta_ref.at[0, here, :], eta_pad.at[here, :]),
            (momenta_ref.at[:, 0, here, :], momenta_in.at[:, here, :]),
            (depth_ref.at[0, here, :], depth_in.at[here, :]),
            (wet_ref.at[0, here, :], wet_in.at[here, :]),
        ], sems.at[part]))
    lane, line = iota((TILE, cols), 1), iota((TILE, cols), 0)
    eta_pad[rows:] = jnp.zeros((TILE, cols), jnp.float32)
    eta_after[rows:] = jnp.zeros((TILE, cols), jnp.float32)
    above = jnp.zeros((1, cols), jnp.float32)
    for copy in loads[0]:
        copy.wait()
    for part in range(parts):
        if part + 1 < parts:
            for copy in loads[part + 1]:
                copy.wait()
        for low in range(part * size, (part + 1) * size, TILE):
            chunk = slice(low, low + TILE)
            mask = wet_in[chunk].astype(jnp.float32)
            depth = courant * mask * depth_in[chunk]
            below = eta_pad[low + 1:low + TILE + 1]
            eta, row, col = advanced(
                eta_pad[chunk], momenta_in[0, chunk], momenta_in[1, chunk], mask, depth,
                lambda eta: jnp.where(lane == cols - 1, 0.0, rolled(eta, -1, 1)), lambda eta: below,
                lambda row: jnp.where(lane == 0, 0.0, rolled(row, 1, 1)),
                lambda col: jnp.where(line == 0, above, rolled(col, 1, 0)))
            above = col[TILE - 1:]
            eta_after[chunk], row_after[chunk], col_after[chunk] = eta, row, col
            wet_after[chunk], depth_after[chunk] = mask, depth
    right = cols - LANES
    turned[0] = wet_after[:, :LANES].T[:TILE]
    turned[1] = depth_after[:, :LANES].T[:TILE]
    turned[2] = wet_after[:, right:].T[LANES - TILE:]
    turned[3] = depth_after[:, right:].T[LANES - TILE:]
    turned[4] = eta_after[:rows, :LANES].T[:TILE]
    turned[5] = row_after[:, right:].T[LANES - TILE:]


def gather_kernel(*refs):
    packets, out_ref = refs[:-2], refs[-1]
    own = lax.axis_index("patch")
    for turn, packet in enumerate(packets):
        out_ref[own ^ turn] = packet[...]


class Segment:
    def __init__(self, patch, flipped):
        self.patch, self.flipped = patch, flipped

    def place(self, patches):
        return self.flipped * patches + self.patch


def below_finest():
    return jnp.where(lax.axis_index("level") < lax.axis_size("level") - 1, 1.0, 0.0)


class Links:
    def __init__(self, links_ref, patches):
        self.links_ref, self.patches = links_ref, patches
        self.half = lax.axis_index("sub")

    def own(self):
        return Segment(lax.axis_index("patch"), 0)

    def all(self):
        return [Segment(patch, flipped) for flipped in range(2) for patch in range(self.patches)]

    def across(self, segment, way):
        patch = self.links_ref[0, segment.patch, way]
        return jnp.maximum(patch, 0), jnp.where(patch >= 0, 1.0, 0.0)

    def other_half(self, segment, way, inner):
        patch, there = self.across(segment, way)
        inside = self.half == (inner ^ segment.flipped)
        return Segment(jnp.where(inside, segment.patch, patch), 1 - segment.flipped), jnp.where(inside, 1.0, there)

    def north(self, segment):
        return self.other_half(segment, 0, 1)

    def south(self, segment):
        return self.other_half(segment, 1, 0)

    def west(self, segment):
        patch, there = self.across(segment, 2)
        return Segment(patch, segment.flipped), there

    def east(self, segment):
        patch, there = self.across(segment, 3)
        return Segment(patch, segment.flipped), there


class Packets:
    def __init__(self, got_refs):
        self.got_refs = got_refs

    def tile(self, segment, row):
        return self.got_refs[segment.flipped][segment.patch, row * TILE:(row + 1) * TILE]

    def line(self, segment, row, line):
        return self.got_refs[segment.flipped][segment.patch, row * TILE + line:row * TILE + line + 1]

    def row(self, segment, row):
        return jnp.concatenate([self.line(segment, row, line) for line in range(TILE)], axis=1)

    def column(self, segment, column):
        return self.line(segment, ROWS, column)


def is_first(shape=(TILE, LANES)):
    return (iota(shape, 0) == 0) & (iota(shape, 1) == 0)


def is_last(shape=(TILE, LANES)):
    return (iota(shape, 0) == shape[0] - 1) & (iota(shape, 1) == shape[1] - 1)


def next_cells(tile, edge):
    lane = iota(tile.shape, 1)
    moved = rolled(tile, -1, 1)
    moved = jnp.where(lane == LANES - 1, rolled(moved, -1, 0), moved)
    return jnp.where(is_last(), edge, moved)


def last_cells(tile, edge):
    lane = iota(tile.shape, 1)
    moved = rolled(tile, 1, 1)
    moved = jnp.where(lane == 0, rolled(moved, 1, 0), moved)
    return jnp.where(is_first(), edge, moved)


def row_of(ref, place):
    return jnp.concatenate([ref[place, line:line + 1] for line in range(TILE)], axis=1)


def nested(flux, index):
    lane, line = index % LANES, index // LANES
    taken = jnp.zeros(index.shape, jnp.float32)
    for source in range(TILE):
        values = jnp.broadcast_to(flux[source:source + 1], index.shape)
        found = jnp.take_along_axis(values, lane, axis=1, mode="promise_in_bounds")
        taken = jnp.where(line == source, found, taken)
    return taken


def strips_kernel(*refs):
    links_ref, mine_ref, other_ref = refs[:3]
    out_ref, strips_ref = refs[-2:]
    finer_ref = refs[3] if len(refs) == 6 else None
    links = Links(links_ref, mine_ref.shape[0])
    patches, count = links.patches, 2 * links.patches
    packets = Packets((mine_ref, other_ref))
    every = links.all()
    strips, inflows = [], []
    for segment in every:
        strip = packets.tile(segment, STRIP)
        if finer_ref is not None:
            place = segment.place(patches)
            gain, index = packets.tile(segment, GAIN) * below_finest(), packets.tile(segment, INDEX).astype(jnp.int32)
            inflow, later = [gain * nested(finer_ref[step * count + place], index) for step in range(2)]
            inflows.append((inflow, later))
            strip = strip + inflow
            strips_ref[place] = strip
        strips.append(strip)

    def strip_at(segment):
        return packets.tile(segment, STRIP) if finer_ref is None else strips_ref[segment.place(patches)]

    totals = []
    for place, segment in enumerate(every):
        eta, depth = strips[place], packets.tile(segment, STRIP_DEPTH)
        mask = wet(depth)
        east, there = links.east(segment)
        edge = there * rolled(rolled(strip_at(east), -1, 1), -1, 0)
        if finer_ref is None:
            row = jnp.where(is_last(), -courant * mask * edge, 0.0)
        else:
            inflow, later = inflows[place]
            row = courant * mask * (inflow - next_cells(inflow, edge))
        west, there = links.west(segment)
        west_eta = rolled(rolled(strip_at(west), 1, 1), 1, 0)
        west_mask = rolled(rolled(wet(packets.tile(west, STRIP_DEPTH)), 1, 1), 1, 0)
        edge = there * west_mask * (packets.column(west, LAST_ROW) - courant * (eta - west_eta))
        north, there = links.north(segment)
        col = there * (packets.tile(north, EDGE_FLOW) - courant * wet(packets.tile(north, EDGE_DEPTH)) * eta)
        total = packets.tile(segment, STRIP_SUM)
        if finer_ref is None:
            total = total - courant * depth * (row - jnp.where(is_first(), edge, 0.0) - col)
        else:
            total = (total + mask * inflow + later
                     - courant * depth * (row - last_cells(row, edge) + courant * mask * inflow - col))
        totals.append(total)
    for place, (strip, total) in enumerate(zip(strips, totals)):
        out_ref[place] = strip
        out_ref[count + place] = total


def beside(links, packets, own, inflow=None):
    lane = iota((1, LANES), 1)
    first, last = lane == 0, lane == LANES - 1

    def field(segment, column):
        return packets.column(segment, column) if inflow is None else 0.0

    def strip(name, turned):
        return 0.0 if inflow is None else jnp.where(first, rolled(inflow[name], turned, 1), 0.0)

    def corner_col(segment, eta, line, turned):
        north, beyond = links.north(segment)
        mask = rolled(wet(packets.line(north, EDGE_DEPTH, line)), turned, 1)
        flow = rolled(packets.line(north, EDGE_FLOW, line), turned, 1) if inflow is None else 0.0
        return beyond * (flow - courant * mask * eta)

    west, there = links.west(own)
    eta = field(west, LAST_ETA) + strip("west", 1)
    next_eta = field(west, NEXT_ETA) + strip("west", 2)
    own_eta = field(own, FIRST_ETA) + strip("own", 0)
    depth = packets.column(west, LAST_DEPTH) * there
    mask = wet(depth)
    next_row = wet(packets.column(west, NEXT_DEPTH)) * (field(west, NEXT_ROW) - courant * (eta - next_eta))
    below, beyond = links.south(west)
    corner = packets.line(below, STRIP, TILE - 1) if inflow is None else inflow["south west"]
    south_eta = jnp.where(last, corner * beyond, rolled(eta, -1, 1))
    col = mask * (field(west, LAST_COL) - courant * (south_eta - eta))
    north_col = jnp.where(first, corner_col(west, eta, TILE - 1, 1), rolled(col, 1, 1))
    west_row = mask * (field(west, LAST_ROW) - courant * (own_eta - eta))
    west_eta = (mask * eta - courant * depth * (west_row - next_row + col - north_col) + strip("west later", 1))
    west_mask = mask

    east, there = links.east(own)
    eta = there * (field(east, FIRST_ETA) + strip("east", 0))
    second_eta = field(east, SECOND_ETA) + strip("east", -1)
    depth = packets.column(east, FIRST_DEPTH) * there
    mask = wet(depth)
    row = mask * (field(east, FIRST_ROW) - courant * (second_eta - eta))
    below, beyond = links.south(east)
    corner = packets.line(below, STRIP, 0) if inflow is None else inflow["south east"]
    south_eta = jnp.where(last, rolled(corner, -1, 1) * beyond, rolled(eta, -1, 1))
    col = mask * (field(east, FIRST_COL) - courant * (south_eta - eta))
    north_col = jnp.where(first, corner_col(east, eta, 0, 0), rolled(col, 1, 1))
    east_sum = mask * eta - courant * depth * (row + col - north_col) + there * strip("east later", 0)
    return west_row, west_mask, west_eta, eta, east_sum, courant * depth


def advanced(eta, row, col, mask, depth, east, south, west, north):
    row = mask * (row - courant * (east(eta) - eta))
    col = mask * (col - courant * (south(eta) - eta))
    return mask * eta - depth * (row - west(row) + col - north(col)), row, col


def two_steps(start, mask, depth, sides, base, north=None, south=None, second=None):
    lane, line = iota(mask.shape, 1), iota(mask.shape, 0)
    cols = mask.shape[1]
    west_row, west_mask, west_eta, east_eta, east_sum, east_depth = sides
    state = start, 0.0, 0.0
    flow, beyond = west_row, east_eta
    above = 0.0 if north is None else north[0]
    for number in range(2):
        below = 0.0 if south is None else south[number]
        state = advanced(
            *state, mask, depth,
            lambda eta: jnp.where(lane == cols - 1, beyond, rolled(eta, -1, 1)),
            lambda eta: jnp.where(line == TILE - 1, below, rolled(eta, -1, 0)),
            lambda row: jnp.where(lane == 0, flow, rolled(row, 1, 1)),
            lambda col: jnp.where(line == 0, above, rolled(col, 1, 0)))
        if number:
            return state
        eta, row, col = state
        if second is not None:
            eta = eta + jnp.where(line == 0, second, 0.0)
            state = eta, row, col
        whole_eta, whole_row = (eta, row) if base is None else (eta + base[0], row + base[1])
        flow = west_mask * (west_row - courant * (whole_eta[:, :1] - west_eta))
        beyond = east_sum + east_depth * whole_row[:, cols - 1:]
        if north is not None:
            above = north[1] * (north[0] - courant * (whole_eta[:1] - north[2]))


def north_of(links, packets, own, own_strip, inflow=None):
    cols = own_strip.shape[1]
    lane = iota((1, LANES), 1)
    north, there = links.north(own)
    depth = packets.row(north, EDGE_DEPTH) * there
    mask = wet(depth)
    if inflow is not None:
        col = -courant * mask * own_strip
        return col, mask, -courant * depth * col
    col = packets.row(north, EDGE_FLOW) * there - courant * mask * own_strip
    north_east, beyond = links.east(north)
    right_eta = beyond * packets.column(north_east, FIRST_ETA)
    north_west, beyond = links.west(north)
    left_row = beyond * wet(packets.column(north_west, LAST_DEPTH)) * (
        packets.column(north_west, LAST_ROW)
        - courant * (packets.column(north, FIRST_ETA) - packets.column(north_west, LAST_ETA)))
    nothing = jnp.zeros((1, cols - LANES), jnp.float32)
    corners = (jnp.concatenate([jnp.where(lane == 0, rolled(left_row, 1, 1), 0.0), nothing], axis=1)
               + jnp.concatenate([nothing, jnp.where(lane == LANES - 1, courant * right_eta, 0.0)], axis=1))
    return col, mask, packets.row(north, EDGE_SUM) + courant * depth * (corners - col)


def as_sublanes(columns):
    rows = columns[0].shape[1]
    count = -len(columns) % TILE
    turned = jnp.concatenate(list(columns) + [jnp.zeros((count, rows), jnp.float32)], axis=0).T
    return [[turned[low:low + TILE, place:place + 1] for place in range(len(columns))]
            for low in (0, rows - TILE)]


def second_kernel(links_ref, mine_ref, other_ref, strips_ref, eta_after, row_after, col_after, wet_after,
                  depth_after, turned, eta_out, momenta_out, ends_out, new_ref, more_ref, sems):
    rows, cols = row_after.shape
    links = Links(links_ref, mine_ref.shape[0])
    own = links.own()
    packets = Packets((mine_ref, other_ref))
    columns = beside(links, packets, own)
    west_row, west_mask, west_eta, east_eta, east_sum, east_depth = columns

    line, lane = iota((TILE, rows), 0), iota((TILE, rows), 1)
    nothing = jnp.zeros((TILE, rows), jnp.float32)

    def column_steps(mask, depth, east, west):
        state = nothing, nothing, nothing
        for number in range(2):
            state = advanced(
                *state, mask, depth,
                lambda eta: jnp.where(line == TILE - 1, east(number, state), rolled(eta, -1, 0)),
                lambda eta: jnp.where(lane == rows - 1, 0.0, rolled(eta, -1, 1)),
                lambda row: jnp.where(line == 0, west(number, state), rolled(row, 1, 0)),
                lambda col: jnp.where(lane == 0, 0.0, rolled(col, 1, 1)))
        return state

    def west_of(number, state):
        if number == 0:
            return west_row
        whole = state[0][:1] + turned[4, :1]
        return west_mask * (west_row - courant * (whole - west_eta))

    def east_of(number, state):
        if number == 0:
            return east_eta
        return east_sum + east_depth * (state[1][TILE - 1:] + turned[5, TILE - 1:])

    left = column_steps(turned[0], turned[1], lambda number, state: 0.0, west_of)
    last = column_steps(turned[2], turned[3], east_of, lambda number, state: 0.0)
    middle = jnp.zeros((LANES - 2 * TILE, rows), jnp.float32)
    for place in range(3):
        more_ref[place] = jnp.concatenate([left[place], middle, last[place]], axis=0).T

    top_sides, low_sides = as_sublanes(columns)
    nothing = jnp.zeros((TILE, cols), jnp.float32)
    end = slice(rows - TILE, rows)
    top = two_steps(
        nothing, wet_after[:TILE], depth_after[:TILE], top_sides, (eta_after[:TILE], row_after[:TILE]),
        north=north_of(links, packets, own, packets.row(own, STRIP)))
    below, there = links.south(own)
    low = two_steps(
        nothing, wet_after[end], depth_after[end], low_sides, (eta_after[end], row_after[end]),
        south=(packets.row(below, STRIP) * there,
               row_of(strips_ref, 2 * links.patches + below.place(links.patches)) * there))

    line, lane = iota((TILE, cols), 0), iota((TILE, cols), 1)
    inside = iota((TILE, LANES), 1)
    outs = eta_out.at[0], momenta_out.at[0, 0], momenta_out.at[1, 0]
    above = jnp.zeros((1, cols), jnp.float32)
    parts = sems.shape[0]
    size = (rows - 2 * TILE) // parts
    copies = []
    for first in range(0, rows, TILE):
        chunk = slice(first, first + TILE)
        south = eta_after[first + 1:first + TILE + 1]
        fields = advanced(
            eta_after[chunk], row_after[chunk], col_after[chunk], wet_after[chunk], depth_after[chunk],
            lambda eta: jnp.where(lane == cols - 1, 0.0, rolled(eta, -1, 1)), lambda eta: south,
            lambda row: jnp.where(lane == 0, 0.0, rolled(row, 1, 1)),
            lambda col: jnp.where(line == 0, above, rolled(col, 1, 0)))
        above = fields[2][TILE - 1:]
        for place, field in enumerate(fields):
            more = more_ref[place, chunk]
            sides = [jnp.where(inside < TILE, more, 0.0), jnp.where(inside >= LANES - TILE, more, 0.0)]
            if first in (0, rows - TILE):
                near, found = (line < TILE // 2, top) if first == 0 else (line >= TILE // 2, low)
                gap = jnp.zeros((TILE, cols - 2 * LANES), jnp.float32)
                wide = jnp.concatenate([sides[0], gap, sides[1]], axis=1)
                ends_out[place, int(first > 0)] = field + jnp.where(near, found[place], wide)
            else:
                new_ref[place, first - TILE:first] = jnp.concatenate(
                    [field[:, :LANES] + sides[0], field[:, LANES:cols - LANES], field[:, cols - LANES:] + sides[1]],
                    axis=1)
        if first and first % size == 0 and first < rows - TILE:
            part = first // size - 1
            here, there = pl.ds(part * size, size), pl.ds(TILE + part * size, size)
            copies += copied([(new_ref.at[place, here], out.at[there, :]) for place, out in enumerate(outs)],
                             sems.at[part])
    for copy in copies:
        copy.wait()


def inflow_kernel(links_ref, mine_ref, other_ref, finer_ref, wet_after, depth_after, ends_ref, eta_hbm, momenta_hbm,
                  eta_out, momenta_out, rows_ref, new_ref, sems):
    del eta_hbm, momenta_hbm
    rows, cols = wet_after.shape
    links = Links(links_ref, mine_ref.shape[0])
    patches = links.patches
    own = links.own()
    packets = Packets((mine_ref, other_ref))
    some = below_finest()

    def flux_place(step, segment):
        return step * 2 * patches + segment.place(patches)

    def inflows(segment):
        gain, index = packets.tile(segment, GAIN) * some, packets.tile(segment, INDEX).astype(jnp.int32)
        return [gain * nested(finer_ref[flux_place(step, segment)], index) for step in range(2)]

    below, there = links.south(own)
    west, east = links.west(own)[0], links.east(own)[0]
    below_west, beyond_west = links.west(below)
    below_east, beyond_east = links.east(below)
    wanted = (
        ("west", 0, west, TILE - 1), ("west later", 1, west, TILE - 1), ("east", 0, east, 0),
        ("east later", 1, east, 0), ("south west", 0, links.south(west)[0], TILE - 1),
        ("south east", 0, links.south(east)[0], 0), ("below west", 0, below_west, TILE - 1),
        ("below east", 0, below_east, 0))
    gain = jnp.concatenate([packets.line(segment, GAIN, line) for _, _, segment, line in wanted], axis=0)
    index = jnp.concatenate([packets.line(segment, INDEX, line) for _, _, segment, line in wanted], axis=0)
    index = index.astype(jnp.int32)
    lane, line = index % LANES, index // LANES
    taken = jnp.zeros((TILE, LANES), jnp.float32)
    for source in range(TILE):
        values = jnp.concatenate(
            [finer_ref[flux_place(step, segment), source:source + 1] for _, step, segment, _ in wanted], axis=0)
        found = jnp.take_along_axis(values, lane, axis=1, mode="promise_in_bounds")
        taken = jnp.where(line == source, found, taken)
    taken = some * gain * taken
    inflow = {name: taken[place:place + 1] for place, (name, _, _, _) in enumerate(wanted)}

    rows_ref[0], rows_ref[1] = inflows(own)
    strip, later = inflows(below)
    strip, later = strip * there, later * there
    inflow["own"] = rows_ref[0, :1]

    depth = packets.tile(below, STRIP_DEPTH)
    mask = wet(depth)
    edge = jnp.broadcast_to(rolled(inflow["below east"] * beyond_east, -1, 1), (TILE, LANES))
    row = courant * mask * (strip - next_cells(strip, edge))
    west_mask = rolled(wet(packets.line(below_west, STRIP_DEPTH, TILE - 1)), 1, 1)
    edge = beyond_west * courant * west_mask * (rolled(inflow["below west"], 1, 1) - strip[:1])
    edge = jnp.broadcast_to(edge, (TILE, LANES))
    north, beyond = links.north(below)
    col = -courant * wet(packets.tile(north, EDGE_DEPTH)) * beyond * strip
    rows_ref[2] = strip
    rows_ref[3] = there * (
        mask * strip - courant * depth * (row - last_cells(row, edge) + courant * mask * strip - col) + later)

    columns = beside(links, packets, own, inflow)
    top_sides, low_sides = as_sublanes(columns)
    line = iota((TILE, cols), 0)
    strip = row_of(rows_ref, 0)
    top = two_steps(
        jnp.where(line == 0, strip, 0.0), wet_after[:TILE], depth_after[:TILE], top_sides, None,
        north=north_of(links, packets, own, strip, inflow), second=row_of(rows_ref, 1))
    low = two_steps(
        jnp.zeros((TILE, cols), jnp.float32), wet_after[rows - TILE:], depth_after[rows - TILE:],
        low_sides, None, south=(row_of(rows_ref, 2), row_of(rows_ref, 3)))
    copies = []
    outs = eta_out.at[0], momenta_out.at[0, 0], momenta_out.at[1, 0]
    for end, (near, found) in enumerate(((line < TILE // 2, top), (line >= TILE // 2, low))):
        for place in range(3):
            new_ref[place, end] = ends_ref[place, end] + jnp.where(near, found[place], 0.0)
        copies += copied([
            (new_ref.at[place, end], out.at[pl.ds(end * (rows - TILE), TILE), :]) for place, out in enumerate(outs)
        ], sems.at[end])
    for copy in copies:
        copy.wait()


def body(adjoint_height, adjoint_momenta, depth, wet_mask, adjacency, nest_gain, nest_index):
    rows, cols = adjoint_height.shape[1:]
    levels = lax.axis_size("level")
    patches = lax.axis_size("patch")
    count = 2 * patches
    params = pltpu.CompilerParams(vmem_limit_bytes=VMEM_LIMIT)
    vmem = pl.BlockSpec(memory_space=pltpu.VMEM)
    smem = pl.BlockSpec(memory_space=pltpu.SMEM)
    hbm = pl.BlockSpec(memory_space=pltpu.HBM)

    def array(*shape):
        return jax.ShapeDtypeStruct(shape, jnp.float32)

    def scratch(*shape):
        return pltpu.VMEM(shape, jnp.float32)

    fields = [pltpu.with_memory_space_constraint(field, pltpu.HBM)
              for field in (adjoint_height, adjoint_momenta, depth, wet_mask, nest_gain, nest_index)]
    packed = pl.pallas_call(
        pack_kernel,
        out_shape=array(LINES, LANES),
        in_specs=[hbm] * 6,
        out_specs=vmem,
        scratch_shapes=[
            scratch(2, 4, TILE, cols), pltpu.VMEM((2, TILE, cols), jnp.int32),
            scratch(2, 4, rows, LANES), pltpu.VMEM((2, rows, LANES), jnp.int32),
            scratch(levels, cols), pltpu.VMEM((levels, cols), jnp.int32),
            pltpu.SemaphoreType.DMA((22,)),
        ],
        compiler_params=params,
        name="pack",
    )(*fields)
    parts = 4
    after = pl.pallas_call(
        first_kernel,
        out_shape=[
            array(rows + TILE, cols), array(rows, cols), array(rows, cols), array(rows, cols), array(rows, cols),
            array(6, TILE, rows),
        ],
        in_specs=[hbm] * 4,
        out_specs=[vmem] * 6,
        scratch_shapes=[
            scratch(rows + TILE, cols), scratch(2, rows, cols), scratch(rows, cols),
            pltpu.VMEM((rows, cols), jnp.int32), pltpu.SemaphoreType.DMA((parts, 4)),
        ],
        compiler_params=params,
        name="first",
    )(*fields[:4])

    sent = [packed] + [
        lax.ppermute(packed, "patch", [(source, source ^ turn) for source in range(patches)])
        for turn in range(1, patches)
    ]
    mine = pl.pallas_call(
        gather_kernel,
        out_shape=array(patches, LINES, LANES),
        in_specs=[vmem] * (patches + 1),
        out_specs=vmem,
        compiler_params=params,
        name="gather",
    )(*sent, after[-1])
    other = lax.ppermute(mine, "sub", [(0, 1), (1, 0)])

    flux = ()
    strips = []
    for turn in range(levels - 1):
        strips.append(pl.pallas_call(
            strips_kernel,
            out_shape=array(2 * count, TILE, LANES),
            in_specs=[smem] + [vmem] * (2 + len(flux)),
            out_specs=vmem,
            scratch_shapes=[scratch(count, TILE, LANES)],
            compiler_params=params,
            name="strips",
        )(adjacency, mine, other, *flux))
        flux = (lax.ppermute(strips[-1], "level", [(source, (source - 1) % levels) for source in range(levels)]),)

    eta_new, momenta_new, ends = pl.pallas_call(
        second_kernel,
        out_shape=[array(*adjoint_height.shape), array(*adjoint_momenta.shape), array(3, 2, TILE, cols)],
        in_specs=[smem] + [vmem] * 9,
        out_specs=[hbm, hbm, vmem],
        scratch_shapes=[
            scratch(3, rows - 2 * TILE, cols), scratch(3, rows, LANES), pltpu.SemaphoreType.DMA((2, 3)),
        ],
        compiler_params=params,
        name="second",
    )(adjacency, mine, other, strips[0], *after)

    return pl.pallas_call(
        inflow_kernel,
        out_shape=[array(*adjoint_height.shape), array(*adjoint_momenta.shape)],
        in_specs=[smem] + [vmem] * 6 + [hbm] * 2,
        out_specs=[hbm, hbm],
        input_output_aliases={7: 0, 8: 1},
        scratch_shapes=[
            scratch(4, TILE, LANES), scratch(3, 2, TILE, cols), pltpu.SemaphoreType.DMA((2, 3)),
        ],
        compiler_params=params,
        name="inflow",
    )(adjacency, mine, other, *flux, after[3], after[4], ends, eta_new, momenta_new)


def solution(mesh):
    in_specs = (
        P(("parts", "level"), ("patch", "sub"), None),
        P(None, ("parts", "level"), ("patch", "sub"), None),
        P("level", ("patch", "sub"), None),
        P("level", ("patch", "sub"), None),
        P("level", None, None),
        P(None, ("patch", "sub")),
        P(None, ("patch", "sub")),
    )
    out_specs = (
        P(("parts", "level"), ("patch", "sub"), None),
        P(None, ("parts", "level"), ("patch", "sub"), None),
    )
    return jax.shard_map(body, mesh=mesh, in_specs=in_specs, out_specs=out_specs, check_vma=False)
```

```python
import jax
import jax.numpy as jnp
from jax import lax
from jax.experimental import pallas as pl
from jax.experimental.pallas import tpu as pltpu
from jax.sharding import PartitionSpec as P

STEPS = 2
LANES = 128
TILE = 8
VMEM_LIMIT = 48 * 1024 * 1024

courant = 0.45

STRIP_SUM, STRIP, STRIP_DEPTH, GAIN, INDEX, EDGE_FLOW, EDGE_DEPTH, EDGE_SUM = range(8)
(FIRST_ETA, SECOND_ETA, FIRST_ROW, FIRST_COL, FIRST_DEPTH, NEXT_ETA, LAST_ETA, NEXT_ROW,
 LAST_ROW, LAST_COL, NEXT_DEPTH, LAST_DEPTH) = range(12)
ROWS, COLUMNS = 8, 16
LINES = ROWS * TILE + COLUMNS
TRIMMED, SPARE = LINES - 2 * TILE, 4


def iota(shape, axis):
    return lax.broadcasted_iota(jnp.int32, shape, axis)


def rolled(value, shift, axis):
    if shift == 0:
        return value
    return pltpu.roll(value, shift % value.shape[axis], axis)


def wet(depth):
    return (depth > 0).astype(jnp.float32)


def copied(pairs, sems):
    copies = [pltpu.make_async_copy(source, target, sems.at[place]) for place, (source, target) in enumerate(pairs)]
    for copy in copies:
        copy.start()
    return copies


def pack_kernel(eta_ref, momenta_ref, depth_ref, wet_ref, gain_ref, index_ref, out_ref, trimmed_ref,
                ends, end_wet, sides, side_wet, gains, indices, sems):
    rows, cols = eta_ref.shape[1:]
    tall, wide = [], []
    for end in range(2):
        here = pl.ds(end * (rows - TILE), TILE)
        tall += [
            (eta_ref.at[0, here, :], ends.at[end, 0]), (momenta_ref.at[:, 0, here, :], ends.at[end, pl.ds(1, 2)]),
            (depth_ref.at[0, here, :], ends.at[end, 3]), (wet_ref.at[0, here, :], end_wet.at[end])]
        here = pl.ds(end * (cols - LANES), LANES)
        wide += [
            (eta_ref.at[0, :, here], sides.at[end, 0]), (momenta_ref.at[:, 0, :, here], sides.at[end, pl.ds(1, 2)]),
            (depth_ref.at[0, :, here], sides.at[end, 3]), (wet_ref.at[0, :, here], side_wet.at[end])]
    tall += [(gain_ref, gains), (index_ref, indices)]
    copies = copied(tall + wide, sems)
    for copy in copies[:len(tall)]:
        copy.wait()
    level = lax.axis_index("level")
    lane = iota((TILE, cols), 1)

    def loaded(end):
        mask = end_wet[end].astype(jnp.float32)
        return ends[end, 0], ends[end, 1], ends[end, 2], mask * ends[end, 3], mask

    def put(row, value):
        for tile in range(TILE):
            out_ref[row * TILE + tile:row * TILE + tile + 1] = value[:, tile * LANES:(tile + 1) * LANES]

    eta, row, col, depth, mask = loaded(0)
    east = jnp.where(lane == cols - 1, 0.0, rolled(eta, -1, 1))
    row = mask * (row - courant * (east - eta))
    west = jnp.where(lane == 0, 0.0, rolled(row, 1, 1))
    col = mask * (col - courant * (rolled(eta, -1, 0) - eta))
    strip_sum = mask * eta - courant * depth * (row - west + col)
    put(STRIP_SUM, strip_sum[:1])
    put(STRIP, eta[:1])
    put(STRIP_DEPTH, depth[:1])
    put(GAIN, gains[pl.ds(level, 1), :])
    put(INDEX, indices[pl.ds(level, 1), :].astype(jnp.float32))

    eta, row, col, depth, mask = loaded(1)
    east = jnp.where(lane == cols - 1, 0.0, rolled(eta, -1, 1))
    row = mask * (row - courant * (east - eta))
    west = jnp.where(lane == 0, 0.0, rolled(row, 1, 1))
    flow = mask * (col + courant * eta)
    above = rolled(flow - courant * mask * rolled(eta, -1, 0), 1, 0)
    edge_sum = mask * eta - courant * depth * (row - west - above)
    put(EDGE_FLOW, flow[TILE - 1:])
    put(EDGE_DEPTH, depth[TILE - 1:])
    put(EDGE_SUM, edge_sum[TILE - 1:])

    for copy in copies[len(tall):]:
        copy.wait()
    lane = iota((rows, LANES), 1)
    columns = jnp.zeros((rows, LANES), jnp.float32)
    depths = [sides[end, 3] * side_wet[end].astype(jnp.float32) for end in range(2)]
    for place, value, at in (
        (FIRST_ETA, sides[0, 0], 0), (SECOND_ETA, sides[0, 0], 1), (FIRST_ROW, sides[0, 1], 0),
        (FIRST_COL, sides[0, 2], 0), (FIRST_DEPTH, depths[0], 0),
        (NEXT_ETA, sides[1, 0], LANES - 2), (LAST_ETA, sides[1, 0], LANES - 1),
        (NEXT_ROW, sides[1, 1], LANES - 2), (LAST_ROW, sides[1, 1], LANES - 1),
        (LAST_COL, sides[1, 2], LANES - 1),
        (NEXT_DEPTH, depths[1], LANES - 2), (LAST_DEPTH, depths[1], LANES - 1),
    ):
        moved = value if place == at else rolled(value, place - at, 1)
        columns = jnp.where(lane == place, moved, columns)
    out_ref[ROWS * TILE:] = columns.T[:COLUMNS]

    def tile(row):
        return out_ref[row * TILE:(row + 1) * TILE]

    tables = sends_tables()
    flow, depth, gain, index = tile(EDGE_FLOW), tile(EDGE_DEPTH), tile(GAIN), tile(INDEX)
    trimmed_ref[:GAIN * TILE] = out_ref[:GAIN * TILE]
    trimmed_ref[GAIN * TILE:INDEX * TILE] = jnp.where(tables, gain, flow)
    trimmed_ref[INDEX * TILE:(INDEX + 1) * TILE] = jnp.where(tables, index, depth)
    trimmed_ref[(INDEX + 1) * TILE:(INDEX + 2) * TILE] = tile(EDGE_SUM)
    trimmed_ref[(INDEX + 2) * TILE:] = out_ref[ROWS * TILE:]
    spare = TRIMMED - SPARE
    for place, (other, own) in enumerate(((flow, gain), (depth, index))):
        chosen = jnp.where(tables, other, own)
        trimmed_ref[spare + 2 * place:spare + 2 * place + 1] = chosen[:1]
        trimmed_ref[spare + 2 * place + 1:spare + 2 * place + 2] = chosen[TILE - 1:]


def first_kernel(eta_ref, momenta_ref, depth_ref, wet_ref, eta_after, row_after, col_after, wet_after, depth_after,
                 turned, eta_pad, momenta_in, depth_in, wet_in, sems):
    rows, cols = row_after.shape
    parts = sems.shape[0]
    size = rows // parts
    loads = []
    for part in range(parts):
        here = pl.ds(part * size, size)
        loads.append(copied([
            (eta_ref.at[0, here, :], eta_pad.at[here, :]),
            (momenta_ref.at[:, 0, here, :], momenta_in.at[:, here, :]),
            (depth_ref.at[0, here, :], depth_in.at[here, :]),
            (wet_ref.at[0, here, :], wet_in.at[here, :]),
        ], sems.at[part]))
    lane, line = iota((TILE, cols), 1), iota((TILE, cols), 0)
    eta_pad[rows:] = jnp.zeros((TILE, cols), jnp.float32)
    eta_after[rows:] = jnp.zeros((TILE, cols), jnp.float32)
    above = jnp.zeros((1, cols), jnp.float32)
    for copy in loads[0]:
        copy.wait()
    for part in range(parts):
        if part + 1 < parts:
            for copy in loads[part + 1]:
                copy.wait()
        for low in range(part * size, (part + 1) * size, TILE):
            chunk = slice(low, low + TILE)
            mask = wet_in[chunk].astype(jnp.float32)
            depth = courant * mask * depth_in[chunk]
            below = eta_pad[low + 1:low + TILE + 1]
            eta, row, col = advanced(
                eta_pad[chunk], momenta_in[0, chunk], momenta_in[1, chunk], mask, depth,
                lambda eta: jnp.where(lane == cols - 1, 0.0, rolled(eta, -1, 1)), lambda eta: below,
                lambda row: jnp.where(lane == 0, 0.0, rolled(row, 1, 1)),
                lambda col: jnp.where(line == 0, above, rolled(col, 1, 0)))
            above = col[TILE - 1:]
            eta_after[chunk], row_after[chunk], col_after[chunk] = eta, row, col
            wet_after[chunk], depth_after[chunk] = mask, depth
    right = cols - LANES
    turned[0] = wet_after[:, :LANES].T[:TILE]
    turned[1] = depth_after[:, :LANES].T[:TILE]
    turned[2] = wet_after[:, right:].T[LANES - TILE:]
    turned[3] = depth_after[:, right:].T[LANES - TILE:]
    turned[4] = eta_after[:rows, :LANES].T[:TILE]
    turned[5] = row_after[:, right:].T[LANES - TILE:]


def sends_tables():
    return (lax.axis_index("level") == 0) & (lax.axis_index("sub") == 0)


def gather_kernel(*refs):
    first, packets, turns, out_ref = refs[0], refs[1:-2], len(refs) - 2, refs[-1]
    own = lax.axis_index("patch")
    out_ref[own] = first[...]
    tables = sends_tables()
    line = iota((TILE, LANES), 0)

    def ends_of(packet, at):
        value = jnp.where(line == 0, packet[at:at + 1], 0.0)
        return jnp.where(line == TILE - 1, packet[at + 1:at + 2], value)

    for place, packet in enumerate(packets):
        patch = own ^ (turns - 1 - place)
        if packet.shape[0] == LINES:
            out_ref[patch] = packet[...]
            continue

        def put(row, value):
            out_ref[patch, row * TILE:(row + 1) * TILE] = value

        out_ref[patch, :GAIN * TILE] = packet[:GAIN * TILE]
        whole = packet[GAIN * TILE:INDEX * TILE], packet[INDEX * TILE:(INDEX + 1) * TILE]
        ends = ends_of(packet, TRIMMED - SPARE), ends_of(packet, TRIMMED - SPARE + 2)
        put(GAIN, jnp.where(tables, whole[0], ends[0]))
        put(INDEX, jnp.where(tables, whole[1], ends[1]))
        put(EDGE_FLOW, jnp.where(tables, ends[0], whole[0]))
        put(EDGE_DEPTH, jnp.where(tables, ends[1], whole[1]))
        put(EDGE_SUM, packet[(INDEX + 1) * TILE:(INDEX + 2) * TILE])
        out_ref[patch, ROWS * TILE:] = packet[(INDEX + 2) * TILE:]


class Segment:
    def __init__(self, patch, flipped):
        self.patch, self.flipped = patch, flipped

    def place(self, patches):
        return self.flipped * patches + self.patch


def below_finest():
    return jnp.where(lax.axis_index("level") < lax.axis_size("level") - 1, 1.0, 0.0)


class Links:
    def __init__(self, links_ref, patches):
        self.links_ref, self.patches = links_ref, patches
        self.half = lax.axis_index("sub")

    def own(self):
        return Segment(lax.axis_index("patch"), 0)

    def all(self):
        return [Segment(patch, flipped) for flipped in range(2) for patch in range(self.patches)]

    def across(self, segment, way):
        patch = self.links_ref[0, segment.patch, way]
        return jnp.maximum(patch, 0), jnp.where(patch >= 0, 1.0, 0.0)

    def other_half(self, segment, way, inner):
        patch, there = self.across(segment, way)
        inside = self.half == (inner ^ segment.flipped)
        return Segment(jnp.where(inside, segment.patch, patch), 1 - segment.flipped), jnp.where(inside, 1.0, there)

    def north(self, segment):
        return self.other_half(segment, 0, 1)

    def south(self, segment):
        return self.other_half(segment, 1, 0)

    def west(self, segment):
        patch, there = self.across(segment, 2)
        return Segment(patch, segment.flipped), there

    def east(self, segment):
        patch, there = self.across(segment, 3)
        return Segment(patch, segment.flipped), there


class Packets:
    def __init__(self, got_refs):
        self.got_refs = got_refs

    def tile(self, segment, row):
        return self.got_refs[segment.flipped][segment.patch, row * TILE:(row + 1) * TILE]

    def line(self, segment, row, line):
        return self.got_refs[segment.flipped][segment.patch, row * TILE + line:row * TILE + line + 1]

    def row(self, segment, row):
        return jnp.concatenate([self.line(segment, row, line) for line in range(TILE)], axis=1)

    def column(self, segment, column):
        return self.line(segment, ROWS, column)


def is_first(shape=(TILE, LANES)):
    return (iota(shape, 0) == 0) & (iota(shape, 1) == 0)


def is_last(shape=(TILE, LANES)):
    return (iota(shape, 0) == shape[0] - 1) & (iota(shape, 1) == shape[1] - 1)


def next_cells(tile, edge):
    lane = iota(tile.shape, 1)
    moved = rolled(tile, -1, 1)
    moved = jnp.where(lane == LANES - 1, rolled(moved, -1, 0), moved)
    return jnp.where(is_last(), edge, moved)


def last_cells(tile, edge):
    lane = iota(tile.shape, 1)
    moved = rolled(tile, 1, 1)
    moved = jnp.where(lane == 0, rolled(moved, 1, 0), moved)
    return jnp.where(is_first(), edge, moved)


def row_of(ref, place):
    return jnp.concatenate([ref[place, line:line + 1] for line in range(TILE)], axis=1)


def nested(flux, index):
    lane, line = index % LANES, index // LANES
    taken = jnp.zeros(index.shape, jnp.float32)
    for source in range(TILE):
        values = jnp.broadcast_to(flux[source:source + 1], index.shape)
        found = jnp.take_along_axis(values, lane, axis=1, mode="promise_in_bounds")
        taken = jnp.where(line == source, found, taken)
    return taken


def strips_kernel(*refs):
    links_ref, mine_ref, other_ref = refs[:3]
    out_ref, strips_ref = refs[-2:]
    finer_ref = refs[3] if len(refs) == 6 else None
    links = Links(links_ref, mine_ref.shape[0])
    patches, count = links.patches, 2 * links.patches
    packets = Packets((mine_ref, other_ref))
    every = links.all()
    strips, inflows = [], []
    for segment in every:
        strip = packets.tile(segment, STRIP)
        if finer_ref is not None:
            place = segment.place(patches)
            gain, index = packets.tile(segment, GAIN) * below_finest(), packets.tile(segment, INDEX).astype(jnp.int32)
            inflow, later = [gain * nested(finer_ref[step * count + place], index) for step in range(2)]
            inflows.append((inflow, later))
            strip = strip + inflow
            strips_ref[place] = strip
        strips.append(strip)

    def strip_at(segment):
        return packets.tile(segment, STRIP) if finer_ref is None else strips_ref[segment.place(patches)]

    totals = []
    for place, segment in enumerate(every):
        eta, depth = strips[place], packets.tile(segment, STRIP_DEPTH)
        mask = wet(depth)
        east, there = links.east(segment)
        edge = there * rolled(rolled(strip_at(east), -1, 1), -1, 0)
        if finer_ref is None:
            row = jnp.where(is_last(), -courant * mask * edge, 0.0)
        else:
            inflow, later = inflows[place]
            row = courant * mask * (inflow - next_cells(inflow, edge))
        west, there = links.west(segment)
        west_eta = rolled(rolled(strip_at(west), 1, 1), 1, 0)
        west_mask = rolled(rolled(wet(packets.tile(west, STRIP_DEPTH)), 1, 1), 1, 0)
        edge = there * west_mask * (packets.column(west, LAST_ROW) - courant * (eta - west_eta))
        north, there = links.north(segment)
        col = there * (packets.tile(north, EDGE_FLOW) - courant * wet(packets.tile(north, EDGE_DEPTH)) * eta)
        total = packets.tile(segment, STRIP_SUM)
        if finer_ref is None:
            total = total - courant * depth * (row - jnp.where(is_first(), edge, 0.0) - col)
        else:
            total = (total + mask * inflow + later
                     - courant * depth * (row - last_cells(row, edge) + courant * mask * inflow - col))
        totals.append(total)
    for place, (strip, total) in enumerate(zip(strips, totals)):
        out_ref[place] = strip
        out_ref[count + place] = total


def beside(links, packets, own, inflow=None):
    lane = iota((1, LANES), 1)
    first, last = lane == 0, lane == LANES - 1

    def field(segment, column):
        return packets.column(segment, column) if inflow is None else 0.0

    def strip(name, turned):
        return 0.0 if inflow is None else jnp.where(first, rolled(inflow[name], turned, 1), 0.0)

    def corner_col(segment, eta, line, turned):
        north, beyond = links.north(segment)
        mask = rolled(wet(packets.line(north, EDGE_DEPTH, line)), turned, 1)
        flow = rolled(packets.line(north, EDGE_FLOW, line), turned, 1) if inflow is None else 0.0
        return beyond * (flow - courant * mask * eta)

    west, there = links.west(own)
    eta = field(west, LAST_ETA) + strip("west", 1)
    next_eta = field(west, NEXT_ETA) + strip("west", 2)
    own_eta = field(own, FIRST_ETA) + strip("own", 0)
    depth = packets.column(west, LAST_DEPTH) * there
    mask = wet(depth)
    next_row = wet(packets.column(west, NEXT_DEPTH)) * (field(west, NEXT_ROW) - courant * (eta - next_eta))
    below, beyond = links.south(west)
    corner = packets.line(below, STRIP, TILE - 1) if inflow is None else inflow["south west"]
    south_eta = jnp.where(last, corner * beyond, rolled(eta, -1, 1))
    col = mask * (field(west, LAST_COL) - courant * (south_eta - eta))
    north_col = jnp.where(first, corner_col(west, eta, TILE - 1, 1), rolled(col, 1, 1))
    west_row = mask * (field(west, LAST_ROW) - courant * (own_eta - eta))
    west_eta = (mask * eta - courant * depth * (west_row - next_row + col - north_col) + strip("west later", 1))
    west_mask = mask

    east, there = links.east(own)
    eta = there * (field(east, FIRST_ETA) + strip("east", 0))
    second_eta = field(east, SECOND_ETA) + strip("east", -1)
    depth = packets.column(east, FIRST_DEPTH) * there
    mask = wet(depth)
    row = mask * (field(east, FIRST_ROW) - courant * (second_eta - eta))
    below, beyond = links.south(east)
    corner = packets.line(below, STRIP, 0) if inflow is None else inflow["south east"]
    south_eta = jnp.where(last, rolled(corner, -1, 1) * beyond, rolled(eta, -1, 1))
    col = mask * (field(east, FIRST_COL) - courant * (south_eta - eta))
    north_col = jnp.where(first, corner_col(east, eta, 0, 0), rolled(col, 1, 1))
    east_sum = mask * eta - courant * depth * (row + col - north_col) + there * strip("east later", 0)
    return west_row, west_mask, west_eta, eta, east_sum, courant * depth


def advanced(eta, row, col, mask, depth, east, south, west, north):
    row = mask * (row - courant * (east(eta) - eta))
    col = mask * (col - courant * (south(eta) - eta))
    return mask * eta - depth * (row - west(row) + col - north(col)), row, col


def two_steps(start, mask, depth, sides, base, north=None, south=None, second=None):
    lane, line = iota(mask.shape, 1), iota(mask.shape, 0)
    cols = mask.shape[1]
    west_row, west_mask, west_eta, east_eta, east_sum, east_depth = sides
    state = start, 0.0, 0.0
    flow, beyond = west_row, east_eta
    above = 0.0 if north is None else north[0]
    for number in range(2):
        below = 0.0 if south is None else south[number]
        state = advanced(
            *state, mask, depth,
            lambda eta: jnp.where(lane == cols - 1, beyond, rolled(eta, -1, 1)),
            lambda eta: jnp.where(line == TILE - 1, below, rolled(eta, -1, 0)),
            lambda row: jnp.where(lane == 0, flow, rolled(row, 1, 1)),
            lambda col: jnp.where(line == 0, above, rolled(col, 1, 0)))
        if number:
            return state
        eta, row, col = state
        if second is not None:
            eta = eta + jnp.where(line == 0, second, 0.0)
            state = eta, row, col
        whole_eta, whole_row = (eta, row) if base is None else (eta + base[0], row + base[1])
        flow = west_mask * (west_row - courant * (whole_eta[:, :1] - west_eta))
        beyond = east_sum + east_depth * whole_row[:, cols - 1:]
        if north is not None:
            above = north[1] * (north[0] - courant * (whole_eta[:1] - north[2]))


def north_of(links, packets, own, own_strip, inflow=None):
    cols = own_strip.shape[1]
    lane = iota((1, LANES), 1)
    north, there = links.north(own)
    depth = packets.row(north, EDGE_DEPTH) * there
    mask = wet(depth)
    if inflow is not None:
        col = -courant * mask * own_strip
        return col, mask, -courant * depth * col
    col = packets.row(north, EDGE_FLOW) * there - courant * mask * own_strip
    north_east, beyond = links.east(north)
    right_eta = beyond * packets.column(north_east, FIRST_ETA)
    north_west, beyond = links.west(north)
    left_row = beyond * wet(packets.column(north_west, LAST_DEPTH)) * (
        packets.column(north_west, LAST_ROW)
        - courant * (packets.column(north, FIRST_ETA) - packets.column(north_west, LAST_ETA)))
    nothing = jnp.zeros((1, cols - LANES), jnp.float32)
    corners = (jnp.concatenate([jnp.where(lane == 0, rolled(left_row, 1, 1), 0.0), nothing], axis=1)
               + jnp.concatenate([nothing, jnp.where(lane == LANES - 1, courant * right_eta, 0.0)], axis=1))
    return col, mask, packets.row(north, EDGE_SUM) + courant * depth * (corners - col)


def as_sublanes(columns):
    rows = columns[0].shape[1]
    count = -len(columns) % TILE
    turned = jnp.concatenate(list(columns) + [jnp.zeros((count, rows), jnp.float32)], axis=0).T
    return [[turned[low:low + TILE, place:place + 1] for place in range(len(columns))]
            for low in (0, rows - TILE)]


def second_kernel(links_ref, mine_ref, other_ref, strips_ref, eta_after, row_after, col_after, wet_after,
                  depth_after, turned, eta_out, momenta_out, ends_out, new_ref, more_ref, sems):
    rows, cols = row_after.shape
    links = Links(links_ref, mine_ref.shape[0])
    own = links.own()
    packets = Packets((mine_ref, other_ref))
    columns = beside(links, packets, own)
    west_row, west_mask, west_eta, east_eta, east_sum, east_depth = columns

    line, lane = iota((TILE, rows), 0), iota((TILE, rows), 1)
    nothing = jnp.zeros((TILE, rows), jnp.float32)

    def column_steps(mask, depth, east, west):
        state = nothing, nothing, nothing
        for number in range(2):
            state = advanced(
                *state, mask, depth,
                lambda eta: jnp.where(line == TILE - 1, east(number, state), rolled(eta, -1, 0)),
                lambda eta: jnp.where(lane == rows - 1, 0.0, rolled(eta, -1, 1)),
                lambda row: jnp.where(line == 0, west(number, state), rolled(row, 1, 0)),
                lambda col: jnp.where(lane == 0, 0.0, rolled(col, 1, 1)))
        return state

    def west_of(number, state):
        if number == 0:
            return west_row
        whole = state[0][:1] + turned[4, :1]
        return west_mask * (west_row - courant * (whole - west_eta))

    def east_of(number, state):
        if number == 0:
            return east_eta
        return east_sum + east_depth * (state[1][TILE - 1:] + turned[5, TILE - 1:])

    left = column_steps(turned[0], turned[1], lambda number, state: 0.0, west_of)
    last = column_steps(turned[2], turned[3], east_of, lambda number, state: 0.0)
    middle = jnp.zeros((LANES - 2 * TILE, rows), jnp.float32)
    for place in range(3):
        more_ref[place] = jnp.concatenate([left[place], middle, last[place]], axis=0).T

    line, lane = iota((TILE, cols), 0), iota((TILE, cols), 1)
    inside = iota((TILE, LANES), 1)
    outs = eta_out.at[0], momenta_out.at[0, 0], momenta_out.at[1, 0]
    above = jnp.zeros((1, cols), jnp.float32)
    parts = sems.shape[0]
    size = (rows - 2 * TILE) // parts
    copies = []
    for first in range(0, rows, TILE):
        chunk = slice(first, first + TILE)
        south = eta_after[first + 1:first + TILE + 1]
        fields = advanced(
            eta_after[chunk], row_after[chunk], col_after[chunk], wet_after[chunk], depth_after[chunk],
            lambda eta: jnp.where(lane == cols - 1, 0.0, rolled(eta, -1, 1)), lambda eta: south,
            lambda row: jnp.where(lane == 0, 0.0, rolled(row, 1, 1)),
            lambda col: jnp.where(line == 0, above, rolled(col, 1, 0)))
        above = fields[2][TILE - 1:]
        for place, field in enumerate(fields):
            more = more_ref[place, chunk]
            sides = [jnp.where(inside < TILE, more, 0.0), jnp.where(inside >= LANES - TILE, more, 0.0)]
            if first in (0, rows - TILE):
                ends_out[place, int(first > 0)] = field
            else:
                new_ref[place, first - TILE:first] = jnp.concatenate(
                    [field[:, :LANES] + sides[0], field[:, LANES:cols - LANES], field[:, cols - LANES:] + sides[1]],
                    axis=1)
        if first and first % size == 0 and first < rows - TILE:
            part = first // size - 1
            here, there = pl.ds(part * size, size), pl.ds(TILE + part * size, size)
            copies += copied([(new_ref.at[place, here], out.at[there, :]) for place, out in enumerate(outs)],
                             sems.at[part])
    top_sides, low_sides = as_sublanes(columns)
    nothing = jnp.zeros((TILE, cols), jnp.float32)
    end = slice(rows - TILE, rows)
    top = two_steps(
        nothing, wet_after[:TILE], depth_after[:TILE], top_sides, (eta_after[:TILE], row_after[:TILE]),
        north=north_of(links, packets, own, packets.row(own, STRIP)))
    below, there = links.south(own)
    low = two_steps(
        nothing, wet_after[end], depth_after[end], low_sides, (eta_after[end], row_after[end]),
        south=(packets.row(below, STRIP) * there,
               row_of(strips_ref, 2 * links.patches + below.place(links.patches)) * there))
    gap = jnp.zeros((TILE, cols - 2 * LANES), jnp.float32)
    for edge, (chunk, near, found) in enumerate(
            ((slice(0, TILE), line < TILE // 2, top), (end, line >= TILE // 2, low))):
        for place in range(3):
            more = more_ref[place, chunk]
            wide = jnp.concatenate(
                [jnp.where(inside < TILE, more, 0.0), gap, jnp.where(inside >= LANES - TILE, more, 0.0)], axis=1)
            ends_out[place, edge] += jnp.where(near, found[place], wide)
    for copy in copies:
        copy.wait()


def inflow_kernel(links_ref, mine_ref, other_ref, finer_ref, wet_after, depth_after, ends_ref, eta_hbm, momenta_hbm,
                  eta_out, momenta_out, rows_ref, new_ref, sems):
    del eta_hbm, momenta_hbm
    rows, cols = wet_after.shape
    links = Links(links_ref, mine_ref.shape[0])
    patches = links.patches
    own = links.own()
    packets = Packets((mine_ref, other_ref))
    some = below_finest()

    def flux_place(step, segment):
        return step * 2 * patches + segment.place(patches)

    def inflows(segment):
        gain, index = packets.tile(segment, GAIN) * some, packets.tile(segment, INDEX).astype(jnp.int32)
        return [gain * nested(finer_ref[flux_place(step, segment)], index) for step in range(2)]

    below, there = links.south(own)
    west, east = links.west(own)[0], links.east(own)[0]
    below_west, beyond_west = links.west(below)
    below_east, beyond_east = links.east(below)
    wanted = (
        ("west", 0, west, TILE - 1), ("west later", 1, west, TILE - 1), ("east", 0, east, 0),
        ("east later", 1, east, 0), ("south west", 0, links.south(west)[0], TILE - 1),
        ("south east", 0, links.south(east)[0], 0), ("below west", 0, below_west, TILE - 1),
        ("below east", 0, below_east, 0))
    gain = jnp.concatenate([packets.line(segment, GAIN, line) for _, _, segment, line in wanted], axis=0)
    index = jnp.concatenate([packets.line(segment, INDEX, line) for _, _, segment, line in wanted], axis=0)
    index = index.astype(jnp.int32)
    lane, line = index % LANES, index // LANES
    taken = jnp.zeros((TILE, LANES), jnp.float32)
    for source in range(TILE):
        values = jnp.concatenate(
            [finer_ref[flux_place(step, segment), source:source + 1] for _, step, segment, _ in wanted], axis=0)
        found = jnp.take_along_axis(values, lane, axis=1, mode="promise_in_bounds")
        taken = jnp.where(line == source, found, taken)
    taken = some * gain * taken
    inflow = {name: taken[place:place + 1] for place, (name, _, _, _) in enumerate(wanted)}

    rows_ref[0], rows_ref[1] = inflows(own)
    strip, later = inflows(below)
    strip, later = strip * there, later * there
    inflow["own"] = rows_ref[0, :1]

    depth = packets.tile(below, STRIP_DEPTH)
    mask = wet(depth)
    edge = jnp.broadcast_to(rolled(inflow["below east"] * beyond_east, -1, 1), (TILE, LANES))
    row = courant * mask * (strip - next_cells(strip, edge))
    west_mask = rolled(wet(packets.line(below_west, STRIP_DEPTH, TILE - 1)), 1, 1)
    edge = beyond_west * courant * west_mask * (rolled(inflow["below west"], 1, 1) - strip[:1])
    edge = jnp.broadcast_to(edge, (TILE, LANES))
    north, beyond = links.north(below)
    col = -courant * wet(packets.tile(north, EDGE_DEPTH)) * beyond * strip
    rows_ref[2] = strip
    rows_ref[3] = there * (
        mask * strip - courant * depth * (row - last_cells(row, edge) + courant * mask * strip - col) + later)

    columns = beside(links, packets, own, inflow)
    top_sides, low_sides = as_sublanes(columns)
    line = iota((TILE, cols), 0)
    strip = row_of(rows_ref, 0)
    top = two_steps(
        jnp.where(line == 0, strip, 0.0), wet_after[:TILE], depth_after[:TILE], top_sides, None,
        north=north_of(links, packets, own, strip, inflow), second=row_of(rows_ref, 1))
    copies = []
    outs = eta_out.at[0], momenta_out.at[0, 0], momenta_out.at[1, 0]

    def write(end, near, found):
        for place in range(3):
            new_ref[place, end] = ends_ref[place, end] + jnp.where(near, found[place], 0.0)
        here = pl.ds(end * (rows - TILE), TILE)
        copies.extend(copied(
            [(new_ref.at[place, end], out.at[here, :]) for place, out in enumerate(outs)], sems.at[end]))

    write(0, line < TILE // 2, top)
    low = two_steps(
        jnp.zeros((TILE, cols), jnp.float32), wet_after[rows - TILE:], depth_after[rows - TILE:],
        low_sides, None, south=(row_of(rows_ref, 2), row_of(rows_ref, 3)))
    write(1, line >= TILE // 2, low)
    for copy in copies:
        copy.wait()


def body(adjoint_height, adjoint_momenta, depth, wet_mask, adjacency, nest_gain, nest_index):
    rows, cols = adjoint_height.shape[1:]
    levels = lax.axis_size("level")
    patches = lax.axis_size("patch")
    count = 2 * patches
    params = pltpu.CompilerParams(vmem_limit_bytes=VMEM_LIMIT)
    vmem = pl.BlockSpec(memory_space=pltpu.VMEM)
    smem = pl.BlockSpec(memory_space=pltpu.SMEM)
    hbm = pl.BlockSpec(memory_space=pltpu.HBM)

    def array(*shape):
        return jax.ShapeDtypeStruct(shape, jnp.float32)

    def scratch(*shape):
        return pltpu.VMEM(shape, jnp.float32)

    fields = [pltpu.with_memory_space_constraint(field, pltpu.HBM)
              for field in (adjoint_height, adjoint_momenta, depth, wet_mask, nest_gain, nest_index)]
    packed, trimmed = pl.pallas_call(
        pack_kernel,
        out_shape=[array(LINES, LANES), array(TRIMMED, LANES)],
        in_specs=[hbm] * 6,
        out_specs=[vmem, vmem],
        scratch_shapes=[
            scratch(2, 4, TILE, cols), pltpu.VMEM((2, TILE, cols), jnp.int32),
            scratch(2, 4, rows, LANES), pltpu.VMEM((2, rows, LANES), jnp.int32),
            scratch(levels, cols), pltpu.VMEM((levels, cols), jnp.int32),
            pltpu.SemaphoreType.DMA((18,)),
        ],
        compiler_params=params,
        name="pack",
    )(*fields)
    parts = 4
    after = pl.pallas_call(
        first_kernel,
        out_shape=[
            array(rows + TILE, cols), array(rows, cols), array(rows, cols), array(rows, cols), array(rows, cols),
            array(6, TILE, rows),
        ],
        in_specs=[hbm] * 4,
        out_specs=[vmem] * 6,
        scratch_shapes=[
            scratch(rows + TILE, cols), scratch(2, rows, cols), scratch(rows, cols),
            pltpu.VMEM((rows, cols), jnp.int32), pltpu.SemaphoreType.DMA((parts, 4)),
        ],
        compiler_params=params,
        name="first",
    )(*fields[:4])

    sent = [packed] + [
        lax.ppermute(trimmed if levels == 2 else packed, "patch",
                     [(source, source ^ turn) for source in range(patches)])
        for turn in range(patches - 1, 0, -1)
    ]
    mine = pl.pallas_call(
        gather_kernel,
        out_shape=array(patches, LINES, LANES),
        in_specs=[vmem] * (patches + 1),
        out_specs=vmem,
        compiler_params=params,
        name="gather",
    )(*sent, after[-1])
    other = lax.ppermute(mine, "sub", [(0, 1), (1, 0)])

    flux = ()
    strips = []
    for turn in range(levels - 1):
        strips.append(pl.pallas_call(
            strips_kernel,
            out_shape=array(2 * count, TILE, LANES),
            in_specs=[smem] + [vmem] * (2 + len(flux)),
            out_specs=vmem,
            scratch_shapes=[scratch(count, TILE, LANES)],
            compiler_params=params,
            name="strips",
        )(adjacency, mine, other, *flux))
        flux = (lax.ppermute(strips[-1], "level", [(source, (source - 1) % levels) for source in range(levels)]),)

    eta_new, momenta_new, ends = pl.pallas_call(
        second_kernel,
        out_shape=[array(*adjoint_height.shape), array(*adjoint_momenta.shape), array(3, 2, TILE, cols)],
        in_specs=[smem] + [vmem] * 9,
        out_specs=[hbm, hbm, vmem],
        scratch_shapes=[
            scratch(3, rows - 2 * TILE, cols), scratch(3, rows, LANES), pltpu.SemaphoreType.DMA((2, 3)),
        ],
        compiler_params=params,
        name="second",
    )(adjacency, mine, other, strips[0], *after)

    return pl.pallas_call(
        inflow_kernel,
        out_shape=[array(*adjoint_height.shape), array(*adjoint_momenta.shape)],
        in_specs=[smem] + [vmem] * 6 + [hbm] * 2,
        out_specs=[hbm, hbm],
        input_output_aliases={7: 0, 8: 1},
        scratch_shapes=[
            scratch(4, TILE, LANES), scratch(3, 2, TILE, cols), pltpu.SemaphoreType.DMA((2, 3)),
        ],
        compiler_params=params,
        name="inflow",
    )(adjacency, mine, other, *flux, after[3], after[4], ends, eta_new, momenta_new)


def solution(mesh):
    in_specs = (
        P(("parts", "level"), ("patch", "sub"), None),
        P(None, ("parts", "level"), ("patch", "sub"), None),
        P("level", ("patch", "sub"), None),
        P("level", ("patch", "sub"), None),
        P("level", None, None),
        P(None, ("patch", "sub")),
        P(None, ("patch", "sub")),
    )
    out_specs = (
        P(("parts", "level"), ("patch", "sub"), None),
        P(None, ("parts", "level"), ("patch", "sub"), None),
    )
    return jax.shard_map(body, mesh=mesh, in_specs=in_specs, out_specs=out_specs, check_vma=False)
```

```python
import jax
import jax.numpy as jnp
from jax import lax
from jax.experimental import pallas as pl
from jax.experimental.pallas import tpu as pltpu
from jax.sharding import PartitionSpec as P

STEPS = 2
LANES = 128
TILE = 8
VMEM_LIMIT = 48 * 1024 * 1024

courant = 0.45

STRIP_SUM, STRIP, STRIP_DEPTH, GAIN, INDEX, EDGE_FLOW, EDGE_DEPTH, EDGE_SUM = range(8)
(FIRST_ETA, SECOND_ETA, FIRST_ROW, FIRST_COL, FIRST_DEPTH, NEXT_ETA, LAST_ETA, NEXT_ROW,
 LAST_ROW, LAST_COL, NEXT_DEPTH, LAST_DEPTH) = range(12)
ROWS, COLUMNS = 8, 16
LINES = ROWS * TILE + COLUMNS
TRIMMED, SPARE = LINES - 2 * TILE, 4


def iota(shape, axis):
    return lax.broadcasted_iota(jnp.int32, shape, axis)


def rolled(value, shift, axis):
    if shift == 0:
        return value
    return pltpu.roll(value, shift % value.shape[axis], axis)


def wet(depth):
    return (depth > 0).astype(jnp.float32)


def copied(pairs, sems):
    copies = [pltpu.make_async_copy(source, target, sems.at[place]) for place, (source, target) in enumerate(pairs)]
    for copy in copies:
        copy.start()
    return copies


def pack_kernel(eta_ref, momenta_ref, depth_ref, wet_ref, gain_ref, index_ref, out_ref, trimmed_ref,
                ends, end_wet, sides, side_wet, gains, indices, sems):
    rows, cols = eta_ref.shape[1:]
    tall, wide = [], []
    for end in range(2):
        here = pl.ds(end * (rows - TILE), TILE)
        tall += [
            (eta_ref.at[0, here, :], ends.at[end, 0]), (momenta_ref.at[:, 0, here, :], ends.at[end, pl.ds(1, 2)]),
            (depth_ref.at[0, here, :], ends.at[end, 3]), (wet_ref.at[0, here, :], end_wet.at[end])]
        here = pl.ds(end * (cols - LANES), LANES)
        wide += [
            (eta_ref.at[0, :, here], sides.at[end, 0]), (momenta_ref.at[:, 0, :, here], sides.at[end, pl.ds(1, 2)]),
            (depth_ref.at[0, :, here], sides.at[end, 3]), (wet_ref.at[0, :, here], side_wet.at[end])]
    tall += [(gain_ref, gains), (index_ref, indices)]
    copies = copied(tall + wide, sems)
    for copy in copies[:len(tall)]:
        copy.wait()
    level = lax.axis_index("level")
    lane = iota((TILE, cols), 1)

    def loaded(end):
        mask = end_wet[end].astype(jnp.float32)
        return ends[end, 0], ends[end, 1], ends[end, 2], mask * ends[end, 3], mask

    def put(row, value):
        for tile in range(TILE):
            out_ref[row * TILE + tile:row * TILE + tile + 1] = value[:, tile * LANES:(tile + 1) * LANES]

    eta, row, col, depth, mask = loaded(0)
    east = jnp.where(lane == cols - 1, 0.0, rolled(eta, -1, 1))
    row = mask * (row - courant * (east - eta))
    west = jnp.where(lane == 0, 0.0, rolled(row, 1, 1))
    col = mask * (col - courant * (rolled(eta, -1, 0) - eta))
    strip_sum = mask * eta - courant * depth * (row - west + col)
    put(STRIP_SUM, strip_sum[:1])
    put(STRIP, eta[:1])
    put(STRIP_DEPTH, depth[:1])
    put(GAIN, gains[pl.ds(level, 1), :])
    put(INDEX, indices[pl.ds(level, 1), :].astype(jnp.float32))

    eta, row, col, depth, mask = loaded(1)
    east = jnp.where(lane == cols - 1, 0.0, rolled(eta, -1, 1))
    row = mask * (row - courant * (east - eta))
    west = jnp.where(lane == 0, 0.0, rolled(row, 1, 1))
    flow = mask * (col + courant * eta)
    above = rolled(flow - courant * mask * rolled(eta, -1, 0), 1, 0)
    edge_sum = mask * eta - courant * depth * (row - west - above)
    put(EDGE_FLOW, flow[TILE - 1:])
    put(EDGE_DEPTH, depth[TILE - 1:])
    put(EDGE_SUM, edge_sum[TILE - 1:])

    for copy in copies[len(tall):]:
        copy.wait()
    lane = iota((rows, LANES), 1)
    columns = jnp.zeros((rows, LANES), jnp.float32)
    depths = [sides[end, 3] * side_wet[end].astype(jnp.float32) for end in range(2)]
    for place, value, at in (
        (FIRST_ETA, sides[0, 0], 0), (SECOND_ETA, sides[0, 0], 1), (FIRST_ROW, sides[0, 1], 0),
        (FIRST_COL, sides[0, 2], 0), (FIRST_DEPTH, depths[0], 0),
        (NEXT_ETA, sides[1, 0], LANES - 2), (LAST_ETA, sides[1, 0], LANES - 1),
        (NEXT_ROW, sides[1, 1], LANES - 2), (LAST_ROW, sides[1, 1], LANES - 1),
        (LAST_COL, sides[1, 2], LANES - 1),
        (NEXT_DEPTH, depths[1], LANES - 2), (LAST_DEPTH, depths[1], LANES - 1),
    ):
        moved = value if place == at else rolled(value, place - at, 1)
        columns = jnp.where(lane == place, moved, columns)
    out_ref[ROWS * TILE:] = columns.T[:COLUMNS]

    def tile(row):
        return out_ref[row * TILE:(row + 1) * TILE]

    tables = sends_tables()
    flow, depth, gain, index = tile(EDGE_FLOW), tile(EDGE_DEPTH), tile(GAIN), tile(INDEX)
    trimmed_ref[:GAIN * TILE] = out_ref[:GAIN * TILE]
    trimmed_ref[GAIN * TILE:INDEX * TILE] = jnp.where(tables, gain, flow)
    trimmed_ref[INDEX * TILE:(INDEX + 1) * TILE] = jnp.where(tables, index, depth)
    trimmed_ref[(INDEX + 1) * TILE:(INDEX + 2) * TILE] = tile(EDGE_SUM)
    trimmed_ref[(INDEX + 2) * TILE:] = out_ref[ROWS * TILE:]
    spare = TRIMMED - SPARE
    for place, (other, own) in enumerate(((flow, gain), (depth, index))):
        chosen = jnp.where(tables, other, own)
        trimmed_ref[spare + 2 * place:spare + 2 * place + 1] = chosen[:1]
        trimmed_ref[spare + 2 * place + 1:spare + 2 * place + 2] = chosen[TILE - 1:]


def bulk_kernel(eta_ref, momenta_ref, depth_ref, wet_ref, eta_after, momenta_after, wet_after, depth_after,
                eta_ends, row_ends, turned, eta_pad, col_pad, momenta_in, depth_in, wet_in, eta_left, row_right, sems):
    rows, cols = eta_ref.shape[1:]
    parts = sems.shape[0]
    size = rows // parts
    loads = []
    for part in range(parts):
        here = pl.ds(part * size, size)
        loads.append(copied([
            (eta_ref.at[0, here, :], eta_pad.at[pl.ds(TILE + part * size, size), :]),
            (momenta_ref.at[:, 0, here, :], momenta_in.at[:, here, :]),
            (depth_ref.at[0, here, :], depth_in.at[here, :]),
            (wet_ref.at[0, here, :], wet_in.at[here, :]),
        ], sems.at[part]))
    lane = iota((TILE, cols), 1)
    eta_pad[TILE + rows:] = jnp.zeros((TILE, cols), jnp.float32)
    col_pad[:TILE] = jnp.zeros((TILE, cols), jnp.float32)

    def step(number, low):
        chunk, padded = slice(low, low + TILE), slice(TILE + low, 2 * TILE + low)
        eta = eta_pad[padded]
        if number == 0:
            mask = wet_in[chunk].astype(jnp.float32)
            depth = courant * mask * depth_in[chunk]
            wet_after[chunk] = mask
            depth_after[chunk] = depth
            row, col = momenta_in[0, chunk], momenta_in[1, chunk]
        else:
            mask, depth = wet_after[chunk], depth_after[chunk]
            row, col = momenta_after[0, chunk], col_pad[padded]
        east = jnp.where(lane == cols - 1, 0.0, rolled(eta, -1, 1))
        south = eta_pad[TILE + low + 1:2 * TILE + low + 1]
        row = mask * (row - courant * (east - eta))
        col = mask * (col - courant * (south - eta))
        momenta_after[0, chunk] = row
        col_pad[padded] = col
        if number:
            momenta_after[1, chunk] = col
        west = jnp.where(lane == 0, 0.0, rolled(row, 1, 1))
        north = col_pad[TILE + low - 1:2 * TILE + low - 1]
        eta = mask * eta - depth * (row - west + (col - north))
        if number:
            eta_after[chunk] = eta
            return
        eta_pad[padded] = eta
        eta_left[chunk] = eta[:, :LANES]
        row_right[chunk] = row[:, cols - LANES:]
        if low in (0, rows - TILE):
            end = int(low > 0)
            eta_ends[end] = eta
            row_ends[end] = row

    for copy in loads[0]:
        copy.wait()
    for part in range(parts + 1):
        if part + 1 < parts:
            for copy in loads[part + 1]:
                copy.wait()
        if part < parts:
            for low in range(part * size, (part + 1) * size, TILE):
                step(0, low)
        if part:
            for low in range((part - 1) * size, part * size, TILE):
                step(1, low)
    right = cols - LANES
    turned[0] = wet_after[:, :LANES].T[:TILE]
    turned[1] = depth_after[:, :LANES].T[:TILE]
    turned[2] = wet_after[:, right:].T[LANES - TILE:]
    turned[3] = depth_after[:, right:].T[LANES - TILE:]
    turned[4] = eta_left[...].T[:TILE]
    turned[5] = row_right[...].T[LANES - TILE:]


def sends_tables():
    return (lax.axis_index("level") == 0) & (lax.axis_index("sub") == 0)


def gather_kernel(*refs):
    first, packets, turns, out_ref = refs[0], refs[1:-2], len(refs) - 2, refs[-1]
    own = lax.axis_index("patch")
    out_ref[own] = first[...]
    tables = sends_tables()
    line = iota((TILE, LANES), 0)

    def ends_of(packet, at):
        value = jnp.where(line == 0, packet[at:at + 1], 0.0)
        return jnp.where(line == TILE - 1, packet[at + 1:at + 2], value)

    for place, packet in enumerate(packets):
        patch = own ^ (turns - 1 - place)
        if packet.shape[0] == LINES:
            out_ref[patch] = packet[...]
            continue

        def put(row, value):
            out_ref[patch, row * TILE:(row + 1) * TILE] = value

        out_ref[patch, :GAIN * TILE] = packet[:GAIN * TILE]
        whole = packet[GAIN * TILE:INDEX * TILE], packet[INDEX * TILE:(INDEX + 1) * TILE]
        ends = ends_of(packet, TRIMMED - SPARE), ends_of(packet, TRIMMED - SPARE + 2)
        put(GAIN, jnp.where(tables, whole[0], ends[0]))
        put(INDEX, jnp.where(tables, whole[1], ends[1]))
        put(EDGE_FLOW, jnp.where(tables, ends[0], whole[0]))
        put(EDGE_DEPTH, jnp.where(tables, ends[1], whole[1]))
        put(EDGE_SUM, packet[(INDEX + 1) * TILE:(INDEX + 2) * TILE])
        out_ref[patch, ROWS * TILE:] = packet[(INDEX + 2) * TILE:]


class Segment:
    def __init__(self, patch, flipped):
        self.patch, self.flipped = patch, flipped

    def place(self, patches):
        return self.flipped * patches + self.patch


def below_finest():
    return jnp.where(lax.axis_index("level") < lax.axis_size("level") - 1, 1.0, 0.0)


class Links:
    def __init__(self, links_ref, patches):
        self.links_ref, self.patches = links_ref, patches
        self.half = lax.axis_index("sub")

    def own(self):
        return Segment(lax.axis_index("patch"), 0)

    def all(self):
        return [Segment(patch, flipped) for flipped in range(2) for patch in range(self.patches)]

    def across(self, segment, way):
        patch = self.links_ref[0, segment.patch, way]
        return jnp.maximum(patch, 0), jnp.where(patch >= 0, 1.0, 0.0)

    def other_half(self, segment, way, inner):
        patch, there = self.across(segment, way)
        inside = self.half == (inner ^ segment.flipped)
        return Segment(jnp.where(inside, segment.patch, patch), 1 - segment.flipped), jnp.where(inside, 1.0, there)

    def north(self, segment):
        return self.other_half(segment, 0, 1)

    def south(self, segment):
        return self.other_half(segment, 1, 0)

    def west(self, segment):
        patch, there = self.across(segment, 2)
        return Segment(patch, segment.flipped), there

    def east(self, segment):
        patch, there = self.across(segment, 3)
        return Segment(patch, segment.flipped), there


class Packets:
    def __init__(self, got_refs):
        self.got_refs = got_refs

    def tile(self, segment, row):
        return self.got_refs[segment.flipped][segment.patch, row * TILE:(row + 1) * TILE]

    def line(self, segment, row, line):
        return self.got_refs[segment.flipped][segment.patch, row * TILE + line:row * TILE + line + 1]

    def row(self, segment, row):
        return jnp.concatenate([self.line(segment, row, line) for line in range(TILE)], axis=1)

    def column(self, segment, column):
        return self.line(segment, ROWS, column)


def is_first(shape=(TILE, LANES)):
    return (iota(shape, 0) == 0) & (iota(shape, 1) == 0)


def is_last(shape=(TILE, LANES)):
    return (iota(shape, 0) == shape[0] - 1) & (iota(shape, 1) == shape[1] - 1)


def next_cells(tile, edge):
    lane = iota(tile.shape, 1)
    moved = rolled(tile, -1, 1)
    moved = jnp.where(lane == LANES - 1, rolled(moved, -1, 0), moved)
    return jnp.where(is_last(), edge, moved)


def last_cells(tile, edge):
    lane = iota(tile.shape, 1)
    moved = rolled(tile, 1, 1)
    moved = jnp.where(lane == 0, rolled(moved, 1, 0), moved)
    return jnp.where(is_first(), edge, moved)


def row_of(ref, place):
    return jnp.concatenate([ref[place, line:line + 1] for line in range(TILE)], axis=1)


def nested(flux, index):
    lane, line = index % LANES, index // LANES
    taken = jnp.zeros(index.shape, jnp.float32)
    for source in range(TILE):
        values = jnp.broadcast_to(flux[source:source + 1], index.shape)
        found = jnp.take_along_axis(values, lane, axis=1, mode="promise_in_bounds")
        taken = jnp.where(line == source, found, taken)
    return taken


def strips_kernel(*refs):
    links_ref, mine_ref, other_ref = refs[:3]
    out_ref, strips_ref = refs[-2:]
    finer_ref = refs[3] if len(refs) == 6 else None
    links = Links(links_ref, mine_ref.shape[0])
    patches, count = links.patches, 2 * links.patches
    packets = Packets((mine_ref, other_ref))
    every = links.all()
    strips, inflows = [], []
    for segment in every:
        strip = packets.tile(segment, STRIP)
        if finer_ref is not None:
            place = segment.place(patches)
            gain, index = packets.tile(segment, GAIN) * below_finest(), packets.tile(segment, INDEX).astype(jnp.int32)
            inflow, later = [gain * nested(finer_ref[step * count + place], index) for step in range(2)]
            inflows.append((inflow, later))
            strip = strip + inflow
            strips_ref[place] = strip
        strips.append(strip)

    def strip_at(segment):
        return packets.tile(segment, STRIP) if finer_ref is None else strips_ref[segment.place(patches)]

    totals = []
    for place, segment in enumerate(every):
        eta, depth = strips[place], packets.tile(segment, STRIP_DEPTH)
        mask = wet(depth)
        east, there = links.east(segment)
        edge = there * rolled(rolled(strip_at(east), -1, 1), -1, 0)
        if finer_ref is None:
            row = jnp.where(is_last(), -courant * mask * edge, 0.0)
        else:
            inflow, later = inflows[place]
            row = courant * mask * (inflow - next_cells(inflow, edge))
        west, there = links.west(segment)
        west_eta = rolled(rolled(strip_at(west), 1, 1), 1, 0)
        west_mask = rolled(rolled(wet(packets.tile(west, STRIP_DEPTH)), 1, 1), 1, 0)
        edge = there * west_mask * (packets.column(west, LAST_ROW) - courant * (eta - west_eta))
        north, there = links.north(segment)
        col = there * (packets.tile(north, EDGE_FLOW) - courant * wet(packets.tile(north, EDGE_DEPTH)) * eta)
        total = packets.tile(segment, STRIP_SUM)
        if finer_ref is None:
            total = total - courant * depth * (row - jnp.where(is_first(), edge, 0.0) - col)
        else:
            total = (total + mask * inflow + later
                     - courant * depth * (row - last_cells(row, edge) + courant * mask * inflow - col))
        totals.append(total)
    for place, (strip, total) in enumerate(zip(strips, totals)):
        out_ref[place] = strip
        out_ref[count + place] = total


def beside(links, packets, own, inflow=None):
    lane = iota((1, LANES), 1)
    first, last = lane == 0, lane == LANES - 1

    def field(segment, column):
        return packets.column(segment, column) if inflow is None else 0.0

    def strip(name, turned):
        return 0.0 if inflow is None else jnp.where(first, rolled(inflow[name], turned, 1), 0.0)

    def corner_col(segment, eta, line, turned):
        north, beyond = links.north(segment)
        mask = rolled(wet(packets.line(north, EDGE_DEPTH, line)), turned, 1)
        flow = rolled(packets.line(north, EDGE_FLOW, line), turned, 1) if inflow is None else 0.0
        return beyond * (flow - courant * mask * eta)

    west, there = links.west(own)
    eta = field(west, LAST_ETA) + strip("west", 1)
    next_eta = field(west, NEXT_ETA) + strip("west", 2)
    own_eta = field(own, FIRST_ETA) + strip("own", 0)
    depth = packets.column(west, LAST_DEPTH) * there
    mask = wet(depth)
    next_row = wet(packets.column(west, NEXT_DEPTH)) * (field(west, NEXT_ROW) - courant * (eta - next_eta))
    below, beyond = links.south(west)
    corner = packets.line(below, STRIP, TILE - 1) if inflow is None else inflow["south west"]
    south_eta = jnp.where(last, corner * beyond, rolled(eta, -1, 1))
    col = mask * (field(west, LAST_COL) - courant * (south_eta - eta))
    north_col = jnp.where(first, corner_col(west, eta, TILE - 1, 1), rolled(col, 1, 1))
    west_row = mask * (field(west, LAST_ROW) - courant * (own_eta - eta))
    west_eta = (mask * eta - courant * depth * (west_row - next_row + col - north_col) + strip("west later", 1))
    west_mask = mask

    east, there = links.east(own)
    eta = there * (field(east, FIRST_ETA) + strip("east", 0))
    second_eta = field(east, SECOND_ETA) + strip("east", -1)
    depth = packets.column(east, FIRST_DEPTH) * there
    mask = wet(depth)
    row = mask * (field(east, FIRST_ROW) - courant * (second_eta - eta))
    below, beyond = links.south(east)
    corner = packets.line(below, STRIP, 0) if inflow is None else inflow["south east"]
    south_eta = jnp.where(last, rolled(corner, -1, 1) * beyond, rolled(eta, -1, 1))
    col = mask * (field(east, FIRST_COL) - courant * (south_eta - eta))
    north_col = jnp.where(first, corner_col(east, eta, 0, 0), rolled(col, 1, 1))
    east_sum = mask * eta - courant * depth * (row + col - north_col) + there * strip("east later", 0)
    return west_row, west_mask, west_eta, eta, east_sum, courant * depth


def advanced(eta, row, col, mask, depth, east, south, west, north):
    row = mask * (row - courant * (east(eta) - eta))
    col = mask * (col - courant * (south(eta) - eta))
    return mask * eta - depth * (row - west(row) + col - north(col)), row, col


def two_steps(start, mask, depth, sides, base, north=None, south=None, second=None):
    lane, line = iota(mask.shape, 1), iota(mask.shape, 0)
    cols = mask.shape[1]
    west_row, west_mask, west_eta, east_eta, east_sum, east_depth = sides
    state = start, 0.0, 0.0
    flow, beyond = west_row, east_eta
    above = 0.0 if north is None else north[0]
    for number in range(2):
        below = 0.0 if south is None else south[number]
        state = advanced(
            *state, mask, depth,
            lambda eta: jnp.where(lane == cols - 1, beyond, rolled(eta, -1, 1)),
            lambda eta: jnp.where(line == TILE - 1, below, rolled(eta, -1, 0)),
            lambda row: jnp.where(lane == 0, flow, rolled(row, 1, 1)),
            lambda col: jnp.where(line == 0, above, rolled(col, 1, 0)))
        if number:
            return state
        eta, row, col = state
        if second is not None:
            eta = eta + jnp.where(line == 0, second, 0.0)
            state = eta, row, col
        whole_eta, whole_row = (eta, row) if base is None else (eta + base[0], row + base[1])
        flow = west_mask * (west_row - courant * (whole_eta[:, :1] - west_eta))
        beyond = east_sum + east_depth * whole_row[:, cols - 1:]
        if north is not None:
            above = north[1] * (north[0] - courant * (whole_eta[:1] - north[2]))


def north_of(links, packets, own, own_strip, inflow=None):
    cols = own_strip.shape[1]
    lane = iota((1, LANES), 1)
    north, there = links.north(own)
    depth = packets.row(north, EDGE_DEPTH) * there
    mask = wet(depth)
    if inflow is not None:
        col = -courant * mask * own_strip
        return col, mask, -courant * depth * col
    col = packets.row(north, EDGE_FLOW) * there - courant * mask * own_strip
    north_east, beyond = links.east(north)
    right_eta = beyond * packets.column(north_east, FIRST_ETA)
    north_west, beyond = links.west(north)
    left_row = beyond * wet(packets.column(north_west, LAST_DEPTH)) * (
        packets.column(north_west, LAST_ROW)
        - courant * (packets.column(north, FIRST_ETA) - packets.column(north_west, LAST_ETA)))
    nothing = jnp.zeros((1, cols - LANES), jnp.float32)
    corners = (jnp.concatenate([jnp.where(lane == 0, rolled(left_row, 1, 1), 0.0), nothing], axis=1)
               + jnp.concatenate([nothing, jnp.where(lane == LANES - 1, courant * right_eta, 0.0)], axis=1))
    return col, mask, packets.row(north, EDGE_SUM) + courant * depth * (corners - col)


def as_sublanes(columns):
    rows = columns[0].shape[1]
    count = -len(columns) % TILE
    turned = jnp.concatenate(list(columns) + [jnp.zeros((count, rows), jnp.float32)], axis=0).T
    return [[turned[low:low + TILE, place:place + 1] for place in range(len(columns))]
            for low in (0, rows - TILE)]


def halo_kernel(links_ref, mine_ref, other_ref, strips_ref, eta_after, momenta_after, wet_after, depth_after,
                eta_ends, row_ends, turned, eta_out, momenta_out, ends_out, sides_new, more_ref, sems):
    rows, cols = eta_after.shape
    fields = eta_after, momenta_after.at[0], momenta_after.at[1]
    outs = eta_out.at[0], momenta_out.at[0, 0], momenta_out.at[1, 0]
    inner, between = pl.ds(TILE, rows - 2 * TILE), pl.ds(LANES, cols - 2 * LANES)
    copies = copied(
        [(field.at[inner, between], out.at[inner, between]) for field, out in zip(fields, outs)], sems.at[0])
    links = Links(links_ref, mine_ref.shape[0])
    own = links.own()
    packets = Packets((mine_ref, other_ref))
    columns = beside(links, packets, own)
    west_row, west_mask, west_eta, east_eta, east_sum, east_depth = columns

    line, lane = iota((TILE, rows), 0), iota((TILE, rows), 1)
    nothing = jnp.zeros((TILE, rows), jnp.float32)

    def column_steps(mask, depth, east, west):
        state = nothing, nothing, nothing
        for number in range(2):
            state = advanced(
                *state, mask, depth,
                lambda eta: jnp.where(line == TILE - 1, east(number, state), rolled(eta, -1, 0)),
                lambda eta: jnp.where(lane == rows - 1, 0.0, rolled(eta, -1, 1)),
                lambda row: jnp.where(line == 0, west(number, state), rolled(row, 1, 0)),
                lambda col: jnp.where(lane == 0, 0.0, rolled(col, 1, 1)))
        return state

    def west_of(number, state):
        if number == 0:
            return west_row
        whole = state[0][:1] + turned[4, :1]
        return west_mask * (west_row - courant * (whole - west_eta))

    def east_of(number, state):
        if number == 0:
            return east_eta
        return east_sum + east_depth * (state[1][TILE - 1:] + turned[5, TILE - 1:])

    left = column_steps(turned[0], turned[1], lambda number, state: 0.0, west_of)
    last = column_steps(turned[2], turned[3], east_of, lambda number, state: 0.0)
    middle = jnp.zeros((LANES - 2 * TILE, rows), jnp.float32)
    body_rows = slice(TILE, rows - TILE)
    inside = iota((rows - 2 * TILE, LANES), 1)
    wides = slice(0, LANES), slice(cols - LANES, cols)
    for place, field in enumerate(fields):
        more_ref[place] = jnp.concatenate([left[place], middle, last[place]], axis=0).T
        more = more_ref[place, body_rows]
        sides_new[0, place] = field[body_rows, wides[0]] + jnp.where(inside < TILE, more, 0.0)
        sides_new[1, place] = field[body_rows, wides[1]] + jnp.where(inside >= LANES - TILE, more, 0.0)
    for side, wide in enumerate(wides):
        copies += copied(
            [(sides_new.at[side, place], out.at[inner, pl.ds(wide.start, LANES)]) for place, out in enumerate(outs)],
            sems.at[1 + side])

    top_sides, low_sides = as_sublanes(columns)
    nothing = jnp.zeros((TILE, cols), jnp.float32)
    end = slice(rows - TILE, rows)
    top = two_steps(
        nothing, wet_after[:TILE], depth_after[:TILE], top_sides, (eta_ends[0], row_ends[0]),
        north=north_of(links, packets, own, packets.row(own, STRIP)))
    below, there = links.south(own)
    low = two_steps(
        nothing, wet_after[end], depth_after[end], low_sides, (eta_ends[1], row_ends[1]),
        south=(packets.row(below, STRIP) * there,
               row_of(strips_ref, 2 * links.patches + below.place(links.patches)) * there))
    line, inside = iota((TILE, cols), 0), iota((TILE, LANES), 1)
    gap = jnp.zeros((TILE, cols - 2 * LANES), jnp.float32)
    for edge, (chunk, near, found) in enumerate(
            ((slice(0, TILE), line < TILE // 2, top), (end, line >= TILE // 2, low))):
        for place in range(3):
            more = more_ref[place, chunk]
            wide = jnp.concatenate(
                [jnp.where(inside < TILE, more, 0.0), gap, jnp.where(inside >= LANES - TILE, more, 0.0)], axis=1)
            ends_out[place, edge] = fields[place][chunk] + jnp.where(near, found[place], wide)
    for copy in copies:
        copy.wait()


def inflow_kernel(links_ref, mine_ref, other_ref, finer_ref, wet_after, depth_after, ends_ref, eta_hbm, momenta_hbm,
                  eta_out, momenta_out, rows_ref, new_ref, sems):
    del eta_hbm, momenta_hbm
    rows, cols = wet_after.shape
    links = Links(links_ref, mine_ref.shape[0])
    patches = links.patches
    own = links.own()
    packets = Packets((mine_ref, other_ref))
    some = below_finest()

    def flux_place(step, segment):
        return step * 2 * patches + segment.place(patches)

    def inflows(segment):
        gain, index = packets.tile(segment, GAIN) * some, packets.tile(segment, INDEX).astype(jnp.int32)
        return [gain * nested(finer_ref[flux_place(step, segment)], index) for step in range(2)]

    below, there = links.south(own)
    west, east = links.west(own)[0], links.east(own)[0]
    below_west, beyond_west = links.west(below)
    below_east, beyond_east = links.east(below)
    wanted = (
        ("west", 0, west, TILE - 1), ("west later", 1, west, TILE - 1), ("east", 0, east, 0),
        ("east later", 1, east, 0), ("south west", 0, links.south(west)[0], TILE - 1),
        ("south east", 0, links.south(east)[0], 0), ("below west", 0, below_west, TILE - 1),
        ("below east", 0, below_east, 0))
    gain = jnp.concatenate([packets.line(segment, GAIN, line) for _, _, segment, line in wanted], axis=0)
    index = jnp.concatenate([packets.line(segment, INDEX, line) for _, _, segment, line in wanted], axis=0)
    index = index.astype(jnp.int32)
    lane, line = index % LANES, index // LANES
    taken = jnp.zeros((TILE, LANES), jnp.float32)
    for source in range(TILE):
        values = jnp.concatenate(
            [finer_ref[flux_place(step, segment), source:source + 1] for _, step, segment, _ in wanted], axis=0)
        found = jnp.take_along_axis(values, lane, axis=1, mode="promise_in_bounds")
        taken = jnp.where(line == source, found, taken)
    taken = some * gain * taken
    inflow = {name: taken[place:place + 1] for place, (name, _, _, _) in enumerate(wanted)}

    rows_ref[0], rows_ref[1] = inflows(own)
    strip, later = inflows(below)
    strip, later = strip * there, later * there
    inflow["own"] = rows_ref[0, :1]

    depth = packets.tile(below, STRIP_DEPTH)
    mask = wet(depth)
    edge = jnp.broadcast_to(rolled(inflow["below east"] * beyond_east, -1, 1), (TILE, LANES))
    row = courant * mask * (strip - next_cells(strip, edge))
    west_mask = rolled(wet(packets.line(below_west, STRIP_DEPTH, TILE - 1)), 1, 1)
    edge = beyond_west * courant * west_mask * (rolled(inflow["below west"], 1, 1) - strip[:1])
    edge = jnp.broadcast_to(edge, (TILE, LANES))
    north, beyond = links.north(below)
    col = -courant * wet(packets.tile(north, EDGE_DEPTH)) * beyond * strip
    rows_ref[2] = strip
    rows_ref[3] = there * (
        mask * strip - courant * depth * (row - last_cells(row, edge) + courant * mask * strip - col) + later)

    columns = beside(links, packets, own, inflow)
    top_sides, low_sides = as_sublanes(columns)
    line = iota((TILE, cols), 0)
    strip = row_of(rows_ref, 0)
    top = two_steps(
        jnp.where(line == 0, strip, 0.0), wet_after[:TILE], depth_after[:TILE], top_sides, None,
        north=north_of(links, packets, own, strip, inflow), second=row_of(rows_ref, 1))
    copies = []
    outs = eta_out.at[0], momenta_out.at[0, 0], momenta_out.at[1, 0]

    def write(end, near, found):
        for place in range(3):
            new_ref[place, end] = ends_ref[place, end] + jnp.where(near, found[place], 0.0)
        here = pl.ds(end * (rows - TILE), TILE)
        copies.extend(copied(
            [(new_ref.at[place, end], out.at[here, :]) for place, out in enumerate(outs)], sems.at[end]))

    write(0, line < TILE // 2, top)
    low = two_steps(
        jnp.zeros((TILE, cols), jnp.float32), wet_after[rows - TILE:], depth_after[rows - TILE:],
        low_sides, None, south=(row_of(rows_ref, 2), row_of(rows_ref, 3)))
    write(1, line >= TILE // 2, low)
    for copy in copies:
        copy.wait()


def body(adjoint_height, adjoint_momenta, depth, wet_mask, adjacency, nest_gain, nest_index):
    rows, cols = adjoint_height.shape[1:]
    levels = lax.axis_size("level")
    patches = lax.axis_size("patch")
    count = 2 * patches
    params = pltpu.CompilerParams(vmem_limit_bytes=VMEM_LIMIT)
    vmem = pl.BlockSpec(memory_space=pltpu.VMEM)
    smem = pl.BlockSpec(memory_space=pltpu.SMEM)
    hbm = pl.BlockSpec(memory_space=pltpu.HBM)

    def array(*shape):
        return jax.ShapeDtypeStruct(shape, jnp.float32)

    def scratch(*shape):
        return pltpu.VMEM(shape, jnp.float32)

    fields = [pltpu.with_memory_space_constraint(field, pltpu.HBM)
              for field in (adjoint_height, adjoint_momenta, depth, wet_mask, nest_gain, nest_index)]
    packed, trimmed = pl.pallas_call(
        pack_kernel,
        out_shape=[array(LINES, LANES), array(TRIMMED, LANES)],
        in_specs=[hbm] * 6,
        out_specs=[vmem, vmem],
        scratch_shapes=[
            scratch(2, 4, TILE, cols), pltpu.VMEM((2, TILE, cols), jnp.int32),
            scratch(2, 4, rows, LANES), pltpu.VMEM((2, rows, LANES), jnp.int32),
            scratch(levels, cols), pltpu.VMEM((levels, cols), jnp.int32),
            pltpu.SemaphoreType.DMA((18,)),
        ],
        compiler_params=params,
        name="pack",
    )(*fields)
    parts = 4
    after = pl.pallas_call(
        bulk_kernel,
        out_shape=[
            array(rows, cols), array(2, rows, cols), array(rows, cols), array(rows, cols),
            array(2, TILE, cols), array(2, TILE, cols), array(6, TILE, rows),
        ],
        in_specs=[hbm] * 4,
        out_specs=[vmem] * 7,
        scratch_shapes=[
            scratch(rows + 2 * TILE, cols), scratch(rows + 2 * TILE, cols),
            scratch(2, rows, cols), scratch(rows, cols), pltpu.VMEM((rows, cols), jnp.int32),
            scratch(rows, LANES), scratch(rows, LANES), pltpu.SemaphoreType.DMA((parts, 4)),
        ],
        compiler_params=params,
        name="bulk",
    )(*fields[:4])

    sent = [packed] + [
        lax.ppermute(trimmed if levels == 2 else packed, "patch",
                     [(source, source ^ turn) for source in range(patches)])
        for turn in range(patches - 1, 0, -1)
    ]
    mine = pl.pallas_call(
        gather_kernel,
        out_shape=array(patches, LINES, LANES),
        in_specs=[vmem] * (patches + 1),
        out_specs=vmem,
        compiler_params=params,
        name="gather",
    )(*sent, after[-1])
    other = lax.ppermute(mine, "sub", [(0, 1), (1, 0)])

    flux = ()
    strips = []
    for turn in range(levels - 1):
        strips.append(pl.pallas_call(
            strips_kernel,
            out_shape=array(2 * count, TILE, LANES),
            in_specs=[smem] + [vmem] * (2 + len(flux)),
            out_specs=vmem,
            scratch_shapes=[scratch(count, TILE, LANES)],
            compiler_params=params,
            name="strips",
        )(adjacency, mine, other, *flux))
        flux = (lax.ppermute(strips[-1], "level", [(source, (source - 1) % levels) for source in range(levels)]),)

    eta_new, momenta_new, ends = pl.pallas_call(
        halo_kernel,
        out_shape=[array(*adjoint_height.shape), array(*adjoint_momenta.shape), array(3, 2, TILE, cols)],
        in_specs=[smem] + [vmem] * 10,
        out_specs=[hbm, hbm, vmem],
        scratch_shapes=[
            scratch(2, 3, rows - 2 * TILE, LANES), scratch(3, rows, LANES), pltpu.SemaphoreType.DMA((3, 3)),
        ],
        compiler_params=params,
        name="halo",
    )(adjacency, mine, other, strips[0], *after)

    return pl.pallas_call(
        inflow_kernel,
        out_shape=[array(*adjoint_height.shape), array(*adjoint_momenta.shape)],
        in_specs=[smem] + [vmem] * 6 + [hbm] * 2,
        out_specs=[hbm, hbm],
        input_output_aliases={7: 0, 8: 1},
        scratch_shapes=[
            scratch(4, TILE, LANES), scratch(3, 2, TILE, cols), pltpu.SemaphoreType.DMA((2, 3)),
        ],
        compiler_params=params,
        name="inflow",
    )(adjacency, mine, other, *flux, after[2], after[3], ends, eta_new, momenta_new)


def solution(mesh):
    in_specs = (
        P(("parts", "level"), ("patch", "sub"), None),
        P(None, ("parts", "level"), ("patch", "sub"), None),
        P("level", ("patch", "sub"), None),
        P("level", ("patch", "sub"), None),
        P("level", None, None),
        P(None, ("patch", "sub")),
        P(None, ("patch", "sub")),
    )
    out_specs = (
        P(("parts", "level"), ("patch", "sub"), None),
        P(None, ("parts", "level"), ("patch", "sub"), None),
    )
    return jax.shard_map(body, mesh=mesh, in_specs=in_specs, out_specs=out_specs, check_vma=False)
```

```python
import jax
import jax.numpy as jnp
from jax import lax
from jax.experimental import pallas as pl
from jax.experimental.pallas import tpu as pltpu
from jax.sharding import PartitionSpec as P

STEPS = 2
LANES = 128
TILE = 8
VMEM_LIMIT = 48 * 1024 * 1024

courant = 0.45

STRIP_SUM, STRIP, STRIP_DEPTH, GAIN, INDEX, EDGE_FLOW, EDGE_DEPTH, EDGE_SUM = range(8)
(FIRST_ETA, SECOND_ETA, FIRST_ROW, FIRST_COL, FIRST_DEPTH, NEXT_ETA, LAST_ETA, NEXT_ROW,
 LAST_ROW, LAST_COL, NEXT_DEPTH, LAST_DEPTH) = range(12)
ROWS, COLUMNS = 8, 16
LINES = ROWS * TILE + COLUMNS
TRIMMED, SPARE = LINES - 2 * TILE, 4


def iota(shape, axis):
    return lax.broadcasted_iota(jnp.int32, shape, axis)


def rolled(value, shift, axis):
    if shift == 0:
        return value
    return pltpu.roll(value, shift % value.shape[axis], axis)


def wet(depth):
    return (depth > 0).astype(jnp.float32)


def copied(pairs, sems):
    copies = [pltpu.make_async_copy(source, target, sems.at[place]) for place, (source, target) in enumerate(pairs)]
    for copy in copies:
        copy.start()
    return copies


def pack_kernel(eta_ref, momenta_ref, depth_ref, wet_ref, gain_ref, index_ref, out_ref, trimmed_ref,
                ends, end_wet, sides, side_wet, gains, indices, sems):
    rows, cols = eta_ref.shape[1:]
    tall, wide = [], []
    for end in range(2):
        here = pl.ds(end * (rows - TILE), TILE)
        tall += [
            (eta_ref.at[0, here, :], ends.at[end, 0]), (momenta_ref.at[:, 0, here, :], ends.at[end, pl.ds(1, 2)]),
            (depth_ref.at[0, here, :], ends.at[end, 3]), (wet_ref.at[0, here, :], end_wet.at[end])]
        here = pl.ds(end * (cols - LANES), LANES)
        wide += [
            (eta_ref.at[0, :, here], sides.at[end, 0]), (momenta_ref.at[:, 0, :, here], sides.at[end, pl.ds(1, 2)]),
            (depth_ref.at[0, :, here], sides.at[end, 3]), (wet_ref.at[0, :, here], side_wet.at[end])]
    tall += [(gain_ref, gains), (index_ref, indices)]
    copies = copied(tall + wide, sems)
    for copy in copies[:len(tall)]:
        copy.wait()
    level = lax.axis_index("level")
    lane = iota((TILE, cols), 1)

    def loaded(end):
        mask = end_wet[end].astype(jnp.float32)
        return ends[end, 0], ends[end, 1], ends[end, 2], mask * ends[end, 3], mask

    def put(row, value):
        for tile in range(TILE):
            out_ref[row * TILE + tile:row * TILE + tile + 1] = value[:, tile * LANES:(tile + 1) * LANES]

    eta, row, col, depth, mask = loaded(0)
    east = jnp.where(lane == cols - 1, 0.0, rolled(eta, -1, 1))
    row = mask * (row - courant * (east - eta))
    west = jnp.where(lane == 0, 0.0, rolled(row, 1, 1))
    col = mask * (col - courant * (rolled(eta, -1, 0) - eta))
    strip_sum = mask * eta - courant * depth * (row - west + col)
    put(STRIP_SUM, strip_sum[:1])
    put(STRIP, eta[:1])
    put(STRIP_DEPTH, depth[:1])
    put(GAIN, gains[pl.ds(level, 1), :])
    put(INDEX, indices[pl.ds(level, 1), :].astype(jnp.float32))

    eta, row, col, depth, mask = loaded(1)
    east = jnp.where(lane == cols - 1, 0.0, rolled(eta, -1, 1))
    row = mask * (row - courant * (east - eta))
    west = jnp.where(lane == 0, 0.0, rolled(row, 1, 1))
    flow = mask * (col + courant * eta)
    above = rolled(flow - courant * mask * rolled(eta, -1, 0), 1, 0)
    edge_sum = mask * eta - courant * depth * (row - west - above)
    put(EDGE_FLOW, flow[TILE - 1:])
    put(EDGE_DEPTH, depth[TILE - 1:])
    put(EDGE_SUM, edge_sum[TILE - 1:])

    for copy in copies[len(tall):]:
        copy.wait()
    lane = iota((rows, LANES), 1)
    columns = jnp.zeros((rows, LANES), jnp.float32)
    depths = [sides[end, 3] * side_wet[end].astype(jnp.float32) for end in range(2)]
    for place, value, at in (
        (FIRST_ETA, sides[0, 0], 0), (SECOND_ETA, sides[0, 0], 1), (FIRST_ROW, sides[0, 1], 0),
        (FIRST_COL, sides[0, 2], 0), (FIRST_DEPTH, depths[0], 0),
        (NEXT_ETA, sides[1, 0], LANES - 2), (LAST_ETA, sides[1, 0], LANES - 1),
        (NEXT_ROW, sides[1, 1], LANES - 2), (LAST_ROW, sides[1, 1], LANES - 1),
        (LAST_COL, sides[1, 2], LANES - 1),
        (NEXT_DEPTH, depths[1], LANES - 2), (LAST_DEPTH, depths[1], LANES - 1),
    ):
        moved = value if place == at else rolled(value, place - at, 1)
        columns = jnp.where(lane == place, moved, columns)
    out_ref[ROWS * TILE:] = columns.T[:COLUMNS]

    def tile(row):
        return out_ref[row * TILE:(row + 1) * TILE]

    tables = sends_tables()
    flow, depth, gain, index = tile(EDGE_FLOW), tile(EDGE_DEPTH), tile(GAIN), tile(INDEX)
    trimmed_ref[:GAIN * TILE] = out_ref[:GAIN * TILE]
    trimmed_ref[GAIN * TILE:INDEX * TILE] = jnp.where(tables, gain, flow)
    trimmed_ref[INDEX * TILE:(INDEX + 1) * TILE] = jnp.where(tables, index, depth)
    trimmed_ref[(INDEX + 1) * TILE:(INDEX + 2) * TILE] = tile(EDGE_SUM)
    trimmed_ref[(INDEX + 2) * TILE:] = out_ref[ROWS * TILE:]
    spare = TRIMMED - SPARE
    for place, (other, own) in enumerate(((flow, gain), (depth, index))):
        chosen = jnp.where(tables, other, own)
        trimmed_ref[spare + 2 * place:spare + 2 * place + 1] = chosen[:1]
        trimmed_ref[spare + 2 * place + 1:spare + 2 * place + 2] = chosen[TILE - 1:]


def bulk_kernel(eta_ref, momenta_ref, depth_ref, wet_ref, eta_after, momenta_after, wet_after, depth_after,
                eta_ends, row_ends, turned, eta_pad, col_pad, momenta_in, depth_in, wet_in, eta_left, row_right, sems):
    rows, cols = eta_ref.shape[1:]
    parts = sems.shape[0]
    size = rows // parts
    loads = []
    for part in range(parts):
        here = pl.ds(part * size, size)
        loads.append(copied([
            (eta_ref.at[0, here, :], eta_pad.at[pl.ds(TILE + part * size, size), :]),
            (momenta_ref.at[:, 0, here, :], momenta_in.at[:, here, :]),
            (depth_ref.at[0, here, :], depth_in.at[here, :]),
            (wet_ref.at[0, here, :], wet_in.at[here, :]),
        ], sems.at[part]))
    lane = iota((TILE, cols), 1)
    eta_pad[TILE + rows:] = jnp.zeros((TILE, cols), jnp.float32)
    col_pad[:TILE] = jnp.zeros((TILE, cols), jnp.float32)

    def step(number, low):
        chunk, padded = slice(low, low + TILE), slice(TILE + low, 2 * TILE + low)
        eta = eta_pad[padded]
        if number == 0:
            mask = wet_in[chunk].astype(jnp.float32)
            depth = courant * mask * depth_in[chunk]
            wet_after[chunk] = mask
            depth_after[chunk] = depth
            row, col = momenta_in[0, chunk], momenta_in[1, chunk]
        else:
            mask, depth = wet_after[chunk], depth_after[chunk]
            row, col = momenta_after[0, chunk], col_pad[padded]
        east = jnp.where(lane == cols - 1, 0.0, rolled(eta, -1, 1))
        south = eta_pad[TILE + low + 1:2 * TILE + low + 1]
        row = mask * (row - courant * (east - eta))
        col = mask * (col - courant * (south - eta))
        momenta_after[0, chunk] = row
        col_pad[padded] = col
        if number:
            momenta_after[1, chunk] = col
        west = jnp.where(lane == 0, 0.0, rolled(row, 1, 1))
        north = col_pad[TILE + low - 1:2 * TILE + low - 1]
        eta = mask * eta - depth * (row - west + (col - north))
        if number:
            eta_after[chunk] = eta
            return
        eta_pad[padded] = eta
        eta_left[chunk] = eta[:, :LANES]
        row_right[chunk] = row[:, cols - LANES:]
        if low in (0, rows - TILE):
            end = int(low > 0)
            eta_ends[end] = eta
            row_ends[end] = row

    for copy in loads[0]:
        copy.wait()
    for part in range(parts + 1):
        if part + 1 < parts:
            for copy in loads[part + 1]:
                copy.wait()
        if part < parts:
            for low in range(part * size, (part + 1) * size, TILE):
                step(0, low)
        if part:
            for low in range((part - 1) * size, part * size, TILE):
                step(1, low)
    right = cols - LANES
    turned[0] = wet_after[:, :LANES].T[:TILE]
    turned[1] = depth_after[:, :LANES].T[:TILE]
    turned[2] = wet_after[:, right:].T[LANES - TILE:]
    turned[3] = depth_after[:, right:].T[LANES - TILE:]
    turned[4] = eta_left[...].T[:TILE]
    turned[5] = row_right[...].T[LANES - TILE:]


def sends_tables():
    return (lax.axis_index("level") == 0) & (lax.axis_index("sub") == 0)


def gather_kernel(*refs):
    first, packets, out_ref = refs[0], refs[1:-2], refs[-1]
    own = lax.axis_index("patch")
    out_ref[own] = first[...]
    tables = sends_tables()
    line = iota((TILE, LANES), 0)

    def ends_of(packet, at):
        value = jnp.where(line == 0, packet[at:at + 1], 0.0)
        return jnp.where(line == TILE - 1, packet[at + 1:at + 2], value)

    for place, packet in enumerate(packets):
        patch = own ^ (place + 1)
        if packet.shape[0] == LINES:
            out_ref[patch] = packet[...]
            continue

        def put(row, value):
            out_ref[patch, row * TILE:(row + 1) * TILE] = value

        out_ref[patch, :GAIN * TILE] = packet[:GAIN * TILE]
        whole = packet[GAIN * TILE:INDEX * TILE], packet[INDEX * TILE:(INDEX + 1) * TILE]
        ends = ends_of(packet, TRIMMED - SPARE), ends_of(packet, TRIMMED - SPARE + 2)
        put(GAIN, jnp.where(tables, whole[0], ends[0]))
        put(INDEX, jnp.where(tables, whole[1], ends[1]))
        put(EDGE_FLOW, jnp.where(tables, ends[0], whole[0]))
        put(EDGE_DEPTH, jnp.where(tables, ends[1], whole[1]))
        put(EDGE_SUM, packet[(INDEX + 1) * TILE:(INDEX + 2) * TILE])
        out_ref[patch, ROWS * TILE:] = packet[(INDEX + 2) * TILE:]


class Segment:
    def __init__(self, patch, flipped):
        self.patch, self.flipped = patch, flipped

    def place(self, patches):
        return self.flipped * patches + self.patch


def below_finest():
    return jnp.where(lax.axis_index("level") < lax.axis_size("level") - 1, 1.0, 0.0)


class Links:
    def __init__(self, links_ref, patches):
        self.links_ref, self.patches = links_ref, patches
        self.half = lax.axis_index("sub")

    def own(self):
        return Segment(lax.axis_index("patch"), 0)

    def all(self):
        return [Segment(patch, flipped) for flipped in range(2) for patch in range(self.patches)]

    def across(self, segment, way):
        patch = self.links_ref[0, segment.patch, way]
        return jnp.maximum(patch, 0), jnp.where(patch >= 0, 1.0, 0.0)

    def other_half(self, segment, way, inner):
        patch, there = self.across(segment, way)
        inside = self.half == (inner ^ segment.flipped)
        return Segment(jnp.where(inside, segment.patch, patch), 1 - segment.flipped), jnp.where(inside, 1.0, there)

    def north(self, segment):
        return self.other_half(segment, 0, 1)

    def south(self, segment):
        return self.other_half(segment, 1, 0)

    def west(self, segment):
        patch, there = self.across(segment, 2)
        return Segment(patch, segment.flipped), there

    def east(self, segment):
        patch, there = self.across(segment, 3)
        return Segment(patch, segment.flipped), there


class Packets:
    def __init__(self, got_refs):
        self.got_refs = got_refs

    def tile(self, segment, row):
        return self.got_refs[segment.flipped][segment.patch, row * TILE:(row + 1) * TILE]

    def line(self, segment, row, line):
        return self.got_refs[segment.flipped][segment.patch, row * TILE + line:row * TILE + line + 1]

    def row(self, segment, row):
        return jnp.concatenate([self.line(segment, row, line) for line in range(TILE)], axis=1)

    def column(self, segment, column):
        return self.line(segment, ROWS, column)


def is_first(shape=(TILE, LANES)):
    return (iota(shape, 0) == 0) & (iota(shape, 1) == 0)


def is_last(shape=(TILE, LANES)):
    return (iota(shape, 0) == shape[0] - 1) & (iota(shape, 1) == shape[1] - 1)


def next_cells(tile, edge):
    lane = iota(tile.shape, 1)
    moved = rolled(tile, -1, 1)
    moved = jnp.where(lane == LANES - 1, rolled(moved, -1, 0), moved)
    return jnp.where(is_last(), edge, moved)


def last_cells(tile, edge):
    lane = iota(tile.shape, 1)
    moved = rolled(tile, 1, 1)
    moved = jnp.where(lane == 0, rolled(moved, 1, 0), moved)
    return jnp.where(is_first(), edge, moved)


def row_of(ref, place):
    return jnp.concatenate([ref[place, line:line + 1] for line in range(TILE)], axis=1)


def nested(flux, index):
    lane, line = index % LANES, index // LANES
    taken = jnp.zeros(index.shape, jnp.float32)
    for source in range(TILE):
        values = jnp.broadcast_to(flux[source:source + 1], index.shape)
        found = jnp.take_along_axis(values, lane, axis=1, mode="promise_in_bounds")
        taken = jnp.where(line == source, found, taken)
    return taken


def strips_kernel(*refs):
    links_ref, mine_ref, other_ref = refs[:3]
    out_ref, strips_ref = refs[-2:]
    finer_ref = refs[3] if len(refs) == 6 else None
    links = Links(links_ref, mine_ref.shape[0])
    patches, count = links.patches, 2 * links.patches
    packets = Packets((mine_ref, other_ref))
    every = links.all()
    strips, inflows = [], []
    for segment in every:
        strip = packets.tile(segment, STRIP)
        if finer_ref is not None:
            place = segment.place(patches)
            gain, index = packets.tile(segment, GAIN) * below_finest(), packets.tile(segment, INDEX).astype(jnp.int32)
            inflow, later = [gain * nested(finer_ref[step * count + place], index) for step in range(2)]
            inflows.append((inflow, later))
            strip = strip + inflow
            strips_ref[place] = strip
        strips.append(strip)

    def strip_at(segment):
        return packets.tile(segment, STRIP) if finer_ref is None else strips_ref[segment.place(patches)]

    totals = []
    for place, segment in enumerate(every):
        eta, depth = strips[place], packets.tile(segment, STRIP_DEPTH)
        mask = wet(depth)
        east, there = links.east(segment)
        edge = there * rolled(rolled(strip_at(east), -1, 1), -1, 0)
        if finer_ref is None:
            row = jnp.where(is_last(), -courant * mask * edge, 0.0)
        else:
            inflow, later = inflows[place]
            row = courant * mask * (inflow - next_cells(inflow, edge))
        west, there = links.west(segment)
        west_eta = rolled(rolled(strip_at(west), 1, 1), 1, 0)
        west_mask = rolled(rolled(wet(packets.tile(west, STRIP_DEPTH)), 1, 1), 1, 0)
        edge = there * west_mask * (packets.column(west, LAST_ROW) - courant * (eta - west_eta))
        north, there = links.north(segment)
        col = there * (packets.tile(north, EDGE_FLOW) - courant * wet(packets.tile(north, EDGE_DEPTH)) * eta)
        total = packets.tile(segment, STRIP_SUM)
        if finer_ref is None:
            total = total - courant * depth * (row - jnp.where(is_first(), edge, 0.0) - col)
        else:
            total = (total + mask * inflow + later
                     - courant * depth * (row - last_cells(row, edge) + courant * mask * inflow - col))
        totals.append(total)
    for place, (strip, total) in enumerate(zip(strips, totals)):
        out_ref[place] = strip
        out_ref[count + place] = total


def beside(links, packets, own, inflow=None):
    lane = iota((1, LANES), 1)
    first, last = lane == 0, lane == LANES - 1

    def field(segment, column):
        return packets.column(segment, column) if inflow is None else 0.0

    def strip(name, turned):
        return 0.0 if inflow is None else jnp.where(first, rolled(inflow[name], turned, 1), 0.0)

    def corner_col(segment, eta, line, turned):
        north, beyond = links.north(segment)
        mask = rolled(wet(packets.line(north, EDGE_DEPTH, line)), turned, 1)
        flow = rolled(packets.line(north, EDGE_FLOW, line), turned, 1) if inflow is None else 0.0
        return beyond * (flow - courant * mask * eta)

    west, there = links.west(own)
    eta = field(west, LAST_ETA) + strip("west", 1)
    next_eta = field(west, NEXT_ETA) + strip("west", 2)
    own_eta = field(own, FIRST_ETA) + strip("own", 0)
    depth = packets.column(west, LAST_DEPTH) * there
    mask = wet(depth)
    next_row = wet(packets.column(west, NEXT_DEPTH)) * (field(west, NEXT_ROW) - courant * (eta - next_eta))
    below, beyond = links.south(west)
    corner = packets.line(below, STRIP, TILE - 1) if inflow is None else inflow["south west"]
    south_eta = jnp.where(last, corner * beyond, rolled(eta, -1, 1))
    col = mask * (field(west, LAST_COL) - courant * (south_eta - eta))
    north_col = jnp.where(first, corner_col(west, eta, TILE - 1, 1), rolled(col, 1, 1))
    west_row = mask * (field(west, LAST_ROW) - courant * (own_eta - eta))
    west_eta = (mask * eta - courant * depth * (west_row - next_row + col - north_col) + strip("west later", 1))
    west_mask = mask

    east, there = links.east(own)
    eta = there * (field(east, FIRST_ETA) + strip("east", 0))
    second_eta = field(east, SECOND_ETA) + strip("east", -1)
    depth = packets.column(east, FIRST_DEPTH) * there
    mask = wet(depth)
    row = mask * (field(east, FIRST_ROW) - courant * (second_eta - eta))
    below, beyond = links.south(east)
    corner = packets.line(below, STRIP, 0) if inflow is None else inflow["south east"]
    south_eta = jnp.where(last, rolled(corner, -1, 1) * beyond, rolled(eta, -1, 1))
    col = mask * (field(east, FIRST_COL) - courant * (south_eta - eta))
    north_col = jnp.where(first, corner_col(east, eta, 0, 0), rolled(col, 1, 1))
    east_sum = mask * eta - courant * depth * (row + col - north_col) + there * strip("east later", 0)
    return west_row, west_mask, west_eta, eta, east_sum, courant * depth


def advanced(eta, row, col, mask, depth, east, south, west, north):
    row = mask * (row - courant * (east(eta) - eta))
    col = mask * (col - courant * (south(eta) - eta))
    return mask * eta - depth * (row - west(row) + col - north(col)), row, col


def two_steps(start, mask, depth, sides, base, north=None, south=None, second=None):
    lane, line = iota(mask.shape, 1), iota(mask.shape, 0)
    cols = mask.shape[1]
    west_row, west_mask, west_eta, east_eta, east_sum, east_depth = sides
    state = start, 0.0, 0.0
    flow, beyond = west_row, east_eta
    above = 0.0 if north is None else north[0]
    for number in range(2):
        below = 0.0 if south is None else south[number]
        state = advanced(
            *state, mask, depth,
            lambda eta: jnp.where(lane == cols - 1, beyond, rolled(eta, -1, 1)),
            lambda eta: jnp.where(line == TILE - 1, below, rolled(eta, -1, 0)),
            lambda row: jnp.where(lane == 0, flow, rolled(row, 1, 1)),
            lambda col: jnp.where(line == 0, above, rolled(col, 1, 0)))
        if number:
            return state
        eta, row, col = state
        if second is not None:
            eta = eta + jnp.where(line == 0, second, 0.0)
            state = eta, row, col
        whole_eta, whole_row = (eta, row) if base is None else (eta + base[0], row + base[1])
        flow = west_mask * (west_row - courant * (whole_eta[:, :1] - west_eta))
        beyond = east_sum + east_depth * whole_row[:, cols - 1:]
        if north is not None:
            above = north[1] * (north[0] - courant * (whole_eta[:1] - north[2]))


def north_of(links, packets, own, own_strip, inflow=None):
    cols = own_strip.shape[1]
    lane = iota((1, LANES), 1)
    north, there = links.north(own)
    depth = packets.row(north, EDGE_DEPTH) * there
    mask = wet(depth)
    if inflow is not None:
        col = -courant * mask * own_strip
        return col, mask, -courant * depth * col
    col = packets.row(north, EDGE_FLOW) * there - courant * mask * own_strip
    north_east, beyond = links.east(north)
    right_eta = beyond * packets.column(north_east, FIRST_ETA)
    north_west, beyond = links.west(north)
    left_row = beyond * wet(packets.column(north_west, LAST_DEPTH)) * (
        packets.column(north_west, LAST_ROW)
        - courant * (packets.column(north, FIRST_ETA) - packets.column(north_west, LAST_ETA)))
    nothing = jnp.zeros((1, cols - LANES), jnp.float32)
    corners = (jnp.concatenate([jnp.where(lane == 0, rolled(left_row, 1, 1), 0.0), nothing], axis=1)
               + jnp.concatenate([nothing, jnp.where(lane == LANES - 1, courant * right_eta, 0.0)], axis=1))
    return col, mask, packets.row(north, EDGE_SUM) + courant * depth * (corners - col)


def as_sublanes(columns):
    rows = columns[0].shape[1]
    count = -len(columns) % TILE
    turned = jnp.concatenate(list(columns) + [jnp.zeros((count, rows), jnp.float32)], axis=0).T
    return [[turned[low:low + TILE, place:place + 1] for place in range(len(columns))]
            for low in (0, rows - TILE)]


def halo_kernel(links_ref, mine_ref, other_ref, strips_ref, eta_after, momenta_after, wet_after, depth_after,
                eta_ends, row_ends, turned, eta_out, momenta_out, ends_out, sides_new, more_ref, sems):
    rows, cols = eta_after.shape
    fields = eta_after, momenta_after.at[0], momenta_after.at[1]
    outs = eta_out.at[0], momenta_out.at[0, 0], momenta_out.at[1, 0]
    inner, between = pl.ds(TILE, rows - 2 * TILE), pl.ds(LANES, cols - 2 * LANES)
    copies = copied(
        [(field.at[inner, between], out.at[inner, between]) for field, out in zip(fields, outs)], sems.at[0])
    links = Links(links_ref, mine_ref.shape[0])
    own = links.own()
    packets = Packets((mine_ref, other_ref))
    columns = beside(links, packets, own)
    west_row, west_mask, west_eta, east_eta, east_sum, east_depth = columns

    line, lane = iota((TILE, rows), 0), iota((TILE, rows), 1)
    nothing = jnp.zeros((TILE, rows), jnp.float32)

    def column_steps(mask, depth, east, west):
        state = nothing, nothing, nothing
        for number in range(2):
            state = advanced(
                *state, mask, depth,
                lambda eta: jnp.where(line == TILE - 1, east(number, state), rolled(eta, -1, 0)),
                lambda eta: jnp.where(lane == rows - 1, 0.0, rolled(eta, -1, 1)),
                lambda row: jnp.where(line == 0, west(number, state), rolled(row, 1, 0)),
                lambda col: jnp.where(lane == 0, 0.0, rolled(col, 1, 1)))
        return state

    def west_of(number, state):
        if number == 0:
            return west_row
        whole = state[0][:1] + turned[4, :1]
        return west_mask * (west_row - courant * (whole - west_eta))

    def east_of(number, state):
        if number == 0:
            return east_eta
        return east_sum + east_depth * (state[1][TILE - 1:] + turned[5, TILE - 1:])

    left = column_steps(turned[0], turned[1], lambda number, state: 0.0, west_of)
    last = column_steps(turned[2], turned[3], east_of, lambda number, state: 0.0)
    middle = jnp.zeros((LANES - 2 * TILE, rows), jnp.float32)
    body_rows = slice(TILE, rows - TILE)
    inside = iota((rows - 2 * TILE, LANES), 1)
    wides = slice(0, LANES), slice(cols - LANES, cols)
    for place, field in enumerate(fields):
        more_ref[place] = jnp.concatenate([left[place], middle, last[place]], axis=0).T
        more = more_ref[place, body_rows]
        sides_new[0, place] = field[body_rows, wides[0]] + jnp.where(inside < TILE, more, 0.0)
        sides_new[1, place] = field[body_rows, wides[1]] + jnp.where(inside >= LANES - TILE, more, 0.0)
    for side, wide in enumerate(wides):
        copies += copied(
            [(sides_new.at[side, place], out.at[inner, pl.ds(wide.start, LANES)]) for place, out in enumerate(outs)],
            sems.at[1 + side])

    top_sides, low_sides = as_sublanes(columns)
    nothing = jnp.zeros((TILE, cols), jnp.float32)
    end = slice(rows - TILE, rows)
    top = two_steps(
        nothing, wet_after[:TILE], depth_after[:TILE], top_sides, (eta_ends[0], row_ends[0]),
        north=north_of(links, packets, own, packets.row(own, STRIP)))
    below, there = links.south(own)
    low = two_steps(
        nothing, wet_after[end], depth_after[end], low_sides, (eta_ends[1], row_ends[1]),
        south=(packets.row(below, STRIP) * there,
               row_of(strips_ref, 2 * links.patches + below.place(links.patches)) * there))
    line, inside = iota((TILE, cols), 0), iota((TILE, LANES), 1)
    gap = jnp.zeros((TILE, cols - 2 * LANES), jnp.float32)
    for edge, (chunk, near, found) in enumerate(
            ((slice(0, TILE), line < TILE // 2, top), (end, line >= TILE // 2, low))):
        for place in range(3):
            more = more_ref[place, chunk]
            wide = jnp.concatenate(
                [jnp.where(inside < TILE, more, 0.0), gap, jnp.where(inside >= LANES - TILE, more, 0.0)], axis=1)
            ends_out[place, edge] = fields[place][chunk] + jnp.where(near, found[place], wide)
    for copy in copies:
        copy.wait()


def inflow_kernel(links_ref, mine_ref, other_ref, finer_ref, wet_after, depth_after, ends_ref, eta_hbm, momenta_hbm,
                  eta_out, momenta_out, rows_ref, new_ref, sems):
    del eta_hbm, momenta_hbm
    rows, cols = wet_after.shape
    links = Links(links_ref, mine_ref.shape[0])
    patches = links.patches
    own = links.own()
    packets = Packets((mine_ref, other_ref))
    some = below_finest()

    def flux_place(step, segment):
        return step * 2 * patches + segment.place(patches)

    def inflows(segment):
        gain, index = packets.tile(segment, GAIN) * some, packets.tile(segment, INDEX).astype(jnp.int32)
        return [gain * nested(finer_ref[flux_place(step, segment)], index) for step in range(2)]

    below, there = links.south(own)
    west, east = links.west(own)[0], links.east(own)[0]
    below_west, beyond_west = links.west(below)
    below_east, beyond_east = links.east(below)
    wanted = (
        ("west", 0, west, TILE - 1), ("west later", 1, west, TILE - 1), ("east", 0, east, 0),
        ("east later", 1, east, 0), ("south west", 0, links.south(west)[0], TILE - 1),
        ("south east", 0, links.south(east)[0], 0), ("below west", 0, below_west, TILE - 1),
        ("below east", 0, below_east, 0))
    gain = jnp.concatenate([packets.line(segment, GAIN, line) for _, _, segment, line in wanted], axis=0)
    index = jnp.concatenate([packets.line(segment, INDEX, line) for _, _, segment, line in wanted], axis=0)
    index = index.astype(jnp.int32)
    lane, line = index % LANES, index // LANES
    taken = jnp.zeros((TILE, LANES), jnp.float32)
    for source in range(TILE):
        values = jnp.concatenate(
            [finer_ref[flux_place(step, segment), source:source + 1] for _, step, segment, _ in wanted], axis=0)
        found = jnp.take_along_axis(values, lane, axis=1, mode="promise_in_bounds")
        taken = jnp.where(line == source, found, taken)
    taken = some * gain * taken
    inflow = {name: taken[place:place + 1] for place, (name, _, _, _) in enumerate(wanted)}

    rows_ref[0], rows_ref[1] = inflows(own)
    strip, later = inflows(below)
    strip, later = strip * there, later * there
    inflow["own"] = rows_ref[0, :1]

    depth = packets.tile(below, STRIP_DEPTH)
    mask = wet(depth)
    edge = jnp.broadcast_to(rolled(inflow["below east"] * beyond_east, -1, 1), (TILE, LANES))
    row = courant * mask * (strip - next_cells(strip, edge))
    west_mask = rolled(wet(packets.line(below_west, STRIP_DEPTH, TILE - 1)), 1, 1)
    edge = beyond_west * courant * west_mask * (rolled(inflow["below west"], 1, 1) - strip[:1])
    edge = jnp.broadcast_to(edge, (TILE, LANES))
    north, beyond = links.north(below)
    col = -courant * wet(packets.tile(north, EDGE_DEPTH)) * beyond * strip
    rows_ref[2] = strip
    rows_ref[3] = there * (
        mask * strip - courant * depth * (row - last_cells(row, edge) + courant * mask * strip - col) + later)

    columns = beside(links, packets, own, inflow)
    top_sides, low_sides = as_sublanes(columns)
    line = iota((TILE, cols), 0)
    strip = row_of(rows_ref, 0)
    top = two_steps(
        jnp.where(line == 0, strip, 0.0), wet_after[:TILE], depth_after[:TILE], top_sides, None,
        north=north_of(links, packets, own, strip, inflow), second=row_of(rows_ref, 1))
    copies = []
    outs = eta_out.at[0], momenta_out.at[0, 0], momenta_out.at[1, 0]

    def write(end, near, found):
        for place in range(3):
            new_ref[place, end] = ends_ref[place, end] + jnp.where(near, found[place], 0.0)
        here = pl.ds(end * (rows - TILE), TILE)
        copies.extend(copied(
            [(new_ref.at[place, end], out.at[here, :]) for place, out in enumerate(outs)], sems.at[end]))

    write(0, line < TILE // 2, top)
    low = two_steps(
        jnp.zeros((TILE, cols), jnp.float32), wet_after[rows - TILE:], depth_after[rows - TILE:],
        low_sides, None, south=(row_of(rows_ref, 2), row_of(rows_ref, 3)))
    write(1, line >= TILE // 2, low)
    for copy in copies:
        copy.wait()


def body(adjoint_height, adjoint_momenta, depth, wet_mask, adjacency, nest_gain, nest_index):
    rows, cols = adjoint_height.shape[1:]
    levels = lax.axis_size("level")
    patches = lax.axis_size("patch")
    count = 2 * patches
    params = pltpu.CompilerParams(vmem_limit_bytes=VMEM_LIMIT)
    vmem = pl.BlockSpec(memory_space=pltpu.VMEM)
    smem = pl.BlockSpec(memory_space=pltpu.SMEM)
    hbm = pl.BlockSpec(memory_space=pltpu.HBM)

    def array(*shape):
        return jax.ShapeDtypeStruct(shape, jnp.float32)

    def scratch(*shape):
        return pltpu.VMEM(shape, jnp.float32)

    fields = [pltpu.with_memory_space_constraint(field, pltpu.HBM)
              for field in (adjoint_height, adjoint_momenta, depth, wet_mask, nest_gain, nest_index)]
    packed, trimmed = pl.pallas_call(
        pack_kernel,
        out_shape=[array(LINES, LANES), array(TRIMMED, LANES)],
        in_specs=[hbm] * 6,
        out_specs=[vmem, vmem],
        scratch_shapes=[
            scratch(2, 4, TILE, cols), pltpu.VMEM((2, TILE, cols), jnp.int32),
            scratch(2, 4, rows, LANES), pltpu.VMEM((2, rows, LANES), jnp.int32),
            scratch(levels, cols), pltpu.VMEM((levels, cols), jnp.int32),
            pltpu.SemaphoreType.DMA((18,)),
        ],
        compiler_params=params,
        name="pack",
    )(*fields)
    parts = 4
    after = pl.pallas_call(
        bulk_kernel,
        out_shape=[
            array(rows, cols), array(2, rows, cols), array(rows, cols), array(rows, cols),
            array(2, TILE, cols), array(2, TILE, cols), array(6, TILE, rows),
        ],
        in_specs=[hbm] * 4,
        out_specs=[vmem] * 7,
        scratch_shapes=[
            scratch(rows + 2 * TILE, cols), scratch(rows + 2 * TILE, cols),
            scratch(2, rows, cols), scratch(rows, cols), pltpu.VMEM((rows, cols), jnp.int32),
            scratch(rows, LANES), scratch(rows, LANES), pltpu.SemaphoreType.DMA((parts, 4)),
        ],
        compiler_params=params,
        name="bulk",
    )(*fields[:4])

    sent = [packed] + [
        lax.ppermute(trimmed if levels == 2 else packed, "patch",
                     [(source, source ^ turn) for source in range(patches)])
        for turn in range(1, patches)
    ]
    mine = pl.pallas_call(
        gather_kernel,
        out_shape=array(patches, LINES, LANES),
        in_specs=[vmem] * (patches + 1),
        out_specs=vmem,
        compiler_params=params,
        name="gather",
    )(*sent, after[-1])
    other = lax.ppermute(mine, "sub", [(0, 1), (1, 0)])

    flux = ()
    strips = []
    for turn in range(levels - 1):
        strips.append(pl.pallas_call(
            strips_kernel,
            out_shape=array(2 * count, TILE, LANES),
            in_specs=[smem] + [vmem] * (2 + len(flux)),
            out_specs=vmem,
            scratch_shapes=[scratch(count, TILE, LANES)],
            compiler_params=params,
            name="strips",
        )(adjacency, mine, other, *flux))
        flux = (lax.ppermute(strips[-1], "level", [(source, (source - 1) % levels) for source in range(levels)]),)

    eta_new, momenta_new, ends = pl.pallas_call(
        halo_kernel,
        out_shape=[array(*adjoint_height.shape), array(*adjoint_momenta.shape), array(3, 2, TILE, cols)],
        in_specs=[smem] + [vmem] * 10,
        out_specs=[hbm, hbm, vmem],
        scratch_shapes=[
            scratch(2, 3, rows - 2 * TILE, LANES), scratch(3, rows, LANES), pltpu.SemaphoreType.DMA((3, 3)),
        ],
        compiler_params=params,
        name="halo",
    )(adjacency, mine, other, strips[0], *after)

    return pl.pallas_call(
        inflow_kernel,
        out_shape=[array(*adjoint_height.shape), array(*adjoint_momenta.shape)],
        in_specs=[smem] + [vmem] * 6 + [hbm] * 2,
        out_specs=[hbm, hbm],
        input_output_aliases={7: 0, 8: 1},
        scratch_shapes=[
            scratch(4, TILE, LANES), scratch(3, 2, TILE, cols), pltpu.SemaphoreType.DMA((2, 3)),
        ],
        compiler_params=params,
        name="inflow",
    )(adjacency, mine, other, *flux, after[2], after[3], ends, eta_new, momenta_new)


def solution(mesh):
    in_specs = (
        P(("parts", "level"), ("patch", "sub"), None),
        P(None, ("parts", "level"), ("patch", "sub"), None),
        P("level", ("patch", "sub"), None),
        P("level", ("patch", "sub"), None),
        P("level", None, None),
        P(None, ("patch", "sub")),
        P(None, ("patch", "sub")),
    )
    out_specs = (
        P(("parts", "level"), ("patch", "sub"), None),
        P(None, ("parts", "level"), ("patch", "sub"), None),
    )
    return jax.shard_map(body, mesh=mesh, in_specs=in_specs, out_specs=out_specs, check_vma=False)
```

```python
import jax
import jax.numpy as jnp
from jax import lax
from jax.experimental import pallas as pl
from jax.experimental.pallas import tpu as pltpu
from jax.sharding import PartitionSpec as P

STEPS = 2
LANES = 128
TILE = 8
LANE_BITS = LANES.bit_length() - 1
VMEM_LIMIT = 48 * 1024 * 1024

courant = 0.45

STRIP_SUM, STRIP, STRIP_DEPTH, GAIN, INDEX, EDGE_FLOW, EDGE_DEPTH, EDGE_SUM = range(8)
(FIRST_ETA, SECOND_ETA, FIRST_ROW, FIRST_COL, FIRST_DEPTH, NEXT_ETA, LAST_ETA, NEXT_ROW,
 LAST_ROW, LAST_COL, NEXT_DEPTH, LAST_DEPTH) = range(12)
ROWS, COLUMNS = 8, 16
LINES = ROWS * TILE + COLUMNS
TRIMMED, SPARE = LINES - 2 * TILE, 4


def iota(shape, axis):
    return lax.broadcasted_iota(jnp.int32, shape, axis)


def rolled(value, shift, axis):
    if shift == 0:
        return value
    return pltpu.roll(value, shift % value.shape[axis], axis)


def wet(depth):
    return (depth > 0).astype(jnp.float32)


def copied(pairs, sems):
    copies = [pltpu.make_async_copy(source, target, sems.at[place]) for place, (source, target) in enumerate(pairs)]
    for copy in copies:
        copy.start()
    return copies


def pack_kernel(eta_ref, momenta_ref, depth_ref, wet_ref, gain_ref, index_ref, out_ref, trimmed_ref,
                ends, end_wet, sides, side_wet, gains, indices, sems):
    rows, cols = eta_ref.shape[1:]
    tall, wide = [], []
    for end in range(2):
        here = pl.ds(end * (rows - TILE), TILE)
        tall += [
            (eta_ref.at[0, here, :], ends.at[end, 0]), (momenta_ref.at[:, 0, here, :], ends.at[end, pl.ds(1, 2)]),
            (depth_ref.at[0, here, :], ends.at[end, 3]), (wet_ref.at[0, here, :], end_wet.at[end])]
        here = pl.ds(end * (cols - LANES), LANES)
        wide += [
            (eta_ref.at[0, :, here], sides.at[end, 0]), (momenta_ref.at[:, 0, :, here], sides.at[end, pl.ds(1, 2)]),
            (depth_ref.at[0, :, here], sides.at[end, 3]), (wet_ref.at[0, :, here], side_wet.at[end])]
    tall += [(gain_ref, gains), (index_ref, indices)]
    copies = copied(tall + wide, sems)
    for copy in copies[:len(tall)]:
        copy.wait()
    level = lax.axis_index("level")
    lane = iota((TILE, cols), 1)

    def loaded(end):
        mask = end_wet[end].astype(jnp.float32)
        return ends[end, 0], ends[end, 1], ends[end, 2], mask * ends[end, 3], mask

    def put(row, value):
        for tile in range(TILE):
            out_ref[row * TILE + tile:row * TILE + tile + 1] = value[:, tile * LANES:(tile + 1) * LANES]

    eta, row, col, depth, mask = loaded(0)
    east = jnp.where(lane == cols - 1, 0.0, rolled(eta, -1, 1))
    row = mask * (row - courant * (east - eta))
    west = jnp.where(lane == 0, 0.0, rolled(row, 1, 1))
    col = mask * (col - courant * (rolled(eta, -1, 0) - eta))
    strip_sum = mask * eta - courant * depth * (row - west + col)
    put(STRIP_SUM, strip_sum[:1])
    put(STRIP, eta[:1])
    put(STRIP_DEPTH, depth[:1])
    put(GAIN, gains[pl.ds(level, 1), :])
    put(INDEX, indices[pl.ds(level, 1), :].astype(jnp.float32))

    eta, row, col, depth, mask = loaded(1)
    east = jnp.where(lane == cols - 1, 0.0, rolled(eta, -1, 1))
    row = mask * (row - courant * (east - eta))
    west = jnp.where(lane == 0, 0.0, rolled(row, 1, 1))
    flow = mask * (col + courant * eta)
    above = rolled(flow - courant * mask * rolled(eta, -1, 0), 1, 0)
    edge_sum = mask * eta - courant * depth * (row - west - above)
    put(EDGE_FLOW, flow[TILE - 1:])
    put(EDGE_DEPTH, depth[TILE - 1:])
    put(EDGE_SUM, edge_sum[TILE - 1:])

    for copy in copies[len(tall):]:
        copy.wait()
    lane = iota((rows, LANES), 1)
    columns = jnp.zeros((rows, LANES), jnp.float32)
    depths = [sides[end, 3] * side_wet[end].astype(jnp.float32) for end in range(2)]
    for place, value, at in (
        (FIRST_ETA, sides[0, 0], 0), (SECOND_ETA, sides[0, 0], 1), (FIRST_ROW, sides[0, 1], 0),
        (FIRST_COL, sides[0, 2], 0), (FIRST_DEPTH, depths[0], 0),
        (NEXT_ETA, sides[1, 0], LANES - 2), (LAST_ETA, sides[1, 0], LANES - 1),
        (NEXT_ROW, sides[1, 1], LANES - 2), (LAST_ROW, sides[1, 1], LANES - 1),
        (LAST_COL, sides[1, 2], LANES - 1),
        (NEXT_DEPTH, depths[1], LANES - 2), (LAST_DEPTH, depths[1], LANES - 1),
    ):
        moved = value if place == at else rolled(value, place - at, 1)
        columns = jnp.where(lane == place, moved, columns)
    out_ref[ROWS * TILE:] = columns.T[:COLUMNS]

    def tile(row):
        return out_ref[row * TILE:(row + 1) * TILE]

    tables = sends_tables()
    flow, depth, gain, index = tile(EDGE_FLOW), tile(EDGE_DEPTH), tile(GAIN), tile(INDEX)
    trimmed_ref[:GAIN * TILE] = out_ref[:GAIN * TILE]
    trimmed_ref[GAIN * TILE:INDEX * TILE] = jnp.where(tables, gain, flow)
    trimmed_ref[INDEX * TILE:(INDEX + 1) * TILE] = jnp.where(tables, index, depth)
    trimmed_ref[(INDEX + 1) * TILE:(INDEX + 2) * TILE] = tile(EDGE_SUM)
    trimmed_ref[(INDEX + 2) * TILE:] = out_ref[ROWS * TILE:]
    spare = TRIMMED - SPARE
    for place, (other, own) in enumerate(((flow, gain), (depth, index))):
        chosen = jnp.where(tables, other, own)
        trimmed_ref[spare + 2 * place:spare + 2 * place + 1] = chosen[:1]
        trimmed_ref[spare + 2 * place + 1:spare + 2 * place + 2] = chosen[TILE - 1:]


def bulk_kernel(eta_ref, momenta_ref, depth_ref, wet_ref, eta_after, momenta_after, wet_after, depth_after,
                eta_ends, row_ends, turned, eta_pad, col_pad, momenta_in, depth_in, wet_in, eta_left, row_right, sems):
    rows, cols = eta_ref.shape[1:]
    parts = sems.shape[0]
    size = rows // parts
    loads = []
    for part in range(parts):
        here = pl.ds(part * size, size)
        loads.append(copied([
            (eta_ref.at[0, here, :], eta_pad.at[pl.ds(TILE + part * size, size), :]),
            (momenta_ref.at[:, 0, here, :], momenta_in.at[:, here, :]),
            (depth_ref.at[0, here, :], depth_in.at[here, :]),
            (wet_ref.at[0, here, :], wet_in.at[here, :]),
        ], sems.at[part]))
    lane = iota((TILE, cols), 1)
    eta_pad[TILE + rows:] = jnp.zeros((TILE, cols), jnp.float32)
    col_pad[:TILE] = jnp.zeros((TILE, cols), jnp.float32)

    def step(number, low):
        chunk, padded = slice(low, low + TILE), slice(TILE + low, 2 * TILE + low)
        eta = eta_pad[padded]
        if number == 0:
            mask = wet_in[chunk].astype(jnp.float32)
            depth = courant * mask * depth_in[chunk]
            wet_after[chunk] = mask
            depth_after[chunk] = depth
            row, col = momenta_in[0, chunk], momenta_in[1, chunk]
        else:
            mask, depth = wet_after[chunk], depth_after[chunk]
            row, col = momenta_after[0, chunk], col_pad[padded]
        east = jnp.where(lane == cols - 1, 0.0, rolled(eta, -1, 1))
        south = eta_pad[TILE + low + 1:2 * TILE + low + 1]
        row = mask * (row - courant * (east - eta))
        col = mask * (col - courant * (south - eta))
        momenta_after[0, chunk] = row
        col_pad[padded] = col
        if number:
            momenta_after[1, chunk] = col
        west = jnp.where(lane == 0, 0.0, rolled(row, 1, 1))
        north = col_pad[TILE + low - 1:2 * TILE + low - 1]
        eta = mask * eta - depth * (row - west + (col - north))
        if number:
            eta_after[chunk] = eta
            return
        eta_pad[padded] = eta
        eta_left[chunk] = eta[:, :LANES]
        row_right[chunk] = row[:, cols - LANES:]
        if low in (0, rows - TILE):
            end = int(low > 0)
            eta_ends[end] = eta
            row_ends[end] = row

    for copy in loads[0]:
        copy.wait()
    for part in range(parts + 1):
        if part + 1 < parts:
            for copy in loads[part + 1]:
                copy.wait()
        if part < parts:
            for low in range(part * size, (part + 1) * size, TILE):
                step(0, low)
        if part:
            for low in range((part - 1) * size, part * size, TILE):
                step(1, low)
    right = cols - LANES
    turned[0] = wet_after[:, :LANES].T[:TILE]
    turned[1] = depth_after[:, :LANES].T[:TILE]
    turned[2] = wet_after[:, right:].T[LANES - TILE:]
    turned[3] = depth_after[:, right:].T[LANES - TILE:]
    turned[4] = eta_left[...].T[:TILE]
    turned[5] = row_right[...].T[LANES - TILE:]


def sends_tables():
    return (lax.axis_index("level") == 0) & (lax.axis_index("sub") == 0)


def gather_kernel(*refs):
    first, packets, out_ref = refs[0], refs[1:-2], refs[-1]
    own = lax.axis_index("patch")
    out_ref[own] = first[...]
    tables = sends_tables()
    line = iota((TILE, LANES), 0)

    def ends_of(packet, at):
        value = jnp.where(line == 0, packet[at:at + 1], 0.0)
        return jnp.where(line == TILE - 1, packet[at + 1:at + 2], value)

    for place, packet in enumerate(packets):
        patch = own ^ (place + 1)
        if packet.shape[0] == LINES:
            out_ref[patch] = packet[...]
            continue

        def put(row, value):
            out_ref[patch, row * TILE:(row + 1) * TILE] = value

        out_ref[patch, :GAIN * TILE] = packet[:GAIN * TILE]
        whole = packet[GAIN * TILE:INDEX * TILE], packet[INDEX * TILE:(INDEX + 1) * TILE]
        ends = ends_of(packet, TRIMMED - SPARE), ends_of(packet, TRIMMED - SPARE + 2)
        put(GAIN, jnp.where(tables, whole[0], ends[0]))
        put(INDEX, jnp.where(tables, whole[1], ends[1]))
        put(EDGE_FLOW, jnp.where(tables, ends[0], whole[0]))
        put(EDGE_DEPTH, jnp.where(tables, ends[1], whole[1]))
        put(EDGE_SUM, packet[(INDEX + 1) * TILE:(INDEX + 2) * TILE])
        out_ref[patch, ROWS * TILE:] = packet[(INDEX + 2) * TILE:]


class Segment:
    def __init__(self, patch, flipped):
        self.patch, self.flipped = patch, flipped

    def place(self, patches):
        return self.flipped * patches + self.patch


def below_finest():
    return jnp.where(lax.axis_index("level") < lax.axis_size("level") - 1, 1.0, 0.0)


class Links:
    def __init__(self, links_ref, patches):
        self.links_ref, self.patches = links_ref, patches
        self.half = lax.axis_index("sub")
        self.known = {}

    def own(self):
        return Segment(lax.axis_index("patch"), 0)

    def all(self):
        return [Segment(patch, flipped) for flipped in range(2) for patch in range(self.patches)]

    def across(self, segment, way):
        key = id(segment.patch) if isinstance(segment.patch, jax.Array) else segment.patch, way
        if key not in self.known:
            patch = self.links_ref[0, segment.patch, way]
            self.known[key] = segment.patch, jnp.maximum(patch, 0), jnp.where(patch >= 0, 1.0, 0.0)
        return self.known[key][1:]

    def other_half(self, segment, way, inner):
        patch, there = self.across(segment, way)
        inside = self.half == (inner ^ segment.flipped)
        return Segment(jnp.where(inside, segment.patch, patch), 1 - segment.flipped), jnp.where(inside, 1.0, there)

    def north(self, segment):
        return self.other_half(segment, 0, 1)

    def south(self, segment):
        return self.other_half(segment, 1, 0)

    def west(self, segment):
        patch, there = self.across(segment, 2)
        return Segment(patch, segment.flipped), there

    def east(self, segment):
        patch, there = self.across(segment, 3)
        return Segment(patch, segment.flipped), there


class Packets:
    def __init__(self, got_refs):
        self.got_refs = got_refs

    def tile(self, segment, row):
        return self.got_refs[segment.flipped][segment.patch, row * TILE:(row + 1) * TILE]

    def line(self, segment, row, line):
        return self.got_refs[segment.flipped][segment.patch, row * TILE + line:row * TILE + line + 1]

    def row(self, segment, row):
        return jnp.concatenate([self.line(segment, row, line) for line in range(TILE)], axis=1)

    def column(self, segment, column):
        return self.line(segment, ROWS, column)


def is_first(shape=(TILE, LANES)):
    return (iota(shape, 0) == 0) & (iota(shape, 1) == 0)


def is_last(shape=(TILE, LANES)):
    return (iota(shape, 0) == shape[0] - 1) & (iota(shape, 1) == shape[1] - 1)


def next_cells(tile, edge):
    lane = iota(tile.shape, 1)
    moved = rolled(tile, -1, 1)
    moved = jnp.where(lane == LANES - 1, rolled(moved, -1, 0), moved)
    return jnp.where(is_last(), edge, moved)


def last_cells(tile, edge):
    lane = iota(tile.shape, 1)
    moved = rolled(tile, 1, 1)
    moved = jnp.where(lane == 0, rolled(moved, 1, 0), moved)
    return jnp.where(is_first(), edge, moved)


def row_of(ref, place):
    return jnp.concatenate([ref[place, line:line + 1] for line in range(TILE)], axis=1)


def split_index(index):
    index = index.astype(jnp.int32)
    return index & (LANES - 1), index >> LANE_BITS


def nested(flux, lane, line):
    taken = jnp.zeros(lane.shape, jnp.float32)
    for source in range(TILE):
        values = jnp.broadcast_to(flux[source:source + 1], lane.shape)
        found = jnp.take_along_axis(values, lane, axis=1, mode="promise_in_bounds")
        taken = jnp.where(line == source, found, taken)
    return taken


def strips_kernel(*refs):
    links_ref, mine_ref, other_ref = refs[:3]
    out_ref, strips_ref = refs[-2:]
    finer_ref = refs[3] if len(refs) == 6 else None
    links = Links(links_ref, mine_ref.shape[0])
    patches, count = links.patches, 2 * links.patches
    packets = Packets((mine_ref, other_ref))
    every = links.all()
    strips, inflows = [], []
    for segment in every:
        strip = packets.tile(segment, STRIP)
        if finer_ref is not None:
            place = segment.place(patches)
            gain, cells = packets.tile(segment, GAIN) * below_finest(), split_index(packets.tile(segment, INDEX))
            inflow, later = [gain * nested(finer_ref[step * count + place], *cells) for step in range(2)]
            inflows.append((inflow, later))
            strip = strip + inflow
            strips_ref[place] = strip
        strips.append(strip)

    def strip_at(segment):
        return packets.tile(segment, STRIP) if finer_ref is None else strips_ref[segment.place(patches)]

    totals = []
    for place, segment in enumerate(every):
        eta, depth = strips[place], packets.tile(segment, STRIP_DEPTH)
        mask = wet(depth)
        east, there = links.east(segment)
        edge = there * rolled(rolled(strip_at(east), -1, 1), -1, 0)
        if finer_ref is None:
            row = jnp.where(is_last(), -courant * mask * edge, 0.0)
        else:
            inflow, later = inflows[place]
            row = courant * mask * (inflow - next_cells(inflow, edge))
        west, there = links.west(segment)
        west_eta = rolled(rolled(strip_at(west), 1, 1), 1, 0)
        west_mask = rolled(rolled(wet(packets.tile(west, STRIP_DEPTH)), 1, 1), 1, 0)
        edge = there * west_mask * (packets.column(west, LAST_ROW) - courant * (eta - west_eta))
        north, there = links.north(segment)
        col = there * (packets.tile(north, EDGE_FLOW) - courant * wet(packets.tile(north, EDGE_DEPTH)) * eta)
        total = packets.tile(segment, STRIP_SUM)
        if finer_ref is None:
            total = total - courant * depth * (row - jnp.where(is_first(), edge, 0.0) - col)
        else:
            total = (total + mask * inflow + later
                     - courant * depth * (row - last_cells(row, edge) + courant * mask * inflow - col))
        totals.append(total)
    for place, (strip, total) in enumerate(zip(strips, totals)):
        out_ref[place] = strip
        out_ref[count + place] = total


def beside(links, packets, own, inflow=None):
    lane = iota((1, LANES), 1)
    first, last = lane == 0, lane == LANES - 1

    def field(segment, column):
        return packets.column(segment, column) if inflow is None else 0.0

    def strip(name, turned):
        return 0.0 if inflow is None else jnp.where(first, rolled(inflow[name], turned, 1), 0.0)

    def corner_col(segment, eta, line, turned):
        north, beyond = links.north(segment)
        mask = rolled(wet(packets.line(north, EDGE_DEPTH, line)), turned, 1)
        flow = rolled(packets.line(north, EDGE_FLOW, line), turned, 1) if inflow is None else 0.0
        return beyond * (flow - courant * mask * eta)

    west, there = links.west(own)
    eta = field(west, LAST_ETA) + strip("west", 1)
    next_eta = field(west, NEXT_ETA) + strip("west", 2)
    own_eta = field(own, FIRST_ETA) + strip("own", 0)
    depth = packets.column(west, LAST_DEPTH) * there
    mask = wet(depth)
    next_row = wet(packets.column(west, NEXT_DEPTH)) * (field(west, NEXT_ROW) - courant * (eta - next_eta))
    below, beyond = links.south(west)
    corner = packets.line(below, STRIP, TILE - 1) if inflow is None else inflow["south west"]
    south_eta = jnp.where(last, corner * beyond, rolled(eta, -1, 1))
    col = mask * (field(west, LAST_COL) - courant * (south_eta - eta))
    north_col = jnp.where(first, corner_col(west, eta, TILE - 1, 1), rolled(col, 1, 1))
    west_row = mask * (field(west, LAST_ROW) - courant * (own_eta - eta))
    west_eta = (mask * eta - courant * depth * (west_row - next_row + col - north_col) + strip("west later", 1))
    west_mask = mask

    east, there = links.east(own)
    eta = there * (field(east, FIRST_ETA) + strip("east", 0))
    second_eta = field(east, SECOND_ETA) + strip("east", -1)
    depth = packets.column(east, FIRST_DEPTH) * there
    mask = wet(depth)
    row = mask * (field(east, FIRST_ROW) - courant * (second_eta - eta))
    below, beyond = links.south(east)
    corner = packets.line(below, STRIP, 0) if inflow is None else inflow["south east"]
    south_eta = jnp.where(last, rolled(corner, -1, 1) * beyond, rolled(eta, -1, 1))
    col = mask * (field(east, FIRST_COL) - courant * (south_eta - eta))
    north_col = jnp.where(first, corner_col(east, eta, 0, 0), rolled(col, 1, 1))
    east_sum = mask * eta - courant * depth * (row + col - north_col) + there * strip("east later", 0)
    return west_row, west_mask, west_eta, eta, east_sum, courant * depth


def advanced(eta, row, col, mask, depth, east, south, west, north):
    row = mask * (row - courant * (east(eta) - eta))
    col = mask * (col - courant * (south(eta) - eta))
    return mask * eta - depth * (row - west(row) + col - north(col)), row, col


def two_steps(start, mask, depth, sides, base, north=None, south=None, second=None):
    lane, line = iota(mask.shape, 1), iota(mask.shape, 0)
    cols = mask.shape[1]
    west_row, west_mask, west_eta, east_eta, east_sum, east_depth = sides
    state = start, 0.0, 0.0
    flow, beyond = west_row, east_eta
    above = 0.0 if north is None else north[0]
    for number in range(2):
        below = 0.0 if south is None else south[number]
        state = advanced(
            *state, mask, depth,
            lambda eta: jnp.where(lane == cols - 1, beyond, rolled(eta, -1, 1)),
            lambda eta: jnp.where(line == TILE - 1, below, rolled(eta, -1, 0)),
            lambda row: jnp.where(lane == 0, flow, rolled(row, 1, 1)),
            lambda col: jnp.where(line == 0, above, rolled(col, 1, 0)))
        if number:
            return state
        eta, row, col = state
        if second is not None:
            eta = eta + jnp.where(line == 0, second, 0.0)
            state = eta, row, col
        whole_eta, whole_row = (eta, row) if base is None else (eta + base[0], row + base[1])
        flow = west_mask * (west_row - courant * (whole_eta[:, :1] - west_eta))
        beyond = east_sum + east_depth * whole_row[:, cols - 1:]
        if north is not None:
            above = north[1] * (north[0] - courant * (whole_eta[:1] - north[2]))


def north_of(links, packets, own, own_strip, inflow=None):
    cols = own_strip.shape[1]
    lane = iota((1, LANES), 1)
    north, there = links.north(own)
    depth = packets.row(north, EDGE_DEPTH) * there
    mask = wet(depth)
    if inflow is not None:
        col = -courant * mask * own_strip
        return col, mask, -courant * depth * col
    col = packets.row(north, EDGE_FLOW) * there - courant * mask * own_strip
    north_east, beyond = links.east(north)
    right_eta = beyond * packets.column(north_east, FIRST_ETA)
    north_west, beyond = links.west(north)
    left_row = beyond * wet(packets.column(north_west, LAST_DEPTH)) * (
        packets.column(north_west, LAST_ROW)
        - courant * (packets.column(north, FIRST_ETA) - packets.column(north_west, LAST_ETA)))
    nothing = jnp.zeros((1, cols - LANES), jnp.float32)
    corners = (jnp.concatenate([jnp.where(lane == 0, rolled(left_row, 1, 1), 0.0), nothing], axis=1)
               + jnp.concatenate([nothing, jnp.where(lane == LANES - 1, courant * right_eta, 0.0)], axis=1))
    return col, mask, packets.row(north, EDGE_SUM) + courant * depth * (corners - col)


def as_sublanes(columns):
    rows = columns[0].shape[1]
    count = -len(columns) % TILE
    turned = jnp.concatenate(list(columns) + [jnp.zeros((count, rows), jnp.float32)], axis=0).T
    return [[turned[low:low + TILE, place:place + 1] for place in range(len(columns))]
            for low in (0, rows - TILE)]


def halo_kernel(links_ref, mine_ref, other_ref, strips_ref, eta_after, momenta_after, wet_after, depth_after,
                eta_ends, row_ends, turned, eta_out, momenta_out, ends_out, sides_new, more_ref, sems):
    rows, cols = eta_after.shape
    fields = eta_after, momenta_after.at[0], momenta_after.at[1]
    outs = eta_out.at[0], momenta_out.at[0, 0], momenta_out.at[1, 0]
    inner, between = pl.ds(TILE, rows - 2 * TILE), pl.ds(LANES, cols - 2 * LANES)
    copies = copied(
        [(field.at[inner, between], out.at[inner, between]) for field, out in zip(fields, outs)], sems.at[0])
    links = Links(links_ref, mine_ref.shape[0])
    own = links.own()
    packets = Packets((mine_ref, other_ref))
    columns = beside(links, packets, own)
    west_row, west_mask, west_eta, east_eta, east_sum, east_depth = columns

    line, lane = iota((TILE, rows), 0), iota((TILE, rows), 1)
    nothing = jnp.zeros((TILE, rows), jnp.float32)

    def column_steps(mask, depth, east, west):
        state = nothing, nothing, nothing
        for number in range(2):
            state = advanced(
                *state, mask, depth,
                lambda eta: jnp.where(line == TILE - 1, east(number, state), rolled(eta, -1, 0)),
                lambda eta: jnp.where(lane == rows - 1, 0.0, rolled(eta, -1, 1)),
                lambda row: jnp.where(line == 0, west(number, state), rolled(row, 1, 0)),
                lambda col: jnp.where(lane == 0, 0.0, rolled(col, 1, 1)))
        return state

    def west_of(number, state):
        if number == 0:
            return west_row
        whole = state[0][:1] + turned[4, :1]
        return west_mask * (west_row - courant * (whole - west_eta))

    def east_of(number, state):
        if number == 0:
            return east_eta
        return east_sum + east_depth * (state[1][TILE - 1:] + turned[5, TILE - 1:])

    left = column_steps(turned[0], turned[1], lambda number, state: 0.0, west_of)
    last = column_steps(turned[2], turned[3], east_of, lambda number, state: 0.0)
    middle = jnp.zeros((LANES - 2 * TILE, rows), jnp.float32)
    body_rows = slice(TILE, rows - TILE)
    inside = iota((rows - 2 * TILE, LANES), 1)
    wides = slice(0, LANES), slice(cols - LANES, cols)
    for place, field in enumerate(fields):
        more_ref[place] = jnp.concatenate([left[place], middle, last[place]], axis=0).T
        more = more_ref[place, body_rows]
        sides_new[0, place] = field[body_rows, wides[0]] + jnp.where(inside < TILE, more, 0.0)
        sides_new[1, place] = field[body_rows, wides[1]] + jnp.where(inside >= LANES - TILE, more, 0.0)
    for side, wide in enumerate(wides):
        copies += copied(
            [(sides_new.at[side, place], out.at[inner, pl.ds(wide.start, LANES)]) for place, out in enumerate(outs)],
            sems.at[1 + side])

    top_sides, low_sides = as_sublanes(columns)
    nothing = jnp.zeros((TILE, cols), jnp.float32)
    end = slice(rows - TILE, rows)
    top = two_steps(
        nothing, wet_after[:TILE], depth_after[:TILE], top_sides, (eta_ends[0], row_ends[0]),
        north=north_of(links, packets, own, packets.row(own, STRIP)))
    below, there = links.south(own)
    low = two_steps(
        nothing, wet_after[end], depth_after[end], low_sides, (eta_ends[1], row_ends[1]),
        south=(packets.row(below, STRIP) * there,
               row_of(strips_ref, 2 * links.patches + below.place(links.patches)) * there))
    line, inside = iota((TILE, cols), 0), iota((TILE, LANES), 1)
    gap = jnp.zeros((TILE, cols - 2 * LANES), jnp.float32)
    for edge, (chunk, near, found) in enumerate(
            ((slice(0, TILE), line < TILE // 2, top), (end, line >= TILE // 2, low))):
        for place in range(3):
            more = more_ref[place, chunk]
            wide = jnp.concatenate(
                [jnp.where(inside < TILE, more, 0.0), gap, jnp.where(inside >= LANES - TILE, more, 0.0)], axis=1)
            ends_out[place, edge] = fields[place][chunk] + jnp.where(near, found[place], wide)
    for copy in copies:
        copy.wait()


def inflow_kernel(links_ref, mine_ref, other_ref, finer_ref, wet_after, depth_after, ends_ref, eta_hbm, momenta_hbm,
                  eta_out, momenta_out, rows_ref, new_ref, sems):
    del eta_hbm, momenta_hbm
    rows, cols = wet_after.shape
    links = Links(links_ref, mine_ref.shape[0])
    patches = links.patches
    own = links.own()
    packets = Packets((mine_ref, other_ref))
    some = below_finest()

    def flux_place(step, segment):
        return step * 2 * patches + segment.place(patches)

    def inflows(segment):
        gain, cells = packets.tile(segment, GAIN) * some, split_index(packets.tile(segment, INDEX))
        return [gain * nested(finer_ref[flux_place(step, segment)], *cells) for step in range(2)]

    below, there = links.south(own)
    west, east = links.west(own)[0], links.east(own)[0]
    below_west, beyond_west = links.west(below)
    below_east, beyond_east = links.east(below)
    wanted = (
        ("west", 0, west, TILE - 1), ("west later", 1, west, TILE - 1), ("east", 0, east, 0),
        ("east later", 1, east, 0), ("south west", 0, links.south(west)[0], TILE - 1),
        ("south east", 0, links.south(east)[0], 0), ("below west", 0, below_west, TILE - 1),
        ("below east", 0, below_east, 0))
    gain = jnp.concatenate([packets.line(segment, GAIN, line) for _, _, segment, line in wanted], axis=0)
    index = jnp.concatenate([packets.line(segment, INDEX, line) for _, _, segment, line in wanted], axis=0)
    lane, line = split_index(index)
    taken = jnp.zeros((TILE, LANES), jnp.float32)
    for source in range(TILE):
        values = jnp.concatenate(
            [finer_ref[flux_place(step, segment), source:source + 1] for _, step, segment, _ in wanted], axis=0)
        found = jnp.take_along_axis(values, lane, axis=1, mode="promise_in_bounds")
        taken = jnp.where(line == source, found, taken)
    taken = some * gain * taken
    inflow = {name: taken[place:place + 1] for place, (name, _, _, _) in enumerate(wanted)}

    rows_ref[0], rows_ref[1] = inflows(own)
    strip, later = inflows(below)
    strip, later = strip * there, later * there
    inflow["own"] = rows_ref[0, :1]

    depth = packets.tile(below, STRIP_DEPTH)
    mask = wet(depth)
    edge = jnp.broadcast_to(rolled(inflow["below east"] * beyond_east, -1, 1), (TILE, LANES))
    row = courant * mask * (strip - next_cells(strip, edge))
    west_mask = rolled(wet(packets.line(below_west, STRIP_DEPTH, TILE - 1)), 1, 1)
    edge = beyond_west * courant * west_mask * (rolled(inflow["below west"], 1, 1) - strip[:1])
    edge = jnp.broadcast_to(edge, (TILE, LANES))
    north, beyond = links.north(below)
    col = -courant * wet(packets.tile(north, EDGE_DEPTH)) * beyond * strip
    rows_ref[2] = strip
    rows_ref[3] = there * (
        mask * strip - courant * depth * (row - last_cells(row, edge) + courant * mask * strip - col) + later)

    columns = beside(links, packets, own, inflow)
    top_sides, low_sides = as_sublanes(columns)
    line = iota((TILE, cols), 0)
    strip = row_of(rows_ref, 0)
    top = two_steps(
        jnp.where(line == 0, strip, 0.0), wet_after[:TILE], depth_after[:TILE], top_sides, None,
        north=north_of(links, packets, own, strip, inflow), second=row_of(rows_ref, 1))
    copies = []
    outs = eta_out.at[0], momenta_out.at[0, 0], momenta_out.at[1, 0]

    def write(end, near, found):
        for place in range(3):
            new_ref[place, end] = ends_ref[place, end] + jnp.where(near, found[place], 0.0)
        here = pl.ds(end * (rows - TILE), TILE)
        copies.extend(copied(
            [(new_ref.at[place, end], out.at[here, :]) for place, out in enumerate(outs)], sems.at[end]))

    write(0, line < TILE // 2, top)
    low = two_steps(
        jnp.zeros((TILE, cols), jnp.float32), wet_after[rows - TILE:], depth_after[rows - TILE:],
        low_sides, None, south=(row_of(rows_ref, 2), row_of(rows_ref, 3)))
    write(1, line >= TILE // 2, low)
    for copy in copies:
        copy.wait()


def body(adjoint_height, adjoint_momenta, depth, wet_mask, adjacency, nest_gain, nest_index):
    rows, cols = adjoint_height.shape[1:]
    levels = lax.axis_size("level")
    patches = lax.axis_size("patch")
    count = 2 * patches
    params = pltpu.CompilerParams(vmem_limit_bytes=VMEM_LIMIT)
    vmem = pl.BlockSpec(memory_space=pltpu.VMEM)
    smem = pl.BlockSpec(memory_space=pltpu.SMEM)
    hbm = pl.BlockSpec(memory_space=pltpu.HBM)

    def array(*shape):
        return jax.ShapeDtypeStruct(shape, jnp.float32)

    def scratch(*shape):
        return pltpu.VMEM(shape, jnp.float32)

    fields = [pltpu.with_memory_space_constraint(field, pltpu.HBM)
              for field in (adjoint_height, adjoint_momenta, depth, wet_mask, nest_gain, nest_index)]
    packed, trimmed = pl.pallas_call(
        pack_kernel,
        out_shape=[array(LINES, LANES), array(TRIMMED, LANES)],
        in_specs=[hbm] * 6,
        out_specs=[vmem, vmem],
        scratch_shapes=[
            scratch(2, 4, TILE, cols), pltpu.VMEM((2, TILE, cols), jnp.int32),
            scratch(2, 4, rows, LANES), pltpu.VMEM((2, rows, LANES), jnp.int32),
            scratch(levels, cols), pltpu.VMEM((levels, cols), jnp.int32),
            pltpu.SemaphoreType.DMA((18,)),
        ],
        compiler_params=params,
        name="pack",
    )(*fields)
    parts = 4
    after = pl.pallas_call(
        bulk_kernel,
        out_shape=[
            array(rows, cols), array(2, rows, cols), array(rows, cols), array(rows, cols),
            array(2, TILE, cols), array(2, TILE, cols), array(6, TILE, rows),
        ],
        in_specs=[hbm] * 4,
        out_specs=[vmem] * 7,
        scratch_shapes=[
            scratch(rows + 2 * TILE, cols), scratch(rows + 2 * TILE, cols),
            scratch(2, rows, cols), scratch(rows, cols), pltpu.VMEM((rows, cols), jnp.int32),
            scratch(rows, LANES), scratch(rows, LANES), pltpu.SemaphoreType.DMA((parts, 4)),
        ],
        compiler_params=params,
        name="bulk",
    )(*fields[:4])

    sent = [packed] + [
        lax.ppermute(trimmed if levels == 2 else packed, "patch",
                     [(source, source ^ turn) for source in range(patches)])
        for turn in range(1, patches)
    ]
    mine = pl.pallas_call(
        gather_kernel,
        out_shape=array(patches, LINES, LANES),
        in_specs=[vmem] * (patches + 1),
        out_specs=vmem,
        compiler_params=params,
        name="gather",
    )(*sent, after[-1])
    other = lax.ppermute(mine, "sub", [(0, 1), (1, 0)])

    flux = ()
    strips = []
    for turn in range(levels - 1):
        strips.append(pl.pallas_call(
            strips_kernel,
            out_shape=array(2 * count, TILE, LANES),
            in_specs=[smem] + [vmem] * (2 + len(flux)),
            out_specs=vmem,
            scratch_shapes=[scratch(count, TILE, LANES)],
            compiler_params=params,
            name="strips",
        )(adjacency, mine, other, *flux))
        flux = (lax.ppermute(strips[-1], "level", [(source, (source - 1) % levels) for source in range(levels)]),)

    eta_new, momenta_new, ends = pl.pallas_call(
        halo_kernel,
        out_shape=[array(*adjoint_height.shape), array(*adjoint_momenta.shape), array(3, 2, TILE, cols)],
        in_specs=[smem] + [vmem] * 10,
        out_specs=[hbm, hbm, vmem],
        scratch_shapes=[
            scratch(2, 3, rows - 2 * TILE, LANES), scratch(3, rows, LANES), pltpu.SemaphoreType.DMA((3, 3)),
        ],
        compiler_params=params,
        name="halo",
    )(adjacency, mine, other, strips[0], *after)

    return pl.pallas_call(
        inflow_kernel,
        out_shape=[array(*adjoint_height.shape), array(*adjoint_momenta.shape)],
        in_specs=[smem] + [vmem] * 6 + [hbm] * 2,
        out_specs=[hbm, hbm],
        input_output_aliases={7: 0, 8: 1},
        scratch_shapes=[
            scratch(4, TILE, LANES), scratch(3, 2, TILE, cols), pltpu.SemaphoreType.DMA((2, 3)),
        ],
        compiler_params=params,
        name="inflow",
    )(adjacency, mine, other, *flux, after[2], after[3], ends, eta_new, momenta_new)


def solution(mesh):
    in_specs = (
        P(("parts", "level"), ("patch", "sub"), None),
        P(None, ("parts", "level"), ("patch", "sub"), None),
        P("level", ("patch", "sub"), None),
        P("level", ("patch", "sub"), None),
        P("level", None, None),
        P(None, ("patch", "sub")),
        P(None, ("patch", "sub")),
    )
    out_specs = (
        P(("parts", "level"), ("patch", "sub"), None),
        P(None, ("parts", "level"), ("patch", "sub"), None),
    )
    return jax.shard_map(body, mesh=mesh, in_specs=in_specs, out_specs=out_specs, check_vma=False)
```

```python
import jax
import jax.numpy as jnp
from jax import lax
from jax.experimental import pallas as pl
from jax.experimental.pallas import tpu as pltpu
from jax.sharding import PartitionSpec as P

STEPS = 2
LANES = 128
TILE = 8
VMEM_LIMIT = 48 * 1024 * 1024

courant = 0.45

STRIP_SUM, STRIP, STRIP_DEPTH, GAIN, INDEX, EDGE_FLOW, EDGE_DEPTH, EDGE_SUM = range(8)
(FIRST_ETA, SECOND_ETA, FIRST_ROW, FIRST_COL, FIRST_DEPTH, NEXT_ETA, LAST_ETA, NEXT_ROW,
 LAST_ROW, LAST_COL, NEXT_DEPTH, LAST_DEPTH) = range(12)
ROWS, COLUMNS = 8, 16
LINES = ROWS * TILE + COLUMNS
TRIMMED, SPARE = LINES - 2 * TILE, 4


def iota(shape, axis):
    return lax.broadcasted_iota(jnp.int32, shape, axis)


def rolled(value, shift, axis):
    if shift == 0:
        return value
    return pltpu.roll(value, shift % value.shape[axis], axis)


def wet(depth):
    return (depth > 0).astype(jnp.float32)


def copied(pairs, sems):
    copies = [pltpu.make_async_copy(source, target, sems.at[place]) for place, (source, target) in enumerate(pairs)]
    for copy in copies:
        copy.start()
    return copies


def pack_kernel(eta_ref, momenta_ref, depth_ref, wet_ref, gain_ref, index_ref, out_ref, trimmed_ref,
                ends, end_wet, sides, side_wet, gains, indices, sems):
    rows, cols = eta_ref.shape[1:]
    tall, wide = [], []
    for end in range(2):
        here = pl.ds(end * (rows - TILE), TILE)
        tall += [
            (eta_ref.at[0, here, :], ends.at[end, 0]), (momenta_ref.at[:, 0, here, :], ends.at[end, pl.ds(1, 2)]),
            (depth_ref.at[0, here, :], ends.at[end, 3]), (wet_ref.at[0, here, :], end_wet.at[end])]
        here = pl.ds(end * (cols - LANES), LANES)
        wide += [
            (eta_ref.at[0, :, here], sides.at[end, 0]), (momenta_ref.at[:, 0, :, here], sides.at[end, pl.ds(1, 2)]),
            (depth_ref.at[0, :, here], sides.at[end, 3]), (wet_ref.at[0, :, here], side_wet.at[end])]
    tall += [(gain_ref, gains), (index_ref, indices)]
    copies = copied(tall + wide, sems)
    for copy in copies[:len(tall)]:
        copy.wait()
    level = lax.axis_index("level")
    lane = iota((TILE, cols), 1)

    def loaded(end):
        mask = end_wet[end].astype(jnp.float32)
        return ends[end, 0], ends[end, 1], ends[end, 2], mask * ends[end, 3], mask

    def put(row, value):
        for tile in range(TILE):
            out_ref[row * TILE + tile:row * TILE + tile + 1] = value[:, tile * LANES:(tile + 1) * LANES]

    eta, row, col, depth, mask = loaded(0)
    east = jnp.where(lane == cols - 1, 0.0, rolled(eta, -1, 1))
    row = mask * (row - courant * (east - eta))
    west = jnp.where(lane == 0, 0.0, rolled(row, 1, 1))
    col = mask * (col - courant * (rolled(eta, -1, 0) - eta))
    strip_sum = mask * eta - courant * depth * (row - west + col)
    put(STRIP_SUM, strip_sum[:1])
    put(STRIP, eta[:1])
    put(STRIP_DEPTH, depth[:1])
    put(GAIN, gains[pl.ds(level, 1), :])
    put(INDEX, indices[pl.ds(level, 1), :].astype(jnp.float32))

    eta, row, col, depth, mask = loaded(1)
    east = jnp.where(lane == cols - 1, 0.0, rolled(eta, -1, 1))
    row = mask * (row - courant * (east - eta))
    west = jnp.where(lane == 0, 0.0, rolled(row, 1, 1))
    flow = mask * (col + courant * eta)
    above = rolled(flow - courant * mask * rolled(eta, -1, 0), 1, 0)
    edge_sum = mask * eta - courant * depth * (row - west - above)
    put(EDGE_FLOW, flow[TILE - 1:])
    put(EDGE_DEPTH, depth[TILE - 1:])
    put(EDGE_SUM, edge_sum[TILE - 1:])

    for copy in copies[len(tall):]:
        copy.wait()
    lane = iota((rows, LANES), 1)
    columns = jnp.zeros((rows, LANES), jnp.float32)
    depths = [sides[end, 3] * side_wet[end].astype(jnp.float32) for end in range(2)]
    for place, value, at in (
        (FIRST_ETA, sides[0, 0], 0), (SECOND_ETA, sides[0, 0], 1), (FIRST_ROW, sides[0, 1], 0),
        (FIRST_COL, sides[0, 2], 0), (FIRST_DEPTH, depths[0], 0),
        (NEXT_ETA, sides[1, 0], LANES - 2), (LAST_ETA, sides[1, 0], LANES - 1),
        (NEXT_ROW, sides[1, 1], LANES - 2), (LAST_ROW, sides[1, 1], LANES - 1),
        (LAST_COL, sides[1, 2], LANES - 1),
        (NEXT_DEPTH, depths[1], LANES - 2), (LAST_DEPTH, depths[1], LANES - 1),
    ):
        moved = value if place == at else rolled(value, place - at, 1)
        columns = jnp.where(lane == place, moved, columns)
    out_ref[ROWS * TILE:] = columns.T[:COLUMNS]

    def tile(row):
        return out_ref[row * TILE:(row + 1) * TILE]

    tables = sends_tables()
    flow, depth, gain, index = tile(EDGE_FLOW), tile(EDGE_DEPTH), tile(GAIN), tile(INDEX)
    trimmed_ref[:GAIN * TILE] = out_ref[:GAIN * TILE]
    trimmed_ref[GAIN * TILE:INDEX * TILE] = jnp.where(tables, gain, flow)
    trimmed_ref[INDEX * TILE:(INDEX + 1) * TILE] = jnp.where(tables, index, depth)
    trimmed_ref[(INDEX + 1) * TILE:(INDEX + 2) * TILE] = tile(EDGE_SUM)
    trimmed_ref[(INDEX + 2) * TILE:] = out_ref[ROWS * TILE:]
    spare = TRIMMED - SPARE
    for place, (other, own) in enumerate(((flow, gain), (depth, index))):
        chosen = jnp.where(tables, other, own)
        trimmed_ref[spare + 2 * place:spare + 2 * place + 1] = chosen[:1]
        trimmed_ref[spare + 2 * place + 1:spare + 2 * place + 2] = chosen[TILE - 1:]


def bulk_kernel(eta_ref, momenta_ref, depth_ref, wet_ref, eta_after, momenta_after, wet_after, depth_after,
                eta_ends, row_ends, turned, eta_pad, col_pad, momenta_in, depth_in, wet_in, eta_left, row_right, sems):
    rows, cols = eta_ref.shape[1:]
    parts = sems.shape[0]
    size = rows // parts
    loads = []
    for part in range(parts):
        here = pl.ds(part * size, size)
        loads.append(copied([
            (eta_ref.at[0, here, :], eta_pad.at[pl.ds(TILE + part * size, size), :]),
            (momenta_ref.at[:, 0, here, :], momenta_in.at[:, here, :]),
            (depth_ref.at[0, here, :], depth_in.at[here, :]),
            (wet_ref.at[0, here, :], wet_in.at[here, :]),
        ], sems.at[part]))
    lane = iota((TILE, cols), 1)
    eta_pad[TILE + rows:] = jnp.zeros((TILE, cols), jnp.float32)
    col_pad[:TILE] = jnp.zeros((TILE, cols), jnp.float32)

    def step(number, low):
        chunk, padded = slice(low, low + TILE), slice(TILE + low, 2 * TILE + low)
        eta = eta_pad[padded]
        if number == 0:
            mask = wet_in[chunk].astype(jnp.float32)
            depth = courant * mask * depth_in[chunk]
            wet_after[chunk] = mask
            depth_after[chunk] = depth
            row, col = momenta_in[0, chunk], momenta_in[1, chunk]
        else:
            mask, depth = wet_after[chunk], depth_after[chunk]
            row, col = momenta_after[0, chunk], col_pad[padded]
        east = jnp.where(lane == cols - 1, 0.0, rolled(eta, -1, 1))
        south = eta_pad[TILE + low + 1:2 * TILE + low + 1]
        row = mask * (row - courant * (east - eta))
        col = mask * (col - courant * (south - eta))
        momenta_after[0, chunk] = row
        col_pad[padded] = col
        if number:
            momenta_after[1, chunk] = col
        west = jnp.where(lane == 0, 0.0, rolled(row, 1, 1))
        north = col_pad[TILE + low - 1:2 * TILE + low - 1]
        eta = mask * eta - depth * (row - west + (col - north))
        if number:
            eta_after[chunk] = eta
            return
        eta_pad[padded] = eta
        eta_left[chunk] = eta[:, :LANES]
        row_right[chunk] = row[:, cols - LANES:]
        if low in (0, rows - TILE):
            end = int(low > 0)
            eta_ends[end] = eta
            row_ends[end] = row

    for copy in loads[0]:
        copy.wait()
    for part in range(parts + 1):
        if part + 1 < parts:
            for copy in loads[part + 1]:
                copy.wait()
        if part < parts:
            for low in range(part * size, (part + 1) * size, TILE):
                step(0, low)
        if part:
            for low in range((part - 1) * size, part * size, TILE):
                step(1, low)
    right = cols - LANES
    turned[0] = wet_after[:, :LANES].T[:TILE]
    turned[1] = depth_after[:, :LANES].T[:TILE]
    turned[2] = wet_after[:, right:].T[LANES - TILE:]
    turned[3] = depth_after[:, right:].T[LANES - TILE:]
    turned[4] = eta_left[...].T[:TILE]
    turned[5] = row_right[...].T[LANES - TILE:]


def sends_tables():
    return (lax.axis_index("level") == 0) & (lax.axis_index("sub") == 0)


def gather_kernel(*refs):
    first, packets, out_ref = refs[0], refs[1:-2], refs[-1]
    own = lax.axis_index("patch")
    out_ref[own] = first[...]
    tables = sends_tables()
    line = iota((TILE, LANES), 0)

    def ends_of(packet, at):
        value = jnp.where(line == 0, packet[at:at + 1], 0.0)
        return jnp.where(line == TILE - 1, packet[at + 1:at + 2], value)

    for place, packet in enumerate(packets):
        patch = own ^ (place + 1)
        if packet.shape[0] == LINES:
            out_ref[patch] = packet[...]
            continue

        def put(row, value):
            out_ref[patch, row * TILE:(row + 1) * TILE] = value

        out_ref[patch, :GAIN * TILE] = packet[:GAIN * TILE]
        whole = packet[GAIN * TILE:INDEX * TILE], packet[INDEX * TILE:(INDEX + 1) * TILE]
        ends = ends_of(packet, TRIMMED - SPARE), ends_of(packet, TRIMMED - SPARE + 2)
        put(GAIN, jnp.where(tables, whole[0], ends[0]))
        put(INDEX, jnp.where(tables, whole[1], ends[1]))
        put(EDGE_FLOW, jnp.where(tables, ends[0], whole[0]))
        put(EDGE_DEPTH, jnp.where(tables, ends[1], whole[1]))
        put(EDGE_SUM, packet[(INDEX + 1) * TILE:(INDEX + 2) * TILE])
        out_ref[patch, ROWS * TILE:] = packet[(INDEX + 2) * TILE:]


class Segment:
    def __init__(self, patch, flipped):
        self.patch, self.flipped = patch, flipped

    def place(self, patches):
        return self.flipped * patches + self.patch


def below_finest():
    return jnp.where(lax.axis_index("level") < lax.axis_size("level") - 1, 1.0, 0.0)


class Links:
    def __init__(self, links_ref, patches):
        self.links_ref, self.patches = links_ref, patches
        self.half = lax.axis_index("sub")

    def own(self):
        return Segment(lax.axis_index("patch"), 0)

    def all(self):
        return [Segment(patch, flipped) for flipped in range(2) for patch in range(self.patches)]

    def across(self, segment, way):
        patch = self.links_ref[0, segment.patch, way]
        return jnp.maximum(patch, 0), jnp.where(patch >= 0, 1.0, 0.0)

    def other_half(self, segment, way, inner):
        patch, there = self.across(segment, way)
        inside = self.half == (inner ^ segment.flipped)
        return Segment(jnp.where(inside, segment.patch, patch), 1 - segment.flipped), jnp.where(inside, 1.0, there)

    def north(self, segment):
        return self.other_half(segment, 0, 1)

    def south(self, segment):
        return self.other_half(segment, 1, 0)

    def west(self, segment):
        patch, there = self.across(segment, 2)
        return Segment(patch, segment.flipped), there

    def east(self, segment):
        patch, there = self.across(segment, 3)
        return Segment(patch, segment.flipped), there


class Packets:
    def __init__(self, got_refs):
        self.got_refs = got_refs

    def tile(self, segment, row):
        return self.got_refs[segment.flipped][segment.patch, row * TILE:(row + 1) * TILE]

    def line(self, segment, row, line):
        return self.got_refs[segment.flipped][segment.patch, row * TILE + line:row * TILE + line + 1]

    def row(self, segment, row):
        return jnp.concatenate([self.line(segment, row, line) for line in range(TILE)], axis=1)

    def column(self, segment, column):
        return self.line(segment, ROWS, column)


def is_first(shape=(TILE, LANES)):
    return (iota(shape, 0) == 0) & (iota(shape, 1) == 0)


def is_last(shape=(TILE, LANES)):
    return (iota(shape, 0) == shape[0] - 1) & (iota(shape, 1) == shape[1] - 1)


def next_cells(tile, edge):
    lane = iota(tile.shape, 1)
    moved = rolled(tile, -1, 1)
    moved = jnp.where(lane == LANES - 1, rolled(moved, -1, 0), moved)
    return jnp.where(is_last(), edge, moved)


def last_cells(tile, edge):
    lane = iota(tile.shape, 1)
    moved = rolled(tile, 1, 1)
    moved = jnp.where(lane == 0, rolled(moved, 1, 0), moved)
    return jnp.where(is_first(), edge, moved)


def row_of(ref, place):
    return jnp.concatenate([ref[place, line:line + 1] for line in range(TILE)], axis=1)


def nested(flux, index):
    lane, line = index % LANES, index // LANES
    taken = jnp.zeros(index.shape, jnp.float32)
    for source in range(TILE):
        values = jnp.broadcast_to(flux[source:source + 1], index.shape)
        found = jnp.take_along_axis(values, lane, axis=1, mode="promise_in_bounds")
        taken = jnp.where(line == source, found, taken)
    return taken


def strips_kernel(*refs):
    links_ref, mine_ref, other_ref = refs[:3]
    out_ref = refs[-1]
    finer_ref = refs[3] if len(refs) == 5 else None
    patches = mine_ref.shape[0]
    count = 2 * patches
    packets = Packets((mine_ref, other_ref))
    links = links_ref[0]
    lower = [lax.axis_index("sub") == 1 ^ flipped for flipped in range(2)]
    every = [Segment(patch, flipped) for flipped in range(2) for patch in range(patches)]

    def matching(patch, way):
        link = jnp.broadcast_to(links[patch:patch + 1, way:way + 1], (TILE, LANES))
        return [link == other for other in range(patches)]

    norths, wests, easts = [[matching(patch, way) for patch in range(patches)] for way in (0, 2, 3)]

    def picked(matches, values):
        total = jnp.zeros((TILE, LANES), jnp.float32)
        for match, value in zip(matches, values):
            total = jnp.where(match, value, total)
        return total

    strips, inflows = [], []
    for segment in every:
        strip = packets.tile(segment, STRIP)
        if finer_ref is not None:
            place = segment.place(patches)
            gain, index = packets.tile(segment, GAIN) * below_finest(), packets.tile(segment, INDEX).astype(jnp.int32)
            inflow, later = [gain * nested(finer_ref[step * count + place], index) for step in range(2)]
            inflows.append((inflow, later))
            strip = strip + inflow
        strips.append(strip)
    masks = [wet(packets.tile(segment, STRIP_DEPTH)) for segment in every]
    flows = [packets.tile(segment, EDGE_FLOW) for segment in every]
    edges = [wet(packets.tile(segment, EDGE_DEPTH)) for segment in every]
    firsts = [rolled(rolled(strip, -1, 1), -1, 0) for strip in strips]
    last_masks = [rolled(rolled(mask, 1, 1), 1, 0) for mask in masks]
    last_rows = [
        last * (packets.column(segment, LAST_ROW) + courant * rolled(rolled(strip, 1, 1), 1, 0))
        for last, segment, strip in zip(last_masks, every, strips)]
    for place, segment in enumerate(every):
        flipped, patch = segment.flipped, segment.patch
        half = slice(flipped * patches, (flipped + 1) * patches)
        other = slice((1 - flipped) * patches, (2 - flipped) * patches)
        eta, mask, depth = strips[place], masks[place], packets.tile(segment, STRIP_DEPTH)
        edge = picked(easts[patch], firsts[half])
        if finer_ref is None:
            row = jnp.where(is_last(), -courant * mask * edge, 0.0)
        else:
            inflow, later = inflows[place]
            row = courant * mask * (inflow - next_cells(inflow, edge))
        edge = picked(wests[patch], last_rows[half]) - courant * picked(wests[patch], last_masks[half]) * eta
        flow = jnp.where(lower[flipped], flows[other][patch], picked(norths[patch], flows[other]))
        above = jnp.where(lower[flipped], edges[other][patch], picked(norths[patch], edges[other]))
        col = flow - courant * above * eta
        total = packets.tile(segment, STRIP_SUM)
        if finer_ref is None:
            total = total - courant * depth * (row - jnp.where(is_first(), edge, 0.0) - col)
        else:
            total = (total + mask * inflow + later
                     - courant * depth * (row - last_cells(row, edge) + courant * mask * inflow - col))
        out_ref[place] = eta
        out_ref[count + place] = total


def beside(links, packets, own, inflow=None):
    lane = iota((1, LANES), 1)
    first, last = lane == 0, lane == LANES - 1

    def field(segment, column):
        return packets.column(segment, column) if inflow is None else 0.0

    def strip(name, turned):
        return 0.0 if inflow is None else jnp.where(first, rolled(inflow[name], turned, 1), 0.0)

    def corner_col(segment, eta, line, turned):
        north, beyond = links.north(segment)
        mask = rolled(wet(packets.line(north, EDGE_DEPTH, line)), turned, 1)
        flow = rolled(packets.line(north, EDGE_FLOW, line), turned, 1) if inflow is None else 0.0
        return beyond * (flow - courant * mask * eta)

    west, there = links.west(own)
    eta = field(west, LAST_ETA) + strip("west", 1)
    next_eta = field(west, NEXT_ETA) + strip("west", 2)
    own_eta = field(own, FIRST_ETA) + strip("own", 0)
    depth = packets.column(west, LAST_DEPTH) * there
    mask = wet(depth)
    next_row = wet(packets.column(west, NEXT_DEPTH)) * (field(west, NEXT_ROW) - courant * (eta - next_eta))
    below, beyond = links.south(west)
    corner = packets.line(below, STRIP, TILE - 1) if inflow is None else inflow["south west"]
    south_eta = jnp.where(last, corner * beyond, rolled(eta, -1, 1))
    col = mask * (field(west, LAST_COL) - courant * (south_eta - eta))
    north_col = jnp.where(first, corner_col(west, eta, TILE - 1, 1), rolled(col, 1, 1))
    west_row = mask * (field(west, LAST_ROW) - courant * (own_eta - eta))
    west_eta = (mask * eta - courant * depth * (west_row - next_row + col - north_col) + strip("west later", 1))
    west_mask = mask

    east, there = links.east(own)
    eta = there * (field(east, FIRST_ETA) + strip("east", 0))
    second_eta = field(east, SECOND_ETA) + strip("east", -1)
    depth = packets.column(east, FIRST_DEPTH) * there
    mask = wet(depth)
    row = mask * (field(east, FIRST_ROW) - courant * (second_eta - eta))
    below, beyond = links.south(east)
    corner = packets.line(below, STRIP, 0) if inflow is None else inflow["south east"]
    south_eta = jnp.where(last, rolled(corner, -1, 1) * beyond, rolled(eta, -1, 1))
    col = mask * (field(east, FIRST_COL) - courant * (south_eta - eta))
    north_col = jnp.where(first, corner_col(east, eta, 0, 0), rolled(col, 1, 1))
    east_sum = mask * eta - courant * depth * (row + col - north_col) + there * strip("east later", 0)
    return west_row, west_mask, west_eta, eta, east_sum, courant * depth


def advanced(eta, row, col, mask, depth, east, south, west, north):
    row = mask * (row - courant * (east(eta) - eta))
    col = mask * (col - courant * (south(eta) - eta))
    return mask * eta - depth * (row - west(row) + col - north(col)), row, col


def two_steps(start, mask, depth, sides, base, north=None, south=None, second=None):
    lane, line = iota(mask.shape, 1), iota(mask.shape, 0)
    cols = mask.shape[1]
    west_row, west_mask, west_eta, east_eta, east_sum, east_depth = sides
    state = start, 0.0, 0.0
    flow, beyond = west_row, east_eta
    above = 0.0 if north is None else north[0]
    for number in range(2):
        below = 0.0 if south is None else south[number]
        state = advanced(
            *state, mask, depth,
            lambda eta: jnp.where(lane == cols - 1, beyond, rolled(eta, -1, 1)),
            lambda eta: jnp.where(line == TILE - 1, below, rolled(eta, -1, 0)),
            lambda row: jnp.where(lane == 0, flow, rolled(row, 1, 1)),
            lambda col: jnp.where(line == 0, above, rolled(col, 1, 0)))
        if number:
            return state
        eta, row, col = state
        if second is not None:
            eta = eta + jnp.where(line == 0, second, 0.0)
            state = eta, row, col
        whole_eta, whole_row = (eta, row) if base is None else (eta + base[0], row + base[1])
        flow = west_mask * (west_row - courant * (whole_eta[:, :1] - west_eta))
        beyond = east_sum + east_depth * whole_row[:, cols - 1:]
        if north is not None:
            above = north[1] * (north[0] - courant * (whole_eta[:1] - north[2]))


def north_of(links, packets, own, own_strip, inflow=None):
    cols = own_strip.shape[1]
    lane = iota((1, LANES), 1)
    north, there = links.north(own)
    depth = packets.row(north, EDGE_DEPTH) * there
    mask = wet(depth)
    if inflow is not None:
        col = -courant * mask * own_strip
        return col, mask, -courant * depth * col
    col = packets.row(north, EDGE_FLOW) * there - courant * mask * own_strip
    north_east, beyond = links.east(north)
    right_eta = beyond * packets.column(north_east, FIRST_ETA)
    north_west, beyond = links.west(north)
    left_row = beyond * wet(packets.column(north_west, LAST_DEPTH)) * (
        packets.column(north_west, LAST_ROW)
        - courant * (packets.column(north, FIRST_ETA) - packets.column(north_west, LAST_ETA)))
    nothing = jnp.zeros((1, cols - LANES), jnp.float32)
    corners = (jnp.concatenate([jnp.where(lane == 0, rolled(left_row, 1, 1), 0.0), nothing], axis=1)
               + jnp.concatenate([nothing, jnp.where(lane == LANES - 1, courant * right_eta, 0.0)], axis=1))
    return col, mask, packets.row(north, EDGE_SUM) + courant * depth * (corners - col)


def as_sublanes(columns):
    rows = columns[0].shape[1]
    count = -len(columns) % TILE
    turned = jnp.concatenate(list(columns) + [jnp.zeros((count, rows), jnp.float32)], axis=0).T
    return [[turned[low:low + TILE, place:place + 1] for place in range(len(columns))]
            for low in (0, rows - TILE)]


def halo_kernel(links_ref, mine_ref, other_ref, strips_ref, eta_after, momenta_after, wet_after, depth_after,
                eta_ends, row_ends, turned, eta_out, momenta_out, ends_out, sides_new, more_ref, sems):
    rows, cols = eta_after.shape
    fields = eta_after, momenta_after.at[0], momenta_after.at[1]
    outs = eta_out.at[0], momenta_out.at[0, 0], momenta_out.at[1, 0]
    inner, between = pl.ds(TILE, rows - 2 * TILE), pl.ds(LANES, cols - 2 * LANES)
    copies = copied(
        [(field.at[inner, between], out.at[inner, between]) for field, out in zip(fields, outs)], sems.at[0])
    links = Links(links_ref, mine_ref.shape[0])
    own = links.own()
    packets = Packets((mine_ref, other_ref))
    columns = beside(links, packets, own)
    west_row, west_mask, west_eta, east_eta, east_sum, east_depth = columns

    line, lane = iota((TILE, rows), 0), iota((TILE, rows), 1)
    nothing = jnp.zeros((TILE, rows), jnp.float32)

    def column_steps(mask, depth, east, west):
        state = nothing, nothing, nothing
        for number in range(2):
            state = advanced(
                *state, mask, depth,
                lambda eta: jnp.where(line == TILE - 1, east(number, state), rolled(eta, -1, 0)),
                lambda eta: jnp.where(lane == rows - 1, 0.0, rolled(eta, -1, 1)),
                lambda row: jnp.where(line == 0, west(number, state), rolled(row, 1, 0)),
                lambda col: jnp.where(lane == 0, 0.0, rolled(col, 1, 1)))
        return state

    def west_of(number, state):
        if number == 0:
            return west_row
        whole = state[0][:1] + turned[4, :1]
        return west_mask * (west_row - courant * (whole - west_eta))

    def east_of(number, state):
        if number == 0:
            return east_eta
        return east_sum + east_depth * (state[1][TILE - 1:] + turned[5, TILE - 1:])

    left = column_steps(turned[0], turned[1], lambda number, state: 0.0, west_of)
    last = column_steps(turned[2], turned[3], east_of, lambda number, state: 0.0)
    middle = jnp.zeros((LANES - 2 * TILE, rows), jnp.float32)
    body_rows = slice(TILE, rows - TILE)
    inside = iota((rows - 2 * TILE, LANES), 1)
    wides = slice(0, LANES), slice(cols - LANES, cols)
    for place, field in enumerate(fields):
        more_ref[place] = jnp.concatenate([left[place], middle, last[place]], axis=0).T
        more = more_ref[place, body_rows]
        sides_new[0, place] = field[body_rows, wides[0]] + jnp.where(inside < TILE, more, 0.0)
        sides_new[1, place] = field[body_rows, wides[1]] + jnp.where(inside >= LANES - TILE, more, 0.0)
    for side, wide in enumerate(wides):
        copies += copied(
            [(sides_new.at[side, place], out.at[inner, pl.ds(wide.start, LANES)]) for place, out in enumerate(outs)],
            sems.at[1 + side])

    top_sides, low_sides = as_sublanes(columns)
    nothing = jnp.zeros((TILE, cols), jnp.float32)
    end = slice(rows - TILE, rows)
    top = two_steps(
        nothing, wet_after[:TILE], depth_after[:TILE], top_sides, (eta_ends[0], row_ends[0]),
        north=north_of(links, packets, own, packets.row(own, STRIP)))
    below, there = links.south(own)
    low = two_steps(
        nothing, wet_after[end], depth_after[end], low_sides, (eta_ends[1], row_ends[1]),
        south=(packets.row(below, STRIP) * there,
               row_of(strips_ref, 2 * links.patches + below.place(links.patches)) * there))
    line, inside = iota((TILE, cols), 0), iota((TILE, LANES), 1)
    gap = jnp.zeros((TILE, cols - 2 * LANES), jnp.float32)
    for edge, (chunk, near, found) in enumerate(
            ((slice(0, TILE), line < TILE // 2, top), (end, line >= TILE // 2, low))):
        for place in range(3):
            more = more_ref[place, chunk]
            wide = jnp.concatenate(
                [jnp.where(inside < TILE, more, 0.0), gap, jnp.where(inside >= LANES - TILE, more, 0.0)], axis=1)
            ends_out[place, edge] = fields[place][chunk] + jnp.where(near, found[place], wide)
    for copy in copies:
        copy.wait()


def inflow_kernel(links_ref, mine_ref, other_ref, finer_ref, wet_after, depth_after, ends_ref, eta_hbm, momenta_hbm,
                  eta_out, momenta_out, rows_ref, new_ref, sems):
    del eta_hbm, momenta_hbm
    rows, cols = wet_after.shape
    links = Links(links_ref, mine_ref.shape[0])
    patches = links.patches
    own = links.own()
    packets = Packets((mine_ref, other_ref))
    some = below_finest()

    def flux_place(step, segment):
        return step * 2 * patches + segment.place(patches)

    def inflows(segment):
        gain, index = packets.tile(segment, GAIN) * some, packets.tile(segment, INDEX).astype(jnp.int32)
        return [gain * nested(finer_ref[flux_place(step, segment)], index) for step in range(2)]

    below, there = links.south(own)
    west, east = links.west(own)[0], links.east(own)[0]
    below_west, beyond_west = links.west(below)
    below_east, beyond_east = links.east(below)
    wanted = (
        ("west", 0, west, TILE - 1), ("west later", 1, west, TILE - 1), ("east", 0, east, 0),
        ("east later", 1, east, 0), ("south west", 0, links.south(west)[0], TILE - 1),
        ("south east", 0, links.south(east)[0], 0), ("below west", 0, below_west, TILE - 1),
        ("below east", 0, below_east, 0))
    gain = jnp.concatenate([packets.line(segment, GAIN, line) for _, _, segment, line in wanted], axis=0)
    index = jnp.concatenate([packets.line(segment, INDEX, line) for _, _, segment, line in wanted], axis=0)
    index = index.astype(jnp.int32)
    lane, line = index % LANES, index // LANES
    taken = jnp.zeros((TILE, LANES), jnp.float32)
    for source in range(TILE):
        values = jnp.concatenate(
            [finer_ref[flux_place(step, segment), source:source + 1] for _, step, segment, _ in wanted], axis=0)
        found = jnp.take_along_axis(values, lane, axis=1, mode="promise_in_bounds")
        taken = jnp.where(line == source, found, taken)
    taken = some * gain * taken
    inflow = {name: taken[place:place + 1] for place, (name, _, _, _) in enumerate(wanted)}

    rows_ref[0], rows_ref[1] = inflows(own)
    strip, later = inflows(below)
    strip, later = strip * there, later * there
    inflow["own"] = rows_ref[0, :1]

    depth = packets.tile(below, STRIP_DEPTH)
    mask = wet(depth)
    edge = jnp.broadcast_to(rolled(inflow["below east"] * beyond_east, -1, 1), (TILE, LANES))
    row = courant * mask * (strip - next_cells(strip, edge))
    west_mask = rolled(wet(packets.line(below_west, STRIP_DEPTH, TILE - 1)), 1, 1)
    edge = beyond_west * courant * west_mask * (rolled(inflow["below west"], 1, 1) - strip[:1])
    edge = jnp.broadcast_to(edge, (TILE, LANES))
    north, beyond = links.north(below)
    col = -courant * wet(packets.tile(north, EDGE_DEPTH)) * beyond * strip
    rows_ref[2] = strip
    rows_ref[3] = there * (
        mask * strip - courant * depth * (row - last_cells(row, edge) + courant * mask * strip - col) + later)

    columns = beside(links, packets, own, inflow)
    top_sides, low_sides = as_sublanes(columns)
    line = iota((TILE, cols), 0)
    strip = row_of(rows_ref, 0)
    top = two_steps(
        jnp.where(line == 0, strip, 0.0), wet_after[:TILE], depth_after[:TILE], top_sides, None,
        north=north_of(links, packets, own, strip, inflow), second=row_of(rows_ref, 1))
    copies = []
    outs = eta_out.at[0], momenta_out.at[0, 0], momenta_out.at[1, 0]

    def write(end, near, found):
        for place in range(3):
            new_ref[place, end] = ends_ref[place, end] + jnp.where(near, found[place], 0.0)
        here = pl.ds(end * (rows - TILE), TILE)
        copies.extend(copied(
            [(new_ref.at[place, end], out.at[here, :]) for place, out in enumerate(outs)], sems.at[end]))

    write(0, line < TILE // 2, top)
    low = two_steps(
        jnp.zeros((TILE, cols), jnp.float32), wet_after[rows - TILE:], depth_after[rows - TILE:],
        low_sides, None, south=(row_of(rows_ref, 2), row_of(rows_ref, 3)))
    write(1, line >= TILE // 2, low)
    for copy in copies:
        copy.wait()


def body(adjoint_height, adjoint_momenta, depth, wet_mask, adjacency, nest_gain, nest_index):
    rows, cols = adjoint_height.shape[1:]
    levels = lax.axis_size("level")
    patches = lax.axis_size("patch")
    count = 2 * patches
    params = pltpu.CompilerParams(vmem_limit_bytes=VMEM_LIMIT)
    vmem = pl.BlockSpec(memory_space=pltpu.VMEM)
    smem = pl.BlockSpec(memory_space=pltpu.SMEM)
    hbm = pl.BlockSpec(memory_space=pltpu.HBM)

    def array(*shape):
        return jax.ShapeDtypeStruct(shape, jnp.float32)

    def scratch(*shape):
        return pltpu.VMEM(shape, jnp.float32)

    fields = [pltpu.with_memory_space_constraint(field, pltpu.HBM)
              for field in (adjoint_height, adjoint_momenta, depth, wet_mask, nest_gain, nest_index)]
    packed, trimmed = pl.pallas_call(
        pack_kernel,
        out_shape=[array(LINES, LANES), array(TRIMMED, LANES)],
        in_specs=[hbm] * 6,
        out_specs=[vmem, vmem],
        scratch_shapes=[
            scratch(2, 4, TILE, cols), pltpu.VMEM((2, TILE, cols), jnp.int32),
            scratch(2, 4, rows, LANES), pltpu.VMEM((2, rows, LANES), jnp.int32),
            scratch(levels, cols), pltpu.VMEM((levels, cols), jnp.int32),
            pltpu.SemaphoreType.DMA((18,)),
        ],
        compiler_params=params,
        name="pack",
    )(*fields)
    parts = 4
    after = pl.pallas_call(
        bulk_kernel,
        out_shape=[
            array(rows, cols), array(2, rows, cols), array(rows, cols), array(rows, cols),
            array(2, TILE, cols), array(2, TILE, cols), array(6, TILE, rows),
        ],
        in_specs=[hbm] * 4,
        out_specs=[vmem] * 7,
        scratch_shapes=[
            scratch(rows + 2 * TILE, cols), scratch(rows + 2 * TILE, cols),
            scratch(2, rows, cols), scratch(rows, cols), pltpu.VMEM((rows, cols), jnp.int32),
            scratch(rows, LANES), scratch(rows, LANES), pltpu.SemaphoreType.DMA((parts, 4)),
        ],
        compiler_params=params,
        name="bulk",
    )(*fields[:4])

    sent = [packed] + [
        lax.ppermute(trimmed if levels == 2 else packed, "patch",
                     [(source, source ^ turn) for source in range(patches)])
        for turn in range(1, patches)
    ]
    mine = pl.pallas_call(
        gather_kernel,
        out_shape=array(patches, LINES, LANES),
        in_specs=[vmem] * (patches + 1),
        out_specs=vmem,
        compiler_params=params,
        name="gather",
    )(*sent, after[-1])
    other = lax.ppermute(mine, "sub", [(0, 1), (1, 0)])

    flux = ()
    strips = []
    for turn in range(levels - 1):
        strips.append(pl.pallas_call(
            strips_kernel,
            out_shape=array(2 * count, TILE, LANES),
            in_specs=[vmem] * (3 + len(flux)),
            out_specs=vmem,
            compiler_params=params,
            name="strips",
        )(adjacency, mine, other, *flux))
        flux = (lax.ppermute(strips[-1], "level", [(source, (source - 1) % levels) for source in range(levels)]),)

    eta_new, momenta_new, ends = pl.pallas_call(
        halo_kernel,
        out_shape=[array(*adjoint_height.shape), array(*adjoint_momenta.shape), array(3, 2, TILE, cols)],
        in_specs=[smem] + [vmem] * 10,
        out_specs=[hbm, hbm, vmem],
        scratch_shapes=[
            scratch(2, 3, rows - 2 * TILE, LANES), scratch(3, rows, LANES), pltpu.SemaphoreType.DMA((3, 3)),
        ],
        compiler_params=params,
        name="halo",
    )(adjacency, mine, other, strips[0], *after)

    return pl.pallas_call(
        inflow_kernel,
        out_shape=[array(*adjoint_height.shape), array(*adjoint_momenta.shape)],
        in_specs=[smem] + [vmem] * 6 + [hbm] * 2,
        out_specs=[hbm, hbm],
        input_output_aliases={7: 0, 8: 1},
        scratch_shapes=[
            scratch(4, TILE, LANES), scratch(3, 2, TILE, cols), pltpu.SemaphoreType.DMA((2, 3)),
        ],
        compiler_params=params,
        name="inflow",
    )(adjacency, mine, other, *flux, after[2], after[3], ends, eta_new, momenta_new)


def solution(mesh):
    in_specs = (
        P(("parts", "level"), ("patch", "sub"), None),
        P(None, ("parts", "level"), ("patch", "sub"), None),
        P("level", ("patch", "sub"), None),
        P("level", ("patch", "sub"), None),
        P("level", None, None),
        P(None, ("patch", "sub")),
        P(None, ("patch", "sub")),
    )
    out_specs = (
        P(("parts", "level"), ("patch", "sub"), None),
        P(None, ("parts", "level"), ("patch", "sub"), None),
    )
    return jax.shard_map(body, mesh=mesh, in_specs=in_specs, out_specs=out_specs, check_vma=False)
```

```python
import jax
import jax.numpy as jnp
from jax import lax
from jax.experimental import pallas as pl
from jax.experimental.pallas import tpu as pltpu
from jax.sharding import PartitionSpec as P

STEPS = 2
LANES = 128
TILE = 8
VMEM_LIMIT = 48 * 1024 * 1024

courant = 0.45

STRIP_SUM, STRIP, STRIP_DEPTH, GAIN, INDEX, EDGE_FLOW, EDGE_DEPTH, EDGE_SUM = range(8)
(FIRST_ETA, SECOND_ETA, FIRST_ROW, FIRST_COL, FIRST_DEPTH, NEXT_ETA, LAST_ETA, NEXT_ROW,
 LAST_ROW, LAST_COL, NEXT_DEPTH, LAST_DEPTH) = range(12)
ROWS, COLUMNS = 8, 16
LINES = ROWS * TILE + COLUMNS
TRIMMED, SPARE = LINES - 2 * TILE, 4
SAVED = 96


def iota(shape, axis):
    return lax.broadcasted_iota(jnp.int32, shape, axis)


def rolled(value, shift, axis):
    if shift == 0:
        return value
    return pltpu.roll(value, shift % value.shape[axis], axis)


def wet(depth):
    return (depth > 0).astype(jnp.float32)


def copied(pairs, sems):
    copies = [pltpu.make_async_copy(source, target, sems.at[place]) for place, (source, target) in enumerate(pairs)]
    for copy in copies:
        copy.start()
    return copies


def pack_kernel(eta_ref, momenta_ref, depth_ref, wet_ref, gain_ref, index_ref, out_ref, trimmed_ref,
                ends, end_wet, sides, side_wet, gains, indices, sems):
    rows, cols = eta_ref.shape[1:]
    tall, wide = [], []
    for end in range(2):
        here = pl.ds(end * (rows - TILE), TILE)
        tall += [
            (eta_ref.at[0, here, :], ends.at[end, 0]), (momenta_ref.at[:, 0, here, :], ends.at[end, pl.ds(1, 2)]),
            (depth_ref.at[0, here, :], ends.at[end, 3]), (wet_ref.at[0, here, :], end_wet.at[end])]
        here = pl.ds(end * (cols - LANES), LANES)
        wide += [
            (eta_ref.at[0, :, here], sides.at[end, 0]), (momenta_ref.at[:, 0, :, here], sides.at[end, pl.ds(1, 2)]),
            (depth_ref.at[0, :, here], sides.at[end, 3]), (wet_ref.at[0, :, here], side_wet.at[end])]
    tall += [(gain_ref, gains), (index_ref, indices)]
    copies = copied(tall + wide, sems)
    for copy in copies[:len(tall)]:
        copy.wait()
    level = lax.axis_index("level")
    lane = iota((TILE, cols), 1)

    def loaded(end):
        mask = end_wet[end].astype(jnp.float32)
        return ends[end, 0], ends[end, 1], ends[end, 2], mask * ends[end, 3], mask

    def put(row, value):
        for tile in range(TILE):
            out_ref[row * TILE + tile:row * TILE + tile + 1] = value[:, tile * LANES:(tile + 1) * LANES]

    eta, row, col, depth, mask = loaded(0)
    east = jnp.where(lane == cols - 1, 0.0, rolled(eta, -1, 1))
    row = mask * (row - courant * (east - eta))
    west = jnp.where(lane == 0, 0.0, rolled(row, 1, 1))
    col = mask * (col - courant * (rolled(eta, -1, 0) - eta))
    strip_sum = mask * eta - courant * depth * (row - west + col)
    put(STRIP_SUM, strip_sum[:1])
    put(STRIP, eta[:1])
    put(STRIP_DEPTH, depth[:1])
    put(GAIN, gains[pl.ds(level, 1), :])
    put(INDEX, indices[pl.ds(level, 1), :].astype(jnp.float32))

    eta, row, col, depth, mask = loaded(1)
    east = jnp.where(lane == cols - 1, 0.0, rolled(eta, -1, 1))
    row = mask * (row - courant * (east - eta))
    west = jnp.where(lane == 0, 0.0, rolled(row, 1, 1))
    flow = mask * (col + courant * eta)
    above = rolled(flow - courant * mask * rolled(eta, -1, 0), 1, 0)
    edge_sum = mask * eta - courant * depth * (row - west - above)
    put(EDGE_FLOW, flow[TILE - 1:])
    put(EDGE_DEPTH, depth[TILE - 1:])
    put(EDGE_SUM, edge_sum[TILE - 1:])

    for copy in copies[len(tall):]:
        copy.wait()
    lane = iota((rows, LANES), 1)
    columns = jnp.zeros((rows, LANES), jnp.float32)
    depths = [sides[end, 3] * side_wet[end].astype(jnp.float32) for end in range(2)]
    for place, value, at in (
        (FIRST_ETA, sides[0, 0], 0), (SECOND_ETA, sides[0, 0], 1), (FIRST_ROW, sides[0, 1], 0),
        (FIRST_COL, sides[0, 2], 0), (FIRST_DEPTH, depths[0], 0),
        (NEXT_ETA, sides[1, 0], LANES - 2), (LAST_ETA, sides[1, 0], LANES - 1),
        (NEXT_ROW, sides[1, 1], LANES - 2), (LAST_ROW, sides[1, 1], LANES - 1),
        (LAST_COL, sides[1, 2], LANES - 1),
        (NEXT_DEPTH, depths[1], LANES - 2), (LAST_DEPTH, depths[1], LANES - 1),
    ):
        moved = value if place == at else rolled(value, place - at, 1)
        columns = jnp.where(lane == place, moved, columns)
    out_ref[ROWS * TILE:] = columns.T[:COLUMNS]

    def tile(row):
        return out_ref[row * TILE:(row + 1) * TILE]

    tables = sends_tables()
    flow, depth, gain, index = tile(EDGE_FLOW), tile(EDGE_DEPTH), tile(GAIN), tile(INDEX)
    trimmed_ref[:GAIN * TILE] = out_ref[:GAIN * TILE]
    trimmed_ref[GAIN * TILE:INDEX * TILE] = jnp.where(tables, gain, flow)
    trimmed_ref[INDEX * TILE:(INDEX + 1) * TILE] = jnp.where(tables, index, depth)
    trimmed_ref[(INDEX + 1) * TILE:(INDEX + 2) * TILE] = tile(EDGE_SUM)
    trimmed_ref[(INDEX + 2) * TILE:] = out_ref[ROWS * TILE:]
    spare = TRIMMED - SPARE
    for place, (other, own) in enumerate(((flow, gain), (depth, index))):
        chosen = jnp.where(tables, other, own)
        trimmed_ref[spare + 2 * place:spare + 2 * place + 1] = chosen[:1]
        trimmed_ref[spare + 2 * place + 1:spare + 2 * place + 2] = chosen[TILE - 1:]


def bulk_kernel(eta_ref, momenta_ref, depth_ref, wet_ref, eta_after, momenta_after, wet_after, depth_after,
                eta_ends, row_ends, turned, eta_pad, col_pad, momenta_in, depth_in, wet_in, eta_left, row_right, sems):
    rows, cols = eta_ref.shape[1:]
    parts = sems.shape[0]
    size = rows // parts
    loads = []
    for part in range(parts):
        here = pl.ds(part * size, size)
        loads.append(copied([
            (eta_ref.at[0, here, :], eta_pad.at[pl.ds(TILE + part * size, size), :]),
            (momenta_ref.at[:, 0, here, :], momenta_in.at[:, here, :]),
            (depth_ref.at[0, here, :], depth_in.at[here, :]),
            (wet_ref.at[0, here, :], wet_in.at[here, :]),
        ], sems.at[part]))
    lane = iota((TILE, cols), 1)
    eta_pad[TILE + rows:] = jnp.zeros((TILE, cols), jnp.float32)
    col_pad[:TILE] = jnp.zeros((TILE, cols), jnp.float32)

    def step(number, low):
        chunk, padded = slice(low, low + TILE), slice(TILE + low, 2 * TILE + low)
        eta = eta_pad[padded]
        if number == 0:
            mask = wet_in[chunk].astype(jnp.float32)
            depth = courant * mask * depth_in[chunk]
            wet_after[chunk] = mask
            depth_after[chunk] = depth
            row, col = momenta_in[0, chunk], momenta_in[1, chunk]
        else:
            mask, depth = wet_after[chunk], depth_after[chunk]
            row, col = momenta_after[0, chunk], col_pad[padded]
        east = jnp.where(lane == cols - 1, 0.0, rolled(eta, -1, 1))
        south = eta_pad[TILE + low + 1:2 * TILE + low + 1]
        row = mask * (row - courant * (east - eta))
        col = mask * (col - courant * (south - eta))
        momenta_after[0, chunk] = row
        col_pad[padded] = col
        if number:
            momenta_after[1, chunk] = col
        west = jnp.where(lane == 0, 0.0, rolled(row, 1, 1))
        north = col_pad[TILE + low - 1:2 * TILE + low - 1]
        eta = mask * eta - depth * (row - west + (col - north))
        if number:
            eta_after[chunk] = eta
            return
        eta_pad[padded] = eta
        eta_left[chunk] = eta[:, :LANES]
        row_right[chunk] = row[:, cols - LANES:]
        if low in (0, rows - TILE):
            end = int(low > 0)
            eta_ends[end] = eta
            row_ends[end] = row

    for copy in loads[0]:
        copy.wait()
    for part in range(parts + 1):
        if part + 1 < parts:
            for copy in loads[part + 1]:
                copy.wait()
        if part < parts:
            for low in range(part * size, (part + 1) * size, TILE):
                step(0, low)
        if part:
            for low in range((part - 1) * size, part * size, TILE):
                step(1, low)
    right = cols - LANES
    turned[0] = wet_after[:, :LANES].T[:TILE]
    turned[1] = depth_after[:, :LANES].T[:TILE]
    turned[2] = wet_after[:, right:].T[LANES - TILE:]
    turned[3] = depth_after[:, right:].T[LANES - TILE:]
    turned[4] = eta_left[...].T[:TILE]
    turned[5] = row_right[...].T[LANES - TILE:]


def sends_tables():
    return (lax.axis_index("level") == 0) & (lax.axis_index("sub") == 0)


def gather_kernel(*refs):
    first, packets, out_ref = refs[0], refs[1:-2], refs[-1]
    own = lax.axis_index("patch")
    out_ref[own] = first[...]
    tables = sends_tables()
    line = iota((TILE, LANES), 0)

    def ends_of(packet, at):
        value = jnp.where(line == 0, packet[at:at + 1], 0.0)
        return jnp.where(line == TILE - 1, packet[at + 1:at + 2], value)

    for place, packet in enumerate(packets):
        patch = own ^ (len(packets) - place)
        if packet.shape[0] == LINES:
            out_ref[patch] = packet[...]
            continue

        def put(row, value):
            out_ref[patch, row * TILE:(row + 1) * TILE] = value

        out_ref[patch, :GAIN * TILE] = packet[:GAIN * TILE]
        whole = packet[GAIN * TILE:INDEX * TILE], packet[INDEX * TILE:(INDEX + 1) * TILE]
        ends = ends_of(packet, TRIMMED - SPARE), ends_of(packet, TRIMMED - SPARE + 2)
        put(GAIN, jnp.where(tables, whole[0], ends[0]))
        put(INDEX, jnp.where(tables, whole[1], ends[1]))
        put(EDGE_FLOW, jnp.where(tables, ends[0], whole[0]))
        put(EDGE_DEPTH, jnp.where(tables, ends[1], whole[1]))
        put(EDGE_SUM, packet[(INDEX + 1) * TILE:(INDEX + 2) * TILE])
        out_ref[patch, ROWS * TILE:] = packet[(INDEX + 2) * TILE:]


class Segment:
    def __init__(self, patch, flipped):
        self.patch, self.flipped = patch, flipped

    def place(self, patches):
        return self.flipped * patches + self.patch


def below_finest():
    return jnp.where(lax.axis_index("level") < lax.axis_size("level") - 1, 1.0, 0.0)


class Links:
    def __init__(self, links_ref, patches):
        self.links_ref, self.patches = links_ref, patches
        self.half = lax.axis_index("sub")

    def own(self):
        return Segment(lax.axis_index("patch"), 0)

    def all(self):
        return [Segment(patch, flipped) for flipped in range(2) for patch in range(self.patches)]

    def across(self, segment, way):
        patch = self.links_ref[0, segment.patch, way]
        return jnp.maximum(patch, 0), jnp.where(patch >= 0, 1.0, 0.0)

    def other_half(self, segment, way, inner):
        patch, there = self.across(segment, way)
        inside = self.half == (inner ^ segment.flipped)
        return Segment(jnp.where(inside, segment.patch, patch), 1 - segment.flipped), jnp.where(inside, 1.0, there)

    def north(self, segment):
        return self.other_half(segment, 0, 1)

    def south(self, segment):
        return self.other_half(segment, 1, 0)

    def west(self, segment):
        patch, there = self.across(segment, 2)
        return Segment(patch, segment.flipped), there

    def east(self, segment):
        patch, there = self.across(segment, 3)
        return Segment(patch, segment.flipped), there


class Packets:
    def __init__(self, got_refs):
        self.got_refs = got_refs

    def tile(self, segment, row):
        return self.got_refs[segment.flipped][segment.patch, row * TILE:(row + 1) * TILE]

    def line(self, segment, row, line):
        return self.got_refs[segment.flipped][segment.patch, row * TILE + line:row * TILE + line + 1]

    def row(self, segment, row):
        return jnp.concatenate([self.line(segment, row, line) for line in range(TILE)], axis=1)

    def column(self, segment, column):
        return self.line(segment, ROWS, column)


class Saver:
    def __init__(self, ref):
        self.ref, self.count = ref, 0

    def put(self, value):
        self.ref[self.count, :value.shape[0]] = value
        self.count += 1

    def take(self, lines=TILE):
        self.count += 1
        return self.ref[self.count - 1, :lines]


class SavingLinks:
    def __init__(self, links, saver):
        self.links, self.saver = links, saver

    def saved(self, found):
        segment, there = found
        self.saver.put(jnp.full((TILE, LANES), there))
        self.saver.put(jnp.full((TILE, LANES), segment.patch).astype(jnp.float32))
        return found

    def north(self, segment):
        return self.saved(self.links.north(segment))

    def south(self, segment):
        return self.saved(self.links.south(segment))

    def west(self, segment):
        return self.saved(self.links.west(segment))

    def east(self, segment):
        return self.saved(self.links.east(segment))


class SavingPackets(Packets):
    def __init__(self, got_refs, saver):
        self.got_refs, self.saver = got_refs, saver

    def tile(self, segment, row):
        value = Packets.tile(self, segment, row)
        self.saver.put(value)
        return value

    def line(self, segment, row, line):
        value = Packets.line(self, segment, row, line)
        self.saver.put(value)
        return value


class SavedLinks:
    def __init__(self, saver):
        self.saver = saver

    def found(self, flipped):
        there = self.saver.take()[:1, :1]
        return Segment(self.saver.take(), flipped), there

    def north(self, segment):
        return self.found(1 - segment.flipped)

    south = north

    def west(self, segment):
        return self.found(segment.flipped)

    east = west


class SavedPackets(Packets):
    def __init__(self, saver):
        self.saver = saver

    def tile(self, segment, row):
        return self.saver.take()

    def line(self, segment, row, line):
        return self.saver.take(1)


def is_first(shape=(TILE, LANES)):
    return (iota(shape, 0) == 0) & (iota(shape, 1) == 0)


def is_last(shape=(TILE, LANES)):
    return (iota(shape, 0) == shape[0] - 1) & (iota(shape, 1) == shape[1] - 1)


def next_cells(tile, edge):
    lane = iota(tile.shape, 1)
    moved = rolled(tile, -1, 1)
    moved = jnp.where(lane == LANES - 1, rolled(moved, -1, 0), moved)
    return jnp.where(is_last(), edge, moved)


def last_cells(tile, edge):
    lane = iota(tile.shape, 1)
    moved = rolled(tile, 1, 1)
    moved = jnp.where(lane == 0, rolled(moved, 1, 0), moved)
    return jnp.where(is_first(), edge, moved)


def row_of(ref, place):
    return jnp.concatenate([ref[place, line:line + 1] for line in range(TILE)], axis=1)


def nested(flux, index):
    lane, line = index % LANES, index // LANES
    taken = jnp.zeros(index.shape, jnp.float32)
    for source in range(TILE):
        values = jnp.broadcast_to(flux[source:source + 1], index.shape)
        found = jnp.take_along_axis(values, lane, axis=1, mode="promise_in_bounds")
        taken = jnp.where(line == source, found, taken)
    return taken


def strips_kernel(*refs):
    links_ref, mine_ref, other_ref = refs[:3]
    out_ref = refs[-1]
    finer_ref = refs[3] if len(refs) == 5 else None
    patches = mine_ref.shape[0]
    count = 2 * patches
    packets = Packets((mine_ref, other_ref))
    links = links_ref[0]
    lower = [lax.axis_index("sub") == 1 ^ flipped for flipped in range(2)]
    every = [Segment(patch, flipped) for flipped in range(2) for patch in range(patches)]

    def matching(patch, way):
        link = jnp.broadcast_to(links[patch:patch + 1, way:way + 1], (TILE, LANES))
        return [link == other for other in range(patches)]

    norths, wests, easts = [[matching(patch, way) for patch in range(patches)] for way in (0, 2, 3)]

    def picked(matches, values):
        total = jnp.zeros((TILE, LANES), jnp.float32)
        for match, value in zip(matches, values):
            total = jnp.where(match, value, total)
        return total

    strips, inflows = [], []
    for segment in every:
        strip = packets.tile(segment, STRIP)
        if finer_ref is not None:
            place = segment.place(patches)
            gain, index = packets.tile(segment, GAIN) * below_finest(), packets.tile(segment, INDEX).astype(jnp.int32)
            inflow, later = [gain * nested(finer_ref[step * count + place], index) for step in range(2)]
            inflows.append((inflow, later))
            strip = strip + inflow
        strips.append(strip)
    masks = [wet(packets.tile(segment, STRIP_DEPTH)) for segment in every]
    flows = [packets.tile(segment, EDGE_FLOW) for segment in every]
    edges = [wet(packets.tile(segment, EDGE_DEPTH)) for segment in every]
    firsts = [rolled(rolled(strip, -1, 1), -1, 0) for strip in strips]
    last_masks = [rolled(rolled(mask, 1, 1), 1, 0) for mask in masks]
    last_rows = [
        last * (packets.column(segment, LAST_ROW) + courant * rolled(rolled(strip, 1, 1), 1, 0))
        for last, segment, strip in zip(last_masks, every, strips)]
    for place, segment in enumerate(every):
        flipped, patch = segment.flipped, segment.patch
        half = slice(flipped * patches, (flipped + 1) * patches)
        other = slice((1 - flipped) * patches, (2 - flipped) * patches)
        eta, mask, depth = strips[place], masks[place], packets.tile(segment, STRIP_DEPTH)
        edge = picked(easts[patch], firsts[half])
        if finer_ref is None:
            row = jnp.where(is_last(), -courant * mask * edge, 0.0)
        else:
            inflow, later = inflows[place]
            row = courant * mask * (inflow - next_cells(inflow, edge))
        edge = picked(wests[patch], last_rows[half]) - courant * picked(wests[patch], last_masks[half]) * eta
        flow = jnp.where(lower[flipped], flows[other][patch], picked(norths[patch], flows[other]))
        above = jnp.where(lower[flipped], edges[other][patch], picked(norths[patch], edges[other]))
        col = flow - courant * above * eta
        total = packets.tile(segment, STRIP_SUM)
        if finer_ref is None:
            total = total - courant * depth * (row - jnp.where(is_first(), edge, 0.0) - col)
        else:
            total = (total + mask * inflow + later
                     - courant * depth * (row - last_cells(row, edge) + courant * mask * inflow - col))
        out_ref[place] = eta
        out_ref[count + place] = total


def beside(links, packets, own, inflow=None):
    lane = iota((1, LANES), 1)
    first, last = lane == 0, lane == LANES - 1

    def field(segment, column):
        return packets.column(segment, column) if inflow is None else 0.0

    def strip(name, turned):
        return 0.0 if inflow is None else jnp.where(first, rolled(inflow[name], turned, 1), 0.0)

    def corner_col(segment, eta, line, turned):
        north, beyond = links.north(segment)
        mask = rolled(wet(packets.line(north, EDGE_DEPTH, line)), turned, 1)
        flow = rolled(packets.line(north, EDGE_FLOW, line), turned, 1) if inflow is None else 0.0
        return beyond * (flow - courant * mask * eta)

    west, there = links.west(own)
    eta = field(west, LAST_ETA) + strip("west", 1)
    next_eta = field(west, NEXT_ETA) + strip("west", 2)
    own_eta = field(own, FIRST_ETA) + strip("own", 0)
    depth = packets.column(west, LAST_DEPTH) * there
    mask = wet(depth)
    next_row = wet(packets.column(west, NEXT_DEPTH)) * (field(west, NEXT_ROW) - courant * (eta - next_eta))
    below, beyond = links.south(west)
    corner = packets.line(below, STRIP, TILE - 1) if inflow is None else inflow["south west"]
    south_eta = jnp.where(last, corner * beyond, rolled(eta, -1, 1))
    col = mask * (field(west, LAST_COL) - courant * (south_eta - eta))
    north_col = jnp.where(first, corner_col(west, eta, TILE - 1, 1), rolled(col, 1, 1))
    west_row = mask * (field(west, LAST_ROW) - courant * (own_eta - eta))
    west_eta = (mask * eta - courant * depth * (west_row - next_row + col - north_col) + strip("west later", 1))
    west_mask = mask

    east, there = links.east(own)
    eta = there * (field(east, FIRST_ETA) + strip("east", 0))
    second_eta = field(east, SECOND_ETA) + strip("east", -1)
    depth = packets.column(east, FIRST_DEPTH) * there
    mask = wet(depth)
    row = mask * (field(east, FIRST_ROW) - courant * (second_eta - eta))
    below, beyond = links.south(east)
    corner = packets.line(below, STRIP, 0) if inflow is None else inflow["south east"]
    south_eta = jnp.where(last, rolled(corner, -1, 1) * beyond, rolled(eta, -1, 1))
    col = mask * (field(east, FIRST_COL) - courant * (south_eta - eta))
    north_col = jnp.where(first, corner_col(east, eta, 0, 0), rolled(col, 1, 1))
    east_sum = mask * eta - courant * depth * (row + col - north_col) + there * strip("east later", 0)
    return west_row, west_mask, west_eta, eta, east_sum, courant * depth


def advanced(eta, row, col, mask, depth, east, south, west, north):
    row = mask * (row - courant * (east(eta) - eta))
    col = mask * (col - courant * (south(eta) - eta))
    return mask * eta - depth * (row - west(row) + col - north(col)), row, col


def two_steps(start, mask, depth, sides, base, north=None, south=None, second=None):
    lane, line = iota(mask.shape, 1), iota(mask.shape, 0)
    cols = mask.shape[1]
    west_row, west_mask, west_eta, east_eta, east_sum, east_depth = sides
    state = start, 0.0, 0.0
    flow, beyond = west_row, east_eta
    above = 0.0 if north is None else north[0]
    for number in range(2):
        below = 0.0 if south is None else south[number]
        state = advanced(
            *state, mask, depth,
            lambda eta: jnp.where(lane == cols - 1, beyond, rolled(eta, -1, 1)),
            lambda eta: jnp.where(line == TILE - 1, below, rolled(eta, -1, 0)),
            lambda row: jnp.where(lane == 0, flow, rolled(row, 1, 1)),
            lambda col: jnp.where(line == 0, above, rolled(col, 1, 0)))
        if number:
            return state
        eta, row, col = state
        if second is not None:
            eta = eta + jnp.where(line == 0, second, 0.0)
            state = eta, row, col
        whole_eta, whole_row = (eta, row) if base is None else (eta + base[0], row + base[1])
        flow = west_mask * (west_row - courant * (whole_eta[:, :1] - west_eta))
        beyond = east_sum + east_depth * whole_row[:, cols - 1:]
        if north is not None:
            above = north[1] * (north[0] - courant * (whole_eta[:1] - north[2]))


def north_of(links, packets, own, own_strip, inflow=None):
    cols = own_strip.shape[1]
    lane = iota((1, LANES), 1)
    north, there = links.north(own)
    depth = packets.row(north, EDGE_DEPTH) * there
    mask = wet(depth)
    if inflow is not None:
        col = -courant * mask * own_strip
        return col, mask, -courant * depth * col
    col = packets.row(north, EDGE_FLOW) * there - courant * mask * own_strip
    north_east, beyond = links.east(north)
    right_eta = beyond * packets.column(north_east, FIRST_ETA)
    north_west, beyond = links.west(north)
    left_row = beyond * wet(packets.column(north_west, LAST_DEPTH)) * (
        packets.column(north_west, LAST_ROW)
        - courant * (packets.column(north, FIRST_ETA) - packets.column(north_west, LAST_ETA)))
    nothing = jnp.zeros((1, cols - LANES), jnp.float32)
    corners = (jnp.concatenate([jnp.where(lane == 0, rolled(left_row, 1, 1), 0.0), nothing], axis=1)
               + jnp.concatenate([nothing, jnp.where(lane == LANES - 1, courant * right_eta, 0.0)], axis=1))
    return col, mask, packets.row(north, EDGE_SUM) + courant * depth * (corners - col)


def as_sublanes(columns):
    rows = columns[0].shape[1]
    count = -len(columns) % TILE
    turned = jnp.concatenate(list(columns) + [jnp.zeros((count, rows), jnp.float32)], axis=0).T
    return [[turned[low:low + TILE, place:place + 1] for place in range(len(columns))]
            for low in (0, rows - TILE)]


def halo_kernel(links_ref, mine_ref, other_ref, strips_ref, eta_after, momenta_after, wet_after, depth_after,
                eta_ends, row_ends, turned, eta_out, momenta_out, ends_out, saved_ref,
                sides_new, more_ref, rows_ref, sems):
    rows, cols = eta_after.shape
    fields = eta_after, momenta_after.at[0], momenta_after.at[1]
    outs = eta_out.at[0], momenta_out.at[0, 0], momenta_out.at[1, 0]
    inner, between = pl.ds(TILE, rows - 2 * TILE), pl.ds(LANES, cols - 2 * LANES)
    copies = copied(
        [(field.at[inner, between], out.at[inner, between]) for field, out in zip(fields, outs)], sems.at[0])
    links = Links(links_ref, mine_ref.shape[0])
    own = links.own()
    packets = Packets((mine_ref, other_ref))
    columns = beside(links, packets, own)
    west_row, west_mask, west_eta, east_eta, east_sum, east_depth = columns

    line, lane = iota((TILE, rows), 0), iota((TILE, rows), 1)
    nothing = jnp.zeros((TILE, rows), jnp.float32)

    def column_steps(mask, depth, east, west):
        state = nothing, nothing, nothing
        for number in range(2):
            state = advanced(
                *state, mask, depth,
                lambda eta: jnp.where(line == TILE - 1, east(number, state), rolled(eta, -1, 0)),
                lambda eta: jnp.where(lane == rows - 1, 0.0, rolled(eta, -1, 1)),
                lambda row: jnp.where(line == 0, west(number, state), rolled(row, 1, 0)),
                lambda col: jnp.where(lane == 0, 0.0, rolled(col, 1, 1)))
        return state

    def west_of(number, state):
        if number == 0:
            return west_row
        whole = state[0][:1] + turned[4, :1]
        return west_mask * (west_row - courant * (whole - west_eta))

    def east_of(number, state):
        if number == 0:
            return east_eta
        return east_sum + east_depth * (state[1][TILE - 1:] + turned[5, TILE - 1:])

    left = column_steps(turned[0], turned[1], lambda number, state: 0.0, west_of)
    last = column_steps(turned[2], turned[3], east_of, lambda number, state: 0.0)
    middle = jnp.zeros((LANES - 2 * TILE, rows), jnp.float32)
    body_rows = slice(TILE, rows - TILE)
    inside = iota((rows - 2 * TILE, LANES), 1)
    wides = slice(0, LANES), slice(cols - LANES, cols)
    for place, field in enumerate(fields):
        more_ref[place] = jnp.concatenate([left[place], middle, last[place]], axis=0).T
        more = more_ref[place, body_rows]
        sides_new[0, place] = field[body_rows, wides[0]] + jnp.where(inside < TILE, more, 0.0)
        sides_new[1, place] = field[body_rows, wides[1]] + jnp.where(inside >= LANES - TILE, more, 0.0)
    for side, wide in enumerate(wides):
        copies += copied(
            [(sides_new.at[side, place], out.at[inner, pl.ds(wide.start, LANES)]) for place, out in enumerate(outs)],
            sems.at[1 + side])

    top_sides, low_sides = as_sublanes(columns)
    nothing = jnp.zeros((TILE, cols), jnp.float32)
    end = slice(rows - TILE, rows)
    top = two_steps(
        nothing, wet_after[:TILE], depth_after[:TILE], top_sides, (eta_ends[0], row_ends[0]),
        north=north_of(links, packets, own, packets.row(own, STRIP)))
    below, there = links.south(own)
    low = two_steps(
        nothing, wet_after[end], depth_after[end], low_sides, (eta_ends[1], row_ends[1]),
        south=(packets.row(below, STRIP) * there,
               row_of(strips_ref, 2 * links.patches + below.place(links.patches)) * there))
    line, inside = iota((TILE, cols), 0), iota((TILE, LANES), 1)
    gap = jnp.zeros((TILE, cols - 2 * LANES), jnp.float32)
    for edge, (chunk, near, found) in enumerate(
            ((slice(0, TILE), line < TILE // 2, top), (end, line >= TILE // 2, low))):
        for place in range(3):
            more = more_ref[place, chunk]
            wide = jnp.concatenate(
                [jnp.where(inside < TILE, more, 0.0), gap, jnp.where(inside >= LANES - TILE, more, 0.0)], axis=1)
            ends_out[place, edge] = fields[place][chunk] + jnp.where(near, found[place], wide)
    saver = Saver(saved_ref)
    inflow_sides(SavingLinks(links, saver), SavingPackets((mine_ref, other_ref), saver), own,
                 lambda step, segment: jnp.zeros((TILE, LANES), jnp.float32), rows_ref)
    assert saver.count <= SAVED
    for copy in copies:
        copy.wait()


def inflow_sides(links, packets, own, flux_of, rows_ref):
    some = below_finest()

    def inflows(segment):
        gain, index = packets.tile(segment, GAIN) * some, packets.tile(segment, INDEX).astype(jnp.int32)
        return [gain * nested(flux_of(step, segment), index) for step in range(2)]

    below, there = links.south(own)
    west, east = links.west(own)[0], links.east(own)[0]
    below_west, beyond_west = links.west(below)
    below_east, beyond_east = links.east(below)
    wanted = (
        ("west", 0, west, TILE - 1), ("west later", 1, west, TILE - 1), ("east", 0, east, 0),
        ("east later", 1, east, 0), ("south west", 0, links.south(west)[0], TILE - 1),
        ("south east", 0, links.south(east)[0], 0), ("below west", 0, below_west, TILE - 1),
        ("below east", 0, below_east, 0))
    gain = jnp.concatenate([packets.line(segment, GAIN, line) for _, _, segment, line in wanted], axis=0)
    index = jnp.concatenate([packets.line(segment, INDEX, line) for _, _, segment, line in wanted], axis=0)
    index = index.astype(jnp.int32)
    lane, line = index % LANES, index // LANES
    fluxes = [flux_of(step, segment) for _, step, segment, _ in wanted]
    taken = jnp.zeros((TILE, LANES), jnp.float32)
    for source in range(TILE):
        values = jnp.concatenate([tile[source:source + 1] for tile in fluxes], axis=0)
        found = jnp.take_along_axis(values, lane, axis=1, mode="promise_in_bounds")
        taken = jnp.where(line == source, found, taken)
    taken = some * gain * taken
    inflow = {name: taken[place:place + 1] for place, (name, _, _, _) in enumerate(wanted)}

    rows_ref[0], rows_ref[1] = inflows(own)
    strip, later = inflows(below)
    strip, later = strip * there, later * there
    inflow["own"] = rows_ref[0, :1]

    depth = packets.tile(below, STRIP_DEPTH)
    mask = wet(depth)
    edge = jnp.broadcast_to(rolled(inflow["below east"] * beyond_east, -1, 1), (TILE, LANES))
    row = courant * mask * (strip - next_cells(strip, edge))
    west_mask = rolled(wet(packets.line(below_west, STRIP_DEPTH, TILE - 1)), 1, 1)
    edge = beyond_west * courant * west_mask * (rolled(inflow["below west"], 1, 1) - strip[:1])
    edge = jnp.broadcast_to(edge, (TILE, LANES))
    north, beyond = links.north(below)
    col = -courant * wet(packets.tile(north, EDGE_DEPTH)) * beyond * strip
    rows_ref[2] = strip
    rows_ref[3] = there * (
        mask * strip - courant * depth * (row - last_cells(row, edge) + courant * mask * strip - col) + later)

    columns = beside(links, packets, own, inflow)
    return columns, north_of(links, packets, own, row_of(rows_ref, 0), inflow)


def inflow_kernel(mine_ref, finer_ref, saved_ref, wet_after, depth_after, ends_ref, eta_hbm, momenta_hbm,
                  eta_out, momenta_out, rows_ref, new_ref, sems):
    del eta_hbm, momenta_hbm
    rows, cols = wet_after.shape
    patches = mine_ref.shape[0]
    saver = Saver(saved_ref)

    def flux_of(step, segment):
        first = (2 * step + segment.flipped) * patches
        if segment is own:
            return finer_ref[first + own.patch]
        flux = jnp.zeros((TILE, LANES), jnp.float32)
        for patch in range(patches):
            flux = jnp.where(segment.patch == patch, finer_ref[first + patch], flux)
        return flux

    own = Segment(lax.axis_index("patch"), 0)
    columns, north = inflow_sides(SavedLinks(saver), SavedPackets(saver), own, flux_of, rows_ref)
    top_sides, low_sides = as_sublanes(columns)
    line = iota((TILE, cols), 0)
    strip = row_of(rows_ref, 0)
    top = two_steps(
        jnp.where(line == 0, strip, 0.0), wet_after[:TILE], depth_after[:TILE], top_sides, None,
        north=north, second=row_of(rows_ref, 1))
    copies = []
    outs = eta_out.at[0], momenta_out.at[0, 0], momenta_out.at[1, 0]

    def write(end, near, found):
        for place in range(3):
            new_ref[place, end] = ends_ref[place, end] + jnp.where(near, found[place], 0.0)
        here = pl.ds(end * (rows - TILE), TILE)
        copies.extend(copied(
            [(new_ref.at[place, end], out.at[here, :]) for place, out in enumerate(outs)], sems.at[end]))

    write(0, line < TILE // 2, top)
    low = two_steps(
        jnp.zeros((TILE, cols), jnp.float32), wet_after[rows - TILE:], depth_after[rows - TILE:],
        low_sides, None, south=(row_of(rows_ref, 2), row_of(rows_ref, 3)))
    write(1, line >= TILE // 2, low)
    for copy in copies:
        copy.wait()


def body(adjoint_height, adjoint_momenta, depth, wet_mask, adjacency, nest_gain, nest_index):
    rows, cols = adjoint_height.shape[1:]
    levels = lax.axis_size("level")
    patches = lax.axis_size("patch")
    count = 2 * patches
    params = pltpu.CompilerParams(vmem_limit_bytes=VMEM_LIMIT)
    vmem = pl.BlockSpec(memory_space=pltpu.VMEM)
    smem = pl.BlockSpec(memory_space=pltpu.SMEM)
    hbm = pl.BlockSpec(memory_space=pltpu.HBM)

    def array(*shape):
        return jax.ShapeDtypeStruct(shape, jnp.float32)

    def scratch(*shape):
        return pltpu.VMEM(shape, jnp.float32)

    fields = [pltpu.with_memory_space_constraint(field, pltpu.HBM)
              for field in (adjoint_height, adjoint_momenta, depth, wet_mask, nest_gain, nest_index)]
    packed, trimmed = pl.pallas_call(
        pack_kernel,
        out_shape=[array(LINES, LANES), array(TRIMMED, LANES)],
        in_specs=[hbm] * 6,
        out_specs=[vmem, vmem],
        scratch_shapes=[
            scratch(2, 4, TILE, cols), pltpu.VMEM((2, TILE, cols), jnp.int32),
            scratch(2, 4, rows, LANES), pltpu.VMEM((2, rows, LANES), jnp.int32),
            scratch(levels, cols), pltpu.VMEM((levels, cols), jnp.int32),
            pltpu.SemaphoreType.DMA((18,)),
        ],
        compiler_params=params,
        name="pack",
    )(*fields)
    parts = 4
    after = pl.pallas_call(
        bulk_kernel,
        out_shape=[
            array(rows, cols), array(2, rows, cols), array(rows, cols), array(rows, cols),
            array(2, TILE, cols), array(2, TILE, cols), array(6, TILE, rows),
        ],
        in_specs=[hbm] * 4,
        out_specs=[vmem] * 7,
        scratch_shapes=[
            scratch(rows + 2 * TILE, cols), scratch(rows + 2 * TILE, cols),
            scratch(2, rows, cols), scratch(rows, cols), pltpu.VMEM((rows, cols), jnp.int32),
            scratch(rows, LANES), scratch(rows, LANES), pltpu.SemaphoreType.DMA((parts, 4)),
        ],
        compiler_params=params,
        name="bulk",
    )(*fields[:4])

    sent = [packed] + [
        lax.ppermute(trimmed if levels == 2 else packed, "patch",
                     [(source, source ^ turn) for source in range(patches)])
        for turn in range(patches - 1, 0, -1)
    ]
    mine = pl.pallas_call(
        gather_kernel,
        out_shape=array(patches, LINES, LANES),
        in_specs=[vmem] * (patches + 1),
        out_specs=vmem,
        compiler_params=params,
        name="gather",
    )(*sent, after[-1])
    other = lax.ppermute(mine, "sub", [(0, 1), (1, 0)])

    flux = ()
    strips = []
    for turn in range(levels - 1):
        strips.append(pl.pallas_call(
            strips_kernel,
            out_shape=array(2 * count, TILE, LANES),
            in_specs=[vmem] * (3 + len(flux)),
            out_specs=vmem,
            compiler_params=params,
            name="strips",
        )(adjacency, mine, other, *flux))
        flux = (lax.ppermute(strips[-1], "level", [(source, (source - 1) % levels) for source in range(levels)]),)

    eta_new, momenta_new, ends, saved = pl.pallas_call(
        halo_kernel,
        out_shape=[
            array(*adjoint_height.shape), array(*adjoint_momenta.shape), array(3, 2, TILE, cols),
            array(SAVED, TILE, LANES),
        ],
        in_specs=[smem] + [vmem] * 10,
        out_specs=[hbm, hbm, vmem, vmem],
        scratch_shapes=[
            scratch(2, 3, rows - 2 * TILE, LANES), scratch(3, rows, LANES), scratch(4, TILE, LANES),
            pltpu.SemaphoreType.DMA((3, 3)),
        ],
        compiler_params=params,
        name="halo",
    )(adjacency, mine, other, strips[0], *after)

    return pl.pallas_call(
        inflow_kernel,
        out_shape=[array(*adjoint_height.shape), array(*adjoint_momenta.shape)],
        in_specs=[vmem] * 6 + [hbm] * 2,
        out_specs=[hbm, hbm],
        input_output_aliases={6: 0, 7: 1},
        scratch_shapes=[
            scratch(4, TILE, LANES), scratch(3, 2, TILE, cols), pltpu.SemaphoreType.DMA((2, 3)),
        ],
        compiler_params=params,
        name="inflow",
    )(mine, *flux, saved, after[2], after[3], ends, eta_new, momenta_new)


def solution(mesh):
    in_specs = (
        P(("parts", "level"), ("patch", "sub"), None),
        P(None, ("parts", "level"), ("patch", "sub"), None),
        P("level", ("patch", "sub"), None),
        P("level", ("patch", "sub"), None),
        P("level", None, None),
        P(None, ("patch", "sub")),
        P(None, ("patch", "sub")),
    )
    out_specs = (
        P(("parts", "level"), ("patch", "sub"), None),
        P(None, ("parts", "level"), ("patch", "sub"), None),
    )
    return jax.shard_map(body, mesh=mesh, in_specs=in_specs, out_specs=out_specs, check_vma=False)
```

```python
import jax
import jax.numpy as jnp
from jax import lax
from jax.experimental import pallas as pl
from jax.experimental.pallas import tpu as pltpu
from jax.sharding import PartitionSpec as P

STEPS = 2
LANES = 128
TILE = 8
VMEM_LIMIT = 48 * 1024 * 1024

courant = 0.45

STRIP_SUM, STRIP, STRIP_DEPTH, GAIN, INDEX, EDGE_FLOW, EDGE_DEPTH, EDGE_SUM = range(8)
(FIRST_ETA, SECOND_ETA, FIRST_ROW, FIRST_COL, FIRST_DEPTH, NEXT_ETA, LAST_ETA, NEXT_ROW,
 LAST_ROW, LAST_COL, NEXT_DEPTH, LAST_DEPTH) = range(12)
ROWS, COLUMNS = 8, 16
LINES = ROWS * TILE + COLUMNS
TRIMMED, SPARE = LINES - 2 * TILE, 4
SAVED = 96


def iota(shape, axis):
    return lax.broadcasted_iota(jnp.int32, shape, axis)


def rolled(value, shift, axis):
    if shift == 0:
        return value
    return pltpu.roll(value, shift % value.shape[axis], axis)


def wet(depth):
    return (depth > 0).astype(jnp.float32)


def copied(pairs, sems):
    copies = [pltpu.make_async_copy(source, target, sems.at[place]) for place, (source, target) in enumerate(pairs)]
    for place, copy in enumerate(copies):
        copy.start(priority=place % 2)
    return copies


def pack_kernel(eta_ref, momenta_ref, depth_ref, wet_ref, gain_ref, index_ref, out_ref, trimmed_ref,
                ends, end_wet, sides, side_wet, gains, indices, sems):
    rows, cols = eta_ref.shape[1:]
    tall, wide = [], []
    for end in range(2):
        here = pl.ds(end * (rows - TILE), TILE)
        tall += [
            (eta_ref.at[0, here, :], ends.at[end, 0]), (momenta_ref.at[:, 0, here, :], ends.at[end, pl.ds(1, 2)]),
            (depth_ref.at[0, here, :], ends.at[end, 3]), (wet_ref.at[0, here, :], end_wet.at[end])]
        here = pl.ds(end * (cols - LANES), LANES)
        wide += [
            (eta_ref.at[0, :, here], sides.at[end, 0]), (momenta_ref.at[:, 0, :, here], sides.at[end, pl.ds(1, 2)]),
            (depth_ref.at[0, :, here], sides.at[end, 3]), (wet_ref.at[0, :, here], side_wet.at[end])]
    tall += [(gain_ref, gains), (index_ref, indices)]
    copies = copied(tall + wide, sems)
    for copy in copies[:len(tall)]:
        copy.wait()
    level = lax.axis_index("level")
    lane = iota((TILE, cols), 1)

    def loaded(end):
        mask = end_wet[end].astype(jnp.float32)
        return ends[end, 0], ends[end, 1], ends[end, 2], mask * ends[end, 3], mask

    def put(row, value):
        for tile in range(TILE):
            out_ref[row * TILE + tile:row * TILE + tile + 1] = value[:, tile * LANES:(tile + 1) * LANES]

    eta, row, col, depth, mask = loaded(0)
    east = jnp.where(lane == cols - 1, 0.0, rolled(eta, -1, 1))
    row = mask * (row - courant * (east - eta))
    west = jnp.where(lane == 0, 0.0, rolled(row, 1, 1))
    col = mask * (col - courant * (rolled(eta, -1, 0) - eta))
    strip_sum = mask * eta - courant * depth * (row - west + col)
    put(STRIP_SUM, strip_sum[:1])
    put(STRIP, eta[:1])
    put(STRIP_DEPTH, depth[:1])
    put(GAIN, gains[pl.ds(level, 1), :])
    put(INDEX, indices[pl.ds(level, 1), :].astype(jnp.float32))

    eta, row, col, depth, mask = loaded(1)
    east = jnp.where(lane == cols - 1, 0.0, rolled(eta, -1, 1))
    row = mask * (row - courant * (east - eta))
    west = jnp.where(lane == 0, 0.0, rolled(row, 1, 1))
    flow = mask * (col + courant * eta)
    above = rolled(flow - courant * mask * rolled(eta, -1, 0), 1, 0)
    edge_sum = mask * eta - courant * depth * (row - west - above)
    put(EDGE_FLOW, flow[TILE - 1:])
    put(EDGE_DEPTH, depth[TILE - 1:])
    put(EDGE_SUM, edge_sum[TILE - 1:])

    for copy in copies[len(tall):]:
        copy.wait()
    lane = iota((rows, LANES), 1)
    columns = jnp.zeros((rows, LANES), jnp.float32)
    depths = [sides[end, 3] * side_wet[end].astype(jnp.float32) for end in range(2)]
    for place, value, at in (
        (FIRST_ETA, sides[0, 0], 0), (SECOND_ETA, sides[0, 0], 1), (FIRST_ROW, sides[0, 1], 0),
        (FIRST_COL, sides[0, 2], 0), (FIRST_DEPTH, depths[0], 0),
        (NEXT_ETA, sides[1, 0], LANES - 2), (LAST_ETA, sides[1, 0], LANES - 1),
        (NEXT_ROW, sides[1, 1], LANES - 2), (LAST_ROW, sides[1, 1], LANES - 1),
        (LAST_COL, sides[1, 2], LANES - 1),
        (NEXT_DEPTH, depths[1], LANES - 2), (LAST_DEPTH, depths[1], LANES - 1),
    ):
        moved = value if place == at else rolled(value, place - at, 1)
        columns = jnp.where(lane == place, moved, columns)
    out_ref[ROWS * TILE:] = columns.T[:COLUMNS]

    def tile(row):
        return out_ref[row * TILE:(row + 1) * TILE]

    tables = sends_tables()
    flow, depth, gain, index = tile(EDGE_FLOW), tile(EDGE_DEPTH), tile(GAIN), tile(INDEX)
    trimmed_ref[:GAIN * TILE] = out_ref[:GAIN * TILE]
    trimmed_ref[GAIN * TILE:INDEX * TILE] = jnp.where(tables, gain, flow)
    trimmed_ref[INDEX * TILE:(INDEX + 1) * TILE] = jnp.where(tables, index, depth)
    trimmed_ref[(INDEX + 1) * TILE:(INDEX + 2) * TILE] = tile(EDGE_SUM)
    trimmed_ref[(INDEX + 2) * TILE:] = out_ref[ROWS * TILE:]
    spare = TRIMMED - SPARE
    for place, (other, own) in enumerate(((flow, gain), (depth, index))):
        chosen = jnp.where(tables, other, own)
        trimmed_ref[spare + 2 * place:spare + 2 * place + 1] = chosen[:1]
        trimmed_ref[spare + 2 * place + 1:spare + 2 * place + 2] = chosen[TILE - 1:]


def bulk_kernel(eta_ref, momenta_ref, depth_ref, wet_ref, eta_after, momenta_after, wet_after, depth_after,
                eta_ends, row_ends, turned, eta_pad, col_pad, momenta_in, depth_in, wet_in, eta_left, row_right, sems):
    rows, cols = eta_ref.shape[1:]
    parts = sems.shape[0]
    size = rows // parts
    loads = []
    for part in range(parts):
        here = pl.ds(part * size, size)
        loads.append(copied([
            (eta_ref.at[0, here, :], eta_pad.at[pl.ds(TILE + part * size, size), :]),
            (momenta_ref.at[:, 0, here, :], momenta_in.at[:, here, :]),
            (depth_ref.at[0, here, :], depth_in.at[here, :]),
            (wet_ref.at[0, here, :], wet_in.at[here, :]),
        ], sems.at[part]))
    lane = iota((TILE, cols), 1)
    eta_pad[TILE + rows:] = jnp.zeros((TILE, cols), jnp.float32)
    col_pad[:TILE] = jnp.zeros((TILE, cols), jnp.float32)

    def step(number, low):
        chunk, padded = slice(low, low + TILE), slice(TILE + low, 2 * TILE + low)
        eta = eta_pad[padded]
        if number == 0:
            mask = wet_in[chunk].astype(jnp.float32)
            depth = courant * mask * depth_in[chunk]
            wet_after[chunk] = mask
            depth_after[chunk] = depth
            row, col = momenta_in[0, chunk], momenta_in[1, chunk]
        else:
            mask, depth = wet_after[chunk], depth_after[chunk]
            row, col = momenta_after[0, chunk], col_pad[padded]
        east = jnp.where(lane == cols - 1, 0.0, rolled(eta, -1, 1))
        south = eta_pad[TILE + low + 1:2 * TILE + low + 1]
        row = mask * (row - courant * (east - eta))
        col = mask * (col - courant * (south - eta))
        momenta_after[0, chunk] = row
        col_pad[padded] = col
        if number:
            momenta_after[1, chunk] = col
        west = jnp.where(lane == 0, 0.0, rolled(row, 1, 1))
        north = col_pad[TILE + low - 1:2 * TILE + low - 1]
        eta = mask * eta - depth * (row - west + (col - north))
        if number:
            eta_after[chunk] = eta
            return
        eta_pad[padded] = eta
        eta_left[chunk] = eta[:, :LANES]
        row_right[chunk] = row[:, cols - LANES:]
        if low in (0, rows - TILE):
            end = int(low > 0)
            eta_ends[end] = eta
            row_ends[end] = row

    for copy in loads[0]:
        copy.wait()
    for part in range(parts + 1):
        if part + 1 < parts:
            for copy in loads[part + 1]:
                copy.wait()
        if part < parts:
            for low in range(part * size, (part + 1) * size, TILE):
                step(0, low)
        if part:
            for low in range((part - 1) * size, part * size, TILE):
                step(1, low)
    right = cols - LANES
    turned[0] = wet_after[:, :LANES].T[:TILE]
    turned[1] = depth_after[:, :LANES].T[:TILE]
    turned[2] = wet_after[:, right:].T[LANES - TILE:]
    turned[3] = depth_after[:, right:].T[LANES - TILE:]
    turned[4] = eta_left[...].T[:TILE]
    turned[5] = row_right[...].T[LANES - TILE:]


def sends_tables():
    return (lax.axis_index("level") == 0) & (lax.axis_index("sub") == 0)


def gather_kernel(*refs):
    first, packets, out_ref = refs[0], refs[1:-2], refs[-1]
    own = lax.axis_index("patch")
    out_ref[own] = first[...]
    tables = sends_tables()
    line = iota((TILE, LANES), 0)

    def ends_of(packet, at):
        value = jnp.where(line == 0, packet[at:at + 1], 0.0)
        return jnp.where(line == TILE - 1, packet[at + 1:at + 2], value)

    for place, packet in enumerate(packets):
        patch = own ^ (len(packets) - place)
        if packet.shape[0] == LINES:
            out_ref[patch] = packet[...]
            continue

        def put(row, value):
            out_ref[patch, row * TILE:(row + 1) * TILE] = value

        out_ref[patch, :GAIN * TILE] = packet[:GAIN * TILE]
        whole = packet[GAIN * TILE:INDEX * TILE], packet[INDEX * TILE:(INDEX + 1) * TILE]
        ends = ends_of(packet, TRIMMED - SPARE), ends_of(packet, TRIMMED - SPARE + 2)
        put(GAIN, jnp.where(tables, whole[0], ends[0]))
        put(INDEX, jnp.where(tables, whole[1], ends[1]))
        put(EDGE_FLOW, jnp.where(tables, ends[0], whole[0]))
        put(EDGE_DEPTH, jnp.where(tables, ends[1], whole[1]))
        put(EDGE_SUM, packet[(INDEX + 1) * TILE:(INDEX + 2) * TILE])
        out_ref[patch, ROWS * TILE:] = packet[(INDEX + 2) * TILE:]


class Segment:
    def __init__(self, patch, flipped):
        self.patch, self.flipped = patch, flipped

    def place(self, patches):
        return self.flipped * patches + self.patch


def below_finest():
    return jnp.where(lax.axis_index("level") < lax.axis_size("level") - 1, 1.0, 0.0)


class Links:
    def __init__(self, links_ref, patches):
        self.links_ref, self.patches = links_ref, patches
        self.half = lax.axis_index("sub")

    def own(self):
        return Segment(lax.axis_index("patch"), 0)

    def all(self):
        return [Segment(patch, flipped) for flipped in range(2) for patch in range(self.patches)]

    def across(self, segment, way):
        patch = self.links_ref[0, segment.patch, way]
        return jnp.maximum(patch, 0), jnp.where(patch >= 0, 1.0, 0.0)

    def other_half(self, segment, way, inner):
        patch, there = self.across(segment, way)
        inside = self.half == (inner ^ segment.flipped)
        return Segment(jnp.where(inside, segment.patch, patch), 1 - segment.flipped), jnp.where(inside, 1.0, there)

    def north(self, segment):
        return self.other_half(segment, 0, 1)

    def south(self, segment):
        return self.other_half(segment, 1, 0)

    def west(self, segment):
        patch, there = self.across(segment, 2)
        return Segment(patch, segment.flipped), there

    def east(self, segment):
        patch, there = self.across(segment, 3)
        return Segment(patch, segment.flipped), there


class Packets:
    def __init__(self, got_refs):
        self.got_refs = got_refs

    def tile(self, segment, row):
        return self.got_refs[segment.flipped][segment.patch, row * TILE:(row + 1) * TILE]

    def line(self, segment, row, line):
        return self.got_refs[segment.flipped][segment.patch, row * TILE + line:row * TILE + line + 1]

    def row(self, segment, row):
        return jnp.concatenate([self.line(segment, row, line) for line in range(TILE)], axis=1)

    def column(self, segment, column):
        return self.line(segment, ROWS, column)


class Saver:
    def __init__(self, ref):
        self.ref, self.count = ref, 0

    def put(self, value):
        self.ref[self.count, :value.shape[0]] = value
        self.count += 1

    def take(self, lines=TILE):
        self.count += 1
        return self.ref[self.count - 1, :lines]


class SavingLinks:
    def __init__(self, links, saver):
        self.links, self.saver = links, saver

    def saved(self, found):
        segment, there = found
        self.saver.put(jnp.full((TILE, LANES), there))
        self.saver.put(jnp.full((TILE, LANES), segment.patch).astype(jnp.float32))
        return found

    def north(self, segment):
        return self.saved(self.links.north(segment))

    def south(self, segment):
        return self.saved(self.links.south(segment))

    def west(self, segment):
        return self.saved(self.links.west(segment))

    def east(self, segment):
        return self.saved(self.links.east(segment))


class SavingPackets(Packets):
    def __init__(self, got_refs, saver):
        self.got_refs, self.saver = got_refs, saver

    def tile(self, segment, row):
        value = Packets.tile(self, segment, row)
        self.saver.put(value)
        return value

    def line(self, segment, row, line):
        value = Packets.line(self, segment, row, line)
        self.saver.put(value)
        return value


class SavedLinks:
    def __init__(self, saver):
        self.saver = saver

    def found(self, flipped):
        there = self.saver.take()[:1, :1]
        return Segment(self.saver.take(), flipped), there

    def north(self, segment):
        return self.found(1 - segment.flipped)

    south = north

    def west(self, segment):
        return self.found(segment.flipped)

    east = west


class SavedPackets(Packets):
    def __init__(self, saver):
        self.saver = saver

    def tile(self, segment, row):
        return self.saver.take()

    def line(self, segment, row, line):
        return self.saver.take(1)


def is_first(shape=(TILE, LANES)):
    return (iota(shape, 0) == 0) & (iota(shape, 1) == 0)


def is_last(shape=(TILE, LANES)):
    return (iota(shape, 0) == shape[0] - 1) & (iota(shape, 1) == shape[1] - 1)


def next_cells(tile, edge):
    lane = iota(tile.shape, 1)
    moved = rolled(tile, -1, 1)
    moved = jnp.where(lane == LANES - 1, rolled(moved, -1, 0), moved)
    return jnp.where(is_last(), edge, moved)


def last_cells(tile, edge):
    lane = iota(tile.shape, 1)
    moved = rolled(tile, 1, 1)
    moved = jnp.where(lane == 0, rolled(moved, 1, 0), moved)
    return jnp.where(is_first(), edge, moved)


def row_of(ref, place):
    return jnp.concatenate([ref[place, line:line + 1] for line in range(TILE)], axis=1)


def nested(flux, index):
    lane, line = index % LANES, index // LANES
    taken = jnp.zeros(index.shape, jnp.float32)
    for source in range(TILE):
        values = jnp.broadcast_to(flux[source:source + 1], index.shape)
        found = jnp.take_along_axis(values, lane, axis=1, mode="promise_in_bounds")
        taken = jnp.where(line == source, found, taken)
    return taken


def strips_kernel(*refs):
    links_ref, mine_ref, other_ref = refs[:3]
    out_ref = refs[-1]
    finer_ref = refs[3] if len(refs) == 5 else None
    patches = mine_ref.shape[0]
    count = 2 * patches
    packets = Packets((mine_ref, other_ref))
    links = links_ref[0]
    lower = [lax.axis_index("sub") == 1 ^ flipped for flipped in range(2)]
    every = [Segment(patch, flipped) for flipped in range(2) for patch in range(patches)]

    def matching(patch, way):
        link = jnp.broadcast_to(links[patch:patch + 1, way:way + 1], (TILE, LANES))
        return [link == other for other in range(patches)]

    norths, wests, easts = [[matching(patch, way) for patch in range(patches)] for way in (0, 2, 3)]

    def picked(matches, values):
        total = jnp.zeros((TILE, LANES), jnp.float32)
        for match, value in zip(matches, values):
            total = jnp.where(match, value, total)
        return total

    strips, inflows = [], []
    for segment in every:
        strip = packets.tile(segment, STRIP)
        if finer_ref is not None:
            place = segment.place(patches)
            gain, index = packets.tile(segment, GAIN) * below_finest(), packets.tile(segment, INDEX).astype(jnp.int32)
            inflow, later = [gain * nested(finer_ref[step * count + place], index) for step in range(2)]
            inflows.append((inflow, later))
            strip = strip + inflow
        strips.append(strip)
    masks = [wet(packets.tile(segment, STRIP_DEPTH)) for segment in every]
    flows = [packets.tile(segment, EDGE_FLOW) for segment in every]
    edges = [wet(packets.tile(segment, EDGE_DEPTH)) for segment in every]
    firsts = [rolled(rolled(strip, -1, 1), -1, 0) for strip in strips]
    last_masks = [rolled(rolled(mask, 1, 1), 1, 0) for mask in masks]
    last_rows = [
        last * (packets.column(segment, LAST_ROW) + courant * rolled(rolled(strip, 1, 1), 1, 0))
        for last, segment, strip in zip(last_masks, every, strips)]
    for place, segment in enumerate(every):
        flipped, patch = segment.flipped, segment.patch
        half = slice(flipped * patches, (flipped + 1) * patches)
        other = slice((1 - flipped) * patches, (2 - flipped) * patches)
        eta, mask, depth = strips[place], masks[place], packets.tile(segment, STRIP_DEPTH)
        edge = picked(easts[patch], firsts[half])
        if finer_ref is None:
            row = jnp.where(is_last(), -courant * mask * edge, 0.0)
        else:
            inflow, later = inflows[place]
            row = courant * mask * (inflow - next_cells(inflow, edge))
        edge = picked(wests[patch], last_rows[half]) - courant * picked(wests[patch], last_masks[half]) * eta
        flow = jnp.where(lower[flipped], flows[other][patch], picked(norths[patch], flows[other]))
        above = jnp.where(lower[flipped], edges[other][patch], picked(norths[patch], edges[other]))
        col = flow - courant * above * eta
        total = packets.tile(segment, STRIP_SUM)
        if finer_ref is None:
            total = total - courant * depth * (row - jnp.where(is_first(), edge, 0.0) - col)
        else:
            total = (total + mask * inflow + later
                     - courant * depth * (row - last_cells(row, edge) + courant * mask * inflow - col))
        out_ref[place] = eta
        out_ref[count + place] = total


def beside(links, packets, own, inflow=None):
    lane = iota((1, LANES), 1)
    first, last = lane == 0, lane == LANES - 1

    def field(segment, column):
        return packets.column(segment, column) if inflow is None else 0.0

    def strip(name, turned):
        return 0.0 if inflow is None else jnp.where(first, rolled(inflow[name], turned, 1), 0.0)

    def corner_col(segment, eta, line, turned):
        north, beyond = links.north(segment)
        mask = rolled(wet(packets.line(north, EDGE_DEPTH, line)), turned, 1)
        flow = rolled(packets.line(north, EDGE_FLOW, line), turned, 1) if inflow is None else 0.0
        return beyond * (flow - courant * mask * eta)

    west, there = links.west(own)
    eta = field(west, LAST_ETA) + strip("west", 1)
    next_eta = field(west, NEXT_ETA) + strip("west", 2)
    own_eta = field(own, FIRST_ETA) + strip("own", 0)
    depth = packets.column(west, LAST_DEPTH) * there
    mask = wet(depth)
    next_row = wet(packets.column(west, NEXT_DEPTH)) * (field(west, NEXT_ROW) - courant * (eta - next_eta))
    below, beyond = links.south(west)
    corner = packets.line(below, STRIP, TILE - 1) if inflow is None else inflow["south west"]
    south_eta = jnp.where(last, corner * beyond, rolled(eta, -1, 1))
    col = mask * (field(west, LAST_COL) - courant * (south_eta - eta))
    north_col = jnp.where(first, corner_col(west, eta, TILE - 1, 1), rolled(col, 1, 1))
    west_row = mask * (field(west, LAST_ROW) - courant * (own_eta - eta))
    west_eta = (mask * eta - courant * depth * (west_row - next_row + col - north_col) + strip("west later", 1))
    west_mask = mask

    east, there = links.east(own)
    eta = there * (field(east, FIRST_ETA) + strip("east", 0))
    second_eta = field(east, SECOND_ETA) + strip("east", -1)
    depth = packets.column(east, FIRST_DEPTH) * there
    mask = wet(depth)
    row = mask * (field(east, FIRST_ROW) - courant * (second_eta - eta))
    below, beyond = links.south(east)
    corner = packets.line(below, STRIP, 0) if inflow is None else inflow["south east"]
    south_eta = jnp.where(last, rolled(corner, -1, 1) * beyond, rolled(eta, -1, 1))
    col = mask * (field(east, FIRST_COL) - courant * (south_eta - eta))
    north_col = jnp.where(first, corner_col(east, eta, 0, 0), rolled(col, 1, 1))
    east_sum = mask * eta - courant * depth * (row + col - north_col) + there * strip("east later", 0)
    return west_row, west_mask, west_eta, eta, east_sum, courant * depth


def advanced(eta, row, col, mask, depth, east, south, west, north):
    row = mask * (row - courant * (east(eta) - eta))
    col = mask * (col - courant * (south(eta) - eta))
    return mask * eta - depth * (row - west(row) + col - north(col)), row, col


def two_steps(start, mask, depth, sides, base, north=None, south=None, second=None):
    lane, line = iota(mask.shape, 1), iota(mask.shape, 0)
    cols = mask.shape[1]
    west_row, west_mask, west_eta, east_eta, east_sum, east_depth = sides
    state = start, 0.0, 0.0
    flow, beyond = west_row, east_eta
    above = 0.0 if north is None else north[0]
    for number in range(2):
        below = 0.0 if south is None else south[number]
        state = advanced(
            *state, mask, depth,
            lambda eta: jnp.where(lane == cols - 1, beyond, rolled(eta, -1, 1)),
            lambda eta: jnp.where(line == TILE - 1, below, rolled(eta, -1, 0)),
            lambda row: jnp.where(lane == 0, flow, rolled(row, 1, 1)),
            lambda col: jnp.where(line == 0, above, rolled(col, 1, 0)))
        if number:
            return state
        eta, row, col = state
        if second is not None:
            eta = eta + jnp.where(line == 0, second, 0.0)
            state = eta, row, col
        whole_eta, whole_row = (eta, row) if base is None else (eta + base[0], row + base[1])
        flow = west_mask * (west_row - courant * (whole_eta[:, :1] - west_eta))
        beyond = east_sum + east_depth * whole_row[:, cols - 1:]
        if north is not None:
            above = north[1] * (north[0] - courant * (whole_eta[:1] - north[2]))


def north_of(links, packets, own, own_strip, inflow=None):
    cols = own_strip.shape[1]
    lane = iota((1, LANES), 1)
    north, there = links.north(own)
    depth = packets.row(north, EDGE_DEPTH) * there
    mask = wet(depth)
    if inflow is not None:
        col = -courant * mask * own_strip
        return col, mask, -courant * depth * col
    col = packets.row(north, EDGE_FLOW) * there - courant * mask * own_strip
    north_east, beyond = links.east(north)
    right_eta = beyond * packets.column(north_east, FIRST_ETA)
    north_west, beyond = links.west(north)
    left_row = beyond * wet(packets.column(north_west, LAST_DEPTH)) * (
        packets.column(north_west, LAST_ROW)
        - courant * (packets.column(north, FIRST_ETA) - packets.column(north_west, LAST_ETA)))
    nothing = jnp.zeros((1, cols - LANES), jnp.float32)
    corners = (jnp.concatenate([jnp.where(lane == 0, rolled(left_row, 1, 1), 0.0), nothing], axis=1)
               + jnp.concatenate([nothing, jnp.where(lane == LANES - 1, courant * right_eta, 0.0)], axis=1))
    return col, mask, packets.row(north, EDGE_SUM) + courant * depth * (corners - col)


def as_sublanes(columns):
    rows = columns[0].shape[1]
    count = -len(columns) % TILE
    turned = jnp.concatenate(list(columns) + [jnp.zeros((count, rows), jnp.float32)], axis=0).T
    return [[turned[low:low + TILE, place:place + 1] for place in range(len(columns))]
            for low in (0, rows - TILE)]


def halo_kernel(links_ref, mine_ref, other_ref, strips_ref, eta_after, momenta_after, wet_after, depth_after,
                eta_ends, row_ends, turned, eta_out, momenta_out, ends_out, saved_ref,
                sides_new, more_ref, rows_ref, sems):
    rows, cols = eta_after.shape
    fields = eta_after, momenta_after.at[0], momenta_after.at[1]
    outs = eta_out.at[0], momenta_out.at[0, 0], momenta_out.at[1, 0]
    inner, between = pl.ds(TILE, rows - 2 * TILE), pl.ds(LANES, cols - 2 * LANES)
    copies = copied(
        [(field.at[inner, between], out.at[inner, between]) for field, out in zip(fields, outs)], sems.at[0])
    links = Links(links_ref, mine_ref.shape[0])
    own = links.own()
    packets = Packets((mine_ref, other_ref))
    columns = beside(links, packets, own)
    west_row, west_mask, west_eta, east_eta, east_sum, east_depth = columns

    line, lane = iota((TILE, rows), 0), iota((TILE, rows), 1)
    nothing = jnp.zeros((TILE, rows), jnp.float32)

    def column_steps(mask, depth, east, west):
        state = nothing, nothing, nothing
        for number in range(2):
            state = advanced(
                *state, mask, depth,
                lambda eta: jnp.where(line == TILE - 1, east(number, state), rolled(eta, -1, 0)),
                lambda eta: jnp.where(lane == rows - 1, 0.0, rolled(eta, -1, 1)),
                lambda row: jnp.where(line == 0, west(number, state), rolled(row, 1, 0)),
                lambda col: jnp.where(lane == 0, 0.0, rolled(col, 1, 1)))
        return state

    def west_of(number, state):
        if number == 0:
            return west_row
        whole = state[0][:1] + turned[4, :1]
        return west_mask * (west_row - courant * (whole - west_eta))

    def east_of(number, state):
        if number == 0:
            return east_eta
        return east_sum + east_depth * (state[1][TILE - 1:] + turned[5, TILE - 1:])

    left = column_steps(turned[0], turned[1], lambda number, state: 0.0, west_of)
    last = column_steps(turned[2], turned[3], east_of, lambda number, state: 0.0)
    middle = jnp.zeros((LANES - 2 * TILE, rows), jnp.float32)
    body_rows = slice(TILE, rows - TILE)
    inside = iota((rows - 2 * TILE, LANES), 1)
    wides = slice(0, LANES), slice(cols - LANES, cols)
    for place, field in enumerate(fields):
        more_ref[place] = jnp.concatenate([left[place], middle, last[place]], axis=0).T
        more = more_ref[place, body_rows]
        sides_new[0, place] = field[body_rows, wides[0]] + jnp.where(inside < TILE, more, 0.0)
        sides_new[1, place] = field[body_rows, wides[1]] + jnp.where(inside >= LANES - TILE, more, 0.0)
    for side, wide in enumerate(wides):
        copies += copied(
            [(sides_new.at[side, place], out.at[inner, pl.ds(wide.start, LANES)]) for place, out in enumerate(outs)],
            sems.at[1 + side])

    top_sides, low_sides = as_sublanes(columns)
    nothing = jnp.zeros((TILE, cols), jnp.float32)
    end = slice(rows - TILE, rows)
    top = two_steps(
        nothing, wet_after[:TILE], depth_after[:TILE], top_sides, (eta_ends[0], row_ends[0]),
        north=north_of(links, packets, own, packets.row(own, STRIP)))
    below, there = links.south(own)
    low = two_steps(
        nothing, wet_after[end], depth_after[end], low_sides, (eta_ends[1], row_ends[1]),
        south=(packets.row(below, STRIP) * there,
               row_of(strips_ref, 2 * links.patches + below.place(links.patches)) * there))
    line, inside = iota((TILE, cols), 0), iota((TILE, LANES), 1)
    gap = jnp.zeros((TILE, cols - 2 * LANES), jnp.float32)
    for edge, (chunk, near, found) in enumerate(
            ((slice(0, TILE), line < TILE // 2, top), (end, line >= TILE // 2, low))):
        for place in range(3):
            more = more_ref[place, chunk]
            wide = jnp.concatenate(
                [jnp.where(inside < TILE, more, 0.0), gap, jnp.where(inside >= LANES - TILE, more, 0.0)], axis=1)
            ends_out[place, edge] = fields[place][chunk] + jnp.where(near, found[place], wide)
    saver = Saver(saved_ref)
    inflow_sides(SavingLinks(links, saver), SavingPackets((mine_ref, other_ref), saver), own,
                 lambda step, segment: jnp.zeros((TILE, LANES), jnp.float32), rows_ref)
    assert saver.count <= SAVED
    for copy in copies:
        copy.wait()


def inflow_sides(links, packets, own, flux_of, rows_ref):
    some = below_finest()

    def inflows(segment):
        gain, index = packets.tile(segment, GAIN) * some, packets.tile(segment, INDEX).astype(jnp.int32)
        return [gain * nested(flux_of(step, segment), index) for step in range(2)]

    below, there = links.south(own)
    west, east = links.west(own)[0], links.east(own)[0]
    below_west, beyond_west = links.west(below)
    below_east, beyond_east = links.east(below)
    wanted = (
        ("west", 0, west, TILE - 1), ("west later", 1, west, TILE - 1), ("east", 0, east, 0),
        ("east later", 1, east, 0), ("south west", 0, links.south(west)[0], TILE - 1),
        ("south east", 0, links.south(east)[0], 0), ("below west", 0, below_west, TILE - 1),
        ("below east", 0, below_east, 0))
    gain = jnp.concatenate([packets.line(segment, GAIN, line) for _, _, segment, line in wanted], axis=0)
    index = jnp.concatenate([packets.line(segment, INDEX, line) for _, _, segment, line in wanted], axis=0)
    index = index.astype(jnp.int32)
    lane, line = index % LANES, index // LANES
    fluxes = [flux_of(step, segment) for _, step, segment, _ in wanted]
    taken = jnp.zeros((TILE, LANES), jnp.float32)
    for source in range(TILE):
        values = jnp.concatenate([tile[source:source + 1] for tile in fluxes], axis=0)
        found = jnp.take_along_axis(values, lane, axis=1, mode="promise_in_bounds")
        taken = jnp.where(line == source, found, taken)
    taken = some * gain * taken
    inflow = {name: taken[place:place + 1] for place, (name, _, _, _) in enumerate(wanted)}

    rows_ref[0], rows_ref[1] = inflows(own)
    strip, later = inflows(below)
    strip, later = strip * there, later * there
    inflow["own"] = rows_ref[0, :1]

    depth = packets.tile(below, STRIP_DEPTH)
    mask = wet(depth)
    edge = jnp.broadcast_to(rolled(inflow["below east"] * beyond_east, -1, 1), (TILE, LANES))
    row = courant * mask * (strip - next_cells(strip, edge))
    west_mask = rolled(wet(packets.line(below_west, STRIP_DEPTH, TILE - 1)), 1, 1)
    edge = beyond_west * courant * west_mask * (rolled(inflow["below west"], 1, 1) - strip[:1])
    edge = jnp.broadcast_to(edge, (TILE, LANES))
    north, beyond = links.north(below)
    col = -courant * wet(packets.tile(north, EDGE_DEPTH)) * beyond * strip
    rows_ref[2] = strip
    rows_ref[3] = there * (
        mask * strip - courant * depth * (row - last_cells(row, edge) + courant * mask * strip - col) + later)

    columns = beside(links, packets, own, inflow)
    return columns, north_of(links, packets, own, row_of(rows_ref, 0), inflow)


def inflow_kernel(mine_ref, finer_ref, saved_ref, wet_after, depth_after, ends_ref, eta_hbm, momenta_hbm,
                  eta_out, momenta_out, rows_ref, new_ref, sems):
    del eta_hbm, momenta_hbm
    rows, cols = wet_after.shape
    patches = mine_ref.shape[0]
    saver = Saver(saved_ref)

    def flux_of(step, segment):
        first = (2 * step + segment.flipped) * patches
        if segment is own:
            return finer_ref[first + own.patch]
        flux = jnp.zeros((TILE, LANES), jnp.float32)
        for patch in range(patches):
            flux = jnp.where(segment.patch == patch, finer_ref[first + patch], flux)
        return flux

    own = Segment(lax.axis_index("patch"), 0)
    columns, north = inflow_sides(SavedLinks(saver), SavedPackets(saver), own, flux_of, rows_ref)
    top_sides, low_sides = as_sublanes(columns)
    line = iota((TILE, cols), 0)
    strip = row_of(rows_ref, 0)
    top = two_steps(
        jnp.where(line == 0, strip, 0.0), wet_after[:TILE], depth_after[:TILE], top_sides, None,
        north=north, second=row_of(rows_ref, 1))
    copies = []
    outs = eta_out.at[0], momenta_out.at[0, 0], momenta_out.at[1, 0]

    def write(end, near, found):
        for place in range(3):
            new_ref[place, end] = ends_ref[place, end] + jnp.where(near, found[place], 0.0)
        here = pl.ds(end * (rows - TILE), TILE)
        copies.extend(copied(
            [(new_ref.at[place, end], out.at[here, :]) for place, out in enumerate(outs)], sems.at[end]))

    write(0, line < TILE // 2, top)
    low = two_steps(
        jnp.zeros((TILE, cols), jnp.float32), wet_after[rows - TILE:], depth_after[rows - TILE:],
        low_sides, None, south=(row_of(rows_ref, 2), row_of(rows_ref, 3)))
    write(1, line >= TILE // 2, low)
    for copy in copies:
        copy.wait()


def body(adjoint_height, adjoint_momenta, depth, wet_mask, adjacency, nest_gain, nest_index):
    rows, cols = adjoint_height.shape[1:]
    levels = lax.axis_size("level")
    patches = lax.axis_size("patch")
    count = 2 * patches
    params = pltpu.CompilerParams(vmem_limit_bytes=VMEM_LIMIT)
    vmem = pl.BlockSpec(memory_space=pltpu.VMEM)
    smem = pl.BlockSpec(memory_space=pltpu.SMEM)
    hbm = pl.BlockSpec(memory_space=pltpu.HBM)

    def array(*shape):
        return jax.ShapeDtypeStruct(shape, jnp.float32)

    def scratch(*shape):
        return pltpu.VMEM(shape, jnp.float32)

    fields = [pltpu.with_memory_space_constraint(field, pltpu.HBM)
              for field in (adjoint_height, adjoint_momenta, depth, wet_mask, nest_gain, nest_index)]
    packed, trimmed = pl.pallas_call(
        pack_kernel,
        out_shape=[array(LINES, LANES), array(TRIMMED, LANES)],
        in_specs=[hbm] * 6,
        out_specs=[vmem, vmem],
        scratch_shapes=[
            scratch(2, 4, TILE, cols), pltpu.VMEM((2, TILE, cols), jnp.int32),
            scratch(2, 4, rows, LANES), pltpu.VMEM((2, rows, LANES), jnp.int32),
            scratch(levels, cols), pltpu.VMEM((levels, cols), jnp.int32),
            pltpu.SemaphoreType.DMA((18,)),
        ],
        compiler_params=params,
        name="pack",
    )(*fields)
    parts = 4
    after = pl.pallas_call(
        bulk_kernel,
        out_shape=[
            array(rows, cols), array(2, rows, cols), array(rows, cols), array(rows, cols),
            array(2, TILE, cols), array(2, TILE, cols), array(6, TILE, rows),
        ],
        in_specs=[hbm] * 4,
        out_specs=[vmem] * 7,
        scratch_shapes=[
            scratch(rows + 2 * TILE, cols), scratch(rows + 2 * TILE, cols),
            scratch(2, rows, cols), scratch(rows, cols), pltpu.VMEM((rows, cols), jnp.int32),
            scratch(rows, LANES), scratch(rows, LANES), pltpu.SemaphoreType.DMA((parts, 4)),
        ],
        compiler_params=params,
        name="bulk",
    )(*fields[:4])

    sent = [packed] + [
        lax.ppermute(trimmed if levels == 2 else packed, "patch",
                     [(source, source ^ turn) for source in range(patches)])
        for turn in range(patches - 1, 0, -1)
    ]
    mine = pl.pallas_call(
        gather_kernel,
        out_shape=array(patches, LINES, LANES),
        in_specs=[vmem] * (patches + 1),
        out_specs=vmem,
        compiler_params=params,
        name="gather",
    )(*sent, after[-1])
    other = lax.ppermute(mine, "sub", [(0, 1), (1, 0)])

    flux = ()
    strips = []
    for turn in range(levels - 1):
        strips.append(pl.pallas_call(
            strips_kernel,
            out_shape=array(2 * count, TILE, LANES),
            in_specs=[vmem] * (3 + len(flux)),
            out_specs=vmem,
            compiler_params=params,
            name="strips",
        )(adjacency, mine, other, *flux))
        flux = (lax.ppermute(strips[-1], "level", [(source, (source - 1) % levels) for source in range(levels)]),)

    eta_new, momenta_new, ends, saved = pl.pallas_call(
        halo_kernel,
        out_shape=[
            array(*adjoint_height.shape), array(*adjoint_momenta.shape), array(3, 2, TILE, cols),
            array(SAVED, TILE, LANES),
        ],
        in_specs=[smem] + [vmem] * 10,
        out_specs=[hbm, hbm, vmem, vmem],
        scratch_shapes=[
            scratch(2, 3, rows - 2 * TILE, LANES), scratch(3, rows, LANES), scratch(4, TILE, LANES),
            pltpu.SemaphoreType.DMA((3, 3)),
        ],
        compiler_params=params,
        name="halo",
    )(adjacency, mine, other, strips[0], *after)

    return pl.pallas_call(
        inflow_kernel,
        out_shape=[array(*adjoint_height.shape), array(*adjoint_momenta.shape)],
        in_specs=[vmem] * 6 + [hbm] * 2,
        out_specs=[hbm, hbm],
        input_output_aliases={6: 0, 7: 1},
        scratch_shapes=[
            scratch(4, TILE, LANES), scratch(3, 2, TILE, cols), pltpu.SemaphoreType.DMA((2, 3)),
        ],
        compiler_params=params,
        name="inflow",
    )(mine, *flux, saved, after[2], after[3], ends, eta_new, momenta_new)


def solution(mesh):
    in_specs = (
        P(("parts", "level"), ("patch", "sub"), None),
        P(None, ("parts", "level"), ("patch", "sub"), None),
        P("level", ("patch", "sub"), None),
        P("level", ("patch", "sub"), None),
        P("level", None, None),
        P(None, ("patch", "sub")),
        P(None, ("patch", "sub")),
    )
    out_specs = (
        P(("parts", "level"), ("patch", "sub"), None),
        P(None, ("parts", "level"), ("patch", "sub"), None),
    )
    return jax.shard_map(body, mesh=mesh, in_specs=in_specs, out_specs=out_specs, check_vma=False)
```

```python
import jax
import jax.numpy as jnp
from jax import lax
from jax.experimental import pallas as pl
from jax.experimental.pallas import tpu as pltpu
from jax.sharding import PartitionSpec as P

STEPS = 2
LANES = 128
TILE = 8
VMEM_LIMIT = 48 * 1024 * 1024

courant = 0.45

STRIP_SUM, STRIP, STRIP_DEPTH, GAIN, INDEX, EDGE_FLOW, EDGE_DEPTH, EDGE_SUM = range(8)
(FIRST_ETA, SECOND_ETA, FIRST_ROW, FIRST_COL, FIRST_DEPTH, NEXT_ETA, LAST_ETA, NEXT_ROW,
 LAST_ROW, LAST_COL, NEXT_DEPTH, LAST_DEPTH) = range(12)
ROWS, COLUMNS = 8, 16
LINES = ROWS * TILE + COLUMNS
TRIMMED, SPARE = LINES - 2 * TILE, 4
SAVED = 96


def iota(shape, axis):
    return lax.broadcasted_iota(jnp.int32, shape, axis)


def rolled(value, shift, axis):
    if shift == 0:
        return value
    return pltpu.roll(value, shift % value.shape[axis], axis)


def wet(depth):
    return (depth > 0).astype(jnp.float32)


def copied(pairs, sems):
    copies = [pltpu.make_async_copy(source, target, sems.at[place]) for place, (source, target) in enumerate(pairs)]
    for copy in copies:
        copy.start()
    return copies


def pack_kernel(eta_ref, momenta_ref, depth_ref, wet_ref, gain_ref, index_ref, out_ref, trimmed_ref,
                ends, end_wet, sides, side_wet, gains, indices, sems):
    rows, cols = eta_ref.shape[1:]
    tall, wide = [], []
    for end in range(2):
        here = pl.ds(end * (rows - TILE), TILE)
        tall += [
            (eta_ref.at[0, here, :], ends.at[end, 0]), (momenta_ref.at[:, 0, here, :], ends.at[end, pl.ds(1, 2)]),
            (depth_ref.at[0, here, :], ends.at[end, 3]), (wet_ref.at[0, here, :], end_wet.at[end])]
        here = pl.ds(end * (cols - LANES), LANES)
        wide += [
            (eta_ref.at[0, :, here], sides.at[end, 0]), (momenta_ref.at[:, 0, :, here], sides.at[end, pl.ds(1, 2)]),
            (depth_ref.at[0, :, here], sides.at[end, 3]), (wet_ref.at[0, :, here], side_wet.at[end])]
    tall += [(gain_ref, gains), (index_ref, indices)]
    copies = copied(tall + wide, sems)
    for copy in copies[:len(tall)]:
        copy.wait()
    level = lax.axis_index("level")
    lane = iota((TILE, cols), 1)

    def loaded(end):
        mask = end_wet[end].astype(jnp.float32)
        return ends[end, 0], ends[end, 1], ends[end, 2], mask * ends[end, 3], mask

    def put(row, value):
        for tile in range(TILE):
            out_ref[row * TILE + tile:row * TILE + tile + 1] = value[:, tile * LANES:(tile + 1) * LANES]

    eta, row, col, depth, mask = loaded(0)
    east = jnp.where(lane == cols - 1, 0.0, rolled(eta, -1, 1))
    row = mask * (row - courant * (east - eta))
    west = jnp.where(lane == 0, 0.0, rolled(row, 1, 1))
    col = mask * (col - courant * (rolled(eta, -1, 0) - eta))
    strip_sum = mask * eta - courant * depth * (row - west + col)
    put(STRIP_SUM, strip_sum[:1])
    put(STRIP, eta[:1])
    put(STRIP_DEPTH, depth[:1])
    put(GAIN, gains[pl.ds(level, 1), :])
    put(INDEX, indices[pl.ds(level, 1), :].astype(jnp.float32))

    eta, row, col, depth, mask = loaded(1)
    east = jnp.where(lane == cols - 1, 0.0, rolled(eta, -1, 1))
    row = mask * (row - courant * (east - eta))
    west = jnp.where(lane == 0, 0.0, rolled(row, 1, 1))
    flow = mask * (col + courant * eta)
    above = rolled(flow - courant * mask * rolled(eta, -1, 0), 1, 0)
    edge_sum = mask * eta - courant * depth * (row - west - above)
    put(EDGE_FLOW, flow[TILE - 1:])
    put(EDGE_DEPTH, depth[TILE - 1:])
    put(EDGE_SUM, edge_sum[TILE - 1:])

    for copy in copies[len(tall):]:
        copy.wait()
    lane = iota((rows, LANES), 1)
    columns = jnp.zeros((rows, LANES), jnp.float32)
    depths = [sides[end, 3] * side_wet[end].astype(jnp.float32) for end in range(2)]
    for place, value, at in (
        (FIRST_ETA, sides[0, 0], 0), (SECOND_ETA, sides[0, 0], 1), (FIRST_ROW, sides[0, 1], 0),
        (FIRST_COL, sides[0, 2], 0), (FIRST_DEPTH, depths[0], 0),
        (NEXT_ETA, sides[1, 0], LANES - 2), (LAST_ETA, sides[1, 0], LANES - 1),
        (NEXT_ROW, sides[1, 1], LANES - 2), (LAST_ROW, sides[1, 1], LANES - 1),
        (LAST_COL, sides[1, 2], LANES - 1),
        (NEXT_DEPTH, depths[1], LANES - 2), (LAST_DEPTH, depths[1], LANES - 1),
    ):
        moved = value if place == at else rolled(value, place - at, 1)
        columns = jnp.where(lane == place, moved, columns)
    out_ref[ROWS * TILE:] = columns.T[:COLUMNS]

    def tile(row):
        return out_ref[row * TILE:(row + 1) * TILE]

    tables = sends_tables()
    flow, depth, gain, index = tile(EDGE_FLOW), tile(EDGE_DEPTH), tile(GAIN), tile(INDEX)
    trimmed_ref[:GAIN * TILE] = out_ref[:GAIN * TILE]
    trimmed_ref[GAIN * TILE:INDEX * TILE] = jnp.where(tables, gain, flow)
    trimmed_ref[INDEX * TILE:(INDEX + 1) * TILE] = jnp.where(tables, index, depth)
    trimmed_ref[(INDEX + 1) * TILE:(INDEX + 2) * TILE] = tile(EDGE_SUM)
    trimmed_ref[(INDEX + 2) * TILE:] = out_ref[ROWS * TILE:]
    spare = TRIMMED - SPARE
    for place, (other, own) in enumerate(((flow, gain), (depth, index))):
        chosen = jnp.where(tables, other, own)
        trimmed_ref[spare + 2 * place:spare + 2 * place + 1] = chosen[:1]
        trimmed_ref[spare + 2 * place + 1:spare + 2 * place + 2] = chosen[TILE - 1:]


def bulk_kernel(eta_ref, momenta_ref, depth_ref, wet_ref, eta_after, momenta_after, wet_after, depth_after,
                eta_ends, row_ends, turned, eta_pad, col_pad, momenta_in, depth_in, wet_in, eta_left, row_right, sems):
    rows, cols = eta_ref.shape[1:]
    parts = sems.shape[0]
    size = rows // parts
    loads = []
    for part in range(parts):
        here = pl.ds(part * size, size)
        loads.append(copied([
            (eta_ref.at[0, here, :], eta_pad.at[pl.ds(TILE + part * size, size), :]),
            (momenta_ref.at[:, 0, here, :], momenta_in.at[:, here, :]),
            (depth_ref.at[0, here, :], depth_in.at[here, :]),
            (wet_ref.at[0, here, :], wet_in.at[here, :]),
        ], sems.at[part]))
    lane = iota((TILE, cols), 1)
    eta_pad[TILE + rows:] = jnp.zeros((TILE, cols), jnp.float32)
    col_pad[:TILE] = jnp.zeros((TILE, cols), jnp.float32)

    def step(number, low):
        chunk, padded = slice(low, low + TILE), slice(TILE + low, 2 * TILE + low)
        eta = eta_pad[padded]
        if number == 0:
            mask = wet_in[chunk].astype(jnp.float32)
            depth = courant * mask * depth_in[chunk]
            wet_after[chunk] = mask
            depth_after[chunk] = depth
            row, col = momenta_in[0, chunk], momenta_in[1, chunk]
        else:
            mask, depth = wet_after[chunk], depth_after[chunk]
            row, col = momenta_after[0, chunk], col_pad[padded]
        east = jnp.where(lane == cols - 1, 0.0, rolled(eta, -1, 1))
        south = eta_pad[TILE + low + 1:2 * TILE + low + 1]
        row = mask * (row - courant * (east - eta))
        col = mask * (col - courant * (south - eta))
        momenta_after[0, chunk] = row
        col_pad[padded] = col
        if number:
            momenta_after[1, chunk] = col
        west = jnp.where(lane == 0, 0.0, rolled(row, 1, 1))
        north = col_pad[TILE + low - 1:2 * TILE + low - 1]
        eta = mask * eta - depth * (row - west + (col - north))
        if number:
            eta_after[chunk] = eta
            return
        eta_pad[padded] = eta
        eta_left[chunk] = eta[:, :LANES]
        row_right[chunk] = row[:, cols - LANES:]
        if low in (0, rows - TILE):
            end = int(low > 0)
            eta_ends[end] = eta
            row_ends[end] = row

    for copy in loads[0]:
        copy.wait()
    for part in range(parts + 1):
        if part + 1 < parts:
            for copy in loads[part + 1]:
                copy.wait()
        if part < parts:
            for low in range(part * size, (part + 1) * size, TILE):
                step(0, low)
        if part:
            for low in range((part - 1) * size, part * size, TILE):
                step(1, low)
    right = cols - LANES
    turned[0] = wet_after[:, :LANES].T[:TILE]
    turned[1] = depth_after[:, :LANES].T[:TILE]
    turned[2] = wet_after[:, right:].T[LANES - TILE:]
    turned[3] = depth_after[:, right:].T[LANES - TILE:]
    turned[4] = eta_left[...].T[:TILE]
    turned[5] = row_right[...].T[LANES - TILE:]


def sends_tables():
    return (lax.axis_index("level") == 0) & (lax.axis_index("sub") == 0)


def send_order(patches):
    return sorted(range(1, patches), key=lambda turn: (turn < patches // 2, turn))


def gather_kernel(*refs):
    first, packets, out_ref = refs[0], refs[1:-2], refs[-1]
    own = lax.axis_index("patch")
    out_ref[own] = first[...]
    tables = sends_tables()
    line = iota((TILE, LANES), 0)

    def ends_of(packet, at):
        value = jnp.where(line == 0, packet[at:at + 1], 0.0)
        return jnp.where(line == TILE - 1, packet[at + 1:at + 2], value)

    for place, packet in enumerate(packets):
        patch = own ^ send_order(len(packets) + 1)[place]
        if packet.shape[0] == LINES:
            out_ref[patch] = packet[...]
            continue

        def put(row, value):
            out_ref[patch, row * TILE:(row + 1) * TILE] = value

        out_ref[patch, :GAIN * TILE] = packet[:GAIN * TILE]
        whole = packet[GAIN * TILE:INDEX * TILE], packet[INDEX * TILE:(INDEX + 1) * TILE]
        ends = ends_of(packet, TRIMMED - SPARE), ends_of(packet, TRIMMED - SPARE + 2)
        put(GAIN, jnp.where(tables, whole[0], ends[0]))
        put(INDEX, jnp.where(tables, whole[1], ends[1]))
        put(EDGE_FLOW, jnp.where(tables, ends[0], whole[0]))
        put(EDGE_DEPTH, jnp.where(tables, ends[1], whole[1]))
        put(EDGE_SUM, packet[(INDEX + 1) * TILE:(INDEX + 2) * TILE])
        out_ref[patch, ROWS * TILE:] = packet[(INDEX + 2) * TILE:]


class Segment:
    def __init__(self, patch, flipped):
        self.patch, self.flipped = patch, flipped

    def place(self, patches):
        return self.flipped * patches + self.patch


def below_finest():
    return jnp.where(lax.axis_index("level") < lax.axis_size("level") - 1, 1.0, 0.0)


class Links:
    def __init__(self, links_ref, patches):
        self.links_ref, self.patches = links_ref, patches
        self.half = lax.axis_index("sub")

    def own(self):
        return Segment(lax.axis_index("patch"), 0)

    def all(self):
        return [Segment(patch, flipped) for flipped in range(2) for patch in range(self.patches)]

    def across(self, segment, way):
        patch = self.links_ref[0, segment.patch, way]
        return jnp.maximum(patch, 0), jnp.where(patch >= 0, 1.0, 0.0)

    def other_half(self, segment, way, inner):
        patch, there = self.across(segment, way)
        inside = self.half == (inner ^ segment.flipped)
        return Segment(jnp.where(inside, segment.patch, patch), 1 - segment.flipped), jnp.where(inside, 1.0, there)

    def north(self, segment):
        return self.other_half(segment, 0, 1)

    def south(self, segment):
        return self.other_half(segment, 1, 0)

    def west(self, segment):
        patch, there = self.across(segment, 2)
        return Segment(patch, segment.flipped), there

    def east(self, segment):
        patch, there = self.across(segment, 3)
        return Segment(patch, segment.flipped), there


class Packets:
    def __init__(self, got_refs):
        self.got_refs = got_refs

    def tile(self, segment, row):
        return self.got_refs[segment.flipped][segment.patch, row * TILE:(row + 1) * TILE]

    def line(self, segment, row, line):
        return self.got_refs[segment.flipped][segment.patch, row * TILE + line:row * TILE + line + 1]

    def row(self, segment, row):
        return jnp.concatenate([self.line(segment, row, line) for line in range(TILE)], axis=1)

    def column(self, segment, column):
        return self.line(segment, ROWS, column)


class Saver:
    def __init__(self, ref):
        self.ref, self.count = ref, 0

    def put(self, value):
        self.ref[self.count, :value.shape[0]] = value
        self.count += 1

    def take(self, lines=TILE):
        self.count += 1
        return self.ref[self.count - 1, :lines]


class SavingLinks:
    def __init__(self, links, saver):
        self.links, self.saver = links, saver

    def saved(self, found):
        segment, there = found
        self.saver.put(jnp.full((TILE, LANES), there))
        self.saver.put(jnp.full((TILE, LANES), segment.patch).astype(jnp.float32))
        return found

    def north(self, segment):
        return self.saved(self.links.north(segment))

    def south(self, segment):
        return self.saved(self.links.south(segment))

    def west(self, segment):
        return self.saved(self.links.west(segment))

    def east(self, segment):
        return self.saved(self.links.east(segment))


class SavingPackets(Packets):
    def __init__(self, got_refs, saver):
        self.got_refs, self.saver = got_refs, saver

    def tile(self, segment, row):
        value = Packets.tile(self, segment, row)
        self.saver.put(value)
        return value

    def line(self, segment, row, line):
        value = Packets.line(self, segment, row, line)
        self.saver.put(value)
        return value


class SavedLinks:
    def __init__(self, saver):
        self.saver = saver

    def found(self, flipped):
        there = self.saver.take()[:1, :1]
        return Segment(self.saver.take(), flipped), there

    def north(self, segment):
        return self.found(1 - segment.flipped)

    south = north

    def west(self, segment):
        return self.found(segment.flipped)

    east = west


class SavedPackets(Packets):
    def __init__(self, saver):
        self.saver = saver

    def tile(self, segment, row):
        return self.saver.take()

    def line(self, segment, row, line):
        return self.saver.take(1)


def is_first(shape=(TILE, LANES)):
    return (iota(shape, 0) == 0) & (iota(shape, 1) == 0)


def is_last(shape=(TILE, LANES)):
    return (iota(shape, 0) == shape[0] - 1) & (iota(shape, 1) == shape[1] - 1)


def next_cells(tile, edge):
    lane = iota(tile.shape, 1)
    moved = rolled(tile, -1, 1)
    moved = jnp.where(lane == LANES - 1, rolled(moved, -1, 0), moved)
    return jnp.where(is_last(), edge, moved)


def last_cells(tile, edge):
    lane = iota(tile.shape, 1)
    moved = rolled(tile, 1, 1)
    moved = jnp.where(lane == 0, rolled(moved, 1, 0), moved)
    return jnp.where(is_first(), edge, moved)


def row_of(ref, place):
    return jnp.concatenate([ref[place, line:line + 1] for line in range(TILE)], axis=1)


def nested(flux, index):
    lane, line = index % LANES, index // LANES
    taken = jnp.zeros(index.shape, jnp.float32)
    for source in range(TILE):
        values = jnp.broadcast_to(flux[source:source + 1], index.shape)
        found = jnp.take_along_axis(values, lane, axis=1, mode="promise_in_bounds")
        taken = jnp.where(line == source, found, taken)
    return taken


def strips_kernel(*refs):
    links_ref, mine_ref, other_ref = refs[:3]
    out_ref = refs[-1]
    finer_ref = refs[3] if len(refs) == 5 else None
    patches = mine_ref.shape[0]
    count = 2 * patches
    packets = Packets((mine_ref, other_ref))
    links = links_ref[0]
    lower = [lax.axis_index("sub") == 1 ^ flipped for flipped in range(2)]
    every = [Segment(patch, flipped) for flipped in range(2) for patch in range(patches)]

    def matching(patch, way):
        link = jnp.broadcast_to(links[patch:patch + 1, way:way + 1], (TILE, LANES))
        return [link == other for other in range(patches)]

    norths, wests, easts = [[matching(patch, way) for patch in range(patches)] for way in (0, 2, 3)]

    def picked(matches, values):
        total = jnp.zeros((TILE, LANES), jnp.float32)
        for match, value in zip(matches, values):
            total = jnp.where(match, value, total)
        return total

    strips, inflows = [], []
    for segment in every:
        strip = packets.tile(segment, STRIP)
        if finer_ref is not None:
            place = segment.place(patches)
            gain, index = packets.tile(segment, GAIN) * below_finest(), packets.tile(segment, INDEX).astype(jnp.int32)
            inflow, later = [gain * nested(finer_ref[step * count + place], index) for step in range(2)]
            inflows.append((inflow, later))
            strip = strip + inflow
        strips.append(strip)
    masks = [wet(packets.tile(segment, STRIP_DEPTH)) for segment in every]
    flows = [packets.tile(segment, EDGE_FLOW) for segment in every]
    edges = [wet(packets.tile(segment, EDGE_DEPTH)) for segment in every]
    firsts = [rolled(rolled(strip, -1, 1), -1, 0) for strip in strips]
    last_masks = [rolled(rolled(mask, 1, 1), 1, 0) for mask in masks]
    last_rows = [
        last * (packets.column(segment, LAST_ROW) + courant * rolled(rolled(strip, 1, 1), 1, 0))
        for last, segment, strip in zip(last_masks, every, strips)]
    for place, segment in enumerate(every):
        flipped, patch = segment.flipped, segment.patch
        half = slice(flipped * patches, (flipped + 1) * patches)
        other = slice((1 - flipped) * patches, (2 - flipped) * patches)
        eta, mask, depth = strips[place], masks[place], packets.tile(segment, STRIP_DEPTH)
        edge = picked(easts[patch], firsts[half])
        if finer_ref is None:
            row = jnp.where(is_last(), -courant * mask * edge, 0.0)
        else:
            inflow, later = inflows[place]
            row = courant * mask * (inflow - next_cells(inflow, edge))
        edge = picked(wests[patch], last_rows[half]) - courant * picked(wests[patch], last_masks[half]) * eta
        flow = jnp.where(lower[flipped], flows[other][patch], picked(norths[patch], flows[other]))
        above = jnp.where(lower[flipped], edges[other][patch], picked(norths[patch], edges[other]))
        col = flow - courant * above * eta
        total = packets.tile(segment, STRIP_SUM)
        if finer_ref is None:
            total = total - courant * depth * (row - jnp.where(is_first(), edge, 0.0) - col)
        else:
            total = (total + mask * inflow + later
                     - courant * depth * (row - last_cells(row, edge) + courant * mask * inflow - col))
        out_ref[place] = eta
        out_ref[count + place] = total


def beside(links, packets, own, inflow=None):
    lane = iota((1, LANES), 1)
    first, last = lane == 0, lane == LANES - 1

    def field(segment, column):
        return packets.column(segment, column) if inflow is None else 0.0

    def strip(name, turned):
        return 0.0 if inflow is None else jnp.where(first, rolled(inflow[name], turned, 1), 0.0)

    def corner_col(segment, eta, line, turned):
        north, beyond = links.north(segment)
        mask = rolled(wet(packets.line(north, EDGE_DEPTH, line)), turned, 1)
        flow = rolled(packets.line(north, EDGE_FLOW, line), turned, 1) if inflow is None else 0.0
        return beyond * (flow - courant * mask * eta)

    west, there = links.west(own)
    eta = field(west, LAST_ETA) + strip("west", 1)
    next_eta = field(west, NEXT_ETA) + strip("west", 2)
    own_eta = field(own, FIRST_ETA) + strip("own", 0)
    depth = packets.column(west, LAST_DEPTH) * there
    mask = wet(depth)
    next_row = wet(packets.column(west, NEXT_DEPTH)) * (field(west, NEXT_ROW) - courant * (eta - next_eta))
    below, beyond = links.south(west)
    corner = packets.line(below, STRIP, TILE - 1) if inflow is None else inflow["south west"]
    south_eta = jnp.where(last, corner * beyond, rolled(eta, -1, 1))
    col = mask * (field(west, LAST_COL) - courant * (south_eta - eta))
    north_col = jnp.where(first, corner_col(west, eta, TILE - 1, 1), rolled(col, 1, 1))
    west_row = mask * (field(west, LAST_ROW) - courant * (own_eta - eta))
    west_eta = (mask * eta - courant * depth * (west_row - next_row + col - north_col) + strip("west later", 1))
    west_mask = mask

    east, there = links.east(own)
    eta = there * (field(east, FIRST_ETA) + strip("east", 0))
    second_eta = field(east, SECOND_ETA) + strip("east", -1)
    depth = packets.column(east, FIRST_DEPTH) * there
    mask = wet(depth)
    row = mask * (field(east, FIRST_ROW) - courant * (second_eta - eta))
    below, beyond = links.south(east)
    corner = packets.line(below, STRIP, 0) if inflow is None else inflow["south east"]
    south_eta = jnp.where(last, rolled(corner, -1, 1) * beyond, rolled(eta, -1, 1))
    col = mask * (field(east, FIRST_COL) - courant * (south_eta - eta))
    north_col = jnp.where(first, corner_col(east, eta, 0, 0), rolled(col, 1, 1))
    east_sum = mask * eta - courant * depth * (row + col - north_col) + there * strip("east later", 0)
    return west_row, west_mask, west_eta, eta, east_sum, courant * depth


def advanced(eta, row, col, mask, depth, east, south, west, north):
    row = mask * (row - courant * (east(eta) - eta))
    col = mask * (col - courant * (south(eta) - eta))
    return mask * eta - depth * (row - west(row) + col - north(col)), row, col


def two_steps(start, mask, depth, sides, base, north=None, south=None, second=None):
    lane, line = iota(mask.shape, 1), iota(mask.shape, 0)
    cols = mask.shape[1]
    west_row, west_mask, west_eta, east_eta, east_sum, east_depth = sides
    state = start, 0.0, 0.0
    flow, beyond = west_row, east_eta
    above = 0.0 if north is None else north[0]
    for number in range(2):
        below = 0.0 if south is None else south[number]
        state = advanced(
            *state, mask, depth,
            lambda eta: jnp.where(lane == cols - 1, beyond, rolled(eta, -1, 1)),
            lambda eta: jnp.where(line == TILE - 1, below, rolled(eta, -1, 0)),
            lambda row: jnp.where(lane == 0, flow, rolled(row, 1, 1)),
            lambda col: jnp.where(line == 0, above, rolled(col, 1, 0)))
        if number:
            return state
        eta, row, col = state
        if second is not None:
            eta = eta + jnp.where(line == 0, second, 0.0)
            state = eta, row, col
        whole_eta, whole_row = (eta, row) if base is None else (eta + base[0], row + base[1])
        flow = west_mask * (west_row - courant * (whole_eta[:, :1] - west_eta))
        beyond = east_sum + east_depth * whole_row[:, cols - 1:]
        if north is not None:
            above = north[1] * (north[0] - courant * (whole_eta[:1] - north[2]))


def north_of(links, packets, own, own_strip, inflow=None):
    cols = own_strip.shape[1]
    lane = iota((1, LANES), 1)
    north, there = links.north(own)
    depth = packets.row(north, EDGE_DEPTH) * there
    mask = wet(depth)
    if inflow is not None:
        col = -courant * mask * own_strip
        return col, mask, -courant * depth * col
    col = packets.row(north, EDGE_FLOW) * there - courant * mask * own_strip
    north_east, beyond = links.east(north)
    right_eta = beyond * packets.column(north_east, FIRST_ETA)
    north_west, beyond = links.west(north)
    left_row = beyond * wet(packets.column(north_west, LAST_DEPTH)) * (
        packets.column(north_west, LAST_ROW)
        - courant * (packets.column(north, FIRST_ETA) - packets.column(north_west, LAST_ETA)))
    nothing = jnp.zeros((1, cols - LANES), jnp.float32)
    corners = (jnp.concatenate([jnp.where(lane == 0, rolled(left_row, 1, 1), 0.0), nothing], axis=1)
               + jnp.concatenate([nothing, jnp.where(lane == LANES - 1, courant * right_eta, 0.0)], axis=1))
    return col, mask, packets.row(north, EDGE_SUM) + courant * depth * (corners - col)


def as_sublanes(columns):
    rows = columns[0].shape[1]
    count = -len(columns) % TILE
    turned = jnp.concatenate(list(columns) + [jnp.zeros((count, rows), jnp.float32)], axis=0).T
    return [[turned[low:low + TILE, place:place + 1] for place in range(len(columns))]
            for low in (0, rows - TILE)]


def halo_kernel(links_ref, mine_ref, other_ref, strips_ref, eta_after, momenta_after, wet_after, depth_after,
                eta_ends, row_ends, turned, eta_out, momenta_out, ends_out, saved_ref,
                sides_new, more_ref, rows_ref, sems):
    rows, cols = eta_after.shape
    fields = eta_after, momenta_after.at[0], momenta_after.at[1]
    outs = eta_out.at[0], momenta_out.at[0, 0], momenta_out.at[1, 0]
    inner, between = pl.ds(TILE, rows - 2 * TILE), pl.ds(LANES, cols - 2 * LANES)
    copies = copied(
        [(field.at[inner, between], out.at[inner, between]) for field, out in zip(fields, outs)], sems.at[0])
    links = Links(links_ref, mine_ref.shape[0])
    own = links.own()
    packets = Packets((mine_ref, other_ref))
    columns = beside(links, packets, own)
    west_row, west_mask, west_eta, east_eta, east_sum, east_depth = columns

    line, lane = iota((TILE, rows), 0), iota((TILE, rows), 1)
    nothing = jnp.zeros((TILE, rows), jnp.float32)

    def column_steps(mask, depth, east, west):
        state = nothing, nothing, nothing
        for number in range(2):
            state = advanced(
                *state, mask, depth,
                lambda eta: jnp.where(line == TILE - 1, east(number, state), rolled(eta, -1, 0)),
                lambda eta: jnp.where(lane == rows - 1, 0.0, rolled(eta, -1, 1)),
                lambda row: jnp.where(line == 0, west(number, state), rolled(row, 1, 0)),
                lambda col: jnp.where(lane == 0, 0.0, rolled(col, 1, 1)))
        return state

    def west_of(number, state):
        if number == 0:
            return west_row
        whole = state[0][:1] + turned[4, :1]
        return west_mask * (west_row - courant * (whole - west_eta))

    def east_of(number, state):
        if number == 0:
            return east_eta
        return east_sum + east_depth * (state[1][TILE - 1:] + turned[5, TILE - 1:])

    left = column_steps(turned[0], turned[1], lambda number, state: 0.0, west_of)
    last = column_steps(turned[2], turned[3], east_of, lambda number, state: 0.0)
    middle = jnp.zeros((LANES - 2 * TILE, rows), jnp.float32)
    body_rows = slice(TILE, rows - TILE)
    inside = iota((rows - 2 * TILE, LANES), 1)
    wides = slice(0, LANES), slice(cols - LANES, cols)
    for place, field in enumerate(fields):
        more_ref[place] = jnp.concatenate([left[place], middle, last[place]], axis=0).T
        more = more_ref[place, body_rows]
        sides_new[0, place] = field[body_rows, wides[0]] + jnp.where(inside < TILE, more, 0.0)
        sides_new[1, place] = field[body_rows, wides[1]] + jnp.where(inside >= LANES - TILE, more, 0.0)
    for side, wide in enumerate(wides):
        copies += copied(
            [(sides_new.at[side, place], out.at[inner, pl.ds(wide.start, LANES)]) for place, out in enumerate(outs)],
            sems.at[1 + side])

    top_sides, low_sides = as_sublanes(columns)
    nothing = jnp.zeros((TILE, cols), jnp.float32)
    end = slice(rows - TILE, rows)
    top = two_steps(
        nothing, wet_after[:TILE], depth_after[:TILE], top_sides, (eta_ends[0], row_ends[0]),
        north=north_of(links, packets, own, packets.row(own, STRIP)))
    below, there = links.south(own)
    low = two_steps(
        nothing, wet_after[end], depth_after[end], low_sides, (eta_ends[1], row_ends[1]),
        south=(packets.row(below, STRIP) * there,
               row_of(strips_ref, 2 * links.patches + below.place(links.patches)) * there))
    line, inside = iota((TILE, cols), 0), iota((TILE, LANES), 1)
    gap = jnp.zeros((TILE, cols - 2 * LANES), jnp.float32)
    for edge, (chunk, near, found) in enumerate(
            ((slice(0, TILE), line < TILE // 2, top), (end, line >= TILE // 2, low))):
        for place in range(3):
            more = more_ref[place, chunk]
            wide = jnp.concatenate(
                [jnp.where(inside < TILE, more, 0.0), gap, jnp.where(inside >= LANES - TILE, more, 0.0)], axis=1)
            ends_out[place, edge] = fields[place][chunk] + jnp.where(near, found[place], wide)
    saver = Saver(saved_ref)
    inflow_sides(SavingLinks(links, saver), SavingPackets((mine_ref, other_ref), saver), own,
                 lambda step, segment: jnp.zeros((TILE, LANES), jnp.float32), rows_ref)
    assert saver.count <= SAVED
    for copy in copies:
        copy.wait()


def inflow_sides(links, packets, own, flux_of, rows_ref):
    some = below_finest()

    def inflows(segment):
        gain, index = packets.tile(segment, GAIN) * some, packets.tile(segment, INDEX).astype(jnp.int32)
        return [gain * nested(flux_of(step, segment), index) for step in range(2)]

    below, there = links.south(own)
    west, east = links.west(own)[0], links.east(own)[0]
    below_west, beyond_west = links.west(below)
    below_east, beyond_east = links.east(below)
    wanted = (
        ("west", 0, west, TILE - 1), ("west later", 1, west, TILE - 1), ("east", 0, east, 0),
        ("east later", 1, east, 0), ("south west", 0, links.south(west)[0], TILE - 1),
        ("south east", 0, links.south(east)[0], 0), ("below west", 0, below_west, TILE - 1),
        ("below east", 0, below_east, 0))
    gain = jnp.concatenate([packets.line(segment, GAIN, line) for _, _, segment, line in wanted], axis=0)
    index = jnp.concatenate([packets.line(segment, INDEX, line) for _, _, segment, line in wanted], axis=0)
    index = index.astype(jnp.int32)
    lane, line = index % LANES, index // LANES
    fluxes = [flux_of(step, segment) for _, step, segment, _ in wanted]
    taken = jnp.zeros((TILE, LANES), jnp.float32)
    for source in range(TILE):
        values = jnp.concatenate([tile[source:source + 1] for tile in fluxes], axis=0)
        found = jnp.take_along_axis(values, lane, axis=1, mode="promise_in_bounds")
        taken = jnp.where(line == source, found, taken)
    taken = some * gain * taken
    inflow = {name: taken[place:place + 1] for place, (name, _, _, _) in enumerate(wanted)}

    rows_ref[0], rows_ref[1] = inflows(own)
    strip, later = inflows(below)
    strip, later = strip * there, later * there
    inflow["own"] = rows_ref[0, :1]

    depth = packets.tile(below, STRIP_DEPTH)
    mask = wet(depth)
    edge = jnp.broadcast_to(rolled(inflow["below east"] * beyond_east, -1, 1), (TILE, LANES))
    row = courant * mask * (strip - next_cells(strip, edge))
    west_mask = rolled(wet(packets.line(below_west, STRIP_DEPTH, TILE - 1)), 1, 1)
    edge = beyond_west * courant * west_mask * (rolled(inflow["below west"], 1, 1) - strip[:1])
    edge = jnp.broadcast_to(edge, (TILE, LANES))
    north, beyond = links.north(below)
    col = -courant * wet(packets.tile(north, EDGE_DEPTH)) * beyond * strip
    rows_ref[2] = strip
    rows_ref[3] = there * (
        mask * strip - courant * depth * (row - last_cells(row, edge) + courant * mask * strip - col) + later)

    columns = beside(links, packets, own, inflow)
    return columns, north_of(links, packets, own, row_of(rows_ref, 0), inflow)


def inflow_kernel(mine_ref, finer_ref, saved_ref, wet_after, depth_after, ends_ref, eta_hbm, momenta_hbm,
                  eta_out, momenta_out, rows_ref, new_ref, sems):
    del eta_hbm, momenta_hbm
    rows, cols = wet_after.shape
    patches = mine_ref.shape[0]
    saver = Saver(saved_ref)

    def flux_of(step, segment):
        first = (2 * step + segment.flipped) * patches
        if segment is own:
            return finer_ref[first + own.patch]
        flux = jnp.zeros((TILE, LANES), jnp.float32)
        for patch in range(patches):
            flux = jnp.where(segment.patch == patch, finer_ref[first + patch], flux)
        return flux

    own = Segment(lax.axis_index("patch"), 0)
    columns, north = inflow_sides(SavedLinks(saver), SavedPackets(saver), own, flux_of, rows_ref)
    top_sides, low_sides = as_sublanes(columns)
    line = iota((TILE, cols), 0)
    strip = row_of(rows_ref, 0)
    top = two_steps(
        jnp.where(line == 0, strip, 0.0), wet_after[:TILE], depth_after[:TILE], top_sides, None,
        north=north, second=row_of(rows_ref, 1))
    copies = []
    outs = eta_out.at[0], momenta_out.at[0, 0], momenta_out.at[1, 0]

    def write(end, near, found):
        for place in range(3):
            new_ref[place, end] = ends_ref[place, end] + jnp.where(near, found[place], 0.0)
        here = pl.ds(end * (rows - TILE), TILE)
        copies.extend(copied(
            [(new_ref.at[place, end], out.at[here, :]) for place, out in enumerate(outs)], sems.at[end]))

    write(0, line < TILE // 2, top)
    low = two_steps(
        jnp.zeros((TILE, cols), jnp.float32), wet_after[rows - TILE:], depth_after[rows - TILE:],
        low_sides, None, south=(row_of(rows_ref, 2), row_of(rows_ref, 3)))
    write(1, line >= TILE // 2, low)
    for copy in copies:
        copy.wait()


def body(adjoint_height, adjoint_momenta, depth, wet_mask, adjacency, nest_gain, nest_index):
    rows, cols = adjoint_height.shape[1:]
    levels = lax.axis_size("level")
    patches = lax.axis_size("patch")
    count = 2 * patches
    params = pltpu.CompilerParams(vmem_limit_bytes=VMEM_LIMIT)
    vmem = pl.BlockSpec(memory_space=pltpu.VMEM)
    smem = pl.BlockSpec(memory_space=pltpu.SMEM)
    hbm = pl.BlockSpec(memory_space=pltpu.HBM)

    def array(*shape):
        return jax.ShapeDtypeStruct(shape, jnp.float32)

    def scratch(*shape):
        return pltpu.VMEM(shape, jnp.float32)

    fields = [pltpu.with_memory_space_constraint(field, pltpu.HBM)
              for field in (adjoint_height, adjoint_momenta, depth, wet_mask, nest_gain, nest_index)]
    packed, trimmed = pl.pallas_call(
        pack_kernel,
        out_shape=[array(LINES, LANES), array(TRIMMED, LANES)],
        in_specs=[hbm] * 6,
        out_specs=[vmem, vmem],
        scratch_shapes=[
            scratch(2, 4, TILE, cols), pltpu.VMEM((2, TILE, cols), jnp.int32),
            scratch(2, 4, rows, LANES), pltpu.VMEM((2, rows, LANES), jnp.int32),
            scratch(levels, cols), pltpu.VMEM((levels, cols), jnp.int32),
            pltpu.SemaphoreType.DMA((18,)),
        ],
        compiler_params=params,
        name="pack",
    )(*fields)
    parts = 4
    after = pl.pallas_call(
        bulk_kernel,
        out_shape=[
            array(rows, cols), array(2, rows, cols), array(rows, cols), array(rows, cols),
            array(2, TILE, cols), array(2, TILE, cols), array(6, TILE, rows),
        ],
        in_specs=[hbm] * 4,
        out_specs=[vmem] * 7,
        scratch_shapes=[
            scratch(rows + 2 * TILE, cols), scratch(rows + 2 * TILE, cols),
            scratch(2, rows, cols), scratch(rows, cols), pltpu.VMEM((rows, cols), jnp.int32),
            scratch(rows, LANES), scratch(rows, LANES), pltpu.SemaphoreType.DMA((parts, 4)),
        ],
        compiler_params=params,
        name="bulk",
    )(*fields[:4])

    sent = [packed] + [
        lax.ppermute(trimmed if levels == 2 else packed, "patch",
                     [(source, source ^ turn) for source in range(patches)])
        for turn in send_order(patches)
    ]
    mine = pl.pallas_call(
        gather_kernel,
        out_shape=array(patches, LINES, LANES),
        in_specs=[vmem] * (patches + 1),
        out_specs=vmem,
        compiler_params=params,
        name="gather",
    )(*sent, after[-1])
    other = lax.ppermute(mine, "sub", [(0, 1), (1, 0)])

    flux = ()
    strips = []
    for turn in range(levels - 1):
        strips.append(pl.pallas_call(
            strips_kernel,
            out_shape=array(2 * count, TILE, LANES),
            in_specs=[vmem] * (3 + len(flux)),
            out_specs=vmem,
            compiler_params=params,
            name="strips",
        )(adjacency, mine, other, *flux))
        flux = (lax.ppermute(strips[-1], "level", [(source, (source - 1) % levels) for source in range(levels)]),)

    eta_new, momenta_new, ends, saved = pl.pallas_call(
        halo_kernel,
        out_shape=[
            array(*adjoint_height.shape), array(*adjoint_momenta.shape), array(3, 2, TILE, cols),
            array(SAVED, TILE, LANES),
        ],
        in_specs=[smem] + [vmem] * 10,
        out_specs=[hbm, hbm, vmem, vmem],
        scratch_shapes=[
            scratch(2, 3, rows - 2 * TILE, LANES), scratch(3, rows, LANES), scratch(4, TILE, LANES),
            pltpu.SemaphoreType.DMA((3, 3)),
        ],
        compiler_params=params,
        name="halo",
    )(adjacency, mine, other, strips[0], *after)

    return pl.pallas_call(
        inflow_kernel,
        out_shape=[array(*adjoint_height.shape), array(*adjoint_momenta.shape)],
        in_specs=[vmem] * 6 + [hbm] * 2,
        out_specs=[hbm, hbm],
        input_output_aliases={6: 0, 7: 1},
        scratch_shapes=[
            scratch(4, TILE, LANES), scratch(3, 2, TILE, cols), pltpu.SemaphoreType.DMA((2, 3)),
        ],
        compiler_params=params,
        name="inflow",
    )(mine, *flux, saved, after[2], after[3], ends, eta_new, momenta_new)


def solution(mesh):
    in_specs = (
        P(("parts", "level"), ("patch", "sub"), None),
        P(None, ("parts", "level"), ("patch", "sub"), None),
        P("level", ("patch", "sub"), None),
        P("level", ("patch", "sub"), None),
        P("level", None, None),
        P(None, ("patch", "sub")),
        P(None, ("patch", "sub")),
    )
    out_specs = (
        P(("parts", "level"), ("patch", "sub"), None),
        P(None, ("parts", "level"), ("patch", "sub"), None),
    )
    return jax.shard_map(body, mesh=mesh, in_specs=in_specs, out_specs=out_specs, check_vma=False)
```
